32 devices in a mesh: fsdp: 16 (over z, x, core), tensor: 2 (over y).
Axes of the slice: x: 2, y: 2, z: 4, core: 2. Of those that a mesh axis runs over, the one named last changes fastest.
Arguments:
- tokens: bfloat16 [2, 3072, 1536], P(None, 'fsdp'), may hold values from -6 to 6
- norm1_gain: bfloat16 [1536], P('fsdp'), may hold values from 0.5 to 1.5
- query_weight: bfloat16 [1536, 1536], P('fsdp', 'tensor'), may hold values from -0.15625 to 0.15625
- query_bias: bfloat16 [12, 128], P('tensor'), may hold values from -3 to 3
- key_weight: bfloat16 [1536, 256], P('fsdp', 'tensor'), may hold values from -0.15625 to 0.15625
- key_bias: bfloat16 [2, 128], P('tensor'), may hold values from -3 to 3
- value_weight: bfloat16 [1536, 256], P('fsdp', 'tensor'), may hold values from -0.15625 to 0.15625
- value_bias: bfloat16 [2, 128], P('tensor'), may hold values from -3 to 3
- output_weight: bfloat16 [1536, 1536], P('tensor', 'fsdp'), may hold values from -0.625 to 0.625
- norm2_gain: bfloat16 [1536], P('fsdp'), may hold values from 0.5 to 1.5
- gate_weight: bfloat16 [1536, 8960], P('fsdp', 'tensor'), may hold values from -0.15625 to 0.15625
- up_weight: bfloat16 [1536, 8960], P('fsdp', 'tensor'), may hold values from -0.15625 to 0.15625
- down_weight: bfloat16 [8960, 1536], P('tensor', 'fsdp'), may hold values from -0.0625 to 0.0625
- cotangent: bfloat16 [2, 3072, 1536], P(None, 'fsdp'), may hold values from -6 to 6
- segments: int32 [2, 3072], replicated, may hold values from 0 to 107, as said below
- positions: int32 [2, 3072], replicated, may hold values from 0 to 799, as said below
Outputs:
- output: bfloat16 [2, 3072, 1536], P(None, 'fsdp')
- input_grad: float32 [2, 3072, 1536], P(None, 'fsdp')
- norm1_gain_grad: float32 [1536], P('fsdp')
- query_weight_grad: float32 [1536, 1536], P('fsdp', 'tensor')
- query_bias_grad: float32 [12, 128], P('tensor')
- key_weight_grad: float32 [1536, 256], P('fsdp', 'tensor')
- key_bias_grad: float32 [2, 128], P('tensor')
- value_weight_grad: float32 [1536, 256], P('fsdp', 'tensor')
- value_bias_grad: float32 [2, 128], P('tensor')
- output_weight_grad: float32 [1536, 1536], P('tensor', 'fsdp')
- norm2_gain_grad: float32 [1536], P('fsdp')
- gate_weight_grad: float32 [1536, 8960], P('fsdp', 'tensor')
- up_weight_grad: float32 [1536, 8960], P('fsdp', 'tensor')
- down_weight_grad: float32 [8960, 1536], P('tensor', 'fsdp')
The draws below stay inside these ranges and needn't reach their ends.
Inputs may be any that keep to these rules, and one draw needn't show every extreme that they name: `segments`: along each micro-batch the numbers never fall; each number marks one document of consecutive tokens inside one sequence of 1024 tokens (sequences start at multiples of 1024); a document has at most 800 tokens, and some document has exactly 800; the documents of sequence j have numbers from j * (18) to (j + 1) * 18 - 1, the last document of each sequence the highest of these. `positions`: the position of each token within its document, counted from 0.
All inputs are finite; a program needn't handle non-finite values.
Results may differ from the reference program's by a relative error of at most 0.02.
Values may be sent and summed in bfloat16 or wider, within the bound.
A program may use at most 160 MiB of HBM per device.

```python
import math
import jax
import jax.numpy as jnp
from jax import lax

D = 1536
QH = 12
KVH = 2
HD = 128
FF = 8960
SEQ_LEN = 1024
WINDOW = 800
DOC_MIN = 60
MICRO = 2
STREAM = 3072


def documents(key):
    sequences = MICRO * STREAM // SEQ_LEN
    per_sequence = SEQ_LEN // DOC_MIN + 1
    lengths = jax.random.randint(key, (sequences, per_sequence), DOC_MIN, WINDOW + 1)
    chosen = jax.random.randint(jax.random.fold_in(key, 11), (), 0, sequences)
    first_doc = (jnp.arange(sequences)[:, None] == chosen) & (jnp.arange(per_sequence)[None, :] == 0)
    lengths = jnp.where(first_doc, WINDOW, lengths).astype(jnp.int32)
    starts = jnp.cumsum(lengths, axis=1) - lengths
    places = jnp.arange(SEQ_LEN, dtype=jnp.int32)
    doc_index = jnp.sum((starts[:, None, :] <= places[None, :, None]).astype(jnp.int32), axis=-1) - 1
    begins = jnp.take_along_axis(starts, doc_index, axis=1)
    offsets = places[None, :] - begins
    last_doc = doc_index[:, SEQ_LEN - 1:SEQ_LEN]
    doc_number = jnp.where(doc_index == last_doc, per_sequence - 1, doc_index)
    segment_ids = jnp.arange(sequences, dtype=jnp.int32)[:, None] * per_sequence + doc_number
    return (segment_ids.reshape(MICRO, STREAM).astype(jnp.int32), offsets.reshape(MICRO, STREAM).astype(jnp.int32))


def draw_segments(key, part):
    segment_ids, offsets = documents(key)
    return segment_ids


def draw_positions(key, part):
    segment_ids, offsets = documents(key)
    return offsets


def block_scale(key, shape, split, least, top_value):
    loudness, own = 1.0, jax.random.fold_in(key, 6)
    for position, shards_of in split:
        steps = jnp.exp(jax.random.uniform(jax.random.fold_in(own, position), (shards_of,), jnp.float32, least / len(split), top_value / len(split)))
        loudness = loudness * jnp.repeat(steps, shape[position] // shards_of).reshape([-1 if axis == position else 1 for axis in range(len(shape))])
    return loudness


def noise(stream_key, extent, deviation, limit, shards=(), kind=jnp.bfloat16):
    level = block_scale(stream_key, extent, shards, -0.22, 0.18) if shards else 1.0
    array = jax.random.normal(stream_key, extent, jnp.float32) * deviation * level
    return jnp.minimum(jnp.maximum(array, -limit), limit).astype(kind)


def setup_inputs(seed: int = 0) -> dict:
    arg_keys = jax.random.split(jax.random.key(seed), 17)
    return {
        "tokens": noise(arg_keys[0], (MICRO, STREAM, D), 1.0, 6.0, ((1, 16),)),
        "norm1_gain": jnp.clip(1.0 + 0.1 * jax.random.normal(arg_keys[1], (D,), jnp.float32), 0.5, 1.5).astype(jnp.bfloat16),
        "query_weight": noise(arg_keys[2], (D, QH * HD), D ** -0.5, 0.15625, ((0, 16), (1, 2))),
        "query_bias": noise(arg_keys[3], (QH, HD), 0.5, 3.0, ((0, 2),)),
        "key_weight": noise(arg_keys[4], (D, KVH * HD), D ** -0.5, 0.15625, ((0, 16), (1, 2))),
        "key_bias": noise(arg_keys[5], (KVH, HD), 0.5, 3.0, ((0, 2),)),
        "value_weight": noise(arg_keys[6], (D, KVH * HD), D ** -0.5, 0.15625, ((0, 16), (1, 2))),
        "value_bias": noise(arg_keys[7], (KVH, HD), 0.5, 3.0, ((0, 2),)),
        "output_weight": noise(arg_keys[8], (QH * HD, D), (QH * HD // 16) ** -0.5, 0.625, ((0, 2), (1, 16))),
        "norm2_gain": jnp.clip(1.0 + 0.1 * jax.random.normal(arg_keys[9], (D,), jnp.float32), 0.5, 1.5).astype(jnp.bfloat16),
        "gate_weight": noise(arg_keys[10], (D, FF), D ** -0.5, 0.15625, ((0, 16), (1, 2))),
        "up_weight": noise(arg_keys[11], (D, FF), D ** -0.5, 0.15625, ((0, 16), (1, 2))),
        "down_weight": noise(arg_keys[12], (FF, D), FF ** -0.5, 0.0625, ((0, 2), (1, 16))),
        "cotangent": noise(arg_keys[13], (MICRO, STREAM, D), 1.0, 6.0, ((1, 16),)),
        "segments": draw_segments(jax.random.fold_in(arg_keys[16], 71), 0),
        "positions": draw_positions(jax.random.fold_in(arg_keys[16], 71), 0),
    }


EPSILON = 1e-06
THETA = 1000000.0
NEGATIVE = -1e+30

@jax.custom_vjp
def low(v):
    return lax.optimization_barrier(v.astype(jnp.bfloat16)).astype(jnp.float32)

@jax.custom_vjp
def low_back(v):
    return v

def low_keep(v):
    return (low(v), None)

def low_pass(kept, grad):
    return (grad,)

def back_keep(v):
    return (v, None)

def back_low(kept, grad):
    return (low(grad),)
low.defvjp(low_keep, low_pass)
low_back.defvjp(back_keep, back_low)

def product(left_side, right_side):
    return jnp.dot(left_side, right_side, precision=lax.Precision.HIGHEST, preferred_element_type=jnp.float32)

def rms_norm(values, gain):
    scale_row = lax.rsqrt(lax.optimization_barrier(jnp.mean(values * values, axis=-1, keepdims=True)) + EPSILON)
    return values * scale_row * gain

def rotate(values, places):
    half_width = HD // 2
    frequency = THETA ** (-(jnp.arange(half_width, dtype=jnp.float32) * 2.0) / HD)
    angles = places.astype(jnp.float32)[:, None] * frequency[None, :]
    cosine = jnp.concatenate([jnp.cos(angles), jnp.cos(angles)], axis=-1)[:, None, :]
    sine_table = jnp.concatenate([jnp.sin(angles), jnp.sin(angles)], axis=-1)[:, None, :]
    turned = jnp.concatenate([-values[..., half_width:], values[..., :half_width]], axis=-1)
    return values * cosine + turned * sine_table

def attend(pieces):
    query_rows, key_rows, value_rows, seg_row, pos_row = pieces
    length = query_rows.shape[0]
    grouped = query_rows.reshape(length, KVH, QH // KVH, HD)
    scores = jnp.einsum('tkgd,skd->kgts', grouped, key_rows, precision=lax.Precision.HIGHEST) * (1.0 / math.sqrt(HD))
    scores = low_back(scores)
    allowed = (seg_row[:, None] == seg_row[None, :]) & (pos_row[None, :] <= pos_row[:, None])
    scores = jnp.where(allowed, scores, NEGATIVE)
    shifted = scores - lax.optimization_barrier(jnp.max(scores, axis=-1, keepdims=True))
    weights_exp = jnp.exp(shifted)
    probs = low(weights_exp / lax.optimization_barrier(jnp.sum(weights_exp, axis=-1, keepdims=True)))
    mixed_heads = jnp.einsum('kgts,skd->tkgd', probs, value_rows, precision=lax.Precision.HIGHEST)
    return mixed_heads.reshape(length, QH * HD)

def reference(tokens, norm1_gain, query_weight, query_bias, key_weight, key_bias, value_weight, value_bias, output_weight, norm2_gain, gate_weight, up_weight, down_weight, cotangent, segments, positions):
    rows_all = MICRO * STREAM
    seq_count = rows_all // SEQ_LEN
    per_group = 4 if seq_count % 4 == 0 else 2 if seq_count % 2 == 0 else 1
    group_rows = per_group * SEQ_LEN
    groups = rows_all // group_rows
    seg_blocks = segments.reshape(groups, per_group, SEQ_LEN)
    pos_blocks = positions.reshape(groups, per_group, SEQ_LEN)

    def forward(inputs, first_norm_gain, w_query, b_query, w_key, b_key, w_value, b_value, w_out, second_norm_gain, w_gate, w_up, w_down):

        def layer_group(pieces):
            group_in, seg_group, pos_group = pieces
            count_rows = group_in.shape[0]
            normed = low(rms_norm(group_in, first_norm_gain))
            query_raw = low_back(product(normed, w_query) + b_query.reshape(-1))
            key_raw = low_back(product(normed, w_key) + b_key.reshape(-1))
            value_raw = low_back(product(normed, w_value) + b_value.reshape(-1))
            places = pos_group.reshape(-1)
            query_rows = low(rotate(query_raw.reshape(count_rows, QH, HD), places))
            key_rows = low(rotate(key_raw.reshape(count_rows, KVH, HD), places))
            value_rows = low(value_raw.reshape(count_rows, KVH, HD))
            mixed_heads = lax.map(jax.checkpoint(attend), (query_rows.reshape(per_group, SEQ_LEN, QH, HD), key_rows.reshape(per_group, SEQ_LEN, KVH, HD), value_rows.reshape(per_group, SEQ_LEN, KVH, HD), seg_group, pos_group))
            heads_out = low(low_back(mixed_heads.reshape(count_rows, QH * HD)))
            residual_state = group_in + low_back(product(heads_out, w_out))
            second_normed_rows = low(rms_norm(residual_state, second_norm_gain))
            gate_value = low_back(product(second_normed_rows, w_gate))
            up_part = low_back(product(second_normed_rows, w_up))
            hidden = low(jax.nn.silu(gate_value) * up_part)
            return residual_state + low_back(product(hidden, w_down))
        blocks = lax.map(jax.checkpoint(layer_group), (inputs.reshape(groups, group_rows, D), seg_blocks, pos_blocks))
        return blocks.reshape(MICRO, STREAM, D)
    result, pull_back = jax.vjp(forward, tokens.astype(jnp.float32), norm1_gain.astype(jnp.float32), query_weight.astype(jnp.float32), query_bias.astype(jnp.float32), key_weight.astype(jnp.float32), key_bias.astype(jnp.float32), value_weight.astype(jnp.float32), value_bias.astype(jnp.float32), output_weight.astype(jnp.float32), norm2_gain.astype(jnp.float32), gate_weight.astype(jnp.float32), up_weight.astype(jnp.float32), down_weight.astype(jnp.float32))
    gradients = pull_back(cotangent.astype(jnp.float32))
    return (result.astype(jnp.bfloat16), gradients[0], gradients[1], gradients[2], gradients[3], gradients[4], gradients[5], gradients[6], gradients[7], gradients[8], gradients[9], gradients[10], gradients[11], gradients[12])
```

```python
import math

import jax
import jax.numpy as jnp
from jax import lax
from jax.sharding import Mesh
from jax.sharding import PartitionSpec as P

BACK = 5
LINE = 4
LANES = 128

EPSILON = 1e-06
THETA = 1000000.0
NEGATIVE = -1e30

RING, PAIR, CORE, TENSOR = "ring", "pair", "core", "tensor"
FSDP = (RING, PAIR, CORE)
SWAP = [(0, 1), (1, 0)]


def low(value):
    return value.astype(jnp.bfloat16)


def wide(value):
    return value.astype(jnp.float32)


def matmul(left_side, right_side):
    return jnp.dot(left_side, right_side, preferred_element_type=jnp.float32)


def contract_rows(left_side, right_side):
    return lax.dot_general(
        left_side, right_side, (((0,), (0,)), ((), ())), preferred_element_type=jnp.float32
    )


def times_transpose(left_side, right_side):
    return lax.dot_general(
        left_side, right_side, (((1,), (1,)), ((), ())), preferred_element_type=jnp.float32
    )


def swapped(value, axis):
    return lax.ppermute(value, axis, SWAP)


def in_order(own, other, place, axis):
    first = jnp.where(place == 0, own, other)
    second = jnp.where(place == 0, other, own)
    return jnp.stack([first, second], axis=axis)


def shifted(value, steps):
    count = lax.axis_size(FSDP)
    first, last = (max(0, -steps), min(count, count - steps))
    return lax.ppermute(value, FSDP, [(source, source + steps) for source in range(first, last)])


def summed_over_fsdp(value):
    count = lax.axis_size(FSDP)
    bit = 1
    while bit < count:
        value = value + lax.ppermute(value, FSDP, [(i, i ^ bit) for i in range(count)])
        bit *= 2
    return value


def line_gather(block):
    count, here = lax.axis_size(RING), lax.axis_index(RING)
    if count > LINE:
        return lax.all_gather(block, RING, axis=0)
    right, left = [block], [block]
    for step in range(1, count):
        right.append(
            lax.ppermute(right[-1], RING, [(i, i + 1) for i in range(step - 1, count - 1)])
        )
        left.append(
            lax.ppermute(left[-1], RING, [(i, i - 1) for i in range(1, count - step + 1)])
        )
    result = jnp.zeros((count,) + block.shape, block.dtype)
    for step in range(count):
        piece = block if step == 0 else jnp.where(here >= step, right[step], left[count - step])
        result = lax.dynamic_update_slice_in_dim(
            result, piece[None], (here - step + count) % count, axis=0
        )
    return result


def line_scatter(parts):
    count, here = lax.axis_size(RING), lax.axis_index(RING)
    if count > LINE:
        return wide(lax.psum_scatter(parts, RING, scatter_dimension=0, tiled=False))

    def part(place):
        return lax.dynamic_index_in_dim(parts, place, axis=0, keepdims=False)

    right, left = None, None
    for step in range(1, count):
        to_right, to_left = part(here + count - step), part(here - count + step)
        if step > 1:
            to_right = low(wide(to_right) + wide(right))
            to_left = low(wide(to_left) + wide(left))
        right = lax.ppermute(to_right, RING, [(i, i + 1) for i in range(step)])
        left = lax.ppermute(to_left, RING, [(i, i - 1) for i in range(count - step, count)])
    return wide(part(here)) + wide(right) + wide(left)


def gather_rows(shard):
    rows = line_gather(shard)
    rows = in_order(rows, swapped(rows, PAIR), lax.axis_index(PAIR), 1)
    rows = in_order(rows, swapped(rows, CORE), lax.axis_index(CORE), 2)
    return rows.reshape((-1,) + shard.shape[1:])


def scatter_rows(total):
    pair, core = lax.axis_index(PAIR), lax.axis_index(CORE)
    parts = low(total).reshape((lax.axis_size(RING), 2, 2, -1) + total.shape[1:])

    def halved(value, axis, place, name):
        mine = lax.dynamic_index_in_dim(value, place, axis=axis, keepdims=False)
        sent = lax.dynamic_index_in_dim(value, 1 - place, axis=axis, keepdims=False)
        return low(wide(mine) + wide(swapped(sent, name)))

    parts = halved(parts, 2, core, CORE)
    parts = halved(parts, 1, pair, PAIR)
    return line_scatter(parts)


def quarter_columns(shard):
    pair, core = lax.axis_index(PAIR), lax.axis_index(CORE)
    half = shard.shape[1] // 2

    def halved(value, place, width):
        mine = lax.dynamic_slice_in_dim(value, place * width, width, axis=value.ndim - 1)
        sent = lax.dynamic_slice_in_dim(value, (1 - place) * width, width, axis=value.ndim - 1)
        return mine, sent

    mine, sent = halved(shard, pair, half)
    rows = in_order(mine, swapped(sent, PAIR), pair, 0)
    mine, sent = halved(rows, core, half // 2)
    rows = in_order(mine, swapped(sent, CORE), core, 1)
    rows = line_gather(rows.reshape(-1, half // 2))
    return rows.reshape(-1, half // 2)


def quarter_to_owner(grad):
    pair, core = lax.axis_index(PAIR), lax.axis_index(CORE)
    width = grad.shape[1]
    block = low(line_scatter(grad.reshape(lax.axis_size(RING), -1, width)))
    block = block.reshape(2, 2, -1, width)

    def halved(value, axis, place):
        mine = lax.dynamic_index_in_dim(value, place, axis=axis, keepdims=False)
        sent = lax.dynamic_index_in_dim(value, 1 - place, axis=axis, keepdims=False)
        return mine, sent

    mine, sent = halved(block, 0, pair)
    block = in_order(mine, swapped(sent, PAIR), pair, 0)
    mine, sent = halved(block, 1, core)
    block = in_order(mine, swapped(sent, CORE), core, 1)
    return jnp.concatenate([wide(block[i, j]) for i in range(2) for j in range(2)], axis=1)


def four_blocks(value):
    over = swapped(value, PAIR)
    return jnp.concatenate([value, over, swapped(value, CORE), swapped(over, CORE)], axis=0)


def four_sums(total):
    half = total.shape[0] // 2
    total = total[:half] + wide(swapped(low(total[half:]), CORE))
    total = total[: half // 2] + wide(swapped(low(total[half // 2 :]), PAIR))
    return tensor_total(total)


def tensor_total(partial_sum):
    own = lax.reduce_precision(partial_sum, 8, 7)
    return own + wide(swapped(low(own), TENSOR))


def rotation(places, width):
    half_width = width // 2
    frequency = THETA ** (-(jnp.arange(half_width, dtype=jnp.float32) * 2.0) / width)
    angles = places.astype(jnp.float32)[:, None] * frequency[None, :]
    cosine = jnp.concatenate([jnp.cos(angles), jnp.cos(angles)], axis=-1)[:, None, :]
    sine_table = jnp.concatenate([jnp.sin(angles), jnp.sin(angles)], axis=-1)[:, None, :]
    return (cosine, sine_table)


def rotate(values, cosine, sine_table):
    half_width = values.shape[-1] // 2
    turned = jnp.concatenate([-values[..., half_width:], values[..., :half_width]], axis=-1)
    return values * cosine + turned * sine_table


def rotate_back(gradient, cosine, sine_table):
    half_width = gradient.shape[-1] // 2
    moved_part = gradient * sine_table
    return gradient * cosine + jnp.concatenate(
        [moved_part[..., half_width:], -moved_part[..., :half_width]], axis=-1
    )


def root_mean_square_parts(values):
    scale_row = lax.rsqrt(jnp.mean(values * values, axis=-1, keepdims=True) + EPSILON)
    return (values * scale_row, scale_row)


def norm_back(grad_normed, normalized, scale_row, gain):
    scaled = grad_normed * gain
    return scale_row * (scaled - normalized * jnp.mean(scaled * normalized, axis=-1, keepdims=True))


def visible(seg_row, pos_row, row_start, count_rows):
    pad_rows = BACK * count_rows
    seg_padded = jnp.concatenate([jnp.full((pad_rows,), -1, jnp.int32), seg_row])
    pos_padded = jnp.concatenate([jnp.zeros((pad_rows,), jnp.int32), pos_row])
    key_seg = lax.dynamic_slice_in_dim(seg_padded, row_start, pad_rows + count_rows)
    key_pos = lax.dynamic_slice_in_dim(pos_padded, row_start, pad_rows + count_rows)
    query_seg = lax.dynamic_slice_in_dim(seg_row, row_start, count_rows)
    query_pos = lax.dynamic_slice_in_dim(pos_row, row_start, count_rows)
    return (query_seg[:, None] == key_seg[None, :]) & (key_pos[None, :] <= query_pos[:, None])


def attend(query_rows, key_rows, value_rows, allowed):
    scores = jnp.einsum("thd,sd->hts", query_rows, key_rows, preferred_element_type=jnp.float32)
    scores = scores * (1.0 / math.sqrt(query_rows.shape[-1]))
    scores = jnp.where(allowed, scores, NEGATIVE)
    row_max = jnp.max(scores, axis=-1, keepdims=True)
    log_total = row_max + jnp.log(jnp.sum(jnp.exp(scores - row_max), axis=-1, keepdims=True))
    probs_low = low(jnp.exp(scores - log_total))
    mixed = jnp.einsum("hts,sd->thd", probs_low, value_rows, preferred_element_type=jnp.float32)
    return low(mixed.reshape(query_rows.shape[0], -1)), log_total


def attend_back(grad_heads, query_rows, key_rows, value_rows, allowed, log_total):
    scale = 1.0 / math.sqrt(query_rows.shape[-1])
    scores = jnp.einsum("thd,sd->hts", query_rows, key_rows, preferred_element_type=jnp.float32)
    probs = jnp.exp(jnp.where(allowed, scores * scale, NEGATIVE) - log_total)
    grad_probs = jnp.einsum(
        "thd,sd->hts", grad_heads, value_rows, preferred_element_type=jnp.float32
    )
    row_inner = jnp.sum(probs * grad_probs, axis=-1, keepdims=True)
    grad_scores = low(probs * (grad_probs - row_inner))
    grad_query = jnp.einsum(
        "hts,sd->thd", grad_scores, key_rows, preferred_element_type=jnp.float32
    )
    grad_keys = jnp.einsum(
        "hts,thd->sd", grad_scores, query_rows, preferred_element_type=jnp.float32
    )
    grad_values = jnp.einsum(
        "hts,thd->sd", low(probs), grad_heads, preferred_element_type=jnp.float32
    )
    return grad_query * scale, grad_keys * scale, grad_values


def body(
    tokens,
    norm1_gain,
    query_weight,
    query_bias,
    key_weight,
    key_bias,
    value_weight,
    value_bias,
    output_weight,
    norm2_gain,
    gate_weight,
    up_weight,
    down_weight,
    cotangent,
    segments,
    positions,
):
    batches, count_rows, width = tokens.shape
    heads, head_size = query_bias.shape
    query_width = heads * head_size
    units = gate_weight.shape[1]
    place = lax.axis_index(FSDP)
    row_start = place * count_rows
    rows = batches * count_rows

    gains = jnp.stack([norm1_gain, norm2_gain], axis=1)
    gains = jnp.pad(gains, ((0, 0), (0, LANES - 2)))
    first_shard = jnp.concatenate([query_weight, key_weight, value_weight, gains], axis=1)
    first_all = gather_rows(first_shard)
    kv_width = query_width + 2 * head_size
    w_qkv = first_all[:, :kv_width]
    first_gain = wide(first_all[:, kv_width])
    second_gain = wide(first_all[:, kv_width + 1])
    w_out = gather_rows(output_weight.T)

    padded = -(-units // (4 * LANES)) * (4 * LANES)

    def quarter(shard):
        return quarter_columns(jnp.pad(shard, ((0, 0), (0, padded - units))))

    w_gate = quarter(gate_weight)
    w_up = quarter(up_weight)
    w_down = quarter(down_weight.T)
    grad_out = cotangent.reshape(rows, width)
    grad_out_four = four_blocks(grad_out)

    inputs = wide(tokens.reshape(rows, width))
    first_unit, first_scale = root_mean_square_parts(inputs)
    first_normed = low(first_unit * first_gain)
    biases = jnp.concatenate(
        [query_bias.reshape(-1), key_bias.reshape(-1), value_bias.reshape(-1)]
    )
    raw = matmul(first_normed, w_qkv) + wide(biases)
    own_places = lax.dynamic_slice_in_dim(positions, row_start, count_rows, axis=1)
    cosine, sine_table = rotation(own_places.reshape(-1), head_size)
    turned = rotate(
        raw[:, : query_width + head_size].reshape(rows, heads + 1, head_size), cosine, sine_table
    )
    turned = low(turned)
    query_rows = turned[:, :heads].reshape(batches, count_rows, heads, head_size)
    key_value = jnp.concatenate([turned[:, heads], low(raw[:, query_width + head_size :])], axis=1)
    key_value = key_value.reshape(batches, count_rows, 2 * head_size)
    window = jnp.concatenate(
        [shifted(key_value, back) for back in range(BACK, 0, -1)] + [key_value], axis=1
    )
    key_rows, value_rows = window[..., :head_size], window[..., head_size:]
    allowed = [
        visible(segments[b], positions[b], row_start, count_rows) for b in range(batches)
    ]
    attended = [
        attend(query_rows[b], key_rows[b], value_rows[b], allowed[b]) for b in range(batches)
    ]
    heads_out = jnp.concatenate([mixed for mixed, _ in attended], axis=0)
    residual = inputs + tensor_total(times_transpose(heads_out, w_out))

    second_unit, second_scale = root_mean_square_parts(residual)
    second_normed = four_blocks(low(second_unit * second_gain))
    gate_value = matmul(second_normed, w_gate)
    up_part = matmul(second_normed, w_up)
    sigmoid_gate = jax.nn.sigmoid(gate_value)
    silu_gate = gate_value * sigmoid_gate
    hidden = low(silu_gate * up_part)
    grad_hidden = matmul(grad_out_four, w_down)
    grad_gate = low(
        grad_hidden * up_part * sigmoid_gate * (1.0 + gate_value * (1.0 - sigmoid_gate))
    )
    grad_up = low(grad_hidden * silu_gate)
    second_back = four_sums(times_transpose(grad_gate, w_gate) + times_transpose(grad_up, w_up))
    grad_w_down = quarter_to_owner(low(contract_rows(grad_out_four, hidden)))
    grad_w_gate = quarter_to_owner(low(contract_rows(second_normed, grad_gate)))
    grad_w_up = quarter_to_owner(low(contract_rows(second_normed, grad_up)))
    output = low(residual + four_sums(times_transpose(hidden, w_down)))

    second_gain_sum = jnp.sum(second_back * second_unit, axis=0)
    grad_state = wide(grad_out) + norm_back(second_back, second_unit, second_scale, second_gain)
    grad_branch = low(grad_state)
    grad_w_out = scatter_rows(contract_rows(grad_branch, heads_out))
    grad_heads = low(matmul(grad_branch, w_out)).reshape(query_rows.shape)
    backs = [
        attend_back(
            grad_heads[b], query_rows[b], key_rows[b], value_rows[b], allowed[b], attended[b][1]
        )
        for b in range(batches)
    ]
    grad_query = jnp.stack([back[0] for back in backs]).reshape(rows, heads, head_size)
    grad_window = jnp.stack([jnp.concatenate([back[1], back[2]], axis=1) for back in backs])
    own_grad = grad_window[:, BACK * count_rows :]
    for back in range(1, BACK + 1):
        first_row = (BACK - back) * count_rows
        own_grad = own_grad + wide(
            shifted(low(grad_window[:, first_row : first_row + count_rows]), -back)
        )
    own_grad = own_grad.reshape(rows, 2, head_size)
    turned_back = rotate_back(
        jnp.concatenate([grad_query, own_grad[:, :1]], axis=1), cosine, sine_table
    )
    grad_raw = low(jnp.concatenate([turned_back, own_grad[:, 1:]], axis=1).reshape(rows, -1))
    grad_w_qkv = scatter_rows(contract_rows(first_normed, grad_raw))
    bias_sum = jnp.sum(wide(grad_raw), axis=0)
    first_back_part = times_transpose(grad_raw, w_qkv)
    first_back = tensor_total(first_back_part)
    first_gain_sum = jnp.sum(first_back * first_unit, axis=0)
    input_grad = grad_state + norm_back(first_back, first_unit, first_scale, first_gain)
    sums = summed_over_fsdp(jnp.concatenate([bias_sum, second_gain_sum, first_gain_sum]))
    bias_total = sums[:kv_width]
    gain_rows = norm1_gain.shape[0]
    second_total = lax.dynamic_slice_in_dim(sums, kv_width + place * gain_rows, gain_rows)
    first_total = lax.dynamic_slice_in_dim(sums, kv_width + width + place * gain_rows, gain_rows)

    return (
        output.reshape(tokens.shape),
        input_grad.reshape(tokens.shape),
        first_total,
        grad_w_qkv[:, :query_width],
        bias_total[:query_width].reshape(query_bias.shape),
        grad_w_qkv[:, query_width : query_width + head_size],
        bias_total[query_width : query_width + head_size].reshape(key_bias.shape),
        grad_w_qkv[:, query_width + head_size :],
        bias_total[query_width + head_size :].reshape(value_bias.shape),
        grad_w_out.T,
        second_total,
        grad_w_gate[:, :units],
        grad_w_up[:, :units],
        grad_w_down[:, :units].T,
    )


def solution(mesh):
    fsdp, tensor = mesh.shape["fsdp"], mesh.shape["tensor"]
    fine = Mesh(mesh.devices.reshape(fsdp // 4, 2, 2, tensor), (RING, PAIR, CORE, TENSOR))
    by_rows, by_columns, by_tensor = P(FSDP, TENSOR), P(TENSOR, FSDP), P(TENSOR, None)
    by_tokens, by_gain = P(None, FSDP, None), P(FSDP)
    placed = (
        by_tokens,
        by_gain,
        by_rows,
        by_tensor,
        by_rows,
        by_tensor,
        by_rows,
        by_tensor,
        by_columns,
        by_gain,
        by_rows,
        by_rows,
        by_columns,
        by_tokens,
        P(),
        P(),
    )
    return jax.shard_map(
        body,
        mesh=fine,
        in_specs=placed,
        out_specs=(
            by_tokens,
            by_tokens,
            by_gain,
            by_rows,
            by_tensor,
            by_rows,
            by_tensor,
            by_rows,
            by_tensor,
            by_columns,
            by_gain,
            by_rows,
            by_rows,
            by_columns,
        ),
        check_vma=False,
    )
```

```python
import functools
import math

import jax
import jax.numpy as jnp
from jax import lax
from jax.experimental import pallas as pl
from jax.experimental.pallas import tpu as pltpu
from jax.sharding import Mesh
from jax.sharding import PartitionSpec as P

BACK = 5
LINE = 4
LANES = 128
VMEM_BYTES = 56 * 1024 * 1024

EPSILON = 1e-06
THETA = 1000000.0
NEGATIVE = -1e30

RING, PAIR, CORE, TENSOR = "ring", "pair", "core", "tensor"
FSDP = (RING, PAIR, CORE)
SWAP = [(0, 1), (1, 0)]


def low(value):
    return value.astype(jnp.bfloat16)


def wide(value):
    return value.astype(jnp.float32)


def matmul(left_side, right_side):
    return jnp.dot(left_side, right_side, preferred_element_type=jnp.float32)


def contract_rows(left_side, right_side):
    return lax.dot_general(
        left_side, right_side, (((0,), (0,)), ((), ())), preferred_element_type=jnp.float32
    )


def times_transpose(left_side, right_side):
    return lax.dot_general(
        left_side, right_side, (((1,), (1,)), ((), ())), preferred_element_type=jnp.float32
    )


def swapped(value, axis):
    return lax.ppermute(value, axis, SWAP)


def in_order(own, other, place, axis):
    first = jnp.where(place == 0, own, other)
    second = jnp.where(place == 0, other, own)
    return jnp.stack([first, second], axis=axis)


def shifted(value, steps):
    count = lax.axis_size(FSDP)
    first, last = (max(0, -steps), min(count, count - steps))
    return lax.ppermute(value, FSDP, [(source, source + steps) for source in range(first, last)])


def summed_over_fsdp(value):
    count = lax.axis_size(FSDP)
    bit = 1
    while bit < count:
        value = value + lax.ppermute(value, FSDP, [(i, i ^ bit) for i in range(count)])
        bit *= 2
    return value


def line_gather(block):
    count, here = lax.axis_size(RING), lax.axis_index(RING)
    if count > LINE:
        return lax.all_gather(block, RING, axis=0)
    right, left = [block], [block]
    for step in range(1, count):
        right.append(
            lax.ppermute(right[-1], RING, [(i, i + 1) for i in range(step - 1, count - 1)])
        )
        left.append(
            lax.ppermute(left[-1], RING, [(i, i - 1) for i in range(1, count - step + 1)])
        )
    result = jnp.zeros((count,) + block.shape, block.dtype)
    for step in range(count):
        piece = block if step == 0 else jnp.where(here >= step, right[step], left[count - step])
        result = lax.dynamic_update_slice_in_dim(
            result, piece[None], (here - step + count) % count, axis=0
        )
    return result


def line_scatter(parts):
    count, here = lax.axis_size(RING), lax.axis_index(RING)
    if count > LINE:
        return wide(lax.psum_scatter(parts, RING, scatter_dimension=0, tiled=False))

    def part(place):
        return lax.dynamic_index_in_dim(parts, place, axis=0, keepdims=False)

    right, left = None, None
    for step in range(1, count):
        to_right, to_left = part(here + count - step), part(here - count + step)
        if step > 1:
            to_right = low(wide(to_right) + wide(right))
            to_left = low(wide(to_left) + wide(left))
        right = lax.ppermute(to_right, RING, [(i, i + 1) for i in range(step)])
        left = lax.ppermute(to_left, RING, [(i, i - 1) for i in range(count - step, count)])
    return wide(part(here)) + wide(right) + wide(left)


def gather_rows(shard):
    rows = line_gather(shard)
    rows = in_order(rows, swapped(rows, PAIR), lax.axis_index(PAIR), 1)
    rows = in_order(rows, swapped(rows, CORE), lax.axis_index(CORE), 2)
    return rows.reshape((-1,) + shard.shape[1:])


def scatter_rows(total):
    pair, core = lax.axis_index(PAIR), lax.axis_index(CORE)
    parts = low(total).reshape((lax.axis_size(RING), 2, 2, -1) + total.shape[1:])

    def halved(value, axis, place, name):
        mine = lax.dynamic_index_in_dim(value, place, axis=axis, keepdims=False)
        sent = lax.dynamic_index_in_dim(value, 1 - place, axis=axis, keepdims=False)
        return low(wide(mine) + wide(swapped(sent, name)))

    parts = halved(parts, 2, core, CORE)
    parts = halved(parts, 1, pair, PAIR)
    return line_scatter(parts)


def quarter_columns(shard):
    pair, core = lax.axis_index(PAIR), lax.axis_index(CORE)
    half = shard.shape[1] // 2

    def halved(value, place, width):
        mine = lax.dynamic_slice_in_dim(value, place * width, width, axis=value.ndim - 1)
        sent = lax.dynamic_slice_in_dim(value, (1 - place) * width, width, axis=value.ndim - 1)
        return mine, sent

    mine, sent = halved(shard, pair, half)
    rows = in_order(mine, swapped(sent, PAIR), pair, 0)
    mine, sent = halved(rows, core, half // 2)
    rows = in_order(mine, swapped(sent, CORE), core, 1)
    rows = line_gather(rows.reshape(-1, half // 2))
    return rows.reshape(-1, half // 2)


def quarter_to_owner(grad):
    pair, core = lax.axis_index(PAIR), lax.axis_index(CORE)
    width = grad.shape[1]
    block = lax.psum_scatter(
        grad.reshape(lax.axis_size(RING), -1, width), RING, scatter_dimension=0, tiled=False
    )
    block = block.reshape(2, 2, -1, width)

    def halved(value, axis, place):
        mine = lax.dynamic_index_in_dim(value, place, axis=axis, keepdims=False)
        sent = lax.dynamic_index_in_dim(value, 1 - place, axis=axis, keepdims=False)
        return mine, sent

    mine, sent = halved(block, 0, pair)
    block = in_order(mine, swapped(sent, PAIR), pair, 0)
    mine, sent = halved(block, 1, core)
    block = in_order(mine, swapped(sent, CORE), core, 1)
    return jnp.concatenate([wide(block[i, j]) for i in range(2) for j in range(2)], axis=1)


def four_blocks(value):
    over = swapped(value, PAIR)
    return jnp.concatenate([value, over, swapped(value, CORE), swapped(over, CORE)], axis=0)


def four_sums(total):
    half = total.shape[0] // 2
    total = total[:half] + wide(swapped(low(total[half:]), CORE))
    total = total[: half // 2] + wide(swapped(low(total[half // 2 :]), PAIR))
    return tensor_total(total)


def tensor_total(partial_sum):
    own = lax.reduce_precision(partial_sum, 8, 7)
    return own + wide(swapped(low(own), TENSOR))


def rotation(places, width):
    half_width = width // 2
    frequency = THETA ** (-(jnp.arange(half_width, dtype=jnp.float32) * 2.0) / width)
    angles = places.astype(jnp.float32)[:, None] * frequency[None, :]
    cosine = jnp.concatenate([jnp.cos(angles), jnp.cos(angles)], axis=-1)[:, None, :]
    sine_table = jnp.concatenate([jnp.sin(angles), jnp.sin(angles)], axis=-1)[:, None, :]
    return (cosine, sine_table)


def rotate(values, cosine, sine_table):
    half_width = values.shape[-1] // 2
    turned = jnp.concatenate([-values[..., half_width:], values[..., :half_width]], axis=-1)
    return values * cosine + turned * sine_table


def rotate_back(gradient, cosine, sine_table):
    half_width = gradient.shape[-1] // 2
    moved_part = gradient * sine_table
    return gradient * cosine + jnp.concatenate(
        [moved_part[..., half_width:], -moved_part[..., :half_width]], axis=-1
    )


def root_mean_square_parts(values):
    scale_row = lax.rsqrt(jnp.mean(values * values, axis=-1, keepdims=True) + EPSILON)
    return (values * scale_row, scale_row)


def norm_back(grad_normed, normalized, scale_row, gain):
    scaled = grad_normed * gain
    return scale_row * (scaled - normalized * jnp.mean(scaled * normalized, axis=-1, keepdims=True))


def visible(seg_row, pos_row, row_start, count_rows):
    pad_rows = BACK * count_rows
    seg_padded = jnp.concatenate([jnp.full((pad_rows,), -1, jnp.int32), seg_row])
    pos_padded = jnp.concatenate([jnp.zeros((pad_rows,), jnp.int32), pos_row])
    key_seg = lax.dynamic_slice_in_dim(seg_padded, row_start, pad_rows + count_rows)
    key_pos = lax.dynamic_slice_in_dim(pos_padded, row_start, pad_rows + count_rows)
    query_seg = lax.dynamic_slice_in_dim(seg_row, row_start, count_rows)
    query_pos = lax.dynamic_slice_in_dim(pos_row, row_start, count_rows)
    return (query_seg[:, None] == key_seg[None, :]) & (key_pos[None, :] <= query_pos[:, None])


def attend(query_rows, key_rows, value_rows, allowed):
    scores = jnp.einsum("thd,sd->hts", query_rows, key_rows, preferred_element_type=jnp.float32)
    scores = scores * (1.0 / math.sqrt(query_rows.shape[-1]))
    scores = jnp.where(allowed, scores, NEGATIVE)
    row_max = jnp.max(scores, axis=-1, keepdims=True)
    log_total = row_max + jnp.log(jnp.sum(jnp.exp(scores - row_max), axis=-1, keepdims=True))
    probs_low = low(jnp.exp(scores - log_total))
    mixed = jnp.einsum("hts,sd->thd", probs_low, value_rows, preferred_element_type=jnp.float32)
    return low(mixed.reshape(query_rows.shape[0], -1)), log_total


def log_total_of(query_rows, key_rows, allowed):
    scores = jnp.einsum("thd,sd->hts", query_rows, key_rows, preferred_element_type=jnp.float32)
    scores = scores * (1.0 / math.sqrt(query_rows.shape[-1]))
    scores = jnp.where(allowed, scores, NEGATIVE)
    row_max = jnp.max(scores, axis=-1, keepdims=True)
    return row_max + jnp.log(jnp.sum(jnp.exp(scores - row_max), axis=-1, keepdims=True))


def attend_back(grad_heads, query_rows, key_rows, value_rows, allowed, log_total):
    scale = 1.0 / math.sqrt(query_rows.shape[-1])
    scores = jnp.einsum("thd,sd->hts", query_rows, key_rows, preferred_element_type=jnp.float32)
    probs = jnp.exp(jnp.where(allowed, scores * scale, NEGATIVE) - log_total)
    grad_probs = jnp.einsum(
        "thd,sd->hts", grad_heads, value_rows, preferred_element_type=jnp.float32
    )
    row_inner = jnp.sum(probs * grad_probs, axis=-1, keepdims=True)
    grad_scores = low(probs * (grad_probs - row_inner))
    grad_query = jnp.einsum(
        "hts,sd->thd", grad_scores, key_rows, preferred_element_type=jnp.float32
    )
    grad_keys = jnp.einsum(
        "hts,thd->sd", grad_scores, query_rows, preferred_element_type=jnp.float32
    )
    grad_values = jnp.einsum(
        "hts,thd->sd", low(probs), grad_heads, preferred_element_type=jnp.float32
    )
    return grad_query * scale, grad_keys * scale, grad_values


def device(**coordinates):
    return {name: place for name, place in coordinates.items()}


class Copies:
    def __init__(self, send_sems, recv_sems):
        self.send_sems, self.recv_sems = send_sems, recv_sems
        self.used = 0
        self.sent = []

    def new(self):
        self.used += 1
        return self.used - 1

    def _make(self, which, source, target, to):
        return pltpu.make_async_remote_copy(
            src_ref=source,
            dst_ref=target,
            send_sem=self.send_sems.at[which],
            recv_sem=self.recv_sems.at[which],
            device_id=to,
            device_id_type=pl.DeviceIdType.MESH,
        )

    def send(self, which, source, target, to, cond=None):
        only(cond, lambda: self._make(which, source, target, to).start())
        self.sent.append((which, source, target, to, cond))

    def receive(self, which, target, via):
        self._make(which, target, target, via).wait_recv()

    def finish(self):
        for which, source, target, to, cond in self.sent:
            only(cond, lambda: self._make(which, source, target, to).wait_send())
        self.sent = []


def only(cond, action):
    if cond is None:
        action()
    else:
        pl.when(cond)(action)


class Place:
    def __init__(self):
        self.z, self.p = lax.axis_index(RING), lax.axis_index(PAIR)
        self.c, self.y = lax.axis_index(CORE), lax.axis_index(TENSOR)
        self.rank = (self.z * 2 + self.p) * 2 + self.c
        self.pair, self.core = {PAIR: 1 - self.p}, {CORE: 1 - self.c}
        self.cross = {PAIR: 1 - self.p, CORE: 1 - self.c}
        self.other = {TENSOR: 1 - self.y}
        self.right, self.left = {RING: self.z + 1}, {RING: self.z - 1}
        self.has_right, self.has_left = self.z < LINE - 1, self.z > 0

    def ranked(self, rank):
        return {RING: rank // 4, PAIR: (rank // 2) % 2, CORE: rank % 2}

    def meet(self):
        barrier = pltpu.get_barrier_semaphore()

        def greet(to, cond=None):
            only(
                cond,
                lambda: pl.semaphore_signal(
                    barrier, inc=1, device_id=to, device_id_type=pl.DeviceIdType.MESH
                ),
            )

        for to in (self.pair, self.core, self.cross, self.other):
            greet(to)
        greet(self.right, self.has_right)
        greet(self.left, self.has_left)
        for back in range(1, BACK + 1):
            greet(self.ranked(self.rank + back), self.rank + back < 4 * LINE)
            greet(self.ranked(self.rank - back), self.rank >= back)
        line = jnp.minimum(self.z, 1) + jnp.minimum(LINE - 1 - self.z, 1)
        reach = jnp.minimum(self.rank, BACK) + jnp.minimum(4 * LINE - 1 - self.rank, BACK)
        pl.semaphore_wait(barrier, 4 + line + reach)


class LineFlow:
    def __init__(self, copies, place, block):
        self.copies, self.place, self.block = copies, place, block
        self.ids = {(way, step): copies.new() for way in (1, -1) for step in range(1, LINE)}

    def valid(self, way, step):
        z = self.place.z
        return z >= step if way == 1 else z + step <= LINE - 1

    def origin(self, way, step):
        return self.place.z - way * step

    def onward(self, way, step, source):
        if step == LINE - 1:
            return
        to = self.place.right if way == 1 else self.place.left
        there = self.place.has_right if way == 1 else self.place.has_left
        if step:
            there = there & self.valid(way, step)
        target = self.block(self.origin(way, step))
        self.copies.send(self.ids[way, step + 1], source, target, to, there)

    def start(self, source):
        self.onward(1, 0, source)
        self.onward(-1, 0, source)

    def arrive(self, step, then=None):
        for way in (1, -1):

            def take(way=way):
                target = self.block(self.origin(way, step))
                via = self.place.left if way == 1 else self.place.right
                self.copies.receive(self.ids[way, step], target, via)

            pl.when(self.valid(way, step))(take)
            if step < LINE - 1:
                self.onward(way, step, self.block(self.origin(way, step)))
            if then is not None:
                then(way, step)


class RowsFlow:
    def __init__(self, copies, place, shard, whole):
        self.copies, self.place, self.shard, self.whole = copies, place, shard, whole
        self.line = LineFlow(copies, place, lambda origin: self.rows(origin, place.p, place.c))
        items = [(0, 0)] + [(way, step) for step in range(1, LINE) for way in (1, -1)]
        self.items = items
        self.pair_ids = {item: copies.new() for item in items}
        self.core_ids = {item: copies.new() for item in items}
        self.cross_ids = {item: copies.new() for item in items}

    def rows(self, origin, p, c):
        count = self.shard.shape[0]
        return self.whole.at[pl.ds(pl.multiple_of((origin * 4 + p * 2 + c) * count, count), count)]

    def valid(self, item):
        return None if item == (0, 0) else self.line.valid(*item)

    def spread(self, way, step):
        item, place = (way, step), self.place
        here = self.rows(self.line.origin(way, step), place.p, place.c)
        self.copies.send(self.pair_ids[item], here, here, place.pair, self.valid(item))
        self.copies.send(self.core_ids[item], here, here, place.core, self.valid(item))

    def start(self, own_copy):
        self.line.start(self.shard)
        own_copy()
        self.spread(0, 0)

    def arrive(self, step):
        self.line.arrive(step, self.spread)

    def crossing(self, step):
        place = self.place
        for item in self.items:
            if item[1] != step:
                continue
            there = self.rows(self.line.origin(*item), 1 - place.p, place.c)
            only(
                self.valid(item),
                lambda: self.copies.receive(self.pair_ids[item], there, place.pair),
            )
            self.copies.send(self.cross_ids[item], there, there, place.core, self.valid(item))

    def end(self):
        place = self.place
        for item in self.items:
            origin = self.line.origin(*item)

            def take(item=item, origin=origin):
                mine = self.rows(origin, place.p, 1 - place.c)
                cross = self.rows(origin, 1 - place.p, 1 - place.c)
                self.copies.receive(self.core_ids[item], mine, place.core)
                self.copies.receive(self.cross_ids[item], cross, place.core)

            only(self.valid(item), take)


class QuarterFlow:
    def __init__(self, copies, place, shard, whole, own_sem):
        self.copies, self.place, self.shard, self.whole = copies, place, shard, whole
        self.count, self.width = shard.shape[0], whole.shape[1]
        self.own = pltpu.make_async_copy(
            self.columns(place.p, place.c), self.rows(place.p, place.c), own_sem
        )
        self.near = (
            (copies.new(), 1 - place.p, place.c, place.pair),
            (copies.new(), place.p, 1 - place.c, place.core),
            (copies.new(), 1 - place.p, 1 - place.c, place.cross),
        )
        self.line = LineFlow(copies, place, self.block)

    def columns(self, p, c):
        width = self.width
        return self.shard.at[:, pl.ds(pl.multiple_of((p * 2 + c) * width, LANES), width)]

    def rows(self, p, c):
        count = self.count
        start = (self.place.z * 4 + p * 2 + c) * count
        return self.whole.at[pl.ds(pl.multiple_of(start, count), count)]

    def block(self, origin):
        count = 4 * self.count
        return self.whole.at[pl.ds(pl.multiple_of(origin * count, count), count)]

    def start(self):
        place = self.place
        self.own.start()
        for which, p, c, to in self.near:
            self.copies.send(which, self.columns(p, c), self.rows(place.p, place.c), to)

    def join(self):
        self.own.wait()
        for which, p, c, to in self.near:
            self.copies.receive(which, self.rows(p, c), to)
        self.line.start(self.block(self.place.z))

    def arrive(self, step):
        self.line.arrive(step)


class FourFlow:
    def __init__(self, copies, place, slots, parts):
        self.copies, self.place, self.slots = copies, place, slots
        self.size = slots.shape[1] // parts
        self.ids = [[copies.new() for _ in range(3)] for _ in range(parts)]

    def slot(self, which, part):
        return self.slots.at[which, pl.ds(part * self.size, self.size)]

    def send(self, part, source):
        self.copies.send(self.ids[part][0], source, self.slot(1, part), self.place.pair)
        self.copies.send(self.ids[part][1], source, self.slot(2, part), self.place.core)

    def cross(self, part):
        got = self.slot(1, part)
        self.copies.receive(self.ids[part][0], got, self.place.pair)
        self.copies.send(self.ids[part][2], got, self.slot(3, part), self.place.core)

    def end(self, part):
        self.copies.receive(self.ids[part][1], self.slot(2, part), self.place.core)
        self.copies.receive(self.ids[part][2], self.slot(3, part), self.place.core)


PARTS = 4
N_REMOTE = 160


def forward_kernel(
    heads,
    head_size,
    tokens,
    first_shard,
    out_shard,
    gate_shard,
    up_shard,
    down_shard,
    grad_out,
    biases,
    cosine,
    sine,
    allowed,
    first_out,
    w_out_out,
    gate_all,
    up_all,
    down_all,
    grad_out_four,
    normed_four,
    query_out,
    window_out,
    heads_out,
    residual_out,
    first_all,
    w_out_all,
    unit,
    window,
    keys,
    values,
    part_own,
    part_other,
    normed,
    send_sems,
    recv_sems,
    local_sems,
):
    place = Place()
    copies = Copies(send_sems, recv_sems)
    rows, width = tokens.shape
    batches = allowed.shape[0]
    per_batch = rows // batches
    query_width = heads * head_size
    kv_width = query_width + 2 * head_size

    window[...] = jnp.zeros_like(window)
    place.meet()

    first = RowsFlow(copies, place, first_shard, first_all)
    outs = RowsFlow(copies, place, out_shard, w_out_all)
    quarters = [
        QuarterFlow(copies, place, shard, whole, local_sems.at[2 + i])
        for i, (shard, whole) in enumerate(
            ((gate_shard, gate_all), (up_shard, up_all), (down_shard, down_all))
        )
    ]
    cot = FourFlow(copies, place, grad_out_four, 1)
    second = FourFlow(copies, place, normed_four, PARTS)
    part_ids = [copies.new() for _ in range(PARTS)]
    window_ids = [copies.new() for _ in range(BACK)]

    def put(flow, sem):
        def run():
            copy = pltpu.make_async_copy(flow.shard, flow.rows(place.z, place.p, place.c), sem)
            copy.start()
            copy.wait()

        return run

    first.start(put(first, local_sems.at[0]))
    quarters[0].start()
    x = wide(tokens[...])
    scale_row = lax.rsqrt(jnp.mean(x * x, axis=-1, keepdims=True) + EPSILON)
    unit[...] = x * scale_row
    first.crossing(0)
    first.arrive(1)
    quarters[1].start()
    first.crossing(1)
    quarters[0].join()
    first.arrive(2)
    first.crossing(2)
    first.arrive(3)
    quarters[2].start()
    first.crossing(3)
    quarters[1].join()
    first.end()

    gains = wide(first_all[:, kv_width:]).T
    first_gain, second_gain = gains[0:1], gains[1:2]
    first_normed = low(unit[...] * first_gain)
    sign = jnp.where(
        lax.broadcasted_iota(jnp.int32, (1, head_size), 1) < head_size // 2, -1.0, 1.0
    )
    turn_sine = sine[...] * sign

    def project(start, size):
        raw = matmul(first_normed, first_all[:, start : start + size])
        return raw + biases[:, start : start + size]

    def turned(raw):
        return low(raw * cosine[...] + pltpu.roll(raw, head_size // 2, 1) * turn_sine)

    kv = project(query_width, 2 * head_size)
    key_now, value_now = turned(kv[:, :head_size]), low(kv[:, head_size:])
    for b in range(batches):
        mine = slice(b * per_batch, (b + 1) * per_batch)
        window[BACK, b, :, :head_size] = key_now[mine]
        window[BACK, b, :, head_size:] = value_now[mine]
    for back in range(1, BACK + 1):
        copies.send(
            window_ids[back - 1],
            window.at[BACK],
            window.at[BACK - back],
            place.ranked(place.rank + back),
            place.rank + back < 4 * LINE,
        )
    outs.start(put(outs, local_sems.at[1]))
    quarters[2].join()
    for h in range(0, heads, 2):
        raw = project(h * head_size, 2 * head_size)
        query_out[:, h * head_size : (h + 1) * head_size] = turned(raw[:, :head_size])
        query_out[:, (h + 1) * head_size : (h + 2) * head_size] = turned(raw[:, head_size:])
    cot_own = pltpu.make_async_copy(grad_out, grad_out_four.at[0], local_sems.at[5])
    cot_own.start()
    cot.send(0, grad_out)
    outs.crossing(0)
    outs.arrive(1)
    outs.crossing(1)
    quarters[0].arrive(1)
    outs.arrive(2)
    outs.crossing(2)
    for back in range(1, BACK + 1):
        only(
            place.rank >= back,
            lambda: copies.receive(
                window_ids[back - 1], window.at[BACK - back], place.ranked(place.rank - back)
            ),
        )

    root = 1.0 / math.sqrt(head_size)
    size = rows // PARTS
    for b in range(batches):
        for slot in range(BACK + 1):
            keys[slot * per_batch : (slot + 1) * per_batch] = window[slot, b, :, :head_size]
            values[slot * per_batch : (slot + 1) * per_batch] = window[slot, b, :, head_size:]

        def attend_head(h, carry, b=b):
            columns = pl.ds(pl.multiple_of(h * head_size, head_size), head_size)
            mine = slice(b * per_batch, (b + 1) * per_batch)
            scores = times_transpose(query_out[mine, columns], keys[...]) * root
            scores = jnp.where(allowed[b] > 0.0, scores, NEGATIVE)
            weights = jnp.exp(scores - jnp.max(scores, axis=-1, keepdims=True))
            probs = low(weights * (1.0 / jnp.sum(weights, axis=-1, keepdims=True)))
            heads_out[mine, columns] = low(matmul(probs, values[...]))
            return carry

        lax.fori_loop(0, heads, attend_head, 0)
        if b == 0:
            outs.arrive(3)
            outs.crossing(3)
            outs.end()
            quarters[1].arrive(1)
        part = low(times_transpose(heads_out[b * per_batch : (b + 1) * per_batch], w_out_all[...]))
        part_own[b * per_batch : (b + 1) * per_batch] = part
        for i in range(b * per_batch // size, (b + 1) * per_batch // size):
            block = pl.ds(i * size, size)
            copies.send(part_ids[i], part_own.at[block], part_other.at[block], place.other)
        if b == 0:
            quarters[2].arrive(1)

    for i in range(PARTS):
        block = pl.ds(i * size, size)
        copies.receive(part_ids[i], part_other.at[block], place.other)
        state = wide(tokens[block]) + (wide(part_own[block]) + wide(part_other[block]))
        residual_out[block] = state
        scale_row = lax.rsqrt(jnp.mean(state * state, axis=-1, keepdims=True) + EPSILON)
        normed[block] = low(state * scale_row * second_gain)
        second.send(i, normed.at[block])
        if i > 0:
            second.cross(i - 1)
    second_own = pltpu.make_async_copy(normed, normed_four.at[0], local_sems.at[6])
    second_own.start()
    second.cross(PARTS - 1)
    for flow in quarters:
        flow.arrive(2)
    cot.cross(0)
    first_copy = pltpu.make_async_copy(first_all, first_out, local_sems.at[0])
    first_copy.start()
    outs_copy = pltpu.make_async_copy(w_out_all, w_out_out, local_sems.at[1])
    outs_copy.start()
    window_out[...] = window[...]
    for i in range(PARTS):
        second.end(i)
    cot.end(0)
    for flow in quarters:
        flow.arrive(3)
    for copy in (cot_own, second_own, first_copy, outs_copy):
        copy.wait()
    copies.finish()


def forward_call(heads, head_size, operands):
    tokens, first_shard, out_shard, gate_shard = operands[:4]
    allowed = operands[-1]
    rows, width = tokens.shape
    batches = allowed.shape[0]
    per_batch = rows // batches
    quarter = gate_shard.shape[1] // 4
    query_width = heads * head_size
    low_type, wide_type = jnp.bfloat16, jnp.float32

    def shape(*dims, kind=low_type):
        return jax.ShapeDtypeStruct(dims, kind)

    in_vmem, anywhere = pl.BlockSpec(memory_space=pltpu.VMEM), pl.BlockSpec(memory_space=pl.ANY)
    window_shape = (BACK + 1, batches, per_batch, 2 * head_size)
    outs = (
        (shape(width, first_shard.shape[1]), anywhere),
        (shape(width, query_width), anywhere),
        (shape(width, quarter), anywhere),
        (shape(width, quarter), anywhere),
        (shape(width, quarter), anywhere),
        (shape(4, rows, width), anywhere),
        (shape(4, rows, width), anywhere),
        (shape(rows, query_width), in_vmem),
        (shape(*window_shape), in_vmem),
        (shape(rows, query_width), in_vmem),
        (shape(rows, width, kind=wide_type), in_vmem),
    )
    return pl.pallas_call(
        functools.partial(forward_kernel, heads, head_size),
        out_shape=[out[0] for out in outs],
        in_specs=[in_vmem] + [anywhere] * 6 + [in_vmem] * 4,
        out_specs=[out[1] for out in outs],
        scratch_shapes=[
            pltpu.VMEM((width, first_shard.shape[1]), low_type),
            pltpu.VMEM((width, query_width), low_type),
            pltpu.VMEM((rows, width), wide_type),
            pltpu.VMEM(window_shape, low_type),
            pltpu.VMEM(((BACK + 1) * per_batch, head_size), low_type),
            pltpu.VMEM(((BACK + 1) * per_batch, head_size), low_type),
            pltpu.VMEM((rows, width), low_type),
            pltpu.VMEM((rows, width), low_type),
            pltpu.VMEM((rows, width), low_type),
            pltpu.SemaphoreType.DMA((N_REMOTE,)),
            pltpu.SemaphoreType.DMA((N_REMOTE,)),
            pltpu.SemaphoreType.DMA((8,)),
        ],
        compiler_params=pltpu.CompilerParams(
            collective_id=0, has_side_effects=True, vmem_limit_bytes=VMEM_BYTES
        ),
    )(*operands)


def body(
    tokens,
    norm1_gain,
    query_weight,
    query_bias,
    key_weight,
    key_bias,
    value_weight,
    value_bias,
    output_weight,
    norm2_gain,
    gate_weight,
    up_weight,
    down_weight,
    cotangent,
    segments,
    positions,
):
    batches, count_rows, width = tokens.shape
    heads, head_size = query_bias.shape
    query_width = heads * head_size
    units = gate_weight.shape[1]
    place = lax.axis_index(FSDP)
    row_start = place * count_rows
    rows = batches * count_rows

    gains = jnp.stack([norm1_gain, norm2_gain], axis=1)
    gains = jnp.pad(gains, ((0, 0), (0, LANES - 2)))
    first_shard = jnp.concatenate([query_weight, key_weight, value_weight, gains], axis=1)
    kv_width = query_width + 2 * head_size
    padded = -(-units // (4 * LANES)) * (4 * LANES)

    def spaced(shard):
        return jnp.pad(shard, ((0, 0), (0, padded - units)))

    grad_out = cotangent.reshape(rows, width)
    inputs = wide(tokens.reshape(rows, width))
    biases = jnp.concatenate(
        [query_bias.reshape(-1), key_bias.reshape(-1), value_bias.reshape(-1)]
    )
    own_places = lax.dynamic_slice_in_dim(positions, row_start, count_rows, axis=1)
    cosine, sine_table = rotation(own_places.reshape(-1), head_size)
    allowed = [
        visible(segments[b], positions[b], row_start, count_rows) for b in range(batches)
    ]
    if lax.axis_size(RING) == LINE:
        (
            first_all,
            w_out,
            w_gate,
            w_up,
            w_down,
            grad_out_four,
            second_normed,
            query_rows,
            window,
            heads_out,
            residual,
        ) = forward_call(
            heads,
            head_size,
            (
                tokens.reshape(rows, width),
                first_shard,
                output_weight.T,
                spaced(gate_weight),
                spaced(up_weight),
                spaced(down_weight.T),
                grad_out,
                wide(biases).reshape(1, -1),
                cosine[:, 0],
                sine_table[:, 0],
                jnp.stack(allowed).astype(jnp.float32),
            ),
        )
        grad_out_four = grad_out_four.reshape(-1, width)
        second_normed = second_normed.reshape(-1, width)
        query_rows = query_rows.reshape(batches, count_rows, heads, head_size)
        window = window.transpose(1, 0, 2, 3).reshape(batches, -1, 2 * head_size)
        w_qkv = first_all[:, :kv_width]
        first_gain = wide(first_all[:, kv_width])
        second_gain = wide(first_all[:, kv_width + 1])
        first_unit, first_scale = root_mean_square_parts(inputs)
        first_normed = low(first_unit * first_gain)
        key_rows, value_rows = window[..., :head_size], window[..., head_size:]
        log_totals = [log_total_of(query_rows[b], key_rows[b], allowed[b]) for b in range(batches)]
    else:
        first_all = gather_rows(first_shard)
        w_qkv = first_all[:, :kv_width]
        first_gain = wide(first_all[:, kv_width])
        second_gain = wide(first_all[:, kv_width + 1])
        w_out = gather_rows(output_weight.T)
        w_gate = quarter_columns(spaced(gate_weight))
        w_up = quarter_columns(spaced(up_weight))
        w_down = quarter_columns(spaced(down_weight.T))
        grad_out_four = four_blocks(grad_out)
        first_unit, first_scale = root_mean_square_parts(inputs)
        first_normed = low(first_unit * first_gain)
        raw = matmul(first_normed, w_qkv) + wide(biases)
        turned = rotate(
            raw[:, : query_width + head_size].reshape(rows, heads + 1, head_size),
            cosine,
            sine_table,
        )
        turned = low(turned)
        query_rows = turned[:, :heads].reshape(batches, count_rows, heads, head_size)
        key_value = jnp.concatenate(
            [turned[:, heads], low(raw[:, query_width + head_size :])], axis=1
        )
        key_value = key_value.reshape(batches, count_rows, 2 * head_size)
        window = jnp.concatenate(
            [shifted(key_value, back) for back in range(BACK, 0, -1)] + [key_value], axis=1
        )
        key_rows, value_rows = window[..., :head_size], window[..., head_size:]
        attended = [
            attend(query_rows[b], key_rows[b], value_rows[b], allowed[b]) for b in range(batches)
        ]
        log_totals = [log_total for _, log_total in attended]
        heads_out = jnp.concatenate([mixed for mixed, _ in attended], axis=0)
        residual = inputs + tensor_total(times_transpose(heads_out, w_out))
        second_unit, second_scale = root_mean_square_parts(residual)
        second_normed = four_blocks(low(second_unit * second_gain))

    second_unit, second_scale = root_mean_square_parts(residual)
    gate_value = matmul(second_normed, w_gate)
    up_part = matmul(second_normed, w_up)
    sigmoid_gate = jax.nn.sigmoid(gate_value)
    silu_gate = gate_value * sigmoid_gate
    hidden = low(silu_gate * up_part)
    grad_hidden = matmul(grad_out_four, w_down)
    grad_gate = low(
        grad_hidden * up_part * sigmoid_gate * (1.0 + gate_value * (1.0 - sigmoid_gate))
    )
    grad_up = low(grad_hidden * silu_gate)
    second_back = four_sums(times_transpose(grad_gate, w_gate) + times_transpose(grad_up, w_up))
    grad_w_down = quarter_to_owner(low(contract_rows(grad_out_four, hidden)))
    grad_w_gate = quarter_to_owner(low(contract_rows(second_normed, grad_gate)))
    grad_w_up = quarter_to_owner(low(contract_rows(second_normed, grad_up)))
    output = low(residual + four_sums(times_transpose(hidden, w_down)))

    second_gain_sum = jnp.sum(second_back * second_unit, axis=0)
    grad_state = wide(grad_out) + norm_back(second_back, second_unit, second_scale, second_gain)
    grad_branch = low(grad_state)
    grad_w_out = scatter_rows(contract_rows(grad_branch, heads_out))
    grad_heads = low(matmul(grad_branch, w_out)).reshape(query_rows.shape)
    backs = [
        attend_back(
            grad_heads[b], query_rows[b], key_rows[b], value_rows[b], allowed[b], log_totals[b]
        )
        for b in range(batches)
    ]
    grad_query = jnp.stack([back[0] for back in backs]).reshape(rows, heads, head_size)
    grad_window = jnp.stack([jnp.concatenate([back[1], back[2]], axis=1) for back in backs])
    own_grad = grad_window[:, BACK * count_rows :]
    for back in range(1, BACK + 1):
        first_row = (BACK - back) * count_rows
        own_grad = own_grad + wide(
            shifted(low(grad_window[:, first_row : first_row + count_rows]), -back)
        )
    own_grad = own_grad.reshape(rows, 2, head_size)
    turned_back = rotate_back(
        jnp.concatenate([grad_query, own_grad[:, :1]], axis=1), cosine, sine_table
    )
    grad_raw = low(jnp.concatenate([turned_back, own_grad[:, 1:]], axis=1).reshape(rows, -1))
    grad_w_qkv = scatter_rows(contract_rows(first_normed, grad_raw))
    bias_sum = jnp.sum(wide(grad_raw), axis=0)
    first_back_part = times_transpose(grad_raw, w_qkv)
    first_back = tensor_total(first_back_part)
    first_gain_sum = jnp.sum(first_back * first_unit, axis=0)
    input_grad = grad_state + norm_back(first_back, first_unit, first_scale, first_gain)
    sums = summed_over_fsdp(jnp.concatenate([bias_sum, second_gain_sum, first_gain_sum]))
    bias_total = sums[:kv_width]
    gain_rows = norm1_gain.shape[0]
    second_total = lax.dynamic_slice_in_dim(sums, kv_width + place * gain_rows, gain_rows)
    first_total = lax.dynamic_slice_in_dim(sums, kv_width + width + place * gain_rows, gain_rows)

    return (
        output.reshape(tokens.shape),
        input_grad.reshape(tokens.shape),
        first_total,
        grad_w_qkv[:, :query_width],
        bias_total[:query_width].reshape(query_bias.shape),
        grad_w_qkv[:, query_width : query_width + head_size],
        bias_total[query_width : query_width + head_size].reshape(key_bias.shape),
        grad_w_qkv[:, query_width + head_size :],
        bias_total[query_width + head_size :].reshape(value_bias.shape),
        grad_w_out.T,
        second_total,
        grad_w_gate[:, :units],
        grad_w_up[:, :units],
        grad_w_down[:, :units].T,
    )


def solution(mesh):
    fsdp, tensor = mesh.shape["fsdp"], mesh.shape["tensor"]
    fine = Mesh(mesh.devices.reshape(fsdp // 4, 2, 2, tensor), (RING, PAIR, CORE, TENSOR))
    by_rows, by_columns, by_tensor = P(FSDP, TENSOR), P(TENSOR, FSDP), P(TENSOR, None)
    by_tokens, by_gain = P(None, FSDP, None), P(FSDP)
    placed = (
        by_tokens,
        by_gain,
        by_rows,
        by_tensor,
        by_rows,
        by_tensor,
        by_rows,
        by_tensor,
        by_columns,
        by_gain,
        by_rows,
        by_rows,
        by_columns,
        by_tokens,
        P(),
        P(),
    )
    return jax.shard_map(
        body,
        mesh=fine,
        in_specs=placed,
        out_specs=(
            by_tokens,
            by_tokens,
            by_gain,
            by_rows,
            by_tensor,
            by_rows,
            by_tensor,
            by_rows,
            by_tensor,
            by_columns,
            by_gain,
            by_rows,
            by_rows,
            by_columns,
        ),
        check_vma=False,
    )
```

```python
import functools
import math

import jax
import jax.numpy as jnp
from jax import lax
from jax.experimental import pallas as pl
from jax.experimental.pallas import tpu as pltpu
from jax.sharding import Mesh
from jax.sharding import PartitionSpec as P

BACK = 5
LINE = 4
LANES = 128
VMEM_BYTES = 62 * 1024 * 1024

EPSILON = 1e-06
THETA = 1000000.0
NEGATIVE = -1e30

RING, PAIR, CORE, TENSOR = "ring", "pair", "core", "tensor"
FSDP = (RING, PAIR, CORE)
SWAP = [(0, 1), (1, 0)]


def low(value):
    return value.astype(jnp.bfloat16)


def wide(value):
    return value.astype(jnp.float32)


def matmul(left_side, right_side):
    return jnp.dot(left_side, right_side, preferred_element_type=jnp.float32)


def contract_rows(left_side, right_side):
    return lax.dot_general(
        left_side, right_side, (((0,), (0,)), ((), ())), preferred_element_type=jnp.float32
    )


def times_transpose(left_side, right_side):
    return lax.dot_general(
        left_side, right_side, (((1,), (1,)), ((), ())), preferred_element_type=jnp.float32
    )


def swapped(value, axis):
    return lax.ppermute(value, axis, SWAP)


def in_order(own, other, place, axis):
    first = jnp.where(place == 0, own, other)
    second = jnp.where(place == 0, other, own)
    return jnp.stack([first, second], axis=axis)


def shifted(value, steps):
    count = lax.axis_size(FSDP)
    first, last = (max(0, -steps), min(count, count - steps))
    return lax.ppermute(value, FSDP, [(source, source + steps) for source in range(first, last)])


def summed_over_fsdp(value):
    count = lax.axis_size(FSDP)
    bit = 1
    while bit < count:
        value = value + lax.ppermute(value, FSDP, [(i, i ^ bit) for i in range(count)])
        bit *= 2
    return value


def line_gather(block):
    count, here = lax.axis_size(RING), lax.axis_index(RING)
    if count > LINE:
        return lax.all_gather(block, RING, axis=0)
    right, left = [block], [block]
    for step in range(1, count):
        right.append(
            lax.ppermute(right[-1], RING, [(i, i + 1) for i in range(step - 1, count - 1)])
        )
        left.append(
            lax.ppermute(left[-1], RING, [(i, i - 1) for i in range(1, count - step + 1)])
        )
    result = jnp.zeros((count,) + block.shape, block.dtype)
    for step in range(count):
        piece = block if step == 0 else jnp.where(here >= step, right[step], left[count - step])
        result = lax.dynamic_update_slice_in_dim(
            result, piece[None], (here - step + count) % count, axis=0
        )
    return result


def line_scatter(parts):
    count, here = lax.axis_size(RING), lax.axis_index(RING)
    if count > LINE:
        return wide(lax.psum_scatter(parts, RING, scatter_dimension=0, tiled=False))

    def part(place):
        return lax.dynamic_index_in_dim(parts, place, axis=0, keepdims=False)

    right, left = None, None
    for step in range(1, count):
        to_right, to_left = part(here + count - step), part(here - count + step)
        if step > 1:
            to_right = low(wide(to_right) + wide(right))
            to_left = low(wide(to_left) + wide(left))
        right = lax.ppermute(to_right, RING, [(i, i + 1) for i in range(step)])
        left = lax.ppermute(to_left, RING, [(i, i - 1) for i in range(count - step, count)])
    return wide(part(here)) + wide(right) + wide(left)


def gather_rows(shard):
    rows = line_gather(shard)
    rows = in_order(rows, swapped(rows, PAIR), lax.axis_index(PAIR), 1)
    rows = in_order(rows, swapped(rows, CORE), lax.axis_index(CORE), 2)
    return rows.reshape((-1,) + shard.shape[1:])


def scatter_rows(total):
    pair, core = lax.axis_index(PAIR), lax.axis_index(CORE)
    parts = low(total).reshape((lax.axis_size(RING), 2, 2, -1) + total.shape[1:])

    def halved(value, axis, place, name):
        mine = lax.dynamic_index_in_dim(value, place, axis=axis, keepdims=False)
        sent = lax.dynamic_index_in_dim(value, 1 - place, axis=axis, keepdims=False)
        return low(wide(mine) + wide(swapped(sent, name)))

    parts = halved(parts, 2, core, CORE)
    parts = halved(parts, 1, pair, PAIR)
    return line_scatter(parts)


def quarter_columns(shard):
    pair, core = lax.axis_index(PAIR), lax.axis_index(CORE)
    half = shard.shape[1] // 2

    def halved(value, place, width):
        mine = lax.dynamic_slice_in_dim(value, place * width, width, axis=value.ndim - 1)
        sent = lax.dynamic_slice_in_dim(value, (1 - place) * width, width, axis=value.ndim - 1)
        return mine, sent

    mine, sent = halved(shard, pair, half)
    rows = in_order(mine, swapped(sent, PAIR), pair, 0)
    mine, sent = halved(rows, core, half // 2)
    rows = in_order(mine, swapped(sent, CORE), core, 1)
    rows = line_gather(rows.reshape(-1, half // 2))
    return rows.reshape(-1, half // 2)


def quarter_to_owner(grad):
    pair, core = lax.axis_index(PAIR), lax.axis_index(CORE)
    width = grad.shape[1]
    block = lax.psum_scatter(
        grad.reshape(lax.axis_size(RING), -1, width), RING, scatter_dimension=0, tiled=False
    )
    block = block.reshape(2, 2, -1, width)

    def halved(value, axis, place):
        mine = lax.dynamic_index_in_dim(value, place, axis=axis, keepdims=False)
        sent = lax.dynamic_index_in_dim(value, 1 - place, axis=axis, keepdims=False)
        return mine, sent

    mine, sent = halved(block, 0, pair)
    block = in_order(mine, swapped(sent, PAIR), pair, 0)
    mine, sent = halved(block, 1, core)
    block = in_order(mine, swapped(sent, CORE), core, 1)
    return jnp.concatenate([wide(block[i, j]) for i in range(2) for j in range(2)], axis=1)


def four_blocks(value):
    over = swapped(value, PAIR)
    return jnp.concatenate([value, over, swapped(value, CORE), swapped(over, CORE)], axis=0)


def four_sums(total):
    half = total.shape[0] // 2
    total = total[:half] + wide(swapped(low(total[half:]), CORE))
    total = total[: half // 2] + wide(swapped(low(total[half // 2 :]), PAIR))
    return tensor_total(total)


def tensor_total(partial_sum):
    own = lax.reduce_precision(partial_sum, 8, 7)
    return own + wide(swapped(low(own), TENSOR))


def rotation(places, width):
    half_width = width // 2
    frequency = THETA ** (-(jnp.arange(half_width, dtype=jnp.float32) * 2.0) / width)
    angles = places.astype(jnp.float32)[:, None] * frequency[None, :]
    cosine = jnp.concatenate([jnp.cos(angles), jnp.cos(angles)], axis=-1)[:, None, :]
    sine_table = jnp.concatenate([jnp.sin(angles), jnp.sin(angles)], axis=-1)[:, None, :]
    return (cosine, sine_table)


def rotate(values, cosine, sine_table):
    half_width = values.shape[-1] // 2
    turned = jnp.concatenate([-values[..., half_width:], values[..., :half_width]], axis=-1)
    return values * cosine + turned * sine_table


def rotate_back(gradient, cosine, sine_table):
    half_width = gradient.shape[-1] // 2
    moved_part = gradient * sine_table
    return gradient * cosine + jnp.concatenate(
        [moved_part[..., half_width:], -moved_part[..., :half_width]], axis=-1
    )


def root_mean_square_parts(values):
    scale_row = lax.rsqrt(jnp.mean(values * values, axis=-1, keepdims=True) + EPSILON)
    return (values * scale_row, scale_row)


def norm_back(grad_normed, normalized, scale_row, gain):
    scaled = grad_normed * gain
    return scale_row * (scaled - normalized * jnp.mean(scaled * normalized, axis=-1, keepdims=True))


def visible(seg_row, pos_row, row_start, count_rows):
    pad_rows = BACK * count_rows
    seg_padded = jnp.concatenate([jnp.full((pad_rows,), -1, jnp.int32), seg_row])
    pos_padded = jnp.concatenate([jnp.zeros((pad_rows,), jnp.int32), pos_row])
    key_seg = lax.dynamic_slice_in_dim(seg_padded, row_start, pad_rows + count_rows)
    key_pos = lax.dynamic_slice_in_dim(pos_padded, row_start, pad_rows + count_rows)
    query_seg = lax.dynamic_slice_in_dim(seg_row, row_start, count_rows)
    query_pos = lax.dynamic_slice_in_dim(pos_row, row_start, count_rows)
    return (query_seg[:, None] == key_seg[None, :]) & (key_pos[None, :] <= query_pos[:, None])


def attend(query_rows, key_rows, value_rows, allowed):
    scores = jnp.einsum("thd,sd->hts", query_rows, key_rows, preferred_element_type=jnp.float32)
    scores = scores * (1.0 / math.sqrt(query_rows.shape[-1]))
    scores = jnp.where(allowed, scores, NEGATIVE)
    row_max = jnp.max(scores, axis=-1, keepdims=True)
    log_total = row_max + jnp.log(jnp.sum(jnp.exp(scores - row_max), axis=-1, keepdims=True))
    probs_low = low(jnp.exp(scores - log_total))
    mixed = jnp.einsum("hts,sd->thd", probs_low, value_rows, preferred_element_type=jnp.float32)
    return low(mixed.reshape(query_rows.shape[0], -1)), log_total


def log_total_of(query_rows, key_rows, allowed):
    scores = jnp.einsum("thd,sd->hts", query_rows, key_rows, preferred_element_type=jnp.float32)
    scores = scores * (1.0 / math.sqrt(query_rows.shape[-1]))
    scores = jnp.where(allowed, scores, NEGATIVE)
    row_max = jnp.max(scores, axis=-1, keepdims=True)
    return row_max + jnp.log(jnp.sum(jnp.exp(scores - row_max), axis=-1, keepdims=True))


def attend_back(grad_heads, query_rows, key_rows, value_rows, allowed, log_total):
    scale = 1.0 / math.sqrt(query_rows.shape[-1])
    scores = jnp.einsum("thd,sd->hts", query_rows, key_rows, preferred_element_type=jnp.float32)
    probs = jnp.exp(jnp.where(allowed, scores * scale, NEGATIVE) - log_total)
    grad_probs = jnp.einsum(
        "thd,sd->hts", grad_heads, value_rows, preferred_element_type=jnp.float32
    )
    row_inner = jnp.sum(probs * grad_probs, axis=-1, keepdims=True)
    grad_scores = low(probs * (grad_probs - row_inner))
    grad_query = jnp.einsum(
        "hts,sd->thd", grad_scores, key_rows, preferred_element_type=jnp.float32
    )
    grad_keys = jnp.einsum(
        "hts,thd->sd", grad_scores, query_rows, preferred_element_type=jnp.float32
    )
    grad_values = jnp.einsum(
        "hts,thd->sd", low(probs), grad_heads, preferred_element_type=jnp.float32
    )
    return grad_query * scale, grad_keys * scale, grad_values


def device(**coordinates):
    return {name: place for name, place in coordinates.items()}


class Copies:
    def __init__(self, send_sems, recv_sems):
        self.send_sems, self.recv_sems = send_sems, recv_sems
        self.used = 0
        self.sent = []

    def new(self):
        self.used += 1
        return self.used - 1

    def _make(self, which, source, target, to):
        return pltpu.make_async_remote_copy(
            src_ref=source,
            dst_ref=target,
            send_sem=self.send_sems.at[which],
            recv_sem=self.recv_sems.at[which],
            device_id=to,
            device_id_type=pl.DeviceIdType.MESH,
        )

    def send(self, which, source, target, to, cond=None):
        only(cond, lambda: self._make(which, source, target, to).start())
        self.sent.append((which, source, target, to, cond))

    def receive(self, which, target, via):
        self._make(which, target, target, via).wait_recv()

    def settle(self, until=None):
        until = len(self.sent) if until is None else until
        for i in range(until):
            if self.sent[i] is not None:
                which, source, target, to, cond = self.sent[i]
                only(cond, lambda: self._make(which, source, target, to).wait_send())
                self.sent[i] = None

    def left(self, which):
        for i, entry in enumerate(self.sent):
            if entry is not None and entry[0] == which:
                _, source, target, to, cond = entry
                only(cond, lambda: self._make(which, source, target, to).wait_send())
                self.sent[i] = None

    def mark(self):
        return len(self.sent)


def only(cond, action):
    if cond is None:
        action()
    else:
        pl.when(cond)(action)


class Place:
    def __init__(self):
        self.z, self.p = lax.axis_index(RING), lax.axis_index(PAIR)
        self.c, self.y = lax.axis_index(CORE), lax.axis_index(TENSOR)
        self.rank = (self.z * 2 + self.p) * 2 + self.c
        self.pair, self.core = {PAIR: 1 - self.p}, {CORE: 1 - self.c}
        self.cross = {PAIR: 1 - self.p, CORE: 1 - self.c}
        self.other = {TENSOR: 1 - self.y}
        self.near = {RING: self.z + 1 - 2 * (self.z % 2)}
        self.far = {RING: self.z + 2 - 4 * (self.z // 2)}
        self.right, self.left = {RING: self.z + 1}, {RING: self.z - 1}
        self.has_right, self.has_left = self.z < LINE - 1, self.z > 0

    def ranked(self, rank):
        return {RING: rank // 4, PAIR: (rank // 2) % 2, CORE: rank % 2}

    def meet(self):
        barrier = pltpu.get_barrier_semaphore()

        def greet(to, cond=None):
            only(
                cond,
                lambda: pl.semaphore_signal(
                    barrier, inc=1, device_id=to, device_id_type=pl.DeviceIdType.MESH
                ),
            )

        for to in (self.pair, self.core, self.cross, self.other):
            greet(to)
        greet(self.far)
        greet(self.right, self.has_right)
        greet(self.left, self.has_left)
        for back in range(1, BACK + 1):
            greet(self.ranked(self.rank + back), self.rank + back < 4 * LINE)
            greet(self.ranked(self.rank - back), self.rank >= back)
        line = jnp.minimum(self.z, 1) + jnp.minimum(LINE - 1 - self.z, 1)
        reach = jnp.minimum(self.rank, BACK) + jnp.minimum(4 * LINE - 1 - self.rank, BACK)
        pl.semaphore_wait(barrier, 5 + line + reach)


class LineFlow:
    def __init__(self, copies, place, block):
        self.copies, self.place, self.block = copies, place, block
        self.ids = {(way, step): copies.new() for way in (1, -1) for step in range(1, LINE)}

    def valid(self, way, step):
        z = self.place.z
        return z >= step if way == 1 else z + step <= LINE - 1

    def origin(self, way, step):
        return self.place.z - way * step

    def onward(self, way, step, source):
        if step == LINE - 1:
            return
        to = self.place.right if way == 1 else self.place.left
        there = self.place.has_right if way == 1 else self.place.has_left
        if step:
            there = there & self.valid(way, step)
        target = self.block(self.origin(way, step))
        self.copies.send(self.ids[way, step + 1], source, target, to, there)

    def start(self, source):
        self.onward(1, 0, source)
        self.onward(-1, 0, source)

    def arrive(self, step, then=None):
        for way in (1, -1):

            def take(way=way):
                target = self.block(self.origin(way, step))
                via = self.place.left if way == 1 else self.place.right
                self.copies.receive(self.ids[way, step], target, via)

            pl.when(self.valid(way, step))(take)
            if step < LINE - 1:
                self.onward(way, step, self.block(self.origin(way, step)))
            if then is not None:
                then(way, step)


class RowsFlow:
    def __init__(self, copies, place, shard, whole):
        self.copies, self.place, self.shard, self.whole = copies, place, shard, whole
        self.line = LineFlow(copies, place, lambda origin: self.rows(origin, place.p, place.c))
        items = [(0, 0)] + [(way, step) for step in range(1, LINE) for way in (1, -1)]
        self.items = items
        self.pair_ids = {item: copies.new() for item in items}
        self.core_ids = {item: copies.new() for item in items}
        self.cross_ids = {item: copies.new() for item in items}

    def rows(self, origin, p, c):
        count = self.shard.shape[0]
        return self.whole.at[pl.ds(pl.multiple_of((origin * 4 + p * 2 + c) * count, count), count)]

    def valid(self, item):
        return None if item == (0, 0) else self.line.valid(*item)

    def spread(self, way, step):
        item, place = (way, step), self.place
        here = self.rows(self.line.origin(way, step), place.p, place.c)
        self.copies.send(self.pair_ids[item], here, here, place.pair, self.valid(item))
        self.copies.send(self.core_ids[item], here, here, place.core, self.valid(item))

    def start(self, own_copy):
        self.line.start(self.shard)
        own_copy()
        self.spread(0, 0)

    def arrive(self, step):
        self.line.arrive(step, self.spread)

    def crossing(self, step):
        place = self.place
        for item in self.items:
            if item[1] != step:
                continue
            there = self.rows(self.line.origin(*item), 1 - place.p, place.c)
            only(
                self.valid(item),
                lambda: self.copies.receive(self.pair_ids[item], there, place.pair),
            )
            self.copies.send(self.cross_ids[item], there, there, place.core, self.valid(item))

    def end(self):
        place = self.place
        for item in self.items:
            origin = self.line.origin(*item)

            def take(item=item, origin=origin):
                mine = self.rows(origin, place.p, 1 - place.c)
                cross = self.rows(origin, 1 - place.p, 1 - place.c)
                self.copies.receive(self.core_ids[item], mine, place.core)
                self.copies.receive(self.cross_ids[item], cross, place.core)

            only(self.valid(item), take)


class QuarterFlow:
    def __init__(self, copies, place, shard, whole, own_sem):
        self.copies, self.place, self.shard, self.whole = copies, place, shard, whole
        self.count, self.width = shard.shape[0], whole.shape[1]
        self.own = pltpu.make_async_copy(
            self.columns(place.p, place.c), self.rows(place.p, place.c), own_sem
        )
        self.near = (
            (copies.new(), 1 - place.p, place.c, place.pair),
            (copies.new(), place.p, 1 - place.c, place.core),
            (copies.new(), 1 - place.p, 1 - place.c, place.cross),
        )
        self.line = LineFlow(copies, place, self.block)

    def columns(self, p, c):
        width = self.width
        return self.shard.at[:, pl.ds(pl.multiple_of((p * 2 + c) * width, LANES), width)]

    def rows(self, p, c):
        count = self.count
        start = (self.place.z * 4 + p * 2 + c) * count
        return self.whole.at[pl.ds(pl.multiple_of(start, count), count)]

    def block(self, origin):
        count = 4 * self.count
        return self.whole.at[pl.ds(pl.multiple_of(origin * count, count), count)]

    def start(self):
        place = self.place
        self.own.start()
        for which, p, c, to in self.near:
            self.copies.send(which, self.columns(p, c), self.rows(place.p, place.c), to)

    def join(self):
        self.own.wait()
        for which, p, c, to in self.near:
            self.copies.receive(which, self.rows(p, c), to)
        self.line.start(self.block(self.place.z))

    def arrive(self, step):
        self.line.arrive(step)


class FourFlow:
    def __init__(self, copies, place, slots, parts):
        self.copies, self.place, self.slots = copies, place, slots
        self.rows = slots.shape[0] // 4
        self.size = self.rows // parts
        self.ids = [[copies.new() for _ in range(3)] for _ in range(parts)]

    def slot(self, which, part):
        return self.slots.at[pl.ds(which * self.rows + part * self.size, self.size)]

    def send(self, part, source):
        self.copies.send(self.ids[part][0], source, self.slot(1, part), self.place.pair)
        self.copies.send(self.ids[part][1], source, self.slot(2, part), self.place.core)

    def cross(self, part):
        got = self.slot(1, part)
        self.copies.receive(self.ids[part][0], got, self.place.pair)
        self.copies.send(self.ids[part][2], got, self.slot(3, part), self.place.core)

    def end(self, part):
        self.copies.receive(self.ids[part][1], self.slot(2, part), self.place.core)
        self.copies.receive(self.ids[part][2], self.slot(3, part), self.place.core)


def fetch(source, target, sem):
    copy = pltpu.make_async_copy(source, target, sem)
    copy.start()
    copy.wait()


def add_to(target, source):
    target[...] = low(wide(target[...]) + wide(source[...]))


class LineScatter:
    def __init__(self, copies, place, block, arrived, stage, sem):
        self.copies, self.place, self.block = copies, place, block
        self.arrived, self.stage, self.sem = arrived, stage, sem
        self.ids = {(way, step): copies.new() for way in (1, -1) for step in range(1, LINE)}

    def landing(self, way, step):
        return self.arrived.at[(1 - way) // 2, step - 1]

    def target(self, way, step):
        return self.block(self.place.z + way * (LINE - step))

    def takes(self, way, step):
        z = self.place.z
        if way == 1:
            return (z >= 1) & (z <= step)
        return (z <= LINE - 2) & (z >= LINE - 1 - step)

    def send(self, way, step, cond):
        to = self.place.right if way == 1 else self.place.left
        self.copies.send(
            self.ids[way, step], self.target(way, step), self.landing(way, step), to, cond
        )

    def start(self):
        for step in range(1, LINE):
            self.send(1, step, self.place.z == 0)
            self.send(-1, step, self.place.z == LINE - 1)

    def take(self, way, step):
        via = self.place.left if way == 1 else self.place.right
        self.copies.receive(self.ids[way, step], self.landing(way, step), via)
        fetch(self.landing(way, step), self.stage, self.sem)

    def step(self, step):
        for way in (1, -1):
            there = self.takes(way, step - 1)

            def add(way=way):
                self.take(way, step - 1)
                add_to(self.target(way, step), self.stage)

            pl.when(there)(add)
            self.send(way, step, there)

    def finish(self, add):
        for way in (1, -1):

            def last(way=way):
                self.take(way, LINE - 1)
                add()

            pl.when(self.takes(way, LINE - 1))(last)


class QuarterScatter:
    def __init__(self, copies, place, grad, owner, arrived, stage, sem):
        self.copies, self.place, self.grad, self.owner, self.sem = copies, place, grad, owner, sem
        self.stage = stage
        self.count, self.width = owner.shape[0], grad.shape[1]
        self.line = LineScatter(copies, place, self.block, arrived, stage, sem)
        self.near = (
            (copies.new(), 1 - place.p, place.c, place.pair),
            (copies.new(), place.p, 1 - place.c, place.core),
            (copies.new(), 1 - place.p, 1 - place.c, place.cross),
        )

    def block(self, origin):
        count = 4 * self.count
        return self.grad.at[pl.ds(pl.multiple_of(origin * count, count), count)]

    def rows(self, p, c):
        count = self.count
        start = (self.place.z * 4 + p * 2 + c) * count
        return self.grad.at[pl.ds(pl.multiple_of(start, count), count)]

    def columns(self, p, c):
        width = self.width
        return self.owner.at[:, pl.ds(pl.multiple_of((p * 2 + c) * width, LANES), width)]

    def finish(self):
        place = self.place
        self.line.finish(lambda: add_to(self.block(place.z), self.stage))
        for which, p, c, to in self.near:
            self.copies.send(which, self.rows(p, c), self.columns(place.p, place.c), to)
        fetch(self.rows(place.p, place.c), self.columns(place.p, place.c), self.sem)

    def end(self):
        for which, p, c, to in self.near:
            self.copies.receive(which, self.columns(p, c), to)


class RowsScatter:
    def __init__(self, copies, place, whole, from_core, from_pair, arrived, stage, sem):
        self.copies, self.place, self.whole, self.sem = copies, place, whole, sem
        self.from_core, self.from_pair = from_core, from_pair
        self.count, self.columns = from_pair.shape[1], from_pair.shape[2]
        self.stage = stage
        self.core_id = copies.new()
        self.pair_ids = [copies.new() for _ in range(LINE)]
        self.line = LineScatter(
            copies, place, lambda d: self.part(place.c, place.p, d), arrived, self.small(1), sem
        )

    def small(self, blocks):
        return self.stage.at[pl.ds(0, blocks * self.count), pl.ds(0, self.columns)]

    def part(self, c, p, origin, blocks=1):
        start = ((c * 2 + p) * LINE + origin) * self.count
        return self.whole.at[
            pl.ds(pl.multiple_of(start, self.count), blocks * self.count), pl.ds(0, self.columns)
        ]

    def fill(self, origin, value):
        for p in range(2):
            for c in range(2):
                start = (p * 2 + c) * self.count
                self.part(c, p, origin)[...] = value[start : start + self.count]

    def start(self):
        place = self.place
        self.copies.send(
            self.core_id, self.part(1 - place.c, 0, 0, 2 * LINE), self.from_core, place.core
        )

    def halve(self):
        place = self.place
        self.copies.receive(self.core_id, self.from_core, place.core)
        size = LINE * self.count
        for p in (1 - place.p, place.p):
            start = pl.multiple_of(p * size, size)
            fetch(self.from_core.at[pl.ds(start, size)], self.small(LINE), self.sem)
            add_to(self.part(place.c, p, 0, LINE), self.small(LINE))
            if p is place.p:
                continue
            for origin in (3, 0, 2, 1):
                self.copies.send(
                    self.pair_ids[origin],
                    self.part(place.c, p, origin),
                    self.from_pair.at[origin],
                    place.pair,
                )

    def quarter(self):
        place = self.place
        for origin in (3, 0, 2, 1):
            self.copies.receive(self.pair_ids[origin], self.from_pair.at[origin], place.pair)
            fetch(self.from_pair.at[origin], self.small(1), self.sem)
            add_to(self.part(place.c, place.p, origin), self.small(1))
        self.line.start()

    def finish(self, out):
        out[...] = wide(self.part(self.place.c, self.place.p, self.place.z)[...])

        def add():
            out[...] += wide(self.small(1)[...])

        self.line.finish(add)


PARTS = 4
N_REMOTE = 200
SUM_ROWS = 32


def eight_rows(value):
    return jnp.sum(value.reshape(-1, 8, value.shape[-1]), axis=0)


def layer_kernel(
    heads,
    head_size,
    tokens,
    first_shard,
    out_shard,
    gate_shard,
    up_shard,
    down_shard,
    grad_out,
    biases,
    cosine,
    sine,
    own_segments,
    own_positions,
    key_segments,
    key_positions,
    output,
    input_grad,
    grad_first,
    grad_w_out,
    grad_w_down,
    grad_w_gate,
    grad_w_up,
    sums_out,
    first_kept,
    line_landing,
    out_core_landing,
    out_pair_landing,
    out_other_landing,
    first_core_landing,
    first_pair_landing,
    first_line_landing,
    wo_core_landing,
    wo_pair_landing,
    wo_line_landing,
    first_all,
    w_out_all,
    state,
    window,
    keys,
    values,
    mail,
    first_normed,
    query,
    heads_out,
    gate_all,
    up_all,
    down_all,
    normed_four,
    grad_four,
    hidden,
    grad_gate,
    grad_up,
    pair_landing,
    other_landing,
    stage,
    grad_keys,
    grad_values,
    own_grad,
    window_landing,
    first_scale,
    second_scale,
    totals,
    sums,
    sums_landing,
    send_sems,
    recv_sems,
    local_sems,
):
    place = Place()
    copies = Copies(send_sems, recv_sems)
    rows, width = tokens.shape
    batches = own_segments.shape[0]
    per_batch = rows // batches
    query_width = heads * head_size
    kv_width = query_width + 2 * head_size
    size = rows // PARTS
    root = 1.0 / math.sqrt(head_size)
    sem = local_sems.at[0]

    window[...] = jnp.zeros_like(window)
    place.meet()

    first = RowsFlow(copies, place, first_shard, first_all)
    outs = RowsFlow(copies, place, out_shard, w_out_all)
    gates, ups, downs = [
        QuarterFlow(copies, place, shard, whole, local_sems.at[2 + i])
        for i, (shard, whole) in enumerate(
            ((gate_shard, gate_all), (up_shard, up_all), (down_shard, down_all))
        )
    ]
    cot = FourFlow(copies, place, grad_four, 1)
    second = FourFlow(copies, place, normed_four, PARTS)
    part_ids = [copies.new() for _ in range(PARTS)]
    window_ids = [copies.new() for _ in range(BACK)]

    def put(flow, sem):
        return lambda: fetch(flow.shard, flow.rows(place.z, place.p, place.c), sem)

    first.start(put(first, sem))
    gates.start()
    x = wide(tokens[...])
    first_scale[...] = lax.rsqrt(jnp.mean(x * x, axis=-1, keepdims=True) + EPSILON)
    state[...] = x * first_scale[...]
    first.crossing(0)
    first.arrive(1)
    ups.start()
    first.crossing(1)
    gates.join()
    first.arrive(2)
    first.crossing(2)
    first.arrive(3)
    downs.start()
    first.crossing(3)
    ups.join()
    first.end()

    gains = wide(first_all[:, kv_width:]).T
    first_gain, second_gain = gains[0:1], gains[1:2]
    first_normed[...] = low(state[...] * first_gain)
    sign = jnp.where(
        lax.broadcasted_iota(jnp.int32, (1, head_size), 1) < head_size // 2, -1.0, 1.0
    )

    def project(start, size):
        raw = matmul(first_normed[...], first_all[:, start : start + size])
        return raw + biases[:, start : start + size]

    def turned(raw):
        half_turn = pltpu.roll(raw, head_size // 2, 1)
        return low(raw * cosine[...] + half_turn * (sine[...] * sign))

    def turned_back(gradient, mine):
        half_turn = pltpu.roll(gradient * sine[mine], head_size // 2, 1)
        return low(gradient * cosine[mine] - half_turn * sign)

    kv = project(query_width, 2 * head_size)
    key_now, value_now = turned(kv[:, :head_size]), low(kv[:, head_size:])
    for b in range(batches):
        mine = slice(b * per_batch, (b + 1) * per_batch)
        window[BACK, b, :, :head_size] = key_now[mine]
        window[BACK, b, :, head_size:] = value_now[mine]
    for back in range(1, BACK + 1):
        copies.send(
            window_ids[back - 1],
            window.at[BACK],
            window.at[BACK - back],
            place.ranked(place.rank + back),
            place.rank + back < 4 * LINE,
        )
    outs.start(put(outs, sem))
    for h in range(0, heads, 2):
        raw = project(h * head_size, 2 * head_size)
        query[:, h * head_size : (h + 1) * head_size] = turned(raw[:, :head_size])
        query[:, (h + 1) * head_size : (h + 2) * head_size] = turned(raw[:, head_size:])
    keep_first = pltpu.make_async_copy(first_all, first_kept, local_sems.at[1])
    keep_first.start()
    cot_own = pltpu.make_async_copy(grad_out, cot.slot(0, 0), local_sems.at[5])
    cot_own.start()
    cot.send(0, grad_out)
    outs.crossing(0)
    outs.arrive(1)
    outs.crossing(1)
    gates.arrive(1)
    outs.arrive(2)
    outs.crossing(2)
    for back in range(1, BACK + 1):
        only(
            place.rank >= back,
            lambda: copies.receive(
                window_ids[back - 1], window.at[BACK - back], place.ranked(place.rank - back)
            ),
        )

    def take_window(b):
        for slot in range(BACK + 1):
            keys[slot * per_batch : (slot + 1) * per_batch] = window[slot, b, :, :head_size]
            values[slot * per_batch : (slot + 1) * per_batch] = window[slot, b, :, head_size:]

    def probabilities(b, mine, columns):
        scores = times_transpose(query[mine, columns], keys[...]) * root
        allowed = (own_segments[b] == key_segments[b]) & (key_positions[b] <= own_positions[b])
        scores = jnp.where(allowed, scores, NEGATIVE)
        weights = jnp.exp(scores - jnp.max(scores, axis=-1, keepdims=True))
        return weights * (1.0 / jnp.sum(weights, axis=-1, keepdims=True))

    part_own, part_other = mail.at[pl.ds(0, rows)], mail.at[pl.ds(rows, rows)]
    for b in range(batches):
        take_window(b)
        mine = slice(b * per_batch, (b + 1) * per_batch)

        def attend_head(h, carry, b=b, mine=mine):
            columns = pl.ds(pl.multiple_of(h * head_size, head_size), head_size)
            probs = low(probabilities(b, mine, columns))
            heads_out[mine, columns] = low(matmul(probs, values[...]))
            return carry

        lax.fori_loop(0, heads, attend_head, 0)
        if b == 0:
            outs.arrive(3)
            outs.crossing(3)
            outs.end()
            ups.arrive(1)
        part = low(times_transpose(heads_out[mine], w_out_all[...]))
        part_own[mine] = part
        for i in range(b * per_batch // size, (b + 1) * per_batch // size):
            block = pl.ds(i * size, size)
            copies.send(part_ids[i], part_own.at[block], part_other.at[block], place.other)
    early = copies.mark()
    gates.arrive(2)

    for i in range(PARTS):
        block = pl.ds(i * size, size)
        copies.receive(part_ids[i], part_other.at[block], place.other)
        copies.left(part_ids[i])
        row_sum = wide(tokens[block]) + (wide(part_own[block]) + wide(part_other[block]))
        state[block] = row_sum
        scale_row = lax.rsqrt(jnp.mean(row_sum * row_sum, axis=-1, keepdims=True) + EPSILON)
        second_scale[block] = scale_row
        second.slot(0, i)[...] = low(row_sum * scale_row * second_gain)
        second.send(i, second.slot(0, i))
        if i > 0:
            second.cross(i - 1)
    ups.arrive(2)
    second.cross(PARTS - 1)
    downs.join()
    cot.cross(0)
    keep_first.wait()
    for i in range(PARTS):
        second.end(i)
    cot_own.wait()
    gates.arrive(3)
    ups.arrive(3)

    tile = 256

    def forward_tile(t, carry):
        block = pl.ds(pl.multiple_of(t * tile, tile), tile)
        gate = matmul(normed_four[block], gate_all[...])
        up = matmul(normed_four[block], up_all[...])
        sigmoid = 1.0 / (1.0 + jnp.exp(-gate))
        silu = gate * sigmoid
        hidden[block] = low(silu * up)
        grad_up[block] = low(silu)
        grad_gate[block] = low(up * sigmoid * (1.0 + gate * (1.0 - sigmoid)))
        return carry

    lax.fori_loop(0, 4 * rows // tile, forward_tile, 0)
    cot.end(0)
    downs.arrive(1)
    copies.settle(early)
    grad_down = first_all

    def columns_of(d):
        return pl.ds(pl.multiple_of(d * rows, rows), rows)

    def weight_grad(target, left_side, right_side):
        def block(d, carry):
            part = contract_rows(left_side[:, columns_of(d)], right_side[...])
            target[columns_of(d)] = low(part)
            return carry

        lax.fori_loop(0, LINE, block, 0)

    scatters = [
        QuarterScatter(copies, place, grad, owner, line_landing.at[i], stage, sem)
        for i, (grad, owner) in enumerate(
            ((grad_down, grad_w_down), (up_all, grad_w_up), (gate_all, grad_w_gate))
        )
    ]
    down_back, up_back, gate_back = scatters
    weight_grad(grad_down, grad_four, hidden)
    late = copies.mark()
    down_back.line.start()
    downs.arrive(2)
    downs.arrive(3)

    def backward_tile(t, carry):
        block = pl.ds(pl.multiple_of(t * tile, tile), tile)
        back = matmul(grad_four[block], down_all[...])
        grad_gate[block] = low(back * wide(grad_gate[block]))
        grad_up[block] = low(back * wide(grad_up[block]))
        return carry

    lax.fori_loop(0, 4 * rows // tile, backward_tile, 0)
    copies.settle(late)

    normed_grad = grad_four
    core_ids = [copies.new() for _ in range(2)]
    pair_ids = [copies.new() for _ in range(PARTS)]
    other_ids = [copies.new() for _ in range(PARTS)]

    def slot(which, part=0, parts=1):
        return pl.ds(which * rows + part * (rows // parts), rows // parts)

    def normed_tile(t, carry):
        block = columns_of(3 - t)
        normed_grad[block] = low(
            times_transpose(grad_gate[block], gate_all[...])
            + times_transpose(grad_up[block], up_all[...])
        )
        return carry

    lax.fori_loop(0, 2, normed_tile, 0)
    for i in (1, 0):
        copies.send(
            core_ids[i],
            normed_grad.at[slot(2 + i)],
            mail.at[pl.ds(i * rows, rows)],
            place.core,
        )
    lax.fori_loop(2, 4, normed_tile, 0)
    copies.receive(core_ids[1], mail.at[pl.ds(rows, rows)], place.core)
    for i in range(PARTS):
        block = slot(1, i, PARTS)
        add_to(normed_grad.at[block], mail.at[pl.ds(rows + i * size, size)])
        copies.send(
            pair_ids[i],
            normed_grad.at[block],
            pair_landing.at[pl.ds(i * size, size)],
            place.pair,
        )
    copies.receive(core_ids[0], mail.at[pl.ds(0, rows)], place.core)
    add_to(normed_grad.at[slot(0)], mail.at[pl.ds(0, rows)])
    weight_grad(up_all, normed_four, grad_up)
    up_back.line.start()
    down_back.line.step(2)
    out_sum = normed_four
    out_core_id, out_pair_id, out_other_id = copies.new(), copies.new(), copies.new()
    first_weights = hidden
    first_fetch = pltpu.make_async_copy(first_kept, first_weights, local_sems.at[6])

    def out_tile(t, carry):
        block = columns_of(t)
        out_sum[block] = low(times_transpose(hidden[block], down_all[...]))
        return carry

    for i in range(PARTS):
        block = pl.ds(i * size, size)
        copies.receive(pair_ids[i], pair_landing.at[block], place.pair)
        add_to(normed_grad.at[block], pair_landing.at[block])
        copies.send(other_ids[i], normed_grad.at[block], other_landing.at[block], place.other)
        if i == 0:
            weight_grad(gate_all, normed_four, grad_gate)
            gate_back.line.start()
        if i == 1:
            lax.fori_loop(0, 4, out_tile, 0)
            copies.send(
                out_core_id, out_sum.at[pl.ds(2 * rows, 2 * rows)], out_core_landing, place.core
            )
            first_fetch.start()
    down_back.line.step(3)
    grad_own = mail.at[pl.ds(rows, rows)]
    grad_branch = mail.at[pl.ds(0, rows)]
    fetch(grad_out, grad_own, sem)
    second_sum = totals.at[:, pl.ds(kv_width, width)]
    second_sum[...] = jnp.zeros_like(second_sum)
    for i in range(PARTS):
        block = pl.ds(i * size, size)
        copies.receive(other_ids[i], other_landing.at[block], place.other)
        back = wide(normed_grad[block]) + wide(other_landing[block])
        scale_row = second_scale[block]
        unit = state[block] * scale_row
        second_sum[...] += eight_rows(back * unit)
        grad_state = wide(grad_own[block]) + norm_back(back, unit, scale_row, second_gain)
        input_grad[block] = grad_state
        grad_branch[block] = low(grad_state)

    grad_heads = grad_up.at[pl.ds(0, rows), pl.ds(0, query_width)]
    grad_raw = grad_up.at[pl.ds(rows, rows), pl.ds(0, kv_width)]
    grad_heads[...] = low(matmul(grad_branch[...], w_out_all[...]))
    wo_back = RowsScatter(
        copies, place, w_out_all, wo_core_landing, wo_pair_landing, wo_line_landing, stage, sem
    )
    for origin in range(LINE):
        branch = grad_branch[:, origin * rows : (origin + 1) * rows]
        wo_back.fill(origin, low(contract_rows(branch, heads_out[...])))
    wo_back.start()
    down_back.finish()
    back_ids = [[copies.new() for _ in range(batches)] for _ in range(BACK)]
    for b in range(batches):
        take_window(b)
        mine = slice(b * per_batch, (b + 1) * per_batch)
        grad_keys[...] = jnp.zeros_like(grad_keys)
        grad_values[...] = jnp.zeros_like(grad_values)

        def attend_back_head(h, carry, b=b, mine=mine):
            columns = pl.ds(pl.multiple_of(h * head_size, head_size), head_size)
            probs = probabilities(b, mine, columns)
            grad_head = grad_heads[mine, columns]
            grad_probs = times_transpose(grad_head, values[...])
            row_inner = jnp.sum(probs * grad_probs, axis=-1, keepdims=True)
            grad_scores = low(probs * (grad_probs - row_inner))
            grad_raw[mine, columns] = turned_back(matmul(grad_scores, keys[...]) * root, mine)
            grad_keys[...] += contract_rows(grad_scores, query[mine, columns])
            grad_values[...] += contract_rows(low(probs), grad_head)
            return carry

        lax.fori_loop(0, heads, attend_back_head, 0)
        for s in range(BACK):
            there = slice(s * per_batch, (s + 1) * per_batch)
            window[s, b, :, :head_size] = low(grad_keys[there] * root)
            window[s, b, :, head_size:] = low(grad_values[there])
        there = slice(BACK * per_batch, (BACK + 1) * per_batch)
        own_grad[mine, :head_size] = grad_keys[there] * root
        own_grad[mine, head_size:] = grad_values[there]
        for back in range(1, BACK + 1):
            copies.send(
                back_ids[back - 1][b],
                window.at[BACK - back, b],
                window_landing.at[back - 1, b],
                place.ranked(place.rank - back),
                place.rank >= back,
            )
        if b == 0:
            wo_back.halve()
            up_back.line.step(2)
    wo_back.quarter()
    for back in range(1, BACK + 1):
        for b in range(batches):
            mine = slice(b * per_batch, (b + 1) * per_batch)

            def take(back=back, b=b, mine=mine):
                landing = window_landing.at[back - 1, b]
                copies.receive(back_ids[back - 1][b], landing, place.ranked(place.rank + back))
                own_grad[mine] += wide(landing[...])

            pl.when(place.rank + back < 4 * LINE)(take)
    every = slice(0, rows)
    grad_raw[:, query_width : query_width + head_size] = turned_back(
        own_grad[:, :head_size], every
    )
    grad_raw[:, query_width + head_size :] = low(own_grad[:, head_size:])
    first_back = RowsScatter(
        copies,
        place,
        grad_gate,
        first_core_landing,
        first_pair_landing,
        first_line_landing,
        stage,
        sem,
    )
    for origin in range(LINE):
        normed = first_normed[:, origin * rows : (origin + 1) * rows]
        first_back.fill(origin, low(contract_rows(normed, grad_raw[...])))
    first_back.start()

    first_ids = [copies.new() for _ in range(PARTS)]
    sum_ids = [copies.new() for _ in range(5)]
    first_at = kv_width + width
    first_own, first_other = mail.at[pl.ds(0, rows)], pair_landing
    first_fetch.wait()

    def first_tile(t, carry):
        block = pl.ds(pl.multiple_of(t * tile, tile), tile)
        part = times_transpose(grad_raw[...], first_weights[block, :kv_width])
        first_own[:, block] = low(part)
        unit = wide(tokens[:, block]) * first_scale[...]
        at = pl.ds(pl.multiple_of(first_at + t * tile, tile), tile)
        totals[:, at] = eight_rows(part * unit)
        return carry

    lax.fori_loop(0, width // tile, first_tile, 0)
    for i in range(PARTS):
        block = pl.ds(i * size, size)
        copies.send(first_ids[i], first_own.at[block], first_other.at[block], place.other)
    totals[:, :kv_width] = eight_rows(wide(grad_raw[...]))

    def sum_row(t, carry):
        columns = pl.ds(pl.multiple_of(t * LANES, LANES), LANES)
        sums[0, pl.ds(t, 1)] = jnp.sum(totals[:, columns], axis=0, keepdims=True)
        return carry

    lax.fori_loop(0, sums.shape[1], sum_row, 0)
    shared = first_at // LANES

    def sum_step(i, to):
        copies.send(sum_ids[i], sums.at[i], sums_landing.at[i], to)

    def sum_take(i, to):
        copies.receive(sum_ids[i], sums_landing.at[i], to)
        if i < 4:
            sums[i + 1] = sums[i] + sums_landing[i]

    sum_step(0, place.core)
    first_back.halve()
    sum_take(0, place.core)
    sum_step(1, place.pair)
    up_back.line.step(3)
    sum_take(1, place.pair)
    sum_step(2, place.near)

    spare = mail.at[pl.ds(rows, rows)]
    copies.receive(out_core_id, out_core_landing, place.core)
    fetch(out_core_landing.at[pl.ds(rows, rows)], spare, sem)
    add_to(out_sum.at[slot(1)], spare)
    copies.send(out_pair_id, out_sum.at[slot(1)], out_pair_landing, place.pair)
    fetch(out_core_landing.at[pl.ds(0, rows)], spare, sem)
    add_to(out_sum.at[slot(0)], spare)
    first_back.quarter()
    sum_take(2, place.near)
    sum_step(3, place.far)
    for i in range(PARTS):
        block = pl.ds(i * size, size)
        copies.receive(first_ids[i], first_other.at[block], place.other)
        unit = wide(tokens[block]) * first_scale[block]
        back = wide(first_own[block]) + wide(first_other[block])
        input_grad[block] += norm_back(back, unit, first_scale[block], first_gain)
    sum_take(3, place.far)
    sum_step(4, place.other)
    copies.receive(out_pair_id, out_pair_landing, place.pair)
    fetch(out_pair_landing, spare, sem)
    add_to(out_sum.at[slot(0)], spare)
    copies.send(out_other_id, out_sum.at[slot(0)], out_other_landing, place.other)
    up_back.finish()
    wo_back.line.step(2)
    first_back.line.step(2)
    wo_back.line.step(3)
    first_back.line.step(3)
    gate_back.line.step(2)
    sum_take(4, place.other)
    sums_out[...] = sums[4]
    sums_out[shared:] += sums_landing[4, shared:]
    copies.receive(out_other_id, out_other_landing, place.other)
    fetch(out_other_landing, spare, sem)
    spare[...] = low(state[...] + (wide(out_sum[slot(0)]) + wide(spare[...])))
    fetch(spare, output, sem)
    wo_back.finish(grad_w_out)
    first_back.finish(grad_first)
    gate_back.line.step(3)
    gate_back.finish()
    for scatter in scatters:
        scatter.end()
    copies.settle()


def layer_call(heads, head_size, operands):
    tokens, first_shard, out_shard, gate_shard = operands[:4]
    own_segments = operands[10]
    rows, width = tokens.shape
    batches = own_segments.shape[0]
    per_batch = rows // batches
    count, padded = gate_shard.shape
    quarter = padded // 4
    query_width = heads * head_size
    kv_width = query_width + 2 * head_size
    low_type, wide_type = jnp.bfloat16, jnp.float32
    in_vmem, anywhere = pl.BlockSpec(memory_space=pltpu.VMEM), pl.BlockSpec(memory_space=pl.ANY)

    def shape(*dims, kind=low_type):
        return jax.ShapeDtypeStruct(dims, kind)

    def vmem(*dims, kind=low_type):
        return pltpu.VMEM(dims, kind)

    sum_rows = (kv_width + 2 * width) // LANES
    outs = (
        (shape(rows, width), anywhere),
        (shape(rows, width, kind=wide_type), in_vmem),
        (shape(count, kv_width, kind=wide_type), in_vmem),
        (shape(count, query_width, kind=wide_type), in_vmem),
        (shape(count, padded), anywhere),
        (shape(count, padded), anywhere),
        (shape(count, padded), anywhere),
        (shape(sum_rows, LANES, kind=wide_type), in_vmem),
    )
    kept = (
        shape(width, first_shard.shape[1]),
        shape(3, 2, LINE - 1, 4 * count, quarter),
        shape(2 * rows, width),
        shape(rows, width),
        shape(rows, width),
        shape(2 * LINE * count, kv_width),
        shape(LINE, count, kv_width),
        shape(2, LINE - 1, count, kv_width),
        shape(2 * LINE * count, query_width),
        shape(LINE, count, query_width),
        shape(2, LINE - 1, count, query_width),
    )
    scratch = (
        vmem(width, first_shard.shape[1]),
        vmem(width, query_width),
        vmem(rows, width, kind=wide_type),
        vmem(BACK + 1, batches, per_batch, 2 * head_size),
        vmem((BACK + 1) * per_batch, head_size),
        vmem((BACK + 1) * per_batch, head_size),
        vmem(2 * rows, width),
        vmem(rows, width),
        vmem(rows, query_width),
        vmem(rows, query_width),
        vmem(width, quarter),
        vmem(width, quarter),
        vmem(width, quarter),
        vmem(4 * rows, width),
        vmem(4 * rows, width),
        vmem(4 * rows, quarter),
        vmem(4 * rows, quarter),
        vmem(4 * rows, quarter),
        vmem(rows, width),
        vmem(rows, width),
        vmem(4 * count, quarter),
        vmem((BACK + 1) * per_batch, head_size, kind=wide_type),
        vmem((BACK + 1) * per_batch, head_size, kind=wide_type),
        vmem(rows, 2 * head_size, kind=wide_type),
        vmem(BACK, batches, per_batch, 2 * head_size),
        vmem(rows, 1, kind=wide_type),
        vmem(rows, 1, kind=wide_type),
        vmem(8, sum_rows * LANES, kind=wide_type),
        vmem(6, sum_rows, LANES, kind=wide_type),
        vmem(5, sum_rows, LANES, kind=wide_type),
        pltpu.SemaphoreType.DMA((N_REMOTE,)),
        pltpu.SemaphoreType.DMA((N_REMOTE,)),
        pltpu.SemaphoreType.DMA((8,)),
    )
    results = pl.pallas_call(
        functools.partial(layer_kernel, heads, head_size),
        out_shape=[out[0] for out in outs] + list(kept),
        in_specs=[in_vmem] + [anywhere] * 6 + [in_vmem] * 7,
        out_specs=[out[1] for out in outs] + [anywhere] * len(kept),
        scratch_shapes=scratch,
        compiler_params=pltpu.CompilerParams(
            collective_id=0, has_side_effects=True, vmem_limit_bytes=VMEM_BYTES
        ),
    )(*operands)
    return results[: len(outs)]


def body(
    tokens,
    norm1_gain,
    query_weight,
    query_bias,
    key_weight,
    key_bias,
    value_weight,
    value_bias,
    output_weight,
    norm2_gain,
    gate_weight,
    up_weight,
    down_weight,
    cotangent,
    segments,
    positions,
):
    batches, count_rows, width = tokens.shape
    heads, head_size = query_bias.shape
    query_width = heads * head_size
    units = gate_weight.shape[1]
    place = lax.axis_index(FSDP)
    row_start = place * count_rows
    rows = batches * count_rows

    gains = jnp.stack([norm1_gain, norm2_gain], axis=1)
    gains = jnp.pad(gains, ((0, 0), (0, LANES - 2)))
    first_shard = jnp.concatenate([query_weight, key_weight, value_weight, gains], axis=1)
    kv_width = query_width + 2 * head_size
    padded = -(-units // (4 * LANES)) * (4 * LANES)

    def spaced(shard):
        return jnp.pad(shard, ((0, 0), (0, padded - units)))

    grad_out = cotangent.reshape(rows, width)
    inputs = wide(tokens.reshape(rows, width))
    biases = jnp.concatenate(
        [query_bias.reshape(-1), key_bias.reshape(-1), value_bias.reshape(-1)]
    )
    own_places = lax.dynamic_slice_in_dim(positions, row_start, count_rows, axis=1)
    cosine, sine_table = rotation(own_places.reshape(-1), head_size)
    if lax.axis_size(RING) == LINE:
        key_segments, key_positions = [], []
        for b in range(batches):
            padding = jnp.full((BACK * count_rows,), -1, jnp.int32)
            for rows_of, padded_rows in ((key_segments, segments), (key_positions, positions)):
                padded_rows = jnp.concatenate([padding, padded_rows[b]])
                rows_of.append(
                    lax.dynamic_slice_in_dim(padded_rows, row_start, (BACK + 1) * count_rows)
                )
        own_segments = lax.dynamic_slice_in_dim(segments, row_start, count_rows, axis=1)
        (
            output,
            input_grad,
            grad_w_qkv,
            grad_w_out,
            grad_w_down,
            grad_w_gate,
            grad_w_up,
            sums,
        ) = layer_call(
            heads,
            head_size,
            (
                tokens.reshape(rows, width),
                first_shard,
                output_weight.T,
                spaced(gate_weight),
                spaced(up_weight),
                spaced(down_weight.T),
                grad_out,
                wide(biases).reshape(1, -1),
                cosine[:, 0],
                sine_table[:, 0],
                own_segments[..., None],
                own_places[..., None],
                jnp.stack(key_segments)[:, None],
                jnp.stack(key_positions)[:, None],
            ),
        )
        sums = sums.reshape(-1)
        grad_w_down, grad_w_gate, grad_w_up = map(wide, (grad_w_down, grad_w_gate, grad_w_up))
    else:
        allowed = [
            visible(segments[b], positions[b], row_start, count_rows) for b in range(batches)
        ]
        first_all = gather_rows(first_shard)
        w_qkv = first_all[:, :kv_width]
        first_gain = wide(first_all[:, kv_width])
        second_gain = wide(first_all[:, kv_width + 1])
        w_out = gather_rows(output_weight.T)
        w_gate = quarter_columns(spaced(gate_weight))
        w_up = quarter_columns(spaced(up_weight))
        w_down = quarter_columns(spaced(down_weight.T))
        grad_out_four = four_blocks(grad_out)
        first_unit, first_scale = root_mean_square_parts(inputs)
        first_normed = low(first_unit * first_gain)
        raw = matmul(first_normed, w_qkv) + wide(biases)
        turned = rotate(
            raw[:, : query_width + head_size].reshape(rows, heads + 1, head_size),
            cosine,
            sine_table,
        )
        turned = low(turned)
        query_rows = turned[:, :heads].reshape(batches, count_rows, heads, head_size)
        key_value = jnp.concatenate(
            [turned[:, heads], low(raw[:, query_width + head_size :])], axis=1
        )
        key_value = key_value.reshape(batches, count_rows, 2 * head_size)
        window = jnp.concatenate(
            [shifted(key_value, back) for back in range(BACK, 0, -1)] + [key_value], axis=1
        )
        key_rows, value_rows = window[..., :head_size], window[..., head_size:]
        attended = [
            attend(query_rows[b], key_rows[b], value_rows[b], allowed[b]) for b in range(batches)
        ]
        log_totals = [log_total for _, log_total in attended]
        heads_out = jnp.concatenate([mixed for mixed, _ in attended], axis=0)
        residual = inputs + tensor_total(times_transpose(heads_out, w_out))
        second_unit, second_scale = root_mean_square_parts(residual)
        second_normed = four_blocks(low(second_unit * second_gain))

        second_unit, second_scale = root_mean_square_parts(residual)
        gate_value = matmul(second_normed, w_gate)
        up_part = matmul(second_normed, w_up)
        sigmoid_gate = jax.nn.sigmoid(gate_value)
        silu_gate = gate_value * sigmoid_gate
        hidden = low(silu_gate * up_part)
        grad_hidden = matmul(grad_out_four, w_down)
        grad_gate = low(
            grad_hidden * up_part * sigmoid_gate * (1.0 + gate_value * (1.0 - sigmoid_gate))
        )
        grad_up = low(grad_hidden * silu_gate)
        second_back = four_sums(times_transpose(grad_gate, w_gate) + times_transpose(grad_up, w_up))
        grad_w_down = quarter_to_owner(low(contract_rows(grad_out_four, hidden)))
        grad_w_gate = quarter_to_owner(low(contract_rows(second_normed, grad_gate)))
        grad_w_up = quarter_to_owner(low(contract_rows(second_normed, grad_up)))
        output = low(residual + four_sums(times_transpose(hidden, w_down)))

        second_gain_sum = jnp.sum(second_back * second_unit, axis=0)
        grad_state = wide(grad_out) + norm_back(second_back, second_unit, second_scale, second_gain)
        grad_branch = low(grad_state)
        grad_w_out = scatter_rows(contract_rows(grad_branch, heads_out))
        grad_heads = low(matmul(grad_branch, w_out)).reshape(query_rows.shape)
        backs = [
            attend_back(
                grad_heads[b], query_rows[b], key_rows[b], value_rows[b], allowed[b], log_totals[b]
            )
            for b in range(batches)
        ]
        grad_query = jnp.stack([back[0] for back in backs]).reshape(rows, heads, head_size)
        grad_window = jnp.stack([jnp.concatenate([back[1], back[2]], axis=1) for back in backs])
        own_grad = grad_window[:, BACK * count_rows :]
        for back in range(1, BACK + 1):
            first_row = (BACK - back) * count_rows
            own_grad = own_grad + wide(
                shifted(low(grad_window[:, first_row : first_row + count_rows]), -back)
            )
        own_grad = own_grad.reshape(rows, 2, head_size)
        turned_back = rotate_back(
            jnp.concatenate([grad_query, own_grad[:, :1]], axis=1), cosine, sine_table
        )
        grad_raw = low(jnp.concatenate([turned_back, own_grad[:, 1:]], axis=1).reshape(rows, -1))
        grad_w_qkv = scatter_rows(contract_rows(first_normed, grad_raw))
        bias_sum = jnp.sum(wide(grad_raw), axis=0)
        first_back_part = times_transpose(grad_raw, w_qkv)
        first_back = tensor_total(first_back_part)
        first_gain_sum = jnp.sum(first_back * first_unit, axis=0)
        input_grad = grad_state + norm_back(first_back, first_unit, first_scale, first_gain)
        sums = summed_over_fsdp(jnp.concatenate([bias_sum, second_gain_sum, first_gain_sum]))
    bias_total = sums[:kv_width]
    gain_rows = norm1_gain.shape[0]
    second_total = lax.dynamic_slice_in_dim(sums, kv_width + place * gain_rows, gain_rows)
    first_total = lax.dynamic_slice_in_dim(sums, kv_width + width + place * gain_rows, gain_rows)

    return (
        output.reshape(tokens.shape),
        input_grad.reshape(tokens.shape),
        first_total,
        grad_w_qkv[:, :query_width],
        bias_total[:query_width].reshape(query_bias.shape),
        grad_w_qkv[:, query_width : query_width + head_size],
        bias_total[query_width : query_width + head_size].reshape(key_bias.shape),
        grad_w_qkv[:, query_width + head_size :],
        bias_total[query_width + head_size :].reshape(value_bias.shape),
        grad_w_out.T,
        second_total,
        grad_w_gate[:, :units],
        grad_w_up[:, :units],
        grad_w_down[:, :units].T,
    )


def solution(mesh):
    fsdp, tensor = mesh.shape["fsdp"], mesh.shape["tensor"]
    fine = Mesh(mesh.devices.reshape(fsdp // 4, 2, 2, tensor), (RING, PAIR, CORE, TENSOR))
    by_rows, by_columns, by_tensor = P(FSDP, TENSOR), P(TENSOR, FSDP), P(TENSOR, None)
    by_tokens, by_gain = P(None, FSDP, None), P(FSDP)
    placed = (
        by_tokens,
        by_gain,
        by_rows,
        by_tensor,
        by_rows,
        by_tensor,
        by_rows,
        by_tensor,
        by_columns,
        by_gain,
        by_rows,
        by_rows,
        by_columns,
        by_tokens,
        P(),
        P(),
    )
    return jax.shard_map(
        body,
        mesh=fine,
        in_specs=placed,
        out_specs=(
            by_tokens,
            by_tokens,
            by_gain,
            by_rows,
            by_tensor,
            by_rows,
            by_tensor,
            by_rows,
            by_tensor,
            by_columns,
            by_gain,
            by_rows,
            by_rows,
            by_columns,
        ),
        check_vma=False,
    )
```

```python
import functools
import math

import jax
import jax.numpy as jnp
from jax import lax
from jax.experimental import pallas as pl
from jax.experimental.pallas import tpu as pltpu
from jax.sharding import Mesh
from jax.sharding import PartitionSpec as P

BACK = 5
LINE = 4
LANES = 128
VMEM_BYTES = 62 * 1024 * 1024

EPSILON = 1e-06
THETA = 1000000.0
NEGATIVE = -1e30

RING, PAIR, CORE, TENSOR = "ring", "pair", "core", "tensor"
FSDP = (RING, PAIR, CORE)
SWAP = [(0, 1), (1, 0)]


def low(value):
    return value.astype(jnp.bfloat16)


def wide(value):
    return value.astype(jnp.float32)


def matmul(left_side, right_side):
    return jnp.dot(left_side, right_side, preferred_element_type=jnp.float32)


def contract_rows(left_side, right_side):
    return lax.dot_general(
        left_side, right_side, (((0,), (0,)), ((), ())), preferred_element_type=jnp.float32
    )


def times_transpose(left_side, right_side):
    return lax.dot_general(
        left_side, right_side, (((1,), (1,)), ((), ())), preferred_element_type=jnp.float32
    )


def swapped(value, axis):
    return lax.ppermute(value, axis, SWAP)


def in_order(own, other, place, axis):
    first = jnp.where(place == 0, own, other)
    second = jnp.where(place == 0, other, own)
    return jnp.stack([first, second], axis=axis)


def shifted(value, steps):
    count = lax.axis_size(FSDP)
    first, last = (max(0, -steps), min(count, count - steps))
    return lax.ppermute(value, FSDP, [(source, source + steps) for source in range(first, last)])


def summed_over_fsdp(value):
    count = lax.axis_size(FSDP)
    bit = 1
    while bit < count:
        value = value + lax.ppermute(value, FSDP, [(i, i ^ bit) for i in range(count)])
        bit *= 2
    return value


def line_gather(block):
    count, here = lax.axis_size(RING), lax.axis_index(RING)
    if count > LINE:
        return lax.all_gather(block, RING, axis=0)
    right, left = [block], [block]
    for step in range(1, count):
        right.append(
            lax.ppermute(right[-1], RING, [(i, i + 1) for i in range(step - 1, count - 1)])
        )
        left.append(
            lax.ppermute(left[-1], RING, [(i, i - 1) for i in range(1, count - step + 1)])
        )
    result = jnp.zeros((count,) + block.shape, block.dtype)
    for step in range(count):
        piece = block if step == 0 else jnp.where(here >= step, right[step], left[count - step])
        result = lax.dynamic_update_slice_in_dim(
            result, piece[None], (here - step + count) % count, axis=0
        )
    return result


def line_scatter(parts):
    count, here = lax.axis_size(RING), lax.axis_index(RING)
    if count > LINE:
        return wide(lax.psum_scatter(parts, RING, scatter_dimension=0, tiled=False))

    def part(place):
        return lax.dynamic_index_in_dim(parts, place, axis=0, keepdims=False)

    right, left = None, None
    for step in range(1, count):
        to_right, to_left = part(here + count - step), part(here - count + step)
        if step > 1:
            to_right = low(wide(to_right) + wide(right))
            to_left = low(wide(to_left) + wide(left))
        right = lax.ppermute(to_right, RING, [(i, i + 1) for i in range(step)])
        left = lax.ppermute(to_left, RING, [(i, i - 1) for i in range(count - step, count)])
    return wide(part(here)) + wide(right) + wide(left)


def gather_rows(shard):
    rows = line_gather(shard)
    rows = in_order(rows, swapped(rows, PAIR), lax.axis_index(PAIR), 1)
    rows = in_order(rows, swapped(rows, CORE), lax.axis_index(CORE), 2)
    return rows.reshape((-1,) + shard.shape[1:])


def scatter_rows(total):
    pair, core = lax.axis_index(PAIR), lax.axis_index(CORE)
    parts = low(total).reshape((lax.axis_size(RING), 2, 2, -1) + total.shape[1:])

    def halved(value, axis, place, name):
        mine = lax.dynamic_index_in_dim(value, place, axis=axis, keepdims=False)
        sent = lax.dynamic_index_in_dim(value, 1 - place, axis=axis, keepdims=False)
        return low(wide(mine) + wide(swapped(sent, name)))

    parts = halved(parts, 2, core, CORE)
    parts = halved(parts, 1, pair, PAIR)
    return line_scatter(parts)


def quarter_columns(shard):
    pair, core = lax.axis_index(PAIR), lax.axis_index(CORE)
    half = shard.shape[1] // 2

    def halved(value, place, width):
        mine = lax.dynamic_slice_in_dim(value, place * width, width, axis=value.ndim - 1)
        sent = lax.dynamic_slice_in_dim(value, (1 - place) * width, width, axis=value.ndim - 1)
        return mine, sent

    mine, sent = halved(shard, pair, half)
    rows = in_order(mine, swapped(sent, PAIR), pair, 0)
    mine, sent = halved(rows, core, half // 2)
    rows = in_order(mine, swapped(sent, CORE), core, 1)
    rows = line_gather(rows.reshape(-1, half // 2))
    return rows.reshape(-1, half // 2)


def quarter_to_owner(grad):
    pair, core = lax.axis_index(PAIR), lax.axis_index(CORE)
    width = grad.shape[1]
    block = lax.psum_scatter(
        grad.reshape(lax.axis_size(RING), -1, width), RING, scatter_dimension=0, tiled=False
    )
    block = block.reshape(2, 2, -1, width)

    def halved(value, axis, place):
        mine = lax.dynamic_index_in_dim(value, place, axis=axis, keepdims=False)
        sent = lax.dynamic_index_in_dim(value, 1 - place, axis=axis, keepdims=False)
        return mine, sent

    mine, sent = halved(block, 0, pair)
    block = in_order(mine, swapped(sent, PAIR), pair, 0)
    mine, sent = halved(block, 1, core)
    block = in_order(mine, swapped(sent, CORE), core, 1)
    return jnp.concatenate([wide(block[i, j]) for i in range(2) for j in range(2)], axis=1)


def four_blocks(value):
    over = swapped(value, PAIR)
    return jnp.concatenate([value, over, swapped(value, CORE), swapped(over, CORE)], axis=0)


def four_sums(total):
    half = total.shape[0] // 2
    total = total[:half] + wide(swapped(low(total[half:]), CORE))
    total = total[: half // 2] + wide(swapped(low(total[half // 2 :]), PAIR))
    return tensor_total(total)


def tensor_total(partial_sum):
    own = lax.reduce_precision(partial_sum, 8, 7)
    return own + wide(swapped(low(own), TENSOR))


def rotation(places, width):
    half_width = width // 2
    frequency = THETA ** (-(jnp.arange(half_width, dtype=jnp.float32) * 2.0) / width)
    angles = places.astype(jnp.float32)[:, None] * frequency[None, :]
    cosine = jnp.concatenate([jnp.cos(angles), jnp.cos(angles)], axis=-1)[:, None, :]
    sine_table = jnp.concatenate([jnp.sin(angles), jnp.sin(angles)], axis=-1)[:, None, :]
    return (cosine, sine_table)


def rotate(values, cosine, sine_table):
    half_width = values.shape[-1] // 2
    turned = jnp.concatenate([-values[..., half_width:], values[..., :half_width]], axis=-1)
    return values * cosine + turned * sine_table


def rotate_back(gradient, cosine, sine_table):
    half_width = gradient.shape[-1] // 2
    moved_part = gradient * sine_table
    return gradient * cosine + jnp.concatenate(
        [moved_part[..., half_width:], -moved_part[..., :half_width]], axis=-1
    )


def root_mean_square_parts(values):
    scale_row = lax.rsqrt(jnp.mean(values * values, axis=-1, keepdims=True) + EPSILON)
    return (values * scale_row, scale_row)


def norm_back(grad_normed, normalized, scale_row, gain):
    scaled = grad_normed * gain
    return scale_row * (scaled - normalized * jnp.mean(scaled * normalized, axis=-1, keepdims=True))


def visible(seg_row, pos_row, row_start, count_rows):
    pad_rows = BACK * count_rows
    seg_padded = jnp.concatenate([jnp.full((pad_rows,), -1, jnp.int32), seg_row])
    pos_padded = jnp.concatenate([jnp.zeros((pad_rows,), jnp.int32), pos_row])
    key_seg = lax.dynamic_slice_in_dim(seg_padded, row_start, pad_rows + count_rows)
    key_pos = lax.dynamic_slice_in_dim(pos_padded, row_start, pad_rows + count_rows)
    query_seg = lax.dynamic_slice_in_dim(seg_row, row_start, count_rows)
    query_pos = lax.dynamic_slice_in_dim(pos_row, row_start, count_rows)
    return (query_seg[:, None] == key_seg[None, :]) & (key_pos[None, :] <= query_pos[:, None])


def attend(query_rows, key_rows, value_rows, allowed):
    scores = jnp.einsum("thd,sd->hts", query_rows, key_rows, preferred_element_type=jnp.float32)
    scores = scores * (1.0 / math.sqrt(query_rows.shape[-1]))
    scores = jnp.where(allowed, scores, NEGATIVE)
    row_max = jnp.max(scores, axis=-1, keepdims=True)
    log_total = row_max + jnp.log(jnp.sum(jnp.exp(scores - row_max), axis=-1, keepdims=True))
    probs_low = low(jnp.exp(scores - log_total))
    mixed = jnp.einsum("hts,sd->thd", probs_low, value_rows, preferred_element_type=jnp.float32)
    return low(mixed.reshape(query_rows.shape[0], -1)), log_total


def log_total_of(query_rows, key_rows, allowed):
    scores = jnp.einsum("thd,sd->hts", query_rows, key_rows, preferred_element_type=jnp.float32)
    scores = scores * (1.0 / math.sqrt(query_rows.shape[-1]))
    scores = jnp.where(allowed, scores, NEGATIVE)
    row_max = jnp.max(scores, axis=-1, keepdims=True)
    return row_max + jnp.log(jnp.sum(jnp.exp(scores - row_max), axis=-1, keepdims=True))


def attend_back(grad_heads, query_rows, key_rows, value_rows, allowed, log_total):
    scale = 1.0 / math.sqrt(query_rows.shape[-1])
    scores = jnp.einsum("thd,sd->hts", query_rows, key_rows, preferred_element_type=jnp.float32)
    probs = jnp.exp(jnp.where(allowed, scores * scale, NEGATIVE) - log_total)
    grad_probs = jnp.einsum(
        "thd,sd->hts", grad_heads, value_rows, preferred_element_type=jnp.float32
    )
    row_inner = jnp.sum(probs * grad_probs, axis=-1, keepdims=True)
    grad_scores = low(probs * (grad_probs - row_inner))
    grad_query = jnp.einsum(
        "hts,sd->thd", grad_scores, key_rows, preferred_element_type=jnp.float32
    )
    grad_keys = jnp.einsum(
        "hts,thd->sd", grad_scores, query_rows, preferred_element_type=jnp.float32
    )
    grad_values = jnp.einsum(
        "hts,thd->sd", low(probs), grad_heads, preferred_element_type=jnp.float32
    )
    return grad_query * scale, grad_keys * scale, grad_values


def device(**coordinates):
    return {name: place for name, place in coordinates.items()}


class Copies:
    def __init__(self, send_sems, recv_sems):
        self.send_sems, self.recv_sems = send_sems, recv_sems
        self.used = 0
        self.sent = []

    def new(self):
        self.used += 1
        return self.used - 1

    def _make(self, which, source, target, to):
        return pltpu.make_async_remote_copy(
            src_ref=source,
            dst_ref=target,
            send_sem=self.send_sems.at[which],
            recv_sem=self.recv_sems.at[which],
            device_id=to,
            device_id_type=pl.DeviceIdType.MESH,
        )

    def send(self, which, source, target, to, cond=None):
        only(cond, lambda: self._make(which, source, target, to).start())
        self.sent.append((which, source, target, to, cond))

    def receive(self, which, target, via):
        self._make(which, target, target, via).wait_recv()

    def settle(self, until=None):
        until = len(self.sent) if until is None else until
        for i in range(until):
            if self.sent[i] is not None:
                which, source, target, to, cond = self.sent[i]
                only(cond, lambda: self._make(which, source, target, to).wait_send())
                self.sent[i] = None

    def left(self, which):
        for i, entry in enumerate(self.sent):
            if entry is not None and entry[0] == which:
                _, source, target, to, cond = entry
                only(cond, lambda: self._make(which, source, target, to).wait_send())
                self.sent[i] = None

    def mark(self):
        return len(self.sent)


def only(cond, action):
    if cond is None:
        action()
    else:
        pl.when(cond)(action)


class Place:
    def __init__(self):
        self.z, self.p = lax.axis_index(RING), lax.axis_index(PAIR)
        self.c, self.y = lax.axis_index(CORE), lax.axis_index(TENSOR)
        self.rank = (self.z * 2 + self.p) * 2 + self.c
        self.pair, self.core = {PAIR: 1 - self.p}, {CORE: 1 - self.c}
        self.cross = {PAIR: 1 - self.p, CORE: 1 - self.c}
        self.other = {TENSOR: 1 - self.y}
        self.near = {RING: self.z + 1 - 2 * (self.z % 2)}
        self.far = {RING: self.z + 2 - 4 * (self.z // 2)}
        self.right, self.left = {RING: self.z + 1}, {RING: self.z - 1}
        self.has_right, self.has_left = self.z < LINE - 1, self.z > 0

    def ranked(self, rank):
        return {RING: rank // 4, PAIR: (rank // 2) % 2, CORE: rank % 2}

    def meet(self):
        barrier = pltpu.get_barrier_semaphore()

        def greet(to, cond=None):
            only(
                cond,
                lambda: pl.semaphore_signal(
                    barrier, inc=1, device_id=to, device_id_type=pl.DeviceIdType.MESH
                ),
            )

        for to in (self.pair, self.core, self.cross, self.other):
            greet(to)
        greet(self.far)
        greet(self.right, self.has_right)
        greet(self.left, self.has_left)
        for back in range(1, BACK + 1):
            greet(self.ranked(self.rank + back), self.rank + back < 4 * LINE)
            greet(self.ranked(self.rank - back), self.rank >= back)
        line = jnp.minimum(self.z, 1) + jnp.minimum(LINE - 1 - self.z, 1)
        reach = jnp.minimum(self.rank, BACK) + jnp.minimum(4 * LINE - 1 - self.rank, BACK)
        pl.semaphore_wait(barrier, 5 + line + reach)


class LineFlow:
    def __init__(self, copies, place, block):
        self.copies, self.place, self.block = copies, place, block
        self.ids = {(way, step): copies.new() for way in (1, -1) for step in range(1, LINE)}

    def valid(self, way, step):
        z = self.place.z
        return z >= step if way == 1 else z + step <= LINE - 1

    def origin(self, way, step):
        return self.place.z - way * step

    def onward(self, way, step, source):
        if step == LINE - 1:
            return
        to = self.place.right if way == 1 else self.place.left
        there = self.place.has_right if way == 1 else self.place.has_left
        if step:
            there = there & self.valid(way, step)
        target = self.block(self.origin(way, step))
        self.copies.send(self.ids[way, step + 1], source, target, to, there)

    def start(self, source):
        self.onward(1, 0, source)
        self.onward(-1, 0, source)

    def arrive(self, step, then=None):
        for way in (1, -1):

            def take(way=way):
                target = self.block(self.origin(way, step))
                via = self.place.left if way == 1 else self.place.right
                self.copies.receive(self.ids[way, step], target, via)

            pl.when(self.valid(way, step))(take)
            if step < LINE - 1:
                self.onward(way, step, self.block(self.origin(way, step)))
            if then is not None:
                then(way, step)


class RowsFlow:
    def __init__(self, copies, place, shard, whole):
        self.copies, self.place, self.shard, self.whole = copies, place, shard, whole
        self.line = LineFlow(copies, place, lambda origin: self.rows(origin, place.p, place.c))
        items = [(0, 0)] + [(way, step) for step in range(1, LINE) for way in (1, -1)]
        self.items = items
        self.pair_ids = {item: copies.new() for item in items}
        self.core_ids = {item: copies.new() for item in items}
        self.cross_ids = {item: copies.new() for item in items}

    def rows(self, origin, p, c):
        count = self.shard.shape[0]
        return self.whole.at[pl.ds(pl.multiple_of((origin * 4 + p * 2 + c) * count, count), count)]

    def valid(self, item):
        return None if item == (0, 0) else self.line.valid(*item)

    def spread(self, way, step):
        item, place = (way, step), self.place
        here = self.rows(self.line.origin(way, step), place.p, place.c)
        self.copies.send(self.pair_ids[item], here, here, place.pair, self.valid(item))
        self.copies.send(self.core_ids[item], here, here, place.core, self.valid(item))

    def start(self, own_copy):
        self.line.start(self.shard)
        own_copy()
        self.spread(0, 0)

    def arrive(self, step):
        self.line.arrive(step, self.spread)

    def crossing(self, step):
        place = self.place
        for item in self.items:
            if item[1] != step:
                continue
            there = self.rows(self.line.origin(*item), 1 - place.p, place.c)
            only(
                self.valid(item),
                lambda: self.copies.receive(self.pair_ids[item], there, place.pair),
            )
            self.copies.send(self.cross_ids[item], there, there, place.core, self.valid(item))

    def end(self):
        place = self.place
        for item in self.items:
            origin = self.line.origin(*item)

            def take(item=item, origin=origin):
                mine = self.rows(origin, place.p, 1 - place.c)
                cross = self.rows(origin, 1 - place.p, 1 - place.c)
                self.copies.receive(self.core_ids[item], mine, place.core)
                self.copies.receive(self.cross_ids[item], cross, place.core)

            only(self.valid(item), take)


class QuarterFlow:
    def __init__(self, copies, place, shard, whole, own_sem):
        self.copies, self.place, self.shard, self.whole = copies, place, shard, whole
        self.count, self.width = shard.shape[0], whole.shape[1]
        self.own = pltpu.make_async_copy(
            self.columns(place.p, place.c), self.rows(place.p, place.c), own_sem
        )
        self.near = (
            (copies.new(), 1 - place.p, place.c, place.pair),
            (copies.new(), place.p, 1 - place.c, place.core),
            (copies.new(), 1 - place.p, 1 - place.c, place.cross),
        )
        self.line = LineFlow(copies, place, self.block)

    def columns(self, p, c):
        width = self.width
        return self.shard.at[:, pl.ds(pl.multiple_of((p * 2 + c) * width, LANES), width)]

    def rows(self, p, c):
        count = self.count
        start = (self.place.z * 4 + p * 2 + c) * count
        return self.whole.at[pl.ds(pl.multiple_of(start, count), count)]

    def block(self, origin):
        count = 4 * self.count
        return self.whole.at[pl.ds(pl.multiple_of(origin * count, count), count)]

    def start(self):
        place = self.place
        self.own.start()
        for which, p, c, to in self.near:
            self.copies.send(which, self.columns(p, c), self.rows(place.p, place.c), to)

    def join(self):
        self.own.wait()
        for which, p, c, to in self.near:
            self.copies.receive(which, self.rows(p, c), to)
        self.line.start(self.block(self.place.z))

    def arrive(self, step):
        self.line.arrive(step)


class FourFlow:
    def __init__(self, copies, place, slots, parts):
        self.copies, self.place, self.slots = copies, place, slots
        self.rows = slots.shape[0] // 4
        self.size = self.rows // parts
        self.ids = [[copies.new() for _ in range(3)] for _ in range(parts)]

    def slot(self, which, part):
        return self.slots.at[pl.ds(which * self.rows + part * self.size, self.size)]

    def send(self, part, source):
        self.copies.send(self.ids[part][0], source, self.slot(1, part), self.place.pair)
        self.copies.send(self.ids[part][1], source, self.slot(2, part), self.place.core)

    def cross(self, part):
        got = self.slot(1, part)
        self.copies.receive(self.ids[part][0], got, self.place.pair)
        self.copies.send(self.ids[part][2], got, self.slot(3, part), self.place.core)

    def end(self, part):
        self.copies.receive(self.ids[part][1], self.slot(2, part), self.place.core)
        self.copies.receive(self.ids[part][2], self.slot(3, part), self.place.core)


def fetch(source, target, sem):
    copy = pltpu.make_async_copy(source, target, sem)
    copy.start()
    copy.wait()


def add_to(target, source):
    target[...] = low(wide(target[...]) + wide(source[...]))


class LineScatter:
    def __init__(self, copies, place, block, arrived, stage, sem):
        self.copies, self.place, self.block = copies, place, block
        self.arrived, self.stage, self.sem = arrived, stage, sem
        self.ids = {(way, step): copies.new() for way in (1, -1) for step in range(1, LINE)}

    def landing(self, way, step):
        return self.arrived.at[(1 - way) // 2, step - 1]

    def target(self, way, step):
        return self.block(self.place.z + way * (LINE - step))

    def takes(self, way, step):
        z = self.place.z
        if way == 1:
            return (z >= 1) & (z <= step)
        return (z <= LINE - 2) & (z >= LINE - 1 - step)

    def send(self, way, step, cond):
        to = self.place.right if way == 1 else self.place.left
        self.copies.send(
            self.ids[way, step], self.target(way, step), self.landing(way, step), to, cond
        )

    def start(self):
        for step in range(1, LINE):
            self.send(1, step, self.place.z == 0)
            self.send(-1, step, self.place.z == LINE - 1)

    def take(self, way, step):
        via = self.place.left if way == 1 else self.place.right
        self.copies.receive(self.ids[way, step], self.landing(way, step), via)
        fetch(self.landing(way, step), self.stage, self.sem)

    def step(self, step):
        for way in (1, -1):
            there = self.takes(way, step - 1)

            def add(way=way):
                self.take(way, step - 1)
                add_to(self.target(way, step), self.stage)

            pl.when(there)(add)
            self.send(way, step, there)

    def finish(self, add):
        for way in (1, -1):

            def last(way=way):
                self.take(way, LINE - 1)
                add()

            pl.when(self.takes(way, LINE - 1))(last)


class QuarterScatter:
    def __init__(self, copies, place, grad, owner, arrived, stage, sem):
        self.copies, self.place, self.grad, self.owner, self.sem = copies, place, grad, owner, sem
        self.stage = stage
        self.count, self.width = owner.shape[0], grad.shape[1]
        self.line = LineScatter(copies, place, self.block, arrived, stage, sem)
        self.near = (
            (copies.new(), 1 - place.p, place.c, place.pair),
            (copies.new(), place.p, 1 - place.c, place.core),
            (copies.new(), 1 - place.p, 1 - place.c, place.cross),
        )

    def block(self, origin):
        count = 4 * self.count
        return self.grad.at[pl.ds(pl.multiple_of(origin * count, count), count)]

    def rows(self, p, c):
        count = self.count
        start = (self.place.z * 4 + p * 2 + c) * count
        return self.grad.at[pl.ds(pl.multiple_of(start, count), count)]

    def columns(self, p, c):
        width = self.width
        return self.owner.at[:, pl.ds(pl.multiple_of((p * 2 + c) * width, LANES), width)]

    def finish(self):
        place = self.place
        self.line.finish(lambda: add_to(self.block(place.z), self.stage))
        for which, p, c, to in self.near:
            self.copies.send(which, self.rows(p, c), self.columns(place.p, place.c), to)
        fetch(self.rows(place.p, place.c), self.columns(place.p, place.c), self.sem)

    def end(self):
        for which, p, c, to in self.near:
            self.copies.receive(which, self.columns(p, c), to)


class RowsScatter:
    def __init__(self, copies, place, whole, from_core, from_pair, arrived, stage, sem):
        self.copies, self.place, self.whole, self.sem = copies, place, whole, sem
        self.from_core, self.from_pair = from_core, from_pair
        self.count, self.columns = from_pair.shape[1], from_pair.shape[2]
        self.stage = stage
        self.core_id = copies.new()
        self.pair_ids = [copies.new() for _ in range(LINE)]
        self.line = LineScatter(
            copies, place, lambda d: self.part(place.c, place.p, d), arrived, self.small(1), sem
        )

    def small(self, blocks):
        return self.stage.at[pl.ds(0, blocks * self.count), pl.ds(0, self.columns)]

    def part(self, c, p, origin, blocks=1):
        start = ((c * 2 + p) * LINE + origin) * self.count
        return self.whole.at[
            pl.ds(pl.multiple_of(start, self.count), blocks * self.count), pl.ds(0, self.columns)
        ]

    def fill(self, origin, value):
        for p in range(2):
            for c in range(2):
                start = (p * 2 + c) * self.count
                self.part(c, p, origin)[...] = value[start : start + self.count]

    def start(self):
        place = self.place
        self.copies.send(
            self.core_id, self.part(1 - place.c, 0, 0, 2 * LINE), self.from_core, place.core
        )

    def halve(self):
        place = self.place
        self.copies.receive(self.core_id, self.from_core, place.core)
        size = LINE * self.count
        for p in (1 - place.p, place.p):
            start = pl.multiple_of(p * size, size)
            fetch(self.from_core.at[pl.ds(start, size)], self.small(LINE), self.sem)
            add_to(self.part(place.c, p, 0, LINE), self.small(LINE))
            if p is place.p:
                continue
            for origin in (3, 0, 2, 1):
                self.copies.send(
                    self.pair_ids[origin],
                    self.part(place.c, p, origin),
                    self.from_pair.at[origin],
                    place.pair,
                )

    def quarter(self):
        place = self.place
        for origin in (3, 0, 2, 1):
            self.copies.receive(self.pair_ids[origin], self.from_pair.at[origin], place.pair)
            fetch(self.from_pair.at[origin], self.small(1), self.sem)
            add_to(self.part(place.c, place.p, origin), self.small(1))
        self.line.start()

    def finish(self, out):
        out[...] = wide(self.part(self.place.c, self.place.p, self.place.z)[...])

        def add():
            out[...] += wide(self.small(1)[...])

        self.line.finish(add)


PARTS = 4
N_REMOTE = 200
SUM_ROWS = 32


def eight_rows(value):
    return jnp.sum(value.reshape(-1, 8, value.shape[-1]), axis=0)


def layer_kernel(
    heads,
    head_size,
    tokens,
    first_shard,
    out_shard,
    gate_shard,
    up_shard,
    down_shard,
    grad_out,
    biases,
    cosine,
    sine,
    own_segments,
    own_positions,
    key_segments,
    key_positions,
    output,
    input_grad,
    grad_first,
    grad_w_out,
    grad_w_down,
    grad_w_gate,
    grad_w_up,
    sums_out,
    first_kept,
    line_landing,
    out_core_landing,
    out_pair_landing,
    out_other_landing,
    first_core_landing,
    first_pair_landing,
    first_line_landing,
    wo_core_landing,
    wo_pair_landing,
    wo_line_landing,
    first_all,
    w_out_all,
    state,
    window,
    keys,
    values,
    mail,
    first_normed,
    query,
    heads_out,
    gate_all,
    up_all,
    down_all,
    normed_four,
    grad_four,
    hidden,
    grad_gate,
    grad_up,
    pair_landing,
    other_landing,
    stage,
    grad_keys,
    grad_values,
    own_grad,
    window_landing,
    first_scale,
    second_scale,
    totals,
    sums,
    sums_landing,
    send_sems,
    recv_sems,
    local_sems,
):
    place = Place()
    copies = Copies(send_sems, recv_sems)
    rows, width = tokens.shape
    batches = own_segments.shape[0]
    per_batch = rows // batches
    query_width = heads * head_size
    kv_width = query_width + 2 * head_size
    size = rows // PARTS
    root = 1.0 / math.sqrt(head_size)
    sem = local_sems.at[0]

    window[...] = jnp.zeros_like(window)
    place.meet()

    first = RowsFlow(copies, place, first_shard, first_all)
    outs = RowsFlow(copies, place, out_shard, w_out_all)
    gates, ups, downs = [
        QuarterFlow(copies, place, shard, whole, local_sems.at[2 + i])
        for i, (shard, whole) in enumerate(
            ((gate_shard, gate_all), (up_shard, up_all), (down_shard, down_all))
        )
    ]
    cot = FourFlow(copies, place, grad_four, 1)
    second = FourFlow(copies, place, normed_four, PARTS)
    part_ids = [copies.new() for _ in range(PARTS)]
    window_ids = [copies.new() for _ in range(BACK)]

    def put(flow, sem):
        return lambda: fetch(flow.shard, flow.rows(place.z, place.p, place.c), sem)

    first.start(put(first, sem))
    gates.start()
    x = wide(tokens[...])
    first_scale[...] = lax.rsqrt(jnp.mean(x * x, axis=-1, keepdims=True) + EPSILON)
    state[...] = x * first_scale[...]
    outs.line.start(out_shard)
    first.crossing(0)
    first.arrive(1)
    outs.line.arrive(1)
    first.arrive(2)
    outs.line.arrive(2)
    first.arrive(3)
    ups.start()
    outs.line.arrive(3)
    gates.join()
    put(outs, sem)()
    for item in outs.items:
        outs.spread(*item)
    for step in range(1, LINE):
        first.crossing(step)
    first.end()

    gains = wide(first_all[:, kv_width:]).T
    first_gain, second_gain = gains[0:1], gains[1:2]
    first_normed[...] = low(state[...] * first_gain)
    sign = jnp.where(
        lax.broadcasted_iota(jnp.int32, (1, head_size), 1) < head_size // 2, -1.0, 1.0
    )

    def project(start, size):
        raw = matmul(first_normed[...], first_all[:, start : start + size])
        return raw + biases[:, start : start + size]

    def turned(raw):
        half_turn = pltpu.roll(raw, head_size // 2, 1)
        return low(raw * cosine[...] + half_turn * (sine[...] * sign))

    def turned_back(gradient, mine):
        half_turn = pltpu.roll(gradient * sine[mine], head_size // 2, 1)
        return low(gradient * cosine[mine] - half_turn * sign)

    kv = project(query_width, 2 * head_size)
    key_now, value_now = turned(kv[:, :head_size]), low(kv[:, head_size:])
    for b in range(batches):
        mine = slice(b * per_batch, (b + 1) * per_batch)
        window[BACK, b, :, :head_size] = key_now[mine]
        window[BACK, b, :, head_size:] = value_now[mine]
    for back in range(1, BACK + 1):
        copies.send(
            window_ids[back - 1],
            window.at[BACK],
            window.at[BACK - back],
            place.ranked(place.rank + back),
            place.rank + back < 4 * LINE,
        )
    for h in range(0, heads, 2):
        raw = project(h * head_size, 2 * head_size)
        query[:, h * head_size : (h + 1) * head_size] = turned(raw[:, :head_size])
        query[:, (h + 1) * head_size : (h + 2) * head_size] = turned(raw[:, head_size:])
    keep_first = pltpu.make_async_copy(first_all, first_kept, local_sems.at[1])
    keep_first.start()
    ups.join()
    downs.start()
    gates.arrive(1)
    for back in range(1, BACK + 1):
        only(
            place.rank >= back,
            lambda: copies.receive(
                window_ids[back - 1], window.at[BACK - back], place.ranked(place.rank - back)
            ),
        )

    def take_window(b):
        for slot in range(BACK + 1):
            keys[slot * per_batch : (slot + 1) * per_batch] = window[slot, b, :, :head_size]
            values[slot * per_batch : (slot + 1) * per_batch] = window[slot, b, :, head_size:]

    def probabilities(b, mine, columns):
        scores = times_transpose(query[mine, columns], keys[...]) * root
        allowed = (own_segments[b] == key_segments[b]) & (key_positions[b] <= own_positions[b])
        scores = jnp.where(allowed, scores, NEGATIVE)
        weights = jnp.exp(scores - jnp.max(scores, axis=-1, keepdims=True))
        return weights * (1.0 / jnp.sum(weights, axis=-1, keepdims=True))

    part_own, part_other = mail.at[pl.ds(0, rows)], mail.at[pl.ds(rows, rows)]
    for b in range(batches):
        take_window(b)
        mine = slice(b * per_batch, (b + 1) * per_batch)

        def attend_head(h, carry, b=b, mine=mine):
            columns = pl.ds(pl.multiple_of(h * head_size, head_size), head_size)
            probs = low(probabilities(b, mine, columns))
            heads_out[mine, columns] = low(matmul(probs, values[...]))
            return carry

        lax.fori_loop(0, heads, attend_head, 0)
        if b == 0:
            for step in range(LINE):
                outs.crossing(step)
            outs.end()
            ups.arrive(1)
        part = low(times_transpose(heads_out[mine], w_out_all[...]))
        part_own[mine] = part
        for i in range(b * per_batch // size, (b + 1) * per_batch // size):
            block = pl.ds(i * size, size)
            copies.send(part_ids[i], part_own.at[block], part_other.at[block], place.other)
    early = copies.mark()

    for i in range(PARTS):
        block = pl.ds(i * size, size)
        copies.receive(part_ids[i], part_other.at[block], place.other)
        copies.left(part_ids[i])
        row_sum = wide(tokens[block]) + (wide(part_own[block]) + wide(part_other[block]))
        state[block] = row_sum
        scale_row = lax.rsqrt(jnp.mean(row_sum * row_sum, axis=-1, keepdims=True) + EPSILON)
        second_scale[block] = scale_row
        second.slot(0, i)[...] = low(row_sum * scale_row * second_gain)
        second.send(i, second.slot(0, i))
        if i > 0:
            second.cross(i - 1)
        if i == 0:
            gates.arrive(2)
        if i == 2:
            ups.arrive(2)
            downs.join()
    cot_own = pltpu.make_async_copy(grad_out, cot.slot(0, 0), local_sems.at[5])
    cot_own.start()
    cot.send(0, grad_out)
    second.cross(PARTS - 1)
    keep_first.wait()
    for i in range(PARTS):
        second.end(i)
    gates.arrive(3)
    ups.arrive(3)

    tile = 256

    def forward_tile(t, carry):
        block = pl.ds(pl.multiple_of(t * tile, tile), tile)
        gate = matmul(normed_four[block], gate_all[...])
        up = matmul(normed_four[block], up_all[...])
        sigmoid = 1.0 / (1.0 + jnp.exp(-gate))
        silu = gate * sigmoid
        hidden[block] = low(silu * up)
        grad_up[block] = low(silu)
        grad_gate[block] = low(up * sigmoid * (1.0 + gate * (1.0 - sigmoid)))
        return carry

    lax.fori_loop(0, 4 * rows // tile, forward_tile, 0)
    cot.cross(0)
    cot_own.wait()
    cot.end(0)
    downs.arrive(1)
    copies.settle(early)
    grad_down = first_all

    def columns_of(d):
        return pl.ds(pl.multiple_of(d * rows, rows), rows)

    def weight_grad(target, left_side, right_side):
        def block(d, carry):
            part = contract_rows(left_side[:, columns_of(d)], right_side[...])
            target[columns_of(d)] = low(part)
            return carry

        lax.fori_loop(0, LINE, block, 0)

    scatters = [
        QuarterScatter(copies, place, grad, owner, line_landing.at[i], stage, sem)
        for i, (grad, owner) in enumerate(
            ((grad_down, grad_w_down), (up_all, grad_w_up), (gate_all, grad_w_gate))
        )
    ]
    down_back, up_back, gate_back = scatters
    weight_grad(grad_down, grad_four, hidden)
    late = copies.mark()
    down_back.line.start()
    downs.arrive(2)
    down_back.line.step(2)
    downs.arrive(3)

    def backward_tile(t, carry):
        block = pl.ds(pl.multiple_of(t * tile, tile), tile)
        back = matmul(grad_four[block], down_all[...])
        grad_gate[block] = low(back * wide(grad_gate[block]))
        grad_up[block] = low(back * wide(grad_up[block]))
        return carry

    lax.fori_loop(0, 4 * rows // tile, backward_tile, 0)
    copies.settle(late)

    normed_grad = grad_four
    core_ids = [copies.new() for _ in range(2)]
    pair_ids = [copies.new() for _ in range(PARTS)]
    other_ids = [copies.new() for _ in range(PARTS)]

    def slot(which, part=0, parts=1):
        return pl.ds(which * rows + part * (rows // parts), rows // parts)

    def normed_tile(t, carry):
        block = columns_of(3 - t)
        normed_grad[block] = low(
            times_transpose(grad_gate[block], gate_all[...])
            + times_transpose(grad_up[block], up_all[...])
        )
        return carry

    lax.fori_loop(0, 2, normed_tile, 0)
    for i in (1, 0):
        copies.send(
            core_ids[i],
            normed_grad.at[slot(2 + i)],
            mail.at[pl.ds(i * rows, rows)],
            place.core,
        )
    lax.fori_loop(2, 4, normed_tile, 0)
    copies.receive(core_ids[1], mail.at[pl.ds(rows, rows)], place.core)
    for i in range(PARTS):
        block = slot(1, i, PARTS)
        add_to(normed_grad.at[block], mail.at[pl.ds(rows + i * size, size)])
        copies.send(
            pair_ids[i],
            normed_grad.at[block],
            pair_landing.at[pl.ds(i * size, size)],
            place.pair,
        )
    copies.receive(core_ids[0], mail.at[pl.ds(0, rows)], place.core)
    add_to(normed_grad.at[slot(0)], mail.at[pl.ds(0, rows)])
    weight_grad(up_all, normed_four, grad_up)
    up_back.line.start()
    down_back.line.step(3)
    out_sum = normed_four
    out_core_id, out_pair_id, out_other_id = copies.new(), copies.new(), copies.new()
    first_weights = hidden
    first_fetch = pltpu.make_async_copy(first_kept, first_weights, local_sems.at[6])

    def out_tile(t, carry):
        block = columns_of(t)
        out_sum[block] = low(times_transpose(hidden[block], down_all[...]))
        return carry

    for i in range(PARTS):
        block = pl.ds(i * size, size)
        copies.receive(pair_ids[i], pair_landing.at[block], place.pair)
        add_to(normed_grad.at[block], pair_landing.at[block])
        copies.send(other_ids[i], normed_grad.at[block], other_landing.at[block], place.other)
        if i == 0:
            weight_grad(gate_all, normed_four, grad_gate)
        if i == 1:
            lax.fori_loop(0, 4, out_tile, 0)
            copies.send(
                out_core_id, out_sum.at[pl.ds(2 * rows, 2 * rows)], out_core_landing, place.core
            )
            first_fetch.start()
    grad_own = mail.at[pl.ds(rows, rows)]
    grad_branch = mail.at[pl.ds(0, rows)]
    fetch(grad_out, grad_own, sem)
    second_sum = totals.at[:, pl.ds(kv_width, width)]
    second_sum[...] = jnp.zeros_like(second_sum)
    for i in range(PARTS):
        block = pl.ds(i * size, size)
        copies.receive(other_ids[i], other_landing.at[block], place.other)
        back = wide(normed_grad[block]) + wide(other_landing[block])
        scale_row = second_scale[block]
        unit = state[block] * scale_row
        second_sum[...] += eight_rows(back * unit)
        grad_state = wide(grad_own[block]) + norm_back(back, unit, scale_row, second_gain)
        input_grad[block] = grad_state
        grad_branch[block] = low(grad_state)

    grad_heads = grad_up.at[pl.ds(0, rows), pl.ds(0, query_width)]
    grad_raw = grad_up.at[pl.ds(rows, rows), pl.ds(0, kv_width)]
    grad_heads[...] = low(matmul(grad_branch[...], w_out_all[...]))
    down_back.finish()
    spare = mail.at[pl.ds(rows, rows)]
    copies.receive(out_core_id, out_core_landing, place.core)
    fetch(out_core_landing.at[pl.ds(rows, rows)], spare, sem)
    add_to(out_sum.at[slot(1)], spare)
    copies.send(out_pair_id, out_sum.at[slot(1)], out_pair_landing, place.pair)
    back_ids = [[copies.new() for _ in range(batches)] for _ in range(BACK)]
    for b in range(batches):
        take_window(b)
        mine = slice(b * per_batch, (b + 1) * per_batch)
        grad_keys[...] = jnp.zeros_like(grad_keys)
        grad_values[...] = jnp.zeros_like(grad_values)

        def attend_back_head(h, carry, b=b, mine=mine):
            columns = pl.ds(pl.multiple_of(h * head_size, head_size), head_size)
            probs = probabilities(b, mine, columns)
            grad_head = grad_heads[mine, columns]
            grad_probs = times_transpose(grad_head, values[...])
            row_inner = jnp.sum(probs * grad_probs, axis=-1, keepdims=True)
            grad_scores = low(probs * (grad_probs - row_inner))
            grad_raw[mine, columns] = turned_back(matmul(grad_scores, keys[...]) * root, mine)
            grad_keys[...] += contract_rows(grad_scores, query[mine, columns])
            grad_values[...] += contract_rows(low(probs), grad_head)
            return carry

        lax.fori_loop(0, heads, attend_back_head, 0)
        for s in range(BACK):
            there = slice(s * per_batch, (s + 1) * per_batch)
            window[s, b, :, :head_size] = low(grad_keys[there] * root)
            window[s, b, :, head_size:] = low(grad_values[there])
        there = slice(BACK * per_batch, (BACK + 1) * per_batch)
        own_grad[mine, :head_size] = grad_keys[there] * root
        own_grad[mine, head_size:] = grad_values[there]
        for back in range(1, BACK + 1):
            copies.send(
                back_ids[back - 1][b],
                window.at[BACK - back, b],
                window_landing.at[back - 1, b],
                place.ranked(place.rank - back),
                place.rank >= back,
            )
        if b == 0:
            up_back.line.step(2)
    gate_back.line.start()
    wo_back = RowsScatter(
        copies, place, w_out_all, wo_core_landing, wo_pair_landing, wo_line_landing, stage, sem
    )
    for origin in range(LINE):
        branch = grad_branch[:, origin * rows : (origin + 1) * rows]
        wo_back.fill(origin, low(contract_rows(branch, heads_out[...])))
    wo_back.start()
    fetch(out_core_landing.at[pl.ds(0, rows)], spare, sem)
    add_to(out_sum.at[slot(0)], spare)
    copies.receive(out_pair_id, out_pair_landing, place.pair)
    fetch(out_pair_landing, spare, sem)
    add_to(out_sum.at[slot(0)], spare)
    copies.send(out_other_id, out_sum.at[slot(0)], out_other_landing, place.other)
    wo_back.halve()
    up_back.line.step(3)
    for back in range(1, BACK + 1):
        for b in range(batches):
            mine = slice(b * per_batch, (b + 1) * per_batch)

            def take(back=back, b=b, mine=mine):
                landing = window_landing.at[back - 1, b]
                copies.receive(back_ids[back - 1][b], landing, place.ranked(place.rank + back))
                own_grad[mine] += wide(landing[...])

            pl.when(place.rank + back < 4 * LINE)(take)
    every = slice(0, rows)
    grad_raw[:, query_width : query_width + head_size] = turned_back(
        own_grad[:, :head_size], every
    )
    grad_raw[:, query_width + head_size :] = low(own_grad[:, head_size:])
    first_back = RowsScatter(
        copies,
        place,
        grad_gate,
        first_core_landing,
        first_pair_landing,
        first_line_landing,
        stage,
        sem,
    )
    for origin in range(LINE):
        normed = first_normed[:, origin * rows : (origin + 1) * rows]
        first_back.fill(origin, low(contract_rows(normed, grad_raw[...])))
    first_back.start()

    first_ids = [copies.new() for _ in range(PARTS)]
    sum_ids = [copies.new() for _ in range(5)]
    first_at = kv_width + width
    first_own, first_other = mail.at[pl.ds(0, rows)], pair_landing
    first_fetch.wait()

    def first_tile(t, carry):
        block = pl.ds(pl.multiple_of(t * tile, tile), tile)
        part = times_transpose(grad_raw[...], first_weights[block, :kv_width])
        first_own[:, block] = low(part)
        unit = wide(tokens[:, block]) * first_scale[...]
        at = pl.ds(pl.multiple_of(first_at + t * tile, tile), tile)
        totals[:, at] = eight_rows(part * unit)
        return carry

    lax.fori_loop(0, width // tile, first_tile, 0)
    for i in range(PARTS):
        block = pl.ds(i * size, size)
        copies.send(first_ids[i], first_own.at[block], first_other.at[block], place.other)
    totals[:, :kv_width] = eight_rows(wide(grad_raw[...]))

    def sum_row(t, carry):
        columns = pl.ds(pl.multiple_of(t * LANES, LANES), LANES)
        sums[0, pl.ds(t, 1)] = jnp.sum(totals[:, columns], axis=0, keepdims=True)
        return carry

    lax.fori_loop(0, sums.shape[1], sum_row, 0)
    shared = first_at // LANES

    def sum_step(i, to):
        copies.send(sum_ids[i], sums.at[i], sums_landing.at[i], to)

    def sum_take(i, to):
        copies.receive(sum_ids[i], sums_landing.at[i], to)
        if i < 4:
            sums[i + 1] = sums[i] + sums_landing[i]

    sum_step(0, place.core)
    first_back.halve()
    sum_take(0, place.core)
    sum_step(1, place.pair)
    wo_back.quarter()
    up_back.finish()
    gate_back.line.step(2)
    sum_take(1, place.pair)
    sum_step(2, place.near)
    first_back.quarter()
    for i in range(PARTS):
        block = pl.ds(i * size, size)
        copies.receive(first_ids[i], first_other.at[block], place.other)
        unit = wide(tokens[block]) * first_scale[block]
        back = wide(first_own[block]) + wide(first_other[block])
        input_grad[block] += norm_back(back, unit, first_scale[block], first_gain)
    gate_back.line.step(3)
    copies.receive(out_other_id, out_other_landing, place.other)
    fetch(out_other_landing, spare, sem)
    spare[...] = low(state[...] + (wide(out_sum[slot(0)]) + wide(spare[...])))
    fetch(spare, output, sem)
    sum_take(2, place.near)
    sum_step(3, place.far)
    wo_back.line.step(2)
    first_back.line.step(2)
    wo_back.line.step(3)
    first_back.line.step(3)
    gate_back.finish()
    sum_take(3, place.far)
    sum_step(4, place.other)
    wo_back.finish(grad_w_out)
    first_back.finish(grad_first)
    sum_take(4, place.other)
    sums_out[...] = sums[4]
    sums_out[shared:] += sums_landing[4, shared:]
    for scatter in scatters:
        scatter.end()
    copies.settle()


def layer_call(heads, head_size, operands):
    tokens, first_shard, out_shard, gate_shard = operands[:4]
    own_segments = operands[10]
    rows, width = tokens.shape
    batches = own_segments.shape[0]
    per_batch = rows // batches
    count, padded = gate_shard.shape
    quarter = padded // 4
    query_width = heads * head_size
    kv_width = query_width + 2 * head_size
    low_type, wide_type = jnp.bfloat16, jnp.float32
    in_vmem, anywhere = pl.BlockSpec(memory_space=pltpu.VMEM), pl.BlockSpec(memory_space=pl.ANY)

    def shape(*dims, kind=low_type):
        return jax.ShapeDtypeStruct(dims, kind)

    def vmem(*dims, kind=low_type):
        return pltpu.VMEM(dims, kind)

    sum_rows = (kv_width + 2 * width) // LANES
    outs = (
        (shape(rows, width), anywhere),
        (shape(rows, width, kind=wide_type), in_vmem),
        (shape(count, kv_width, kind=wide_type), in_vmem),
        (shape(count, query_width, kind=wide_type), in_vmem),
        (shape(count, padded), anywhere),
        (shape(count, padded), anywhere),
        (shape(count, padded), anywhere),
        (shape(sum_rows, LANES, kind=wide_type), in_vmem),
    )
    kept = (
        shape(width, first_shard.shape[1]),
        shape(3, 2, LINE - 1, 4 * count, quarter),
        shape(2 * rows, width),
        shape(rows, width),
        shape(rows, width),
        shape(2 * LINE * count, kv_width),
        shape(LINE, count, kv_width),
        shape(2, LINE - 1, count, kv_width),
        shape(2 * LINE * count, query_width),
        shape(LINE, count, query_width),
        shape(2, LINE - 1, count, query_width),
    )
    scratch = (
        vmem(width, first_shard.shape[1]),
        vmem(width, query_width),
        vmem(rows, width, kind=wide_type),
        vmem(BACK + 1, batches, per_batch, 2 * head_size),
        vmem((BACK + 1) * per_batch, head_size),
        vmem((BACK + 1) * per_batch, head_size),
        vmem(2 * rows, width),
        vmem(rows, width),
        vmem(rows, query_width),
        vmem(rows, query_width),
        vmem(width, quarter),
        vmem(width, quarter),
        vmem(width, quarter),
        vmem(4 * rows, width),
        vmem(4 * rows, width),
        vmem(4 * rows, quarter),
        vmem(4 * rows, quarter),
        vmem(4 * rows, quarter),
        vmem(rows, width),
        vmem(rows, width),
        vmem(4 * count, quarter),
        vmem((BACK + 1) * per_batch, head_size, kind=wide_type),
        vmem((BACK + 1) * per_batch, head_size, kind=wide_type),
        vmem(rows, 2 * head_size, kind=wide_type),
        vmem(BACK, batches, per_batch, 2 * head_size),
        vmem(rows, 1, kind=wide_type),
        vmem(rows, 1, kind=wide_type),
        vmem(8, sum_rows * LANES, kind=wide_type),
        vmem(6, sum_rows, LANES, kind=wide_type),
        vmem(5, sum_rows, LANES, kind=wide_type),
        pltpu.SemaphoreType.DMA((N_REMOTE,)),
        pltpu.SemaphoreType.DMA((N_REMOTE,)),
        pltpu.SemaphoreType.DMA((8,)),
    )
    results = pl.pallas_call(
        functools.partial(layer_kernel, heads, head_size),
        out_shape=[out[0] for out in outs] + list(kept),
        in_specs=[in_vmem] + [anywhere] * 6 + [in_vmem] * 7,
        out_specs=[out[1] for out in outs] + [anywhere] * len(kept),
        scratch_shapes=scratch,
        compiler_params=pltpu.CompilerParams(
            collective_id=0, has_side_effects=True, vmem_limit_bytes=VMEM_BYTES
        ),
    )(*operands)
    return results[: len(outs)]


def body(
    tokens,
    norm1_gain,
    query_weight,
    query_bias,
    key_weight,
    key_bias,
    value_weight,
    value_bias,
    output_weight,
    norm2_gain,
    gate_weight,
    up_weight,
    down_weight,
    cotangent,
    segments,
    positions,
):
    batches, count_rows, width = tokens.shape
    heads, head_size = query_bias.shape
    query_width = heads * head_size
    units = gate_weight.shape[1]
    place = lax.axis_index(FSDP)
    row_start = place * count_rows
    rows = batches * count_rows

    gains = jnp.stack([norm1_gain, norm2_gain], axis=1)
    gains = jnp.pad(gains, ((0, 0), (0, LANES - 2)))
    first_shard = jnp.concatenate([query_weight, key_weight, value_weight, gains], axis=1)
    kv_width = query_width + 2 * head_size
    padded = -(-units // (4 * LANES)) * (4 * LANES)

    def spaced(shard):
        return jnp.pad(shard, ((0, 0), (0, padded - units)))

    grad_out = cotangent.reshape(rows, width)
    inputs = wide(tokens.reshape(rows, width))
    biases = jnp.concatenate(
        [query_bias.reshape(-1), key_bias.reshape(-1), value_bias.reshape(-1)]
    )
    own_places = lax.dynamic_slice_in_dim(positions, row_start, count_rows, axis=1)
    cosine, sine_table = rotation(own_places.reshape(-1), head_size)
    if lax.axis_size(RING) == LINE:
        key_segments, key_positions = [], []
        for b in range(batches):
            padding = jnp.full((BACK * count_rows,), -1, jnp.int32)
            for rows_of, padded_rows in ((key_segments, segments), (key_positions, positions)):
                padded_rows = jnp.concatenate([padding, padded_rows[b]])
                rows_of.append(
                    lax.dynamic_slice_in_dim(padded_rows, row_start, (BACK + 1) * count_rows)
                )
        own_segments = lax.dynamic_slice_in_dim(segments, row_start, count_rows, axis=1)
        (
            output,
            input_grad,
            grad_w_qkv,
            grad_w_out,
            grad_w_down,
            grad_w_gate,
            grad_w_up,
            sums,
        ) = layer_call(
            heads,
            head_size,
            (
                tokens.reshape(rows, width),
                first_shard,
                output_weight.T,
                spaced(gate_weight),
                spaced(up_weight),
                spaced(down_weight.T),
                grad_out,
                wide(biases).reshape(1, -1),
                cosine[:, 0],
                sine_table[:, 0],
                own_segments[..., None],
                own_places[..., None],
                jnp.stack(key_segments)[:, None],
                jnp.stack(key_positions)[:, None],
            ),
        )
        sums = sums.reshape(-1)
        grad_w_down, grad_w_gate, grad_w_up = map(wide, (grad_w_down, grad_w_gate, grad_w_up))
    else:
        allowed = [
            visible(segments[b], positions[b], row_start, count_rows) for b in range(batches)
        ]
        first_all = gather_rows(first_shard)
        w_qkv = first_all[:, :kv_width]
        first_gain = wide(first_all[:, kv_width])
        second_gain = wide(first_all[:, kv_width + 1])
        w_out = gather_rows(output_weight.T)
        w_gate = quarter_columns(spaced(gate_weight))
        w_up = quarter_columns(spaced(up_weight))
        w_down = quarter_columns(spaced(down_weight.T))
        grad_out_four = four_blocks(grad_out)
        first_unit, first_scale = root_mean_square_parts(inputs)
        first_normed = low(first_unit * first_gain)
        raw = matmul(first_normed, w_qkv) + wide(biases)
        turned = rotate(
            raw[:, : query_width + head_size].reshape(rows, heads + 1, head_size),
            cosine,
            sine_table,
        )
        turned = low(turned)
        query_rows = turned[:, :heads].reshape(batches, count_rows, heads, head_size)
        key_value = jnp.concatenate(
            [turned[:, heads], low(raw[:, query_width + head_size :])], axis=1
        )
        key_value = key_value.reshape(batches, count_rows, 2 * head_size)
        window = jnp.concatenate(
            [shifted(key_value, back) for back in range(BACK, 0, -1)] + [key_value], axis=1
        )
        key_rows, value_rows = window[..., :head_size], window[..., head_size:]
        attended = [
            attend(query_rows[b], key_rows[b], value_rows[b], allowed[b]) for b in range(batches)
        ]
        log_totals = [log_total for _, log_total in attended]
        heads_out = jnp.concatenate([mixed for mixed, _ in attended], axis=0)
        residual = inputs + tensor_total(times_transpose(heads_out, w_out))
        second_unit, second_scale = root_mean_square_parts(residual)
        second_normed = four_blocks(low(second_unit * second_gain))

        second_unit, second_scale = root_mean_square_parts(residual)
        gate_value = matmul(second_normed, w_gate)
        up_part = matmul(second_normed, w_up)
        sigmoid_gate = jax.nn.sigmoid(gate_value)
        silu_gate = gate_value * sigmoid_gate
        hidden = low(silu_gate * up_part)
        grad_hidden = matmul(grad_out_four, w_down)
        grad_gate = low(
            grad_hidden * up_part * sigmoid_gate * (1.0 + gate_value * (1.0 - sigmoid_gate))
        )
        grad_up = low(grad_hidden * silu_gate)
        second_back = four_sums(times_transpose(grad_gate, w_gate) + times_transpose(grad_up, w_up))
        grad_w_down = quarter_to_owner(low(contract_rows(grad_out_four, hidden)))
        grad_w_gate = quarter_to_owner(low(contract_rows(second_normed, grad_gate)))
        grad_w_up = quarter_to_owner(low(contract_rows(second_normed, grad_up)))
        output = low(residual + four_sums(times_transpose(hidden, w_down)))

        second_gain_sum = jnp.sum(second_back * second_unit, axis=0)
        grad_state = wide(grad_out) + norm_back(second_back, second_unit, second_scale, second_gain)
        grad_branch = low(grad_state)
        grad_w_out = scatter_rows(contract_rows(grad_branch, heads_out))
        grad_heads = low(matmul(grad_branch, w_out)).reshape(query_rows.shape)
        backs = [
            attend_back(
                grad_heads[b], query_rows[b], key_rows[b], value_rows[b], allowed[b], log_totals[b]
            )
            for b in range(batches)
        ]
        grad_query = jnp.stack([back[0] for back in backs]).reshape(rows, heads, head_size)
        grad_window = jnp.stack([jnp.concatenate([back[1], back[2]], axis=1) for back in backs])
        own_grad = grad_window[:, BACK * count_rows :]
        for back in range(1, BACK + 1):
            first_row = (BACK - back) * count_rows
            own_grad = own_grad + wide(
                shifted(low(grad_window[:, first_row : first_row + count_rows]), -back)
            )
        own_grad = own_grad.reshape(rows, 2, head_size)
        turned_back = rotate_back(
            jnp.concatenate([grad_query, own_grad[:, :1]], axis=1), cosine, sine_table
        )
        grad_raw = low(jnp.concatenate([turned_back, own_grad[:, 1:]], axis=1).reshape(rows, -1))
        grad_w_qkv = scatter_rows(contract_rows(first_normed, grad_raw))
        bias_sum = jnp.sum(wide(grad_raw), axis=0)
        first_back_part = times_transpose(grad_raw, w_qkv)
        first_back = tensor_total(first_back_part)
        first_gain_sum = jnp.sum(first_back * first_unit, axis=0)
        input_grad = grad_state + norm_back(first_back, first_unit, first_scale, first_gain)
        sums = summed_over_fsdp(jnp.concatenate([bias_sum, second_gain_sum, first_gain_sum]))
    bias_total = sums[:kv_width]
    gain_rows = norm1_gain.shape[0]
    second_total = lax.dynamic_slice_in_dim(sums, kv_width + place * gain_rows, gain_rows)
    first_total = lax.dynamic_slice_in_dim(sums, kv_width + width + place * gain_rows, gain_rows)

    return (
        output.reshape(tokens.shape),
        input_grad.reshape(tokens.shape),
        first_total,
        grad_w_qkv[:, :query_width],
        bias_total[:query_width].reshape(query_bias.shape),
        grad_w_qkv[:, query_width : query_width + head_size],
        bias_total[query_width : query_width + head_size].reshape(key_bias.shape),
        grad_w_qkv[:, query_width + head_size :],
        bias_total[query_width + head_size :].reshape(value_bias.shape),
        grad_w_out.T,
        second_total,
        grad_w_gate[:, :units],
        grad_w_up[:, :units],
        grad_w_down[:, :units].T,
    )


def solution(mesh):
    fsdp, tensor = mesh.shape["fsdp"], mesh.shape["tensor"]
    fine = Mesh(mesh.devices.reshape(fsdp // 4, 2, 2, tensor), (RING, PAIR, CORE, TENSOR))
    by_rows, by_columns, by_tensor = P(FSDP, TENSOR), P(TENSOR, FSDP), P(TENSOR, None)
    by_tokens, by_gain = P(None, FSDP, None), P(FSDP)
    placed = (
        by_tokens,
        by_gain,
        by_rows,
        by_tensor,
        by_rows,
        by_tensor,
        by_rows,
        by_tensor,
        by_columns,
        by_gain,
        by_rows,
        by_rows,
        by_columns,
        by_tokens,
        P(),
        P(),
    )
    return jax.shard_map(
        body,
        mesh=fine,
        in_specs=placed,
        out_specs=(
            by_tokens,
            by_tokens,
            by_gain,
            by_rows,
            by_tensor,
            by_rows,
            by_tensor,
            by_rows,
            by_tensor,
            by_columns,
            by_gain,
            by_rows,
            by_rows,
            by_columns,
        ),
        check_vma=False,
    )
```

```python
import functools
import math

import jax
import jax.numpy as jnp
from jax import lax
from jax.experimental import pallas as pl
from jax.experimental.pallas import tpu as pltpu
from jax.sharding import Mesh
from jax.sharding import PartitionSpec as P

BACK = 5
LINE = 4
LANES = 128
VMEM_BYTES = 63 * 1024 * 1024

EPSILON = 1e-06
THETA = 1000000.0
NEGATIVE = -1e30

RING, PAIR, CORE, TENSOR = "ring", "pair", "core", "tensor"
FSDP = (RING, PAIR, CORE)
SWAP = [(0, 1), (1, 0)]


def low(value):
    return value.astype(jnp.bfloat16)


def wide(value):
    return value.astype(jnp.float32)


def matmul(left_side, right_side):
    return jnp.dot(left_side, right_side, preferred_element_type=jnp.float32)


def contract_rows(left_side, right_side):
    return lax.dot_general(
        left_side, right_side, (((0,), (0,)), ((), ())), preferred_element_type=jnp.float32
    )


def times_transpose(left_side, right_side):
    return lax.dot_general(
        left_side, right_side, (((1,), (1,)), ((), ())), preferred_element_type=jnp.float32
    )


def swapped(value, axis):
    return lax.ppermute(value, axis, SWAP)


def in_order(own, other, place, axis):
    first = jnp.where(place == 0, own, other)
    second = jnp.where(place == 0, other, own)
    return jnp.stack([first, second], axis=axis)


def shifted(value, steps):
    count = lax.axis_size(FSDP)
    first, last = (max(0, -steps), min(count, count - steps))
    return lax.ppermute(value, FSDP, [(source, source + steps) for source in range(first, last)])


def summed_over_fsdp(value):
    count = lax.axis_size(FSDP)
    bit = 1
    while bit < count:
        value = value + lax.ppermute(value, FSDP, [(i, i ^ bit) for i in range(count)])
        bit *= 2
    return value


def line_gather(block):
    count, here = lax.axis_size(RING), lax.axis_index(RING)
    if count > LINE:
        return lax.all_gather(block, RING, axis=0)
    right, left = [block], [block]
    for step in range(1, count):
        right.append(
            lax.ppermute(right[-1], RING, [(i, i + 1) for i in range(step - 1, count - 1)])
        )
        left.append(
            lax.ppermute(left[-1], RING, [(i, i - 1) for i in range(1, count - step + 1)])
        )
    result = jnp.zeros((count,) + block.shape, block.dtype)
    for step in range(count):
        piece = block if step == 0 else jnp.where(here >= step, right[step], left[count - step])
        result = lax.dynamic_update_slice_in_dim(
            result, piece[None], (here - step + count) % count, axis=0
        )
    return result


def line_scatter(parts):
    count, here = lax.axis_size(RING), lax.axis_index(RING)
    if count > LINE:
        return wide(lax.psum_scatter(parts, RING, scatter_dimension=0, tiled=False))

    def part(place):
        return lax.dynamic_index_in_dim(parts, place, axis=0, keepdims=False)

    right, left = None, None
    for step in range(1, count):
        to_right, to_left = part(here + count - step), part(here - count + step)
        if step > 1:
            to_right = low(wide(to_right) + wide(right))
            to_left = low(wide(to_left) + wide(left))
        right = lax.ppermute(to_right, RING, [(i, i + 1) for i in range(step)])
        left = lax.ppermute(to_left, RING, [(i, i - 1) for i in range(count - step, count)])
    return wide(part(here)) + wide(right) + wide(left)


def gather_rows(shard):
    rows = line_gather(shard)
    rows = in_order(rows, swapped(rows, PAIR), lax.axis_index(PAIR), 1)
    rows = in_order(rows, swapped(rows, CORE), lax.axis_index(CORE), 2)
    return rows.reshape((-1,) + shard.shape[1:])


def scatter_rows(total):
    pair, core = lax.axis_index(PAIR), lax.axis_index(CORE)
    parts = low(total).reshape((lax.axis_size(RING), 2, 2, -1) + total.shape[1:])

    def halved(value, axis, place, name):
        mine = lax.dynamic_index_in_dim(value, place, axis=axis, keepdims=False)
        sent = lax.dynamic_index_in_dim(value, 1 - place, axis=axis, keepdims=False)
        return low(wide(mine) + wide(swapped(sent, name)))

    parts = halved(parts, 2, core, CORE)
    parts = halved(parts, 1, pair, PAIR)
    return line_scatter(parts)


def quarter_columns(shard):
    pair, core = lax.axis_index(PAIR), lax.axis_index(CORE)
    half = shard.shape[1] // 2

    def halved(value, place, width):
        mine = lax.dynamic_slice_in_dim(value, place * width, width, axis=value.ndim - 1)
        sent = lax.dynamic_slice_in_dim(value, (1 - place) * width, width, axis=value.ndim - 1)
        return mine, sent

    mine, sent = halved(shard, pair, half)
    rows = in_order(mine, swapped(sent, PAIR), pair, 0)
    mine, sent = halved(rows, core, half // 2)
    rows = in_order(mine, swapped(sent, CORE), core, 1)
    rows = line_gather(rows.reshape(-1, half // 2))
    return rows.reshape(-1, half // 2)


def quarter_to_owner(grad):
    pair, core = lax.axis_index(PAIR), lax.axis_index(CORE)
    width = grad.shape[1]
    block = lax.psum_scatter(
        grad.reshape(lax.axis_size(RING), -1, width), RING, scatter_dimension=0, tiled=False
    )
    block = block.reshape(2, 2, -1, width)

    def halved(value, axis, place):
        mine = lax.dynamic_index_in_dim(value, place, axis=axis, keepdims=False)
        sent = lax.dynamic_index_in_dim(value, 1 - place, axis=axis, keepdims=False)
        return mine, sent

    mine, sent = halved(block, 0, pair)
    block = in_order(mine, swapped(sent, PAIR), pair, 0)
    mine, sent = halved(block, 1, core)
    block = in_order(mine, swapped(sent, CORE), core, 1)
    return jnp.concatenate([wide(block[i, j]) for i in range(2) for j in range(2)], axis=1)


def four_blocks(value):
    over = swapped(value, PAIR)
    return jnp.concatenate([value, over, swapped(value, CORE), swapped(over, CORE)], axis=0)


def four_sums(total):
    half = total.shape[0] // 2
    total = total[:half] + wide(swapped(low(total[half:]), CORE))
    total = total[: half // 2] + wide(swapped(low(total[half // 2 :]), PAIR))
    return tensor_total(total)


def tensor_total(partial_sum):
    own = lax.reduce_precision(partial_sum, 8, 7)
    return own + wide(swapped(low(own), TENSOR))


def rotation(places, width):
    half_width = width // 2
    frequency = THETA ** (-(jnp.arange(half_width, dtype=jnp.float32) * 2.0) / width)
    angles = places.astype(jnp.float32)[:, None] * frequency[None, :]
    cosine = jnp.concatenate([jnp.cos(angles), jnp.cos(angles)], axis=-1)[:, None, :]
    sine_table = jnp.concatenate([jnp.sin(angles), jnp.sin(angles)], axis=-1)[:, None, :]
    return (cosine, sine_table)


def rotate(values, cosine, sine_table):
    half_width = values.shape[-1] // 2
    turned = jnp.concatenate([-values[..., half_width:], values[..., :half_width]], axis=-1)
    return values * cosine + turned * sine_table


def rotate_back(gradient, cosine, sine_table):
    half_width = gradient.shape[-1] // 2
    moved_part = gradient * sine_table
    return gradient * cosine + jnp.concatenate(
        [moved_part[..., half_width:], -moved_part[..., :half_width]], axis=-1
    )


def root_mean_square_parts(values):
    scale_row = lax.rsqrt(jnp.mean(values * values, axis=-1, keepdims=True) + EPSILON)
    return (values * scale_row, scale_row)


def norm_back(grad_normed, normalized, scale_row, gain):
    scaled = grad_normed * gain
    return scale_row * (scaled - normalized * jnp.mean(scaled * normalized, axis=-1, keepdims=True))


def visible(seg_row, pos_row, row_start, count_rows):
    pad_rows = BACK * count_rows
    seg_padded = jnp.concatenate([jnp.full((pad_rows,), -1, jnp.int32), seg_row])
    pos_padded = jnp.concatenate([jnp.zeros((pad_rows,), jnp.int32), pos_row])
    key_seg = lax.dynamic_slice_in_dim(seg_padded, row_start, pad_rows + count_rows)
    key_pos = lax.dynamic_slice_in_dim(pos_padded, row_start, pad_rows + count_rows)
    query_seg = lax.dynamic_slice_in_dim(seg_row, row_start, count_rows)
    query_pos = lax.dynamic_slice_in_dim(pos_row, row_start, count_rows)
    return (query_seg[:, None] == key_seg[None, :]) & (key_pos[None, :] <= query_pos[:, None])


def attend(query_rows, key_rows, value_rows, allowed):
    scores = jnp.einsum("thd,sd->hts", query_rows, key_rows, preferred_element_type=jnp.float32)
    scores = scores * (1.0 / math.sqrt(query_rows.shape[-1]))
    scores = jnp.where(allowed, scores, NEGATIVE)
    row_max = jnp.max(scores, axis=-1, keepdims=True)
    log_total = row_max + jnp.log(jnp.sum(jnp.exp(scores - row_max), axis=-1, keepdims=True))
    probs_low = low(jnp.exp(scores - log_total))
    mixed = jnp.einsum("hts,sd->thd", probs_low, value_rows, preferred_element_type=jnp.float32)
    return low(mixed.reshape(query_rows.shape[0], -1)), log_total


def log_total_of(query_rows, key_rows, allowed):
    scores = jnp.einsum("thd,sd->hts", query_rows, key_rows, preferred_element_type=jnp.float32)
    scores = scores * (1.0 / math.sqrt(query_rows.shape[-1]))
    scores = jnp.where(allowed, scores, NEGATIVE)
    row_max = jnp.max(scores, axis=-1, keepdims=True)
    return row_max + jnp.log(jnp.sum(jnp.exp(scores - row_max), axis=-1, keepdims=True))


def attend_back(grad_heads, query_rows, key_rows, value_rows, allowed, log_total):
    scale = 1.0 / math.sqrt(query_rows.shape[-1])
    scores = jnp.einsum("thd,sd->hts", query_rows, key_rows, preferred_element_type=jnp.float32)
    probs = jnp.exp(jnp.where(allowed, scores * scale, NEGATIVE) - log_total)
    grad_probs = jnp.einsum(
        "thd,sd->hts", grad_heads, value_rows, preferred_element_type=jnp.float32
    )
    row_inner = jnp.sum(probs * grad_probs, axis=-1, keepdims=True)
    grad_scores = low(probs * (grad_probs - row_inner))
    grad_query = jnp.einsum(
        "hts,sd->thd", grad_scores, key_rows, preferred_element_type=jnp.float32
    )
    grad_keys = jnp.einsum(
        "hts,thd->sd", grad_scores, query_rows, preferred_element_type=jnp.float32
    )
    grad_values = jnp.einsum(
        "hts,thd->sd", low(probs), grad_heads, preferred_element_type=jnp.float32
    )
    return grad_query * scale, grad_keys * scale, grad_values


def device(**coordinates):
    return {name: place for name, place in coordinates.items()}


class Copies:
    def __init__(self, send_sems, recv_sems):
        self.send_sems, self.recv_sems = send_sems, recv_sems
        self.used = 0
        self.sent = []

    def new(self):
        self.used += 1
        return self.used - 1

    def _make(self, which, source, target, to):
        return pltpu.make_async_remote_copy(
            src_ref=source,
            dst_ref=target,
            send_sem=self.send_sems.at[which],
            recv_sem=self.recv_sems.at[which],
            device_id=to,
            device_id_type=pl.DeviceIdType.MESH,
        )

    def send(self, which, source, target, to, cond=None):
        only(cond, lambda: self._make(which, source, target, to).start())
        self.sent.append((which, source, target, to, cond))

    def receive(self, which, target, via):
        self._make(which, target, target, via).wait_recv()

    def settle(self, until=None):
        until = len(self.sent) if until is None else until
        for i in range(until):
            if self.sent[i] is not None:
                which, source, target, to, cond = self.sent[i]
                only(cond, lambda: self._make(which, source, target, to).wait_send())
                self.sent[i] = None

    def left(self, which):
        for i, entry in enumerate(self.sent):
            if entry is not None and entry[0] == which:
                _, source, target, to, cond = entry
                only(cond, lambda: self._make(which, source, target, to).wait_send())
                self.sent[i] = None

    def settle_of(self, ids):
        for which in ids:
            self.left(which)

    def mark(self):
        return len(self.sent)


def only(cond, action):
    if cond is None:
        action()
    else:
        pl.when(cond)(action)


class Place:
    def __init__(self):
        self.z, self.p = lax.axis_index(RING), lax.axis_index(PAIR)
        self.c, self.y = lax.axis_index(CORE), lax.axis_index(TENSOR)
        self.q = self.p * 2 + self.c
        self.q_pair, self.q_core = (1 - self.p) * 2 + self.c, self.p * 2 + 1 - self.c
        self.q_cross = (1 - self.p) * 2 + 1 - self.c
        self.pair, self.core = {PAIR: 1 - self.p}, {CORE: 1 - self.c}
        self.cross = {PAIR: 1 - self.p, CORE: 1 - self.c}
        self.other = {TENSOR: 1 - self.y}
        self.near = {RING: self.z + 1 - 2 * (self.z % 2)}
        self.far = {RING: self.z + 2 - 4 * (self.z // 2)}
        self.right, self.left = {RING: self.z + 1}, {RING: self.z - 1}
        self.right_cross = {RING: self.z + 1, PAIR: 1 - self.p}
        self.left_cross = {RING: self.z - 1, PAIR: 1 - self.p}
        self.far_right = {RING: self.z + 2, PAIR: 0, CORE: 0}
        self.far_left = {RING: self.z - 2, PAIR: 1, CORE: 1}
        self.has_right, self.has_left = self.z < LINE - 1, self.z > 0
        self.has_far_right = (self.q == 3) & (self.z < LINE - 2)
        self.has_far_left = (self.q == 0) & (self.z > 1)

    def meet(self):
        barrier = pltpu.get_barrier_semaphore()

        def greet(to, cond=None):
            only(
                cond,
                lambda: pl.semaphore_signal(
                    barrier, inc=1, device_id=to, device_id_type=pl.DeviceIdType.MESH
                ),
            )

        for to in (self.pair, self.core, self.cross, self.other):
            greet(to)
        for far in (2, 3):
            greet({RING: self.z + far}, self.z + far < LINE)
            greet({RING: self.z - far}, self.z >= far)
        for there, to, cross in (
            (self.has_right, self.right, self.right_cross),
            (self.has_left, self.left, self.left_cross),
        ):
            greet(to, there)
            greet(cross, there)
        greet(self.far_right, self.has_far_right)
        greet(self.far_left, self.has_far_left)
        line = jnp.minimum(self.z, 1) + jnp.minimum(LINE - 1 - self.z, 1)
        upper = self.z // 2
        reach = self.p * self.c * (1 - upper) + (1 - self.p) * (1 - self.c) * upper
        pl.semaphore_wait(barrier, 4 + LINE - 1 + line + reach)


class LineFlow:
    def __init__(self, copies, place, block):
        self.copies, self.place, self.block = copies, place, block
        self.ids = {(way, step): copies.new() for way in (1, -1) for step in range(1, LINE)}

    def valid(self, way, step):
        z = self.place.z
        return z >= step if way == 1 else z + step <= LINE - 1

    def origin(self, way, step):
        return self.place.z - way * step

    def onward(self, way, step, source):
        if step == LINE - 1:
            return
        to = self.place.right if way == 1 else self.place.left
        there = self.place.has_right if way == 1 else self.place.has_left
        if step:
            there = there & self.valid(way, step)
        target = self.block(self.origin(way, step))
        self.copies.send(self.ids[way, step + 1], source, target, to, there)

    def start(self, source):
        self.onward(1, 0, source)
        self.onward(-1, 0, source)

    def arrive(self, step, then=None):
        for way in (1, -1):

            def take(way=way):
                target = self.block(self.origin(way, step))
                via = self.place.left if way == 1 else self.place.right
                self.copies.receive(self.ids[way, step], target, via)

            pl.when(self.valid(way, step))(take)
            if step < LINE - 1:
                self.onward(way, step, self.block(self.origin(way, step)))
            if then is not None:
                then(way, step)


class RowsFlow:
    def __init__(self, copies, place, shard, whole):
        self.copies, self.place, self.shard, self.whole = copies, place, shard, whole
        self.line = LineFlow(copies, place, lambda origin: self.rows(origin, place.p, place.c))
        items = [(0, 0)] + [(way, step) for step in range(1, LINE) for way in (1, -1)]
        self.items = items
        self.pair_ids = {item: copies.new() for item in items}
        self.core_ids = {item: copies.new() for item in items}
        self.cross_ids = {item: copies.new() for item in items}

    def rows(self, origin, p, c):
        count = self.shard.shape[0]
        return self.whole.at[pl.ds(pl.multiple_of((origin * 4 + p * 2 + c) * count, count), count)]

    def valid(self, item):
        return None if item == (0, 0) else self.line.valid(*item)

    def spread(self, way, step):
        item, place = (way, step), self.place
        here = self.rows(self.line.origin(way, step), place.p, place.c)
        self.copies.send(self.pair_ids[item], here, here, place.pair, self.valid(item))
        self.copies.send(self.core_ids[item], here, here, place.core, self.valid(item))

    def start(self, own_copy):
        self.line.start(self.shard)
        own_copy()
        self.spread(0, 0)

    def arrive(self, step):
        self.line.arrive(step, self.spread)

    def crossing(self, step):
        place = self.place
        for item in self.items:
            if item[1] != step:
                continue
            there = self.rows(self.line.origin(*item), 1 - place.p, place.c)
            only(
                self.valid(item),
                lambda: self.copies.receive(self.pair_ids[item], there, place.pair),
            )
            self.copies.send(self.cross_ids[item], there, there, place.core, self.valid(item))

    def end(self):
        place = self.place
        for item in self.items:
            origin = self.line.origin(*item)

            def take(item=item, origin=origin):
                mine = self.rows(origin, place.p, 1 - place.c)
                cross = self.rows(origin, 1 - place.p, 1 - place.c)
                self.copies.receive(self.core_ids[item], mine, place.core)
                self.copies.receive(self.cross_ids[item], cross, place.core)

            only(self.valid(item), take)


class QuarterFlow:
    def __init__(self, copies, place, shard, whole, columns, own_sem):
        self.copies, self.place, self.shard, self.whole = copies, place, shard, whole
        self.count, self.whole_width = shard.shape[0], shard.shape[1] // 4
        self.start_column, self.width = columns
        self.own = pltpu.make_async_copy(
            self.columns(place.p, place.c), self.rows(place.p, place.c), own_sem
        )
        self.near = (
            (copies.new(), 1 - place.p, place.c, place.pair),
            (copies.new(), place.p, 1 - place.c, place.core),
            (copies.new(), 1 - place.p, 1 - place.c, place.cross),
        )
        self.line = LineFlow(copies, place, self.block)

    def columns(self, p, c):
        start = (p * 2 + c) * self.whole_width + self.start_column
        return self.shard.at[:, pl.ds(pl.multiple_of(start, LANES), self.width)]

    def rows(self, p, c):
        count = self.count
        start = (self.place.z * 4 + p * 2 + c) * count
        return self.whole.at[pl.ds(pl.multiple_of(start, count), count)]

    def block(self, origin):
        count = 4 * self.count
        return self.whole.at[pl.ds(pl.multiple_of(origin * count, count), count)]

    def start(self):
        place = self.place
        self.own.start()
        for which, p, c, to in self.near:
            self.copies.send(which, self.columns(p, c), self.rows(place.p, place.c), to)

    def join(self):
        self.own.wait()
        for which, p, c, to in self.near:
            self.copies.receive(which, self.rows(p, c), to)
        self.line.start(self.block(self.place.z))

    def arrive(self, step):
        self.line.arrive(step)


class FourFlow:
    def __init__(self, copies, place, slots, parts):
        self.copies, self.place, self.slots = copies, place, slots
        self.rows = slots.shape[0] // 4
        self.size = self.rows // parts
        self.ids = [[copies.new() for _ in range(3)] for _ in range(parts)]

    def slot(self, which, part):
        return self.slots.at[pl.ds(which * self.rows + part * self.size, self.size)]

    def send(self, part, source):
        self.copies.send(self.ids[part][0], source, self.slot(1, part), self.place.pair)
        self.copies.send(self.ids[part][1], source, self.slot(2, part), self.place.core)

    def cross(self, part):
        got = self.slot(1, part)
        self.copies.receive(self.ids[part][0], got, self.place.pair)
        self.copies.send(self.ids[part][2], got, self.slot(3, part), self.place.core)

    def end(self, part):
        self.copies.receive(self.ids[part][1], self.slot(2, part), self.place.core)
        self.copies.receive(self.ids[part][2], self.slot(3, part), self.place.core)


def fetch(source, target, sem):
    copy = pltpu.make_async_copy(source, target, sem)
    copy.start()
    copy.wait()


def add_to(target, source):
    target[...] = low(wide(target[...]) + wide(source[...]))


class LineScatter:
    def __init__(self, copies, place, block, arrived, stage, sem):
        self.copies, self.place, self.block = copies, place, block
        self.arrived, self.stage, self.sem = arrived, stage, sem
        self.ids = {(way, step): copies.new() for way in (1, -1) for step in range(1, LINE)}

    def landing(self, way, step):
        return self.arrived.at[(1 - way) // 2, step - 1]

    def target(self, way, step):
        return self.block(self.place.z + way * (LINE - step))

    def takes(self, way, step):
        z = self.place.z
        if way == 1:
            return (z >= 1) & (z <= step)
        return (z <= LINE - 2) & (z >= LINE - 1 - step)

    def send(self, way, step, cond):
        to = self.place.right if way == 1 else self.place.left
        self.copies.send(
            self.ids[way, step], self.target(way, step), self.landing(way, step), to, cond
        )

    def start(self, ways=(1, -1)):
        for way in ways:
            for step in range(1, LINE):
                self.send(way, step, self.place.z == (0 if way == 1 else LINE - 1))

    def take(self, way, step):
        via = self.place.left if way == 1 else self.place.right
        self.copies.receive(self.ids[way, step], self.landing(way, step), via)
        fetch(self.landing(way, step), self.stage, self.sem)

    def step(self, step, ways=(1, -1)):
        for way in ways:
            there = self.takes(way, step - 1)

            def add(way=way):
                self.take(way, step - 1)
                add_to(self.target(way, step), self.stage)

            pl.when(there)(add)
            self.send(way, step, there)

    def finish(self, add):
        for way in (1, -1):

            def last(way=way):
                self.take(way, LINE - 1)
                add()

            pl.when(self.takes(way, LINE - 1))(last)


class QuarterScatter:
    def __init__(self, copies, place, grad, owner, columns, arrived, stage, sem, line=LineScatter):
        self.copies, self.place, self.grad, self.owner, self.sem = copies, place, grad, owner, sem
        self.stage = stage
        self.count, self.whole_width = owner.shape[0], owner.shape[1] // 4
        self.start_column, self.width = columns
        self.line = line(copies, place, self.block, arrived, stage, sem)
        self.near = (
            (copies.new(), 1 - place.p, place.c, place.pair),
            (copies.new(), place.p, 1 - place.c, place.core),
            (copies.new(), 1 - place.p, 1 - place.c, place.cross),
        )

    def block(self, origin):
        count = 4 * self.count
        return self.grad.at[pl.ds(pl.multiple_of(origin * count, count), count)]

    def rows(self, p, c):
        count = self.count
        start = (self.place.z * 4 + p * 2 + c) * count
        return self.grad.at[pl.ds(pl.multiple_of(start, count), count)]

    def columns(self, p, c):
        start = (p * 2 + c) * self.whole_width + self.start_column
        return self.owner.at[:, pl.ds(pl.multiple_of(start, LANES), self.width)]

    def finish(self):
        place = self.place
        self.line.finish(lambda: add_to(self.block(place.z), self.stage))
        for which, p, c, to in self.near:
            self.copies.send(which, self.rows(p, c), self.columns(place.p, place.c), to)
        fetch(self.rows(place.p, place.c), self.columns(place.p, place.c), self.sem)

    def end(self):
        for which, p, c, to in self.near:
            self.copies.receive(which, self.columns(p, c), to)


class ShortScatter:
    def __init__(self, copies, place, block, arrived, stage, sem):
        self.copies, self.place, self.block = copies, place, block
        self.arrived, self.stage, self.sem = arrived, stage, sem
        self.ids = {way: {name: copies.new() for name in "abcdef"} for way in (1, -1)}

    def at(self, way, k):
        return self.place.z == (k if way == 1 else LINE - 1 - k)

    def there(self, way, k):
        return k if way == 1 else LINE - 1 - k

    def landing(self, way, name):
        return self.arrived.at[(1 - way) // 2, 0 if name in "abc" else 1]

    def send(self, way, name, head, k, to):
        self.copies.send(
            self.ids[way][name],
            self.block(self.there(way, k)),
            self.landing(way, name),
            {RING: self.there(way, to)},
            self.at(way, head),
        )

    def take(self, way, name, source):
        landing = self.landing(way, name)
        self.copies.receive(self.ids[way][name], landing, {RING: self.there(way, source)})
        fetch(landing, self.stage, self.sem)

    def start(self, ways=(1, -1), names="abcd"):
        for name, head, k, to in (("a", 0, 2, 1), ("b", 1, 3, 2), ("c", 0, 3, 3), ("d", 0, 1, 1)):
            for way in ways:
                if name in names:
                    self.send(way, name, head, k, to)

    def step(self, ways=(1, -1)):
        for way in ways:
            for k, name, onward in ((1, "a", "e"), (2, "b", "f")):

                def add(way=way, k=k, name=name):
                    self.take(way, name, k - 1)
                    add_to(self.block(self.there(way, k + 1)), self.stage)

                pl.when(self.at(way, k))(add)
                self.send(way, onward, k, k + 1, k + 1)

    def finish(self, add):
        for way in (1, -1):
            for k, name, source in ((1, "d", 0), (2, "e", 1), (3, "c", 0), (3, "f", 2)):

                def last(way=way, name=name, source=source):
                    self.take(way, name, source)
                    add()

                pl.when(self.at(way, k))(last)


class DirectScatter:
    def __init__(self, copies, place, block, arrived, stage, sem):
        self.copies, self.place, self.block = copies, place, block
        self.arrived, self.stage, self.sem = arrived, stage, sem
        self.ids = {(way, far): copies.new() for way in (1, -1) for far in range(1, LINE)}

    def landing(self, way, far):
        return self.arrived.at[(1 - way) // 2, far - 1]

    def reaches(self, way, far):
        return self.place.z + far < LINE if way == 1 else self.place.z >= far

    def start(self):
        for far in range(LINE - 1, 0, -1):
            for way in (1, -1):
                there = self.place.z + way * far
                self.copies.send(
                    self.ids[way, far],
                    self.block(there),
                    self.landing(way, far),
                    {RING: there},
                    self.reaches(way, far),
                )

    def finish(self, add):
        for way in (1, -1):
            for far in range(1, LINE):

                def take(way=way, far=far):
                    via = {RING: self.place.z - way * far}
                    self.copies.receive(self.ids[way, far], self.landing(way, far), via)
                    fetch(self.landing(way, far), self.stage, self.sem)
                    add()

                pl.when(self.reaches(-way, far))(take)


class RowsScatter:
    def __init__(self, copies, place, whole, from_core, from_pair, arrived, stage, sem):
        self.copies, self.place, self.whole, self.sem = copies, place, whole, sem
        self.from_core, self.from_pair = from_core, from_pair
        self.count, self.columns = from_pair.shape[1], from_pair.shape[2]
        self.stage = stage
        self.core_id = copies.new()
        self.pair_ids = [copies.new() for _ in range(LINE)]
        self.line = DirectScatter(
            copies, place, lambda d: self.part(place.c, place.p, d), arrived, self.small(1), sem
        )

    def small(self, blocks):
        return self.stage.at[pl.ds(0, blocks * self.count), pl.ds(0, self.columns)]

    def part(self, c, p, origin, blocks=1):
        start = ((c * 2 + p) * LINE + origin) * self.count
        return self.whole.at[
            pl.ds(pl.multiple_of(start, self.count), blocks * self.count), pl.ds(0, self.columns)
        ]

    def fill(self, origin, value):
        for p in range(2):
            for c in range(2):
                start = (p * 2 + c) * self.count
                self.part(c, p, origin)[...] = value[start : start + self.count]

    def start(self):
        place = self.place
        self.copies.send(
            self.core_id, self.part(1 - place.c, 0, 0, 2 * LINE), self.from_core, place.core
        )

    def halve(self):
        place = self.place
        self.copies.receive(self.core_id, self.from_core, place.core)
        size = LINE * self.count
        for p in (1 - place.p, place.p):
            start = pl.multiple_of(p * size, size)
            fetch(self.from_core.at[pl.ds(start, size)], self.small(LINE), self.sem)
            add_to(self.part(place.c, p, 0, LINE), self.small(LINE))
            if p is place.p:
                continue
            for origin in (3, 0, 2, 1):
                self.copies.send(
                    self.pair_ids[origin],
                    self.part(place.c, p, origin),
                    self.from_pair.at[origin],
                    place.pair,
                )

    def quarter(self):
        place = self.place
        for origin in (3, 0, 2, 1):
            self.copies.receive(self.pair_ids[origin], self.from_pair.at[origin], place.pair)
            fetch(self.from_pair.at[origin], self.small(1), self.sem)
            add_to(self.part(place.c, place.p, origin), self.small(1))

    def finish(self, out):
        out[...] = wide(self.part(self.place.c, self.place.p, self.place.z)[...])

        def add():
            out[...] += wide(self.small(1)[...])

        self.line.finish(add)


PARTS = 4
NORMED_TILE = 768
BEFORE, NOW = 1, 5
N_REMOTE = 300
SUM_ROWS = 32


def eight_rows(value):
    return jnp.sum(value.reshape(-1, 8, value.shape[-1]), axis=0)


def layer_kernel(
    heads,
    head_size,
    tokens,
    first_shard,
    out_shard,
    gate_shard,
    up_shard,
    down_shard,
    grad_out,
    biases,
    cosine,
    sine,
    own_segments,
    own_positions,
    key_segments,
    key_positions,
    output,
    input_grad,
    grad_first,
    grad_w_out,
    grad_w_down,
    grad_w_gate,
    grad_w_up,
    sums_out,
    first_kept,
    normed_kept,
    line_landing,
    out_core_landing,
    out_pair_landing,
    out_other_landing,
    first_core_landing,
    first_pair_landing,
    first_line_landing,
    wo_core_landing,
    wo_pair_landing,
    wo_line_landing,
    first_all,
    w_out_all,
    state,
    window,
    keys,
    values,
    mail,
    query,
    heads_out,
    gate_all,
    up_all,
    down_all,
    normed_four,
    grad_four,
    hidden,
    grad_gate,
    grad_up,
    early_up,
    early_gate,
    pair_landing,
    other_landing,
    stage,
    grad_keys,
    grad_values,
    own_grad,
    window_landing,
    core_window,
    first_scale,
    second_scale,
    totals,
    sums,
    sums_landing,
    line_sums,
    send_sems,
    recv_sems,
    local_sems,
):
    place = Place()
    copies = Copies(send_sems, recv_sems)
    rows, width = tokens.shape
    batches = own_segments.shape[0]
    per_batch = rows // batches
    query_width = heads * head_size
    kv_width = query_width + 2 * head_size
    size = rows // PARTS
    root = 1.0 / math.sqrt(head_size)
    sem = local_sems.at[0]

    window[...] = jnp.zeros_like(window)
    place.meet()

    first = RowsFlow(copies, place, first_shard, first_all)
    outs = RowsFlow(copies, place, out_shard, w_out_all)
    quarter = gate_all.shape[1]
    first_half = -(-quarter // (2 * LANES)) * LANES
    halves = ((0, first_half), (first_half, quarter - first_half))

    def part_of(whole, half):
        return whole.at[:, pl.ds(*halves[half])]

    gates, ups, downs = [
        [
            QuarterFlow(
                copies, place, shard, part_of(whole, half), halves[half], local_sems.at[2 + i * 2 + half]
            )
            for half in range(2)
        ]
        for i, (shard, whole) in enumerate(
            ((gate_shard, gate_all), (up_shard, up_all), (down_shard, down_all))
        )
    ]
    cot = FourFlow(copies, place, grad_four, PARTS)
    second = FourFlow(copies, place, normed_four, PARTS)
    part_ids = [copies.new() for _ in range(PARTS)]
    window_ids = [copies.new() for _ in range(4)]
    window_core_ids = [copies.new() for _ in range(4)]

    def put(flow, sem):
        return lambda: fetch(flow.shard, flow.rows(place.z, place.p, place.c), sem)

    first.start(put(first, sem))
    gates[0].start()
    x = wide(tokens[...])
    first_scale[...] = lax.rsqrt(jnp.mean(x * x, axis=-1, keepdims=True) + EPSILON)
    state[...] = x * first_scale[...]
    outs.line.start(out_shard)
    first.crossing(0)
    first.arrive(1)
    outs.line.arrive(1)
    first.arrive(2)
    outs.line.arrive(2)
    first.arrive(3)
    ups[0].start()
    outs.line.arrive(3)
    gates[0].join()
    put(outs, sem)()
    for step in range(1, LINE):
        first.crossing(step)
    first.end()

    gains = wide(first_all[:, kv_width:]).T
    first_gain, second_gain = gains[0:1], gains[1:2]
    first_normed = mail.at[pl.ds(0, rows)]
    first_normed[...] = low(state[...] * first_gain)
    sign = jnp.where(
        lax.broadcasted_iota(jnp.int32, (1, head_size), 1) < head_size // 2, -1.0, 1.0
    )

    def project(start, size):
        raw = matmul(first_normed[...], first_all[:, start : start + size])
        return raw + biases[:, start : start + size]

    def turned(raw):
        half_turn = pltpu.roll(raw, head_size // 2, 1)
        return low(raw * cosine[...] + half_turn * (sine[...] * sign))

    def turned_back(gradient, mine):
        half_turn = pltpu.roll(gradient * sine[mine], head_size // 2, 1)
        return low(gradient * cosine[mine] - half_turn * sign)

    kv = project(query_width, 2 * head_size)
    key_now, value_now = turned(kv[:, :head_size]), low(kv[:, head_size:])
    for b in range(batches):
        mine = slice(b * per_batch, (b + 1) * per_batch)
        window[NOW + place.q, b, :, :head_size] = key_now[mine]
        window[NOW + place.q, b, :, head_size:] = value_now[mine]
    mine_now = window.at[NOW + place.q]
    copies.send(window_ids[0], mine_now, mine_now, place.pair)
    copies.send(window_core_ids[0], mine_now, mine_now, place.core)
    before = window.at[BEFORE + place.q]
    copies.send(window_ids[1], mine_now, before, place.right, place.has_right)
    copies.send(window_ids[2], mine_now, before, place.right_cross, place.has_right)
    copies.send(window_ids[3], mine_now, window.at[0], place.far_right, place.has_far_right)
    for h in range(0, heads, 2):
        raw = project(h * head_size, 2 * head_size)
        query[:, h * head_size : (h + 1) * head_size] = turned(raw[:, :head_size])
        query[:, (h + 1) * head_size : (h + 2) * head_size] = turned(raw[:, head_size:])
    keep_first = pltpu.make_async_copy(first_all, first_kept, local_sems.at[1])
    keep_first.start()
    for item in outs.items:
        outs.spread(*item)
    downs[0].start()
    ups[0].join()
    gates[0].arrive(1)
    copies.receive(window_ids[0], window.at[NOW + place.q_pair], place.pair)
    copies.send(
        window_core_ids[1],
        window.at[NOW + place.q_pair],
        window.at[NOW + place.q_pair],
        place.core,
    )

    def take_before():
        copies.receive(window_ids[1], window.at[BEFORE + place.q], place.left)
        copies.receive(window_ids[2], window.at[BEFORE + place.q_pair], place.left_cross)

    pl.when(place.has_left)(take_before)
    for i, at in ((2, BEFORE + place.q), (3, BEFORE + place.q_pair)):
        copies.send(window_core_ids[i], window.at[at], window.at[at], place.core, place.has_left)
    only(
        place.has_far_left,
        lambda: copies.receive(window_ids[3], window.at[0], place.far_left),
    )
    copies.receive(window_core_ids[0], window.at[NOW + place.q_core], place.core)
    copies.receive(window_core_ids[1], window.at[NOW + place.q_cross], place.core)

    def take_before_core():
        copies.receive(window_core_ids[2], window.at[BEFORE + place.q_core], place.core)
        copies.receive(window_core_ids[3], window.at[BEFORE + place.q_cross], place.core)

    pl.when(place.has_left)(take_before_core)
    cot_own = pltpu.make_async_copy(grad_out, grad_four.at[pl.ds(0, rows)], local_sems.at[8])
    cot_own.start()
    for i in range(PARTS):
        cot.send(i, grad_out.at[pl.ds(i * size, size)])

    def take_window(b):
        for slot in range(BACK + 1):
            at, there = place.q + slot, slice(slot * per_batch, (slot + 1) * per_batch)
            keys[there] = window[at, b, :, :head_size]
            values[there] = window[at, b, :, head_size:]

    def probabilities(b, mine, columns):
        scores = times_transpose(query[mine, columns], keys[...]) * root
        allowed = (own_segments[b] == key_segments[b]) & (key_positions[b] <= own_positions[b])
        scores = jnp.where(allowed, scores, NEGATIVE)
        weights = jnp.exp(scores - jnp.max(scores, axis=-1, keepdims=True))
        return weights * (1.0 / jnp.sum(weights, axis=-1, keepdims=True))

    part_own, part_other = mail.at[pl.ds(0, rows)], mail.at[pl.ds(rows, rows)]
    for b in range(batches):
        take_window(b)
        mine = slice(b * per_batch, (b + 1) * per_batch)

        def attend_head(h, carry, b=b, mine=mine):
            columns = pl.ds(pl.multiple_of(h * head_size, head_size), head_size)
            probs = low(probabilities(b, mine, columns))
            heads_out[mine, columns] = low(matmul(probs, values[...]))
            return carry

        lax.fori_loop(0, heads, attend_head, 0)
        if b == 0:
            for step in range(LINE):
                outs.crossing(step)
            outs.end()
            ups[0].arrive(1)
        part = low(times_transpose(heads_out[mine], w_out_all[...]))
        part_own[mine] = part
        for i in range(b * per_batch // size, (b + 1) * per_batch // size):
            block = pl.ds(i * size, size)
            copies.send(part_ids[i], part_own.at[block], part_other.at[block], place.other)
    early = copies.mark()

    for i in range(PARTS):
        block = pl.ds(i * size, size)
        copies.receive(part_ids[i], part_other.at[block], place.other)
        copies.left(part_ids[i])
        row_sum = wide(tokens[block]) + (wide(part_own[block]) + wide(part_other[block]))
        state[block] = row_sum
        scale_row = lax.rsqrt(jnp.mean(row_sum * row_sum, axis=-1, keepdims=True) + EPSILON)
        second_scale[block] = scale_row
        second.slot(0, i)[...] = low(row_sum * scale_row * second_gain)
        second.send(i, second.slot(0, i))
        if i == 0:
            gates[0].arrive(2)
            downs[0].join()
        if i == PARTS // 2:
            ups[0].arrive(2)
    downs[0].arrive(1)
    for flow in (gates[1], ups[1], downs[1]):
        flow.start()
    for part in range(PARTS):
        cot.cross(part)
        cot.end(part)
    for part in range(PARTS):
        second.cross(part)
    downs[0].arrive(2)
    keep_first.wait()
    for i in range(PARTS):
        second.end(i)
    gates[0].arrive(3)
    ups[0].arrive(3)

    tile = 256

    def forward_half(half):
        columns = pl.ds(*halves[half])

        def forward_tile(t, carry):
            block = pl.ds(pl.multiple_of(t * tile, tile), tile)
            gate = matmul(normed_four[block], gate_all[:, columns])
            up = matmul(normed_four[block], up_all[:, columns])
            sigmoid = 1.0 / (1.0 + jnp.exp(-gate))
            silu = gate * sigmoid
            hidden[block, columns] = low(silu * up)
            grad_up[block, columns] = low(silu)
            grad_gate[block, columns] = low(up * sigmoid * (1.0 + gate * (1.0 - sigmoid)))
            return carry

        lax.fori_loop(0, 4 * rows // tile, forward_tile, 0)

    def backward_half(half):
        columns = pl.ds(*halves[half])

        def backward_tile(t, carry):
            block = pl.ds(pl.multiple_of(t * tile, tile), tile)
            back = matmul(grad_four[block], down_all[:, columns])
            grad_gate[block, columns] = low(back * wide(grad_gate[block, columns]))
            grad_up[block, columns] = low(back * wide(grad_up[block, columns]))
            return carry

        lax.fori_loop(0, 4 * rows // tile, backward_tile, 0)

    def columns_of(d):
        return pl.ds(pl.multiple_of(d * rows, rows), rows)

    def weight_grad(target, left_side, right_side, half):
        columns = pl.ds(*halves[half])

        def block(d, carry):
            part = contract_rows(left_side[:, columns_of(d)], right_side[:, columns])
            target[columns_of(d)] = low(part)
            return carry

        lax.fori_loop(0, LINE, block, 0)

    grad_down = first_all
    down_backs, up_backs, gate_backs = [
        [
            QuarterScatter(
                copies,
                place,
                grads[half],
                owner,
                halves[half],
                line_landing.at[i * 2 + half, :, :, :, pl.ds(0, halves[half][1])],
                stage.at[:, pl.ds(0, halves[half][1])],
                sem,
                (LineScatter, ShortScatter)[half],
            )
            for half in range(2)
        ]
        for i, (grads, owner) in enumerate(
            (
                ([part_of(grad_down, 0), part_of(grad_down, 1)], grad_w_down),
                ([early_up, part_of(up_all, 1)], grad_w_up),
                ([early_gate, part_of(gate_all, 1)], grad_w_gate),
            )
        )
    ]

    forward_half(0)
    copies.settle(early)
    cot_own.wait()
    for flow in (gates[1], ups[1], downs[1]):
        flow.join()
    weight_grad(down_backs[0].grad, grad_four, hidden, 0)
    down_backs[0].line.start()
    downs[0].arrive(3)
    backward_half(0)
    weight_grad(up_backs[0].grad, normed_four, grad_up, 0)
    up_backs[0].line.start()
    weight_grad(gate_backs[0].grad, normed_four, grad_gate, 0)
    gate_backs[0].line.start()
    for flow in (gates[1], ups[1], downs[1]):
        flow.arrive(1)

    first_columns, later_columns = pl.ds(*halves[0]), pl.ds(*halves[1])
    step = halves[1][1]
    spares = (hidden, grad_gate, grad_up)[: width // step]
    for i, spare in enumerate(spares):

        def first_normed_tile(t, carry, i=i, spare=spare):
            block = columns_of(t)
            spare[block, later_columns] = low(
                times_transpose(grad_gate[block, first_columns], gate_all[i * step : (i + 1) * step, first_columns])
                + times_transpose(grad_up[block, first_columns], up_all[i * step : (i + 1) * step, first_columns])
            )
            return carry

        lax.fori_loop(0, 4, first_normed_tile, 0)
    keeps = [
        pltpu.make_async_copy(
            spare.at[:, later_columns],
            normed_kept.at[:, pl.ds(i * step, step)],
            local_sems.at[10 + i],
        )
        for i, spare in enumerate(spares)
    ]
    for keep in keeps:
        keep.start()
    down_backs[0].line.step(2)
    for flow in (gates[1], ups[1], downs[1]):
        flow.arrive(2)
    down_backs[0].line.step(3)
    for keep in keeps:
        keep.wait()
    gates[1].arrive(3)
    ups[1].arrive(3)

    forward_half(1)
    weight_grad(down_backs[1].grad, grad_four, hidden, 1)
    down_backs[1].line.start()
    up_backs[0].line.step(2)
    downs[1].arrive(3)
    backward_half(1)
    for flow in (cot, second):
        for ids in flow.ids:
            copies.settle_of(ids)
    for flow in (gates[1], ups[1]):
        copies.settle_of(flow.line.ids.values())

    normed_grad = grad_four
    core_ids = [copies.new() for _ in range(2)]
    pair_ids = [copies.new() for _ in range(PARTS)]
    other_ids = [copies.new() for _ in range(PARTS)]

    def slot(which, part=0, parts=1):
        return pl.ds(which * rows + part * (rows // parts), rows // parts)

    order = (3, 1, 2, 0)
    backs = [
        pltpu.make_async_copy(
            normed_kept.at[slot(which)], normed_grad.at[slot(which)], local_sems.at[10 + which]
        )
        for which in range(4)
    ]
    for which in order:
        backs[which].start()

    def normed_slot(which):
        backs[which].wait()

        def column_tile(t, carry):
            columns = pl.ds(pl.multiple_of(t * NORMED_TILE, NORMED_TILE), NORMED_TILE)
            normed_grad[slot(which), columns] = low(
                wide(normed_grad[slot(which), columns])
                + times_transpose(grad_gate[slot(which), later_columns], gate_all[columns, later_columns])
                + times_transpose(grad_up[slot(which), later_columns], up_all[columns, later_columns])
            )
            return carry

        lax.fori_loop(0, width // NORMED_TILE, column_tile, 0)

    def send_core(i):
        copies.send(
            core_ids[i], normed_grad.at[slot(2 + i)], mail.at[pl.ds(i * rows, rows)], place.core
        )

    normed_slot(3)
    send_core(1)
    normed_slot(1)
    copies.receive(core_ids[1], mail.at[pl.ds(rows, rows)], place.core)
    for i in range(PARTS):
        block = slot(1, i, PARTS)
        add_to(normed_grad.at[block], mail.at[pl.ds(rows + i * size, size)])
        copies.send(
            pair_ids[i],
            normed_grad.at[block],
            pair_landing.at[pl.ds(i * size, size)],
            place.pair,
        )
    normed_slot(2)
    send_core(0)
    normed_slot(0)
    copies.receive(core_ids[0], mail.at[pl.ds(0, rows)], place.core)
    add_to(normed_grad.at[slot(0)], mail.at[pl.ds(0, rows)])
    weight_grad(up_backs[1].grad, normed_four, grad_up, 1)
    up_backs[1].line.start((1,))
    up_backs[1].line.start((-1,), "b")
    down_backs[0].finish()
    up_backs[0].line.step(3)
    out_sum = normed_four
    out_core_id, out_pair_id, out_other_id = copies.new(), copies.new(), copies.new()
    first_weights = hidden
    first_fetch = pltpu.make_async_copy(first_kept, first_weights, local_sems.at[9])

    def out_tile(t, carry):
        block = columns_of(t)
        out_sum[block] = low(times_transpose(hidden[block], down_all[...]))
        return carry

    for i in range(PARTS):
        block = pl.ds(i * size, size)
        copies.receive(pair_ids[i], pair_landing.at[block], place.pair)
        add_to(normed_grad.at[block], pair_landing.at[block])
        copies.send(other_ids[i], normed_grad.at[block], other_landing.at[block], place.other)
        if i == 0:
            weight_grad(gate_backs[1].grad, normed_four, grad_gate, 1)
            gate_backs[1].line.start((1,))
            gate_backs[1].line.start((-1,), "b")
        if i == 1:
            lax.fori_loop(0, 4, out_tile, 0)
            copies.send(
                out_core_id, out_sum.at[pl.ds(2 * rows, 2 * rows)], out_core_landing, place.core
            )
            first_fetch.start()
        if i == 2:
            gate_backs[0].line.step(2)
    spare = mail.at[pl.ds(rows, rows)]
    copies.receive(out_core_id, out_core_landing, place.core)
    fetch(out_core_landing.at[pl.ds(rows, rows)], spare, sem)
    add_to(out_sum.at[slot(1)], spare)
    copies.send(out_pair_id, out_sum.at[slot(1)], out_pair_landing, place.pair)
    grad_own = mail.at[pl.ds(rows, rows)]
    grad_branch = mail.at[pl.ds(0, rows)]
    fetch(grad_out, grad_own, sem)
    second_sum = totals.at[:, pl.ds(kv_width, width)]
    second_sum[...] = jnp.zeros_like(second_sum)
    for i in range(PARTS):
        block = pl.ds(i * size, size)
        copies.receive(other_ids[i], other_landing.at[block], place.other)
        back = wide(normed_grad[block]) + wide(other_landing[block])
        scale_row = second_scale[block]
        unit = state[block] * scale_row
        second_sum[...] += eight_rows(back * unit)
        grad_state = wide(grad_own[block]) + norm_back(back, unit, scale_row, second_gain)
        input_grad[block] = grad_state
        grad_branch[block] = low(grad_state)

    grad_heads = grad_up.at[pl.ds(0, rows), pl.ds(0, query_width)]
    grad_raw = grad_up.at[pl.ds(rows, rows), pl.ds(0, kv_width)]
    grad_heads[...] = low(matmul(grad_branch[...], w_out_all[...]))
    back_ids = [copies.new() for _ in range(4)]
    back_core_ids = [copies.new() for _ in range(4)]
    for b in range(batches):
        take_window(b)
        mine = slice(b * per_batch, (b + 1) * per_batch)
        grad_keys[...] = jnp.zeros_like(grad_keys)
        grad_values[...] = jnp.zeros_like(grad_values)

        def attend_back_head(h, carry, b=b, mine=mine):
            columns = pl.ds(pl.multiple_of(h * head_size, head_size), head_size)
            probs = probabilities(b, mine, columns)
            grad_head = grad_heads[mine, columns]
            grad_probs = times_transpose(grad_head, values[...])
            row_inner = jnp.sum(probs * grad_probs, axis=-1, keepdims=True)
            grad_scores = low(probs * (grad_probs - row_inner))
            grad_raw[mine, columns] = turned_back(matmul(grad_scores, keys[...]) * root, mine)
            grad_keys[...] += contract_rows(grad_scores, query[mine, columns])
            grad_values[...] += contract_rows(low(probs), grad_head)
            return carry

        lax.fori_loop(0, heads, attend_back_head, 0)
        for at in range(NOW + 4):
            window[at, b] = jnp.zeros_like(window[at, b])
        for back in range(BACK + 1):
            at, there = place.q + back, slice(back * per_batch, (back + 1) * per_batch)
            window[at, b, :, :head_size] = low(grad_keys[there] * root)
            window[at, b, :, head_size:] = low(grad_values[there])
        own_grad[mine, :head_size] = grad_keys[there] * root
        own_grad[mine, head_size:] = grad_values[there]
    theirs = (NOW + place.q_core, NOW + place.q_cross, BEFORE + place.q_core, BEFORE + place.q_cross)
    ours = (NOW + place.q, NOW + place.q_pair, BEFORE + place.q, BEFORE + place.q_pair)
    for i in range(4):
        copies.send(back_core_ids[i], window.at[theirs[i]], core_window.at[i], place.core)
    copies.send(
        back_ids[3], window.at[0], window_landing.at[3], place.far_left, place.has_far_left
    )


    def add_own(landing):
        for b in range(batches):
            own_grad[b * per_batch : (b + 1) * per_batch] += wide(landing[b])

    for i in (1, 2, 3):
        copies.receive(back_core_ids[i], core_window.at[i], place.core)
        for b in range(batches):
            add_to(window.at[ours[i], b], core_window.at[i, b])
    copies.send(back_ids[0], window.at[ours[1]], window_landing.at[0], place.pair)
    copies.send(back_ids[1], window.at[ours[2]], window_landing.at[1], place.left, place.has_left)
    copies.send(
        back_ids[2], window.at[ours[3]], window_landing.at[2], place.left_cross, place.has_left
    )
    up_backs[0].finish()
    gate_backs[0].line.step(3)
    for name in "acd":
        up_backs[1].line.start((-1,), name)
        gate_backs[1].line.start((-1,), name)
    copies.receive(back_core_ids[0], core_window.at[0], place.core)
    add_own(core_window.at[0])
    wo_back = RowsScatter(
        copies, place, w_out_all, wo_core_landing, wo_pair_landing, wo_line_landing, stage, sem
    )
    for origin in range(LINE):
        branch = grad_branch[:, origin * rows : (origin + 1) * rows]
        wo_back.fill(origin, low(contract_rows(branch, heads_out[...])))
    wo_back.start()
    wo_back.halve()
    down_backs[1].line.step()
    up_backs[1].line.step((1,))
    fetch(out_core_landing.at[pl.ds(0, rows)], spare, sem)
    add_to(out_sum.at[slot(0)], spare)
    copies.receive(out_pair_id, out_pair_landing, place.pair)
    fetch(out_pair_landing, spare, sem)
    add_to(out_sum.at[slot(0)], spare)
    copies.send(out_other_id, out_sum.at[slot(0)], out_other_landing, place.other)
    copies.receive(back_ids[0], window_landing.at[0], place.pair)
    add_own(window_landing.at[0])

    def take_after():
        copies.receive(back_ids[1], window_landing.at[1], place.right)
        add_own(window_landing.at[1])
        copies.receive(back_ids[2], window_landing.at[2], place.right_cross)
        add_own(window_landing.at[2])

    pl.when(place.has_right)(take_after)

    def take_far():
        copies.receive(back_ids[3], window_landing.at[3], place.far_right)
        add_own(window_landing.at[3])

    pl.when(place.has_far_right)(take_far)
    every = slice(0, rows)
    grad_raw[:, query_width : query_width + head_size] = turned_back(
        own_grad[:, :head_size], every
    )
    grad_raw[:, query_width + head_size :] = low(own_grad[:, head_size:])
    first_back = RowsScatter(
        copies,
        place,
        grad_gate,
        first_core_landing,
        first_pair_landing,
        first_line_landing,
        stage,
        sem,
    )
    first_normed[...] = low(wide(tokens[...]) * first_scale[...] * first_gain)
    for origin in range(LINE):
        normed = first_normed[:, origin * rows : (origin + 1) * rows]
        first_back.fill(origin, low(contract_rows(normed, grad_raw[...])))
    first_back.start()

    first_ids = [copies.new() for _ in range(PARTS)]
    sum_ids = [copies.new() for _ in range(3)]
    first_at = kv_width + width
    first_own, first_other = mail.at[pl.ds(0, rows)], pair_landing
    first_fetch.wait()

    def first_tile(t, carry):
        block = pl.ds(pl.multiple_of(t * tile, tile), tile)
        part = times_transpose(grad_raw[...], first_weights[block, :kv_width])
        first_own[:, block] = low(part)
        unit = wide(tokens[:, block]) * first_scale[...]
        at = pl.ds(pl.multiple_of(first_at + t * tile, tile), tile)
        totals[:, at] = eight_rows(part * unit)
        return carry

    lax.fori_loop(0, width // tile, first_tile, 0)
    totals[:, :kv_width] = eight_rows(wide(grad_raw[...]))

    def sum_row(t, carry):
        columns = pl.ds(pl.multiple_of(t * LANES, LANES), LANES)
        sums[0, pl.ds(t, 1)] = jnp.sum(totals[:, columns], axis=0, keepdims=True)
        return carry

    lax.fori_loop(0, sums.shape[1], sum_row, 0)
    shared = first_at // LANES

    def sum_step(i, to):
        copies.send(sum_ids[i], sums.at[i], sums_landing.at[i], to)

    def sum_take(i, to):
        copies.receive(sum_ids[i], sums_landing.at[i], to)
        sums[i + 1] = sums[i]
        if i == 0:
            sums[1, shared:] += sums_landing[0, shared:]
        else:
            sums[i + 1] += sums_landing[i]

    def sum_line(way, far):
        return place.z + far < LINE if way == 1 else place.z >= far

    line_sum_ids = {(way, far): copies.new() for way in (1, -1) for far in range(1, LINE)}
    sum_step(0, place.other)
    for i in range(PARTS):
        block = pl.ds(i * size, size)
        copies.send(first_ids[i], first_own.at[block], first_other.at[block], place.other)
    first_back.halve()
    gate_backs[0].finish()
    gate_backs[1].line.step((1,))
    wo_back.quarter()
    wo_back.line.start()
    up_backs[1].line.step((-1,))
    first_back.quarter()
    gate_backs[1].line.step((-1,))
    first_back.line.start()
    sum_take(0, place.other)
    sum_step(1, place.pair)
    for i in range(PARTS):
        block = pl.ds(i * size, size)
        copies.receive(first_ids[i], first_other.at[block], place.other)
        unit = wide(tokens[block]) * first_scale[block]
        back = wide(first_own[block]) + wide(first_other[block])
        input_grad[block] += norm_back(back, unit, first_scale[block], first_gain)
    sum_take(1, place.pair)
    sum_step(2, place.core)
    sum_take(2, place.core)
    line_sums[place.z] = sums[3]
    for way in (1, -1):
        for far in range(1, LINE):
            copies.send(
                line_sum_ids[way, far],
                sums.at[3],
                line_sums.at[place.z],
                {RING: place.z + way * far},
                sum_line(way, far),
            )
    down_backs[1].finish()
    up_backs[1].finish()
    copies.receive(out_other_id, out_other_landing, place.other)
    fetch(out_other_landing, spare, sem)
    spare[...] = low(state[...] + (wide(out_sum[slot(0)]) + wide(spare[...])))
    fetch(spare, output, sem)
    gate_backs[1].finish()
    wo_back.finish(grad_w_out)
    first_back.finish(grad_first)
    for way in (1, -1):
        for far in range(1, LINE):
            source = place.z - way * far

            def take_sums(way=way, far=far, source=source):
                copies.receive(line_sum_ids[way, far], line_sums.at[source], {RING: source})

            pl.when(sum_line(-way, far))(take_sums)
    total = line_sums[0]
    for origin in range(1, LINE):
        total += line_sums[origin]
    sums_out[...] = total
    for scatter in down_backs + up_backs + gate_backs:
        scatter.end()
    copies.settle()


def layer_call(heads, head_size, operands):
    tokens, first_shard, out_shard, gate_shard = operands[:4]
    own_segments = operands[10]
    rows, width = tokens.shape
    batches = own_segments.shape[0]
    per_batch = rows // batches
    count, padded = gate_shard.shape
    quarter = padded // 4
    first_half = -(-quarter // (2 * LANES)) * LANES
    query_width = heads * head_size
    kv_width = query_width + 2 * head_size
    low_type, wide_type = jnp.bfloat16, jnp.float32
    in_vmem, anywhere = pl.BlockSpec(memory_space=pltpu.VMEM), pl.BlockSpec(memory_space=pl.ANY)

    def shape(*dims, kind=low_type):
        return jax.ShapeDtypeStruct(dims, kind)

    def vmem(*dims, kind=low_type):
        return pltpu.VMEM(dims, kind)

    sum_rows = (kv_width + 2 * width) // LANES
    outs = (
        (shape(rows, width), anywhere),
        (shape(rows, width, kind=wide_type), in_vmem),
        (shape(count, kv_width, kind=wide_type), in_vmem),
        (shape(count, query_width, kind=wide_type), in_vmem),
        (shape(count, padded), anywhere),
        (shape(count, padded), anywhere),
        (shape(count, padded), anywhere),
        (shape(sum_rows, LANES, kind=wide_type), in_vmem),
    )
    kept = (
        shape(width, first_shard.shape[1]),
        shape(4 * rows, width),
        shape(6, 2, LINE - 1, 4 * count, first_half),
        shape(2 * rows, width),
        shape(rows, width),
        shape(rows, width),
        shape(2 * LINE * count, kv_width),
        shape(LINE, count, kv_width),
        shape(2, LINE - 1, count, kv_width),
        shape(2 * LINE * count, query_width),
        shape(LINE, count, query_width),
        shape(2, LINE - 1, count, query_width),
    )
    scratch = (
        vmem(width, first_shard.shape[1]),
        vmem(width, query_width),
        vmem(rows, width, kind=wide_type),
        vmem(NOW + 4, batches, per_batch, 2 * head_size),
        vmem((BACK + 1) * per_batch, head_size),
        vmem((BACK + 1) * per_batch, head_size),
        vmem(2 * rows, width),
        vmem(rows, query_width),
        vmem(rows, query_width),
        vmem(width, quarter),
        vmem(width, quarter),
        vmem(width, quarter),
        vmem(4 * rows, width),
        vmem(4 * rows, width),
        vmem(4 * rows, quarter),
        vmem(4 * rows, quarter),
        vmem(4 * rows, quarter),
        vmem(width, first_half),
        vmem(width, first_half),
        vmem(rows, width),
        vmem(rows, width),
        vmem(4 * count, quarter),
        vmem((BACK + 1) * per_batch, head_size, kind=wide_type),
        vmem((BACK + 1) * per_batch, head_size, kind=wide_type),
        vmem(rows, 2 * head_size, kind=wide_type),
        vmem(4, batches, per_batch, 2 * head_size),
        vmem(4, batches, per_batch, 2 * head_size),
        vmem(rows, 1, kind=wide_type),
        vmem(rows, 1, kind=wide_type),
        vmem(8, sum_rows * LANES, kind=wide_type),
        vmem(4, sum_rows, LANES, kind=wide_type),
        vmem(3, sum_rows, LANES, kind=wide_type),
        vmem(LINE, sum_rows, LANES, kind=wide_type),
        pltpu.SemaphoreType.DMA((N_REMOTE,)),
        pltpu.SemaphoreType.DMA((N_REMOTE,)),
        pltpu.SemaphoreType.DMA((14,)),
    )
    results = pl.pallas_call(
        functools.partial(layer_kernel, heads, head_size),
        out_shape=[out[0] for out in outs] + list(kept),
        in_specs=[in_vmem] + [anywhere] * 6 + [in_vmem] * 7,
        out_specs=[out[1] for out in outs] + [anywhere] * len(kept),
        scratch_shapes=scratch,
        compiler_params=pltpu.CompilerParams(
            collective_id=0, has_side_effects=True, vmem_limit_bytes=VMEM_BYTES
        ),
    )(*operands)
    return results[: len(outs)]


def body(
    tokens,
    norm1_gain,
    query_weight,
    query_bias,
    key_weight,
    key_bias,
    value_weight,
    value_bias,
    output_weight,
    norm2_gain,
    gate_weight,
    up_weight,
    down_weight,
    cotangent,
    segments,
    positions,
):
    batches, count_rows, width = tokens.shape
    heads, head_size = query_bias.shape
    query_width = heads * head_size
    units = gate_weight.shape[1]
    place = lax.axis_index(FSDP)
    row_start = place * count_rows
    rows = batches * count_rows

    gains = jnp.stack([norm1_gain, norm2_gain], axis=1)
    gains = jnp.pad(gains, ((0, 0), (0, LANES - 2)))
    first_shard = jnp.concatenate([query_weight, key_weight, value_weight, gains], axis=1)
    kv_width = query_width + 2 * head_size
    padded = -(-units // (4 * LANES)) * (4 * LANES)

    def spaced(shard):
        return jnp.pad(shard, ((0, 0), (0, padded - units)))

    grad_out = cotangent.reshape(rows, width)
    inputs = wide(tokens.reshape(rows, width))
    biases = jnp.concatenate(
        [query_bias.reshape(-1), key_bias.reshape(-1), value_bias.reshape(-1)]
    )
    own_places = lax.dynamic_slice_in_dim(positions, row_start, count_rows, axis=1)
    cosine, sine_table = rotation(own_places.reshape(-1), head_size)
    if lax.axis_size(RING) == LINE:
        key_segments, key_positions = [], []
        for b in range(batches):
            padding = jnp.full((BACK * count_rows,), -1, jnp.int32)
            for rows_of, padded_rows in ((key_segments, segments), (key_positions, positions)):
                padded_rows = jnp.concatenate([padding, padded_rows[b]])
                rows_of.append(
                    lax.dynamic_slice_in_dim(padded_rows, row_start, (BACK + 1) * count_rows)
                )
        own_segments = lax.dynamic_slice_in_dim(segments, row_start, count_rows, axis=1)
        (
            output,
            input_grad,
            grad_w_qkv,
            grad_w_out,
            grad_w_down,
            grad_w_gate,
            grad_w_up,
            sums,
        ) = layer_call(
            heads,
            head_size,
            (
                tokens.reshape(rows, width),
                first_shard,
                output_weight.T,
                spaced(gate_weight),
                spaced(up_weight),
                spaced(down_weight.T),
                grad_out,
                wide(biases).reshape(1, -1),
                cosine[:, 0],
                sine_table[:, 0],
                own_segments[..., None],
                own_places[..., None],
                jnp.stack(key_segments)[:, None],
                jnp.stack(key_positions)[:, None],
            ),
        )
        sums = sums.reshape(-1)
        grad_w_down, grad_w_gate, grad_w_up = map(wide, (grad_w_down, grad_w_gate, grad_w_up))
    else:
        allowed = [
            visible(segments[b], positions[b], row_start, count_rows) for b in range(batches)
        ]
        first_all = gather_rows(first_shard)
        w_qkv = first_all[:, :kv_width]
        first_gain = wide(first_all[:, kv_width])
        second_gain = wide(first_all[:, kv_width + 1])
        w_out = gather_rows(output_weight.T)
        w_gate = quarter_columns(spaced(gate_weight))
        w_up = quarter_columns(spaced(up_weight))
        w_down = quarter_columns(spaced(down_weight.T))
        grad_out_four = four_blocks(grad_out)
        first_unit, first_scale = root_mean_square_parts(inputs)
        first_normed = low(first_unit * first_gain)
        raw = matmul(first_normed, w_qkv) + wide(biases)
        turned = rotate(
            raw[:, : query_width + head_size].reshape(rows, heads + 1, head_size),
            cosine,
            sine_table,
        )
        turned = low(turned)
        query_rows = turned[:, :heads].reshape(batches, count_rows, heads, head_size)
        key_value = jnp.concatenate(
            [turned[:, heads], low(raw[:, query_width + head_size :])], axis=1
        )
        key_value = key_value.reshape(batches, count_rows, 2 * head_size)
        window = jnp.concatenate(
            [shifted(key_value, back) for back in range(BACK, 0, -1)] + [key_value], axis=1
        )
        key_rows, value_rows = window[..., :head_size], window[..., head_size:]
        attended = [
            attend(query_rows[b], key_rows[b], value_rows[b], allowed[b]) for b in range(batches)
        ]
        log_totals = [log_total for _, log_total in attended]
        heads_out = jnp.concatenate([mixed for mixed, _ in attended], axis=0)
        residual = inputs + tensor_total(times_transpose(heads_out, w_out))
        second_unit, second_scale = root_mean_square_parts(residual)
        second_normed = four_blocks(low(second_unit * second_gain))

        second_unit, second_scale = root_mean_square_parts(residual)
        gate_value = matmul(second_normed, w_gate)
        up_part = matmul(second_normed, w_up)
        sigmoid_gate = jax.nn.sigmoid(gate_value)
        silu_gate = gate_value * sigmoid_gate
        hidden = low(silu_gate * up_part)
        grad_hidden = matmul(grad_out_four, w_down)
        grad_gate = low(
            grad_hidden * up_part * sigmoid_gate * (1.0 + gate_value * (1.0 - sigmoid_gate))
        )
        grad_up = low(grad_hidden * silu_gate)
        second_back = four_sums(times_transpose(grad_gate, w_gate) + times_transpose(grad_up, w_up))
        grad_w_down = quarter_to_owner(low(contract_rows(grad_out_four, hidden)))
        grad_w_gate = quarter_to_owner(low(contract_rows(second_normed, grad_gate)))
        grad_w_up = quarter_to_owner(low(contract_rows(second_normed, grad_up)))
        output = low(residual + four_sums(times_transpose(hidden, w_down)))

        second_gain_sum = jnp.sum(second_back * second_unit, axis=0)
        grad_state = wide(grad_out) + norm_back(second_back, second_unit, second_scale, second_gain)
        grad_branch = low(grad_state)
        grad_w_out = scatter_rows(contract_rows(grad_branch, heads_out))
        grad_heads = low(matmul(grad_branch, w_out)).reshape(query_rows.shape)
        backs = [
            attend_back(
                grad_heads[b], query_rows[b], key_rows[b], value_rows[b], allowed[b], log_totals[b]
            )
            for b in range(batches)
        ]
        grad_query = jnp.stack([back[0] for back in backs]).reshape(rows, heads, head_size)
        grad_window = jnp.stack([jnp.concatenate([back[1], back[2]], axis=1) for back in backs])
        own_grad = grad_window[:, BACK * count_rows :]
        for back in range(1, BACK + 1):
            first_row = (BACK - back) * count_rows
            own_grad = own_grad + wide(
                shifted(low(grad_window[:, first_row : first_row + count_rows]), -back)
            )
        own_grad = own_grad.reshape(rows, 2, head_size)
        turned_back = rotate_back(
            jnp.concatenate([grad_query, own_grad[:, :1]], axis=1), cosine, sine_table
        )
        grad_raw = low(jnp.concatenate([turned_back, own_grad[:, 1:]], axis=1).reshape(rows, -1))
        grad_w_qkv = scatter_rows(contract_rows(first_normed, grad_raw))
        bias_sum = jnp.sum(wide(grad_raw), axis=0)
        first_back_part = times_transpose(grad_raw, w_qkv)
        first_back = tensor_total(first_back_part)
        first_gain_sum = jnp.sum(first_back * first_unit, axis=0)
        input_grad = grad_state + norm_back(first_back, first_unit, first_scale, first_gain)
        sums = summed_over_fsdp(jnp.concatenate([bias_sum, second_gain_sum, first_gain_sum]))
    bias_total = sums[:kv_width]
    gain_rows = norm1_gain.shape[0]
    second_total = lax.dynamic_slice_in_dim(sums, kv_width + place * gain_rows, gain_rows)
    first_total = lax.dynamic_slice_in_dim(sums, kv_width + width + place * gain_rows, gain_rows)

    return (
        output.reshape(tokens.shape),
        input_grad.reshape(tokens.shape),
        first_total,
        grad_w_qkv[:, :query_width],
        bias_total[:query_width].reshape(query_bias.shape),
        grad_w_qkv[:, query_width : query_width + head_size],
        bias_total[query_width : query_width + head_size].reshape(key_bias.shape),
        grad_w_qkv[:, query_width + head_size :],
        bias_total[query_width + head_size :].reshape(value_bias.shape),
        grad_w_out.T,
        second_total,
        grad_w_gate[:, :units],
        grad_w_up[:, :units],
        grad_w_down[:, :units].T,
    )


def solution(mesh):
    fsdp, tensor = mesh.shape["fsdp"], mesh.shape["tensor"]
    fine = Mesh(mesh.devices.reshape(fsdp // 4, 2, 2, tensor), (RING, PAIR, CORE, TENSOR))
    by_rows, by_columns, by_tensor = P(FSDP, TENSOR), P(TENSOR, FSDP), P(TENSOR, None)
    by_tokens, by_gain = P(None, FSDP, None), P(FSDP)
    placed = (
        by_tokens,
        by_gain,
        by_rows,
        by_tensor,
        by_rows,
        by_tensor,
        by_rows,
        by_tensor,
        by_columns,
        by_gain,
        by_rows,
        by_rows,
        by_columns,
        by_tokens,
        P(),
        P(),
    )
    return jax.shard_map(
        body,
        mesh=fine,
        in_specs=placed,
        out_specs=(
            by_tokens,
            by_tokens,
            by_gain,
            by_rows,
            by_tensor,
            by_rows,
            by_tensor,
            by_rows,
            by_tensor,
            by_columns,
            by_gain,
            by_rows,
            by_rows,
            by_columns,
        ),
        check_vma=False,
    )
```

```python
import functools
import math

import jax
import jax.numpy as jnp
from jax import lax
from jax.experimental import pallas as pl
from jax.experimental.pallas import tpu as pltpu
from jax.sharding import Mesh
from jax.sharding import PartitionSpec as P

BACK = 5
LINE = 4
LANES = 128
VMEM_BYTES = 65350 * 1024

EPSILON = 1e-06
THETA = 1000000.0
NEGATIVE = -1e30

RING, PAIR, CORE, TENSOR = "ring", "pair", "core", "tensor"
FSDP = (RING, PAIR, CORE)
SWAP = [(0, 1), (1, 0)]


def low(value):
    return value.astype(jnp.bfloat16)


def wide(value):
    return value.astype(jnp.float32)


def matmul(left_side, right_side):
    return jnp.dot(left_side, right_side, preferred_element_type=jnp.float32)


def contract_rows(left_side, right_side):
    return lax.dot_general(
        left_side, right_side, (((0,), (0,)), ((), ())), preferred_element_type=jnp.float32
    )


def times_transpose(left_side, right_side):
    return lax.dot_general(
        left_side, right_side, (((1,), (1,)), ((), ())), preferred_element_type=jnp.float32
    )


def swapped(value, axis):
    return lax.ppermute(value, axis, SWAP)


def in_order(own, other, place, axis):
    first = jnp.where(place == 0, own, other)
    second = jnp.where(place == 0, other, own)
    return jnp.stack([first, second], axis=axis)


def shifted(value, steps):
    count = lax.axis_size(FSDP)
    first, last = (max(0, -steps), min(count, count - steps))
    return lax.ppermute(value, FSDP, [(source, source + steps) for source in range(first, last)])


def summed_over_fsdp(value):
    count = lax.axis_size(FSDP)
    bit = 1
    while bit < count:
        value = value + lax.ppermute(value, FSDP, [(i, i ^ bit) for i in range(count)])
        bit *= 2
    return value


def line_gather(block):
    count, here = lax.axis_size(RING), lax.axis_index(RING)
    if count > LINE:
        return lax.all_gather(block, RING, axis=0)
    right, left = [block], [block]
    for step in range(1, count):
        right.append(
            lax.ppermute(right[-1], RING, [(i, i + 1) for i in range(step - 1, count - 1)])
        )
        left.append(
            lax.ppermute(left[-1], RING, [(i, i - 1) for i in range(1, count - step + 1)])
        )
    result = jnp.zeros((count,) + block.shape, block.dtype)
    for step in range(count):
        piece = block if step == 0 else jnp.where(here >= step, right[step], left[count - step])
        result = lax.dynamic_update_slice_in_dim(
            result, piece[None], (here - step + count) % count, axis=0
        )
    return result


def line_scatter(parts):
    count, here = lax.axis_size(RING), lax.axis_index(RING)
    if count > LINE:
        return wide(lax.psum_scatter(parts, RING, scatter_dimension=0, tiled=False))

    def part(place):
        return lax.dynamic_index_in_dim(parts, place, axis=0, keepdims=False)

    right, left = None, None
    for step in range(1, count):
        to_right, to_left = part(here + count - step), part(here - count + step)
        if step > 1:
            to_right = low(wide(to_right) + wide(right))
            to_left = low(wide(to_left) + wide(left))
        right = lax.ppermute(to_right, RING, [(i, i + 1) for i in range(step)])
        left = lax.ppermute(to_left, RING, [(i, i - 1) for i in range(count - step, count)])
    return wide(part(here)) + wide(right) + wide(left)


def gather_rows(shard):
    rows = line_gather(shard)
    rows = in_order(rows, swapped(rows, PAIR), lax.axis_index(PAIR), 1)
    rows = in_order(rows, swapped(rows, CORE), lax.axis_index(CORE), 2)
    return rows.reshape((-1,) + shard.shape[1:])


def scatter_rows(total):
    pair, core = lax.axis_index(PAIR), lax.axis_index(CORE)
    parts = low(total).reshape((lax.axis_size(RING), 2, 2, -1) + total.shape[1:])

    def halved(value, axis, place, name):
        mine = lax.dynamic_index_in_dim(value, place, axis=axis, keepdims=False)
        sent = lax.dynamic_index_in_dim(value, 1 - place, axis=axis, keepdims=False)
        return low(wide(mine) + wide(swapped(sent, name)))

    parts = halved(parts, 2, core, CORE)
    parts = halved(parts, 1, pair, PAIR)
    return line_scatter(parts)


def quarter_columns(shard):
    pair, core = lax.axis_index(PAIR), lax.axis_index(CORE)
    half = shard.shape[1] // 2

    def halved(value, place, width):
        mine = lax.dynamic_slice_in_dim(value, place * width, width, axis=value.ndim - 1)
        sent = lax.dynamic_slice_in_dim(value, (1 - place) * width, width, axis=value.ndim - 1)
        return mine, sent

    mine, sent = halved(shard, pair, half)
    rows = in_order(mine, swapped(sent, PAIR), pair, 0)
    mine, sent = halved(rows, core, half // 2)
    rows = in_order(mine, swapped(sent, CORE), core, 1)
    rows = line_gather(rows.reshape(-1, half // 2))
    return rows.reshape(-1, half // 2)


def quarter_to_owner(grad):
    pair, core = lax.axis_index(PAIR), lax.axis_index(CORE)
    width = grad.shape[1]
    block = lax.psum_scatter(
        grad.reshape(lax.axis_size(RING), -1, width), RING, scatter_dimension=0, tiled=False
    )
    block = block.reshape(2, 2, -1, width)

    def halved(value, axis, place):
        mine = lax.dynamic_index_in_dim(value, place, axis=axis, keepdims=False)
        sent = lax.dynamic_index_in_dim(value, 1 - place, axis=axis, keepdims=False)
        return mine, sent

    mine, sent = halved(block, 0, pair)
    block = in_order(mine, swapped(sent, PAIR), pair, 0)
    mine, sent = halved(block, 1, core)
    block = in_order(mine, swapped(sent, CORE), core, 1)
    return jnp.concatenate([wide(block[i, j]) for i in range(2) for j in range(2)], axis=1)


def four_blocks(value):
    over = swapped(value, PAIR)
    return jnp.concatenate([value, over, swapped(value, CORE), swapped(over, CORE)], axis=0)


def four_sums(total):
    half = total.shape[0] // 2
    total = total[:half] + wide(swapped(low(total[half:]), CORE))
    total = total[: half // 2] + wide(swapped(low(total[half // 2 :]), PAIR))
    return tensor_total(total)


def tensor_total(partial_sum):
    own = lax.reduce_precision(partial_sum, 8, 7)
    return own + wide(swapped(low(own), TENSOR))


def rotation(places, width):
    half_width = width // 2
    frequency = THETA ** (-(jnp.arange(half_width, dtype=jnp.float32) * 2.0) / width)
    angles = places.astype(jnp.float32)[:, None] * frequency[None, :]
    cosine = jnp.concatenate([jnp.cos(angles), jnp.cos(angles)], axis=-1)[:, None, :]
    sine_table = jnp.concatenate([jnp.sin(angles), jnp.sin(angles)], axis=-1)[:, None, :]
    return (cosine, sine_table)


def rotate(values, cosine, sine_table):
    half_width = values.shape[-1] // 2
    turned = jnp.concatenate([-values[..., half_width:], values[..., :half_width]], axis=-1)
    return values * cosine + turned * sine_table


def rotate_back(gradient, cosine, sine_table):
    half_width = gradient.shape[-1] // 2
    moved_part = gradient * sine_table
    return gradient * cosine + jnp.concatenate(
        [moved_part[..., half_width:], -moved_part[..., :half_width]], axis=-1
    )


def root_mean_square_parts(values):
    scale_row = lax.rsqrt(jnp.mean(values * values, axis=-1, keepdims=True) + EPSILON)
    return (values * scale_row, scale_row)


def norm_back(grad_normed, normalized, scale_row, gain):
    scaled = grad_normed * gain
    return scale_row * (scaled - normalized * jnp.mean(scaled * normalized, axis=-1, keepdims=True))


def visible(seg_row, pos_row, row_start, count_rows):
    pad_rows = BACK * count_rows
    seg_padded = jnp.concatenate([jnp.full((pad_rows,), -1, jnp.int32), seg_row])
    pos_padded = jnp.concatenate([jnp.zeros((pad_rows,), jnp.int32), pos_row])
    key_seg = lax.dynamic_slice_in_dim(seg_padded, row_start, pad_rows + count_rows)
    key_pos = lax.dynamic_slice_in_dim(pos_padded, row_start, pad_rows + count_rows)
    query_seg = lax.dynamic_slice_in_dim(seg_row, row_start, count_rows)
    query_pos = lax.dynamic_slice_in_dim(pos_row, row_start, count_rows)
    return (query_seg[:, None] == key_seg[None, :]) & (key_pos[None, :] <= query_pos[:, None])


def attend(query_rows, key_rows, value_rows, allowed):
    scores = jnp.einsum("thd,sd->hts", query_rows, key_rows, preferred_element_type=jnp.float32)
    scores = scores * (1.0 / math.sqrt(query_rows.shape[-1]))
    scores = jnp.where(allowed, scores, NEGATIVE)
    row_max = jnp.max(scores, axis=-1, keepdims=True)
    log_total = row_max + jnp.log(jnp.sum(jnp.exp(scores - row_max), axis=-1, keepdims=True))
    probs_low = low(jnp.exp(scores - log_total))
    mixed = jnp.einsum("hts,sd->thd", probs_low, value_rows, preferred_element_type=jnp.float32)
    return low(mixed.reshape(query_rows.shape[0], -1)), log_total


def log_total_of(query_rows, key_rows, allowed):
    scores = jnp.einsum("thd,sd->hts", query_rows, key_rows, preferred_element_type=jnp.float32)
    scores = scores * (1.0 / math.sqrt(query_rows.shape[-1]))
    scores = jnp.where(allowed, scores, NEGATIVE)
    row_max = jnp.max(scores, axis=-1, keepdims=True)
    return row_max + jnp.log(jnp.sum(jnp.exp(scores - row_max), axis=-1, keepdims=True))


def attend_back(grad_heads, query_rows, key_rows, value_rows, allowed, log_total):
    scale = 1.0 / math.sqrt(query_rows.shape[-1])
    scores = jnp.einsum("thd,sd->hts", query_rows, key_rows, preferred_element_type=jnp.float32)
    probs = jnp.exp(jnp.where(allowed, scores * scale, NEGATIVE) - log_total)
    grad_probs = jnp.einsum(
        "thd,sd->hts", grad_heads, value_rows, preferred_element_type=jnp.float32
    )
    row_inner = jnp.sum(probs * grad_probs, axis=-1, keepdims=True)
    grad_scores = low(probs * (grad_probs - row_inner))
    grad_query = jnp.einsum(
        "hts,sd->thd", grad_scores, key_rows, preferred_element_type=jnp.float32
    )
    grad_keys = jnp.einsum(
        "hts,thd->sd", grad_scores, query_rows, preferred_element_type=jnp.float32
    )
    grad_values = jnp.einsum(
        "hts,thd->sd", low(probs), grad_heads, preferred_element_type=jnp.float32
    )
    return grad_query * scale, grad_keys * scale, grad_values


def device(**coordinates):
    return {name: place for name, place in coordinates.items()}


class Copies:
    def __init__(self, send_sems, recv_sems):
        self.send_sems, self.recv_sems = send_sems, recv_sems
        self.used = 0
        self.sent = []

    def new(self):
        self.used += 1
        return self.used - 1

    def _make(self, which, source, target, to):
        return pltpu.make_async_remote_copy(
            src_ref=source,
            dst_ref=target,
            send_sem=self.send_sems.at[which],
            recv_sem=self.recv_sems.at[which],
            device_id=to,
            device_id_type=pl.DeviceIdType.MESH,
        )

    def send(self, which, source, target, to, cond=None):
        only(cond, lambda: self._make(which, source, target, to).start())
        self.sent.append((which, source, target, to, cond))

    def receive(self, which, target, via):
        self._make(which, target, target, via).wait_recv()

    def settle(self, until=None):
        until = len(self.sent) if until is None else until
        for i in range(until):
            if self.sent[i] is not None:
                which, source, target, to, cond = self.sent[i]
                only(cond, lambda: self._make(which, source, target, to).wait_send())
                self.sent[i] = None

    def left(self, which):
        for i, entry in enumerate(self.sent):
            if entry is not None and entry[0] == which:
                _, source, target, to, cond = entry
                only(cond, lambda: self._make(which, source, target, to).wait_send())
                self.sent[i] = None

    def settle_of(self, ids):
        for which in ids:
            self.left(which)

    def mark(self):
        return len(self.sent)


def only(cond, action):
    if cond is None:
        action()
    else:
        pl.when(cond)(action)


class Place:
    def __init__(self):
        self.z, self.p = lax.axis_index(RING), lax.axis_index(PAIR)
        self.c, self.y = lax.axis_index(CORE), lax.axis_index(TENSOR)
        self.q = self.p * 2 + self.c
        self.q_pair, self.q_core = (1 - self.p) * 2 + self.c, self.p * 2 + 1 - self.c
        self.q_cross = (1 - self.p) * 2 + 1 - self.c
        self.pair, self.core = {PAIR: 1 - self.p}, {CORE: 1 - self.c}
        self.cross = {PAIR: 1 - self.p, CORE: 1 - self.c}
        self.other = {TENSOR: 1 - self.y}
        self.near = {RING: self.z + 1 - 2 * (self.z % 2)}
        self.far = {RING: self.z + 2 - 4 * (self.z // 2)}
        self.right, self.left = {RING: self.z + 1}, {RING: self.z - 1}
        self.right_cross = {RING: self.z + 1, PAIR: 1 - self.p}
        self.left_cross = {RING: self.z - 1, PAIR: 1 - self.p}
        self.far_right = {RING: self.z + 2, PAIR: 0, CORE: 0}
        self.far_left = {RING: self.z - 2, PAIR: 1, CORE: 1}
        self.has_right, self.has_left = self.z < LINE - 1, self.z > 0
        self.has_far_right = (self.q == 3) & (self.z < LINE - 2)
        self.has_far_left = (self.q == 0) & (self.z > 1)

    def meet(self):
        barrier = pltpu.get_barrier_semaphore()

        def greet(to, cond=None):
            only(
                cond,
                lambda: pl.semaphore_signal(
                    barrier, inc=1, device_id=to, device_id_type=pl.DeviceIdType.MESH
                ),
            )

        for to in (self.pair, self.core, self.cross, self.other):
            greet(to)
        for far in (2, 3):
            greet({RING: self.z + far}, self.z + far < LINE)
            greet({RING: self.z - far}, self.z >= far)
        for there, to, cross in (
            (self.has_right, self.right, self.right_cross),
            (self.has_left, self.left, self.left_cross),
        ):
            greet(to, there)
            greet(cross, there)
        greet(self.far_right, self.has_far_right)
        greet(self.far_left, self.has_far_left)
        line = jnp.minimum(self.z, 1) + jnp.minimum(LINE - 1 - self.z, 1)
        upper = self.z // 2
        reach = self.p * self.c * (1 - upper) + (1 - self.p) * (1 - self.c) * upper
        pl.semaphore_wait(barrier, 4 + LINE - 1 + line + reach)


class LineFlow:
    def __init__(self, copies, place, block):
        self.copies, self.place, self.block = copies, place, block
        self.ids = {(way, step): copies.new() for way in (1, -1) for step in range(1, LINE)}

    def valid(self, way, step):
        z = self.place.z
        return z >= step if way == 1 else z + step <= LINE - 1

    def origin(self, way, step):
        return self.place.z - way * step

    def onward(self, way, step, source):
        if step == LINE - 1:
            return
        to = self.place.right if way == 1 else self.place.left
        there = self.place.has_right if way == 1 else self.place.has_left
        if step:
            there = there & self.valid(way, step)
        target = self.block(self.origin(way, step))
        self.copies.send(self.ids[way, step + 1], source, target, to, there)

    def start(self, source):
        self.onward(1, 0, source)
        self.onward(-1, 0, source)

    def arrive(self, step, then=None):
        for way in (1, -1):

            def take(way=way):
                target = self.block(self.origin(way, step))
                via = self.place.left if way == 1 else self.place.right
                self.copies.receive(self.ids[way, step], target, via)

            pl.when(self.valid(way, step))(take)
            if step < LINE - 1:
                self.onward(way, step, self.block(self.origin(way, step)))
            if then is not None:
                then(way, step)


class RowsFlow:
    def __init__(self, copies, place, shard, whole):
        self.copies, self.place, self.shard, self.whole = copies, place, shard, whole
        self.line = LineFlow(copies, place, lambda origin: self.rows(origin, place.p, place.c))
        items = [(0, 0)] + [(way, step) for step in range(1, LINE) for way in (1, -1)]
        self.items = items
        self.pair_ids = {item: copies.new() for item in items}
        self.core_ids = {item: copies.new() for item in items}
        self.cross_ids = {item: copies.new() for item in items}

    def rows(self, origin, p, c):
        count = self.shard.shape[0]
        return self.whole.at[pl.ds(pl.multiple_of((origin * 4 + p * 2 + c) * count, count), count)]

    def valid(self, item):
        return None if item == (0, 0) else self.line.valid(*item)

    def spread(self, way, step):
        item, place = (way, step), self.place
        here = self.rows(self.line.origin(way, step), place.p, place.c)
        self.copies.send(self.pair_ids[item], here, here, place.pair, self.valid(item))
        self.copies.send(self.core_ids[item], here, here, place.core, self.valid(item))

    def start(self, own_copy):
        self.line.start(self.shard)
        own_copy()
        self.spread(0, 0)

    def arrive(self, step):
        self.line.arrive(step, self.spread)

    def crossing(self, step):
        place = self.place
        for item in self.items:
            if item[1] != step:
                continue
            there = self.rows(self.line.origin(*item), 1 - place.p, place.c)
            only(
                self.valid(item),
                lambda: self.copies.receive(self.pair_ids[item], there, place.pair),
            )
            self.copies.send(self.cross_ids[item], there, there, place.core, self.valid(item))

    def end(self):
        place = self.place
        for item in self.items:
            origin = self.line.origin(*item)

            def take(item=item, origin=origin):
                mine = self.rows(origin, place.p, 1 - place.c)
                cross = self.rows(origin, 1 - place.p, 1 - place.c)
                self.copies.receive(self.core_ids[item], mine, place.core)
                self.copies.receive(self.cross_ids[item], cross, place.core)

            only(self.valid(item), take)


class QuarterFlow:
    def __init__(self, copies, place, shard, whole, columns, own_sem):
        self.copies, self.place, self.shard, self.whole = copies, place, shard, whole
        self.count, self.quarter = shard.shape[0], -(-shard.shape[1] // (4 * LANES)) * LANES
        self.start_column, self.width = columns
        self.last = min(self.width, shard.shape[1] - 3 * self.quarter - self.start_column)
        self.own_sem = own_sem
        self.near = (
            (copies.new(), 1 - place.p, place.c, place.pair),
            (copies.new(), place.p, 1 - place.c, place.core),
            (copies.new(), 1 - place.p, 1 - place.c, place.cross),
        )
        self.line = LineFlow(copies, place, self.block)

    def columns(self, q, width):
        start = q * self.quarter + self.start_column
        return self.shard.at[:, pl.ds(pl.multiple_of(start, LANES), width)]

    def rows(self, p, c, width):
        start = (self.place.z * 4 + p * 2 + c) * self.count
        rows = pl.ds(pl.multiple_of(start, self.count), self.count)
        return self.whole.at[rows, pl.ds(0, width)]

    def block(self, origin):
        count = 4 * self.count
        return self.whole.at[pl.ds(pl.multiple_of(origin * count, count), count)]

    def widths(self, q):
        if self.last == self.width:
            return ((None, self.width),)
        return ((q == 3, self.last), (q != 3, self.width))

    def own(self, width):
        place = self.place
        return pltpu.make_async_copy(
            self.columns(place.q, width), self.rows(place.p, place.c, width), self.own_sem
        )

    def start(self):
        place = self.place
        for cond, width in self.widths(place.q):
            only(cond, lambda: self.own(width).start())
        for which, p, c, to in self.near:
            for cond, width in self.widths(p * 2 + c):
                target = self.rows(place.p, place.c, width)
                self.copies.send(which, self.columns(p * 2 + c, width), target, to, cond)

    def join(self):
        def take(width):
            self.own(width).wait()
            for which, p, c, to in self.near:
                self.copies.receive(which, self.rows(p, c, width), to)

        for cond, width in self.widths(self.place.q):
            only(cond, lambda: take(width))
        self.line.start(self.block(self.place.z))

    def arrive(self, step):
        self.line.arrive(step)


class FourFlow:
    def __init__(self, copies, place, slots, parts):
        self.copies, self.place, self.slots = copies, place, slots
        self.rows = slots.shape[0] // 4
        self.size = self.rows // parts
        self.ids = [[copies.new() for _ in range(3)] for _ in range(parts)]

    def slot(self, which, part):
        return self.slots.at[pl.ds(which * self.rows + part * self.size, self.size)]

    def send(self, part, source):
        self.copies.send(self.ids[part][0], source, self.slot(1, part), self.place.pair)
        self.copies.send(self.ids[part][1], source, self.slot(2, part), self.place.core)

    def cross(self, part):
        got = self.slot(1, part)
        self.copies.receive(self.ids[part][0], got, self.place.pair)
        self.copies.send(self.ids[part][2], got, self.slot(3, part), self.place.core)

    def end(self, part):
        self.copies.receive(self.ids[part][1], self.slot(2, part), self.place.core)
        self.copies.receive(self.ids[part][2], self.slot(3, part), self.place.core)


def fetch(source, target, sem):
    copy = pltpu.make_async_copy(source, target, sem)
    copy.start()
    copy.wait()


def add_to(target, source):
    target[...] = low(wide(target[...]) + wide(source[...]))


class LineScatter:
    def __init__(self, copies, place, block, arrived, stage, sem):
        self.copies, self.place, self.block = copies, place, block
        self.arrived, self.stage, self.sem = arrived, stage, sem
        self.ids = {(way, step): copies.new() for way in (1, -1) for step in range(1, LINE)}

    def landing(self, way, step):
        return self.arrived.at[(1 - way) // 2, step - 1]

    def target(self, way, step):
        return self.block(self.place.z + way * (LINE - step))

    def takes(self, way, step):
        z = self.place.z
        if way == 1:
            return (z >= 1) & (z <= step)
        return (z <= LINE - 2) & (z >= LINE - 1 - step)

    def send(self, way, step, cond):
        to = self.place.right if way == 1 else self.place.left
        self.copies.send(
            self.ids[way, step], self.target(way, step), self.landing(way, step), to, cond
        )

    def start(self, ways=(1, -1)):
        for way in ways:
            for step in range(1, LINE):
                self.send(way, step, self.place.z == (0 if way == 1 else LINE - 1))

    def take(self, way, step):
        via = self.place.left if way == 1 else self.place.right
        self.copies.receive(self.ids[way, step], self.landing(way, step), via)
        fetch(self.landing(way, step), self.stage, self.sem)

    def step(self, step, ways=(1, -1)):
        for way in ways:
            there = self.takes(way, step - 1)

            def add(way=way):
                self.take(way, step - 1)
                add_to(self.target(way, step), self.stage)

            pl.when(there)(add)
            self.send(way, step, there)

    def finish(self, add):
        for way in (1, -1):

            def last(way=way):
                self.take(way, LINE - 1)
                add()

            pl.when(self.takes(way, LINE - 1))(last)


class QuarterScatter:
    def __init__(self, copies, place, grad, owner, columns, arrived, stage, sem, line=LineScatter):
        self.copies, self.place, self.grad, self.owner, self.sem = copies, place, grad, owner, sem
        self.stage = stage
        self.count, self.whole_width = owner.shape[0], owner.shape[1] // 4
        self.start_column, self.width = columns
        self.line = line(copies, place, self.block, arrived, stage, sem)
        self.near = (
            (copies.new(), 1 - place.p, place.c, place.pair),
            (copies.new(), place.p, 1 - place.c, place.core),
            (copies.new(), 1 - place.p, 1 - place.c, place.cross),
        )

    def block(self, origin):
        count = 4 * self.count
        return self.grad.at[pl.ds(pl.multiple_of(origin * count, count), count)]

    def rows(self, p, c):
        count = self.count
        start = (self.place.z * 4 + p * 2 + c) * count
        return self.grad.at[pl.ds(pl.multiple_of(start, count), count)]

    def columns(self, p, c):
        start = (p * 2 + c) * self.whole_width + self.start_column
        return self.owner.at[:, pl.ds(pl.multiple_of(start, LANES), self.width)]

    def finish(self):
        place = self.place
        self.line.finish(lambda: add_to(self.block(place.z), self.stage))
        for which, p, c, to in self.near:
            self.copies.send(which, self.rows(p, c), self.columns(place.p, place.c), to)
        fetch(self.rows(place.p, place.c), self.columns(place.p, place.c), self.sem)

    def end(self):
        for which, p, c, to in self.near:
            self.copies.receive(which, self.columns(p, c), to)


class ShortScatter:
    def __init__(self, copies, place, block, arrived, stage, sem):
        self.copies, self.place, self.block = copies, place, block
        self.arrived, self.stage, self.sem = arrived, stage, sem
        self.ids = {way: {name: copies.new() for name in "abcdef"} for way in (1, -1)}

    def at(self, way, k):
        return self.place.z == (k if way == 1 else LINE - 1 - k)

    def there(self, way, k):
        return k if way == 1 else LINE - 1 - k

    def landing(self, way, name):
        return self.arrived.at[(1 - way) // 2, 0 if name in "abc" else 1]

    def send(self, way, name, head, k, to):
        self.copies.send(
            self.ids[way][name],
            self.block(self.there(way, k)),
            self.landing(way, name),
            {RING: self.there(way, to)},
            self.at(way, head),
        )

    def take(self, way, name, source):
        landing = self.landing(way, name)
        self.copies.receive(self.ids[way][name], landing, {RING: self.there(way, source)})
        fetch(landing, self.stage, self.sem)

    def start(self, ways=(1, -1), names="abcd"):
        for name, head, k, to in (("a", 0, 2, 1), ("b", 1, 3, 2), ("c", 0, 3, 3), ("d", 0, 1, 1)):
            for way in ways:
                if name in names:
                    self.send(way, name, head, k, to)

    def step(self, ways=(1, -1)):
        for way in ways:
            for k, name, onward in ((1, "a", "e"), (2, "b", "f")):

                def add(way=way, k=k, name=name):
                    self.take(way, name, k - 1)
                    add_to(self.block(self.there(way, k + 1)), self.stage)

                pl.when(self.at(way, k))(add)
                self.send(way, onward, k, k + 1, k + 1)

    def finish(self, add):
        for way in (1, -1):
            for k, name, source in ((1, "d", 0), (2, "e", 1), (3, "c", 0), (3, "f", 2)):

                def last(way=way, name=name, source=source):
                    self.take(way, name, source)
                    add()

                pl.when(self.at(way, k))(last)


class DirectScatter:
    def __init__(self, copies, place, block, arrived, stage, sem):
        self.copies, self.place, self.block = copies, place, block
        self.arrived, self.stage, self.sem = arrived, stage, sem
        self.ids = {(way, far): copies.new() for way in (1, -1) for far in range(1, LINE)}

    def landing(self, way, far):
        return self.arrived.at[(1 - way) // 2, far - 1]

    def reaches(self, way, far):
        return self.place.z + far < LINE if way == 1 else self.place.z >= far

    def start(self):
        for far in range(LINE - 1, 0, -1):
            for way in (1, -1):
                there = self.place.z + way * far
                self.copies.send(
                    self.ids[way, far],
                    self.block(there),
                    self.landing(way, far),
                    {RING: there},
                    self.reaches(way, far),
                )

    def finish(self, add):
        for way in (1, -1):
            for far in range(1, LINE):

                def take(way=way, far=far):
                    via = {RING: self.place.z - way * far}
                    self.copies.receive(self.ids[way, far], self.landing(way, far), via)
                    fetch(self.landing(way, far), self.stage, self.sem)
                    add()

                pl.when(self.reaches(-way, far))(take)


class RowsScatter:
    def __init__(self, copies, place, whole, from_core, from_pair, arrived, stage, sem):
        self.copies, self.place, self.whole, self.sem = copies, place, whole, sem
        self.from_core, self.from_pair = from_core, from_pair
        self.count, self.columns = from_pair.shape[1], from_pair.shape[2]
        self.stage = stage
        self.core_id = copies.new()
        self.pair_ids = [copies.new() for _ in range(LINE)]
        self.line = DirectScatter(
            copies, place, lambda d: self.part(place.c, place.p, d), arrived, self.small(1), sem
        )

    def small(self, blocks):
        return self.stage.at[pl.ds(0, blocks * self.count), pl.ds(0, self.columns)]

    def part(self, c, p, origin, blocks=1):
        start = ((c * 2 + p) * LINE + origin) * self.count
        return self.whole.at[
            pl.ds(pl.multiple_of(start, self.count), blocks * self.count), pl.ds(0, self.columns)
        ]

    def fill(self, origin, value):
        for p in range(2):
            for c in range(2):
                start = (p * 2 + c) * self.count
                self.part(c, p, origin)[...] = value[start : start + self.count]

    def start(self):
        place = self.place
        self.copies.send(
            self.core_id, self.part(1 - place.c, 0, 0, 2 * LINE), self.from_core, place.core
        )

    def halve(self):
        place = self.place
        self.copies.receive(self.core_id, self.from_core, place.core)
        size = LINE * self.count
        for p in (1 - place.p, place.p):
            start = pl.multiple_of(p * size, size)
            fetch(self.from_core.at[pl.ds(start, size)], self.small(LINE), self.sem)
            add_to(self.part(place.c, p, 0, LINE), self.small(LINE))
            if p is place.p:
                continue
            for origin in (3, 0, 2, 1):
                self.copies.send(
                    self.pair_ids[origin],
                    self.part(place.c, p, origin),
                    self.from_pair.at[origin],
                    place.pair,
                )

    def quarter(self):
        place = self.place
        for origin in (3, 0, 2, 1):
            self.copies.receive(self.pair_ids[origin], self.from_pair.at[origin], place.pair)
            fetch(self.from_pair.at[origin], self.small(1), self.sem)
            add_to(self.part(place.c, place.p, origin), self.small(1))

    def finish(self, *outs):
        start = 0
        columns = []
        for out in outs:
            columns.append((out, slice(start, start + out.shape[1])))
            start += out.shape[1]
        for out, at in columns:
            out[...] = wide(self.part(self.place.c, self.place.p, self.place.z)[:, at])

        def add():
            for out, at in columns:
                out[...] += wide(self.small(1)[:, at])

        self.line.finish(add)


PARTS = 4
NORMED_TILE = 768
BEFORE, NOW = 1, 5
N_REMOTE = 300
SUM_ROWS = 32


def clear_last(*wholes_and_shard):
    *wholes, shard = wholes_and_shard
    quarter = wholes[0].shape[1]
    last = shard.shape[1] - 3 * quarter
    if last < quarter:
        for whole in wholes:
            whole[:, last:] = jnp.zeros((whole.shape[0], quarter - last), whole.dtype)


def eight_rows(value):
    return jnp.sum(value.reshape(-1, 8, value.shape[-1]), axis=0)


def layer_kernel(
    heads,
    head_size,
    tokens,
    first_shard,
    out_shard,
    gate_shard,
    up_shard,
    down_shard,
    grad_out,
    query_bias,
    key_bias,
    value_bias,
    cosine,
    sine,
    marks,
    output,
    input_grad,
    grad_query_weight,
    grad_key_weight,
    grad_value_weight,
    grad_w_out,
    grad_w_down,
    grad_w_gate,
    grad_w_up,
    query_bias_sum,
    key_bias_sum,
    value_bias_sum,
    first_gain_out,
    second_gain_out,
    first_kept,
    normed_kept,
    line_landing,
    out_core_landing,
    out_pair_landing,
    out_other_landing,
    first_core_landing,
    first_pair_landing,
    first_line_landing,
    wo_core_landing,
    wo_pair_landing,
    wo_line_landing,
    first_all,
    w_out_all,
    state,
    window,
    keys,
    values,
    mail,
    query,
    heads_out,
    gate_all,
    up_all,
    down_all,
    normed_four,
    grad_four,
    hidden,
    grad_gate,
    grad_up,
    early_up,
    early_gate,
    pair_landing,
    other_landing,
    stage,
    grad_keys,
    grad_values,
    own_grad,
    window_landing,
    core_window,
    own_marks,
    scales,
    totals,
    sums,
    sums_landing,
    line_sums,
    send_sems,
    recv_sems,
    local_sems,
):
    place = Place()
    copies = Copies(send_sems, recv_sems)
    rows, width = tokens.shape
    batches = marks.shape[0] // 4
    per_batch = rows // batches
    query_width = heads * head_size
    kv_width = query_width + 2 * head_size
    size = rows // PARTS
    root = 1.0 / math.sqrt(head_size)
    sem = local_sems.at[0]

    window[...] = jnp.zeros_like(window)
    clear_last(gate_all, up_all, down_all, gate_shard)
    place.meet()

    first = RowsFlow(copies, place, first_shard, first_all)
    outs = RowsFlow(copies, place, out_shard, w_out_all)
    quarter = gate_all.shape[1]
    first_half = -(-quarter // (2 * LANES)) * LANES
    halves = ((0, first_half), (first_half, quarter - first_half))

    def part_of(whole, half):
        return whole.at[:, pl.ds(*halves[half])]

    gates, ups, downs = [
        [
            QuarterFlow(
                copies, place, shard, part_of(whole, half), halves[half], local_sems.at[2 + i * 2 + half]
            )
            for half in range(2)
        ]
        for i, (shard, whole) in enumerate(
            ((gate_shard, gate_all), (up_shard, up_all), (down_shard, down_all))
        )
    ]
    cot = FourFlow(copies, place, grad_four, PARTS)
    second = FourFlow(copies, place, normed_four, PARTS)
    part_ids = [copies.new() for _ in range(PARTS)]
    window_ids = [copies.new() for _ in range(4)]
    window_core_ids = [copies.new() for _ in range(4)]

    def put(flow, sem):
        return lambda: fetch(flow.shard, flow.rows(place.z, place.p, place.c), sem)

    first.start(put(first, sem))
    gates[0].start()
    x = wide(tokens[...])
    scales[:, 0:1] = lax.rsqrt(jnp.mean(x * x, axis=-1, keepdims=True) + EPSILON)
    state[...] = x * scales[:, 0:1]
    outs.line.start(out_shard)
    first.crossing(0)
    first.arrive(1)
    outs.line.arrive(1)
    first.arrive(2)
    outs.line.arrive(2)
    first.arrive(3)
    ups[0].start()
    outs.line.arrive(3)
    gates[0].join()
    put(outs, sem)()
    for step in range(1, LINE):
        first.crossing(step)
    first.end()

    gains = wide(first_all[:, kv_width:]).T
    first_gain, second_gain = gains[0:1], gains[1:2]
    first_normed = mail.at[pl.ds(0, rows)]
    first_normed[...] = low(state[...] * first_gain)
    sign = jnp.where(
        lax.broadcasted_iota(jnp.int32, (1, head_size), 1) < head_size // 2, -1.0, 1.0
    )

    def project(start, size):
        return matmul(first_normed[...], first_all[:, start : start + size])

    def turned(raw):
        half_turn = pltpu.roll(raw, head_size // 2, 1)
        return low(raw * cosine[...] + half_turn * (sine[...] * sign))

    def turned_back(gradient, mine):
        half_turn = pltpu.roll(gradient * sine[mine], head_size // 2, 1)
        return low(gradient * cosine[mine] - half_turn * sign)

    kv = project(query_width, 2 * head_size)
    key_now = turned(kv[:, :head_size] + wide(key_bias[...]))
    value_now = low(kv[:, head_size:] + wide(value_bias[...]))
    for b in range(batches):
        mine = slice(b * per_batch, (b + 1) * per_batch)
        window[NOW + place.q, b, :, :head_size] = key_now[mine]
        window[NOW + place.q, b, :, head_size:] = value_now[mine]
    mine_now = window.at[NOW + place.q]
    copies.send(window_ids[0], mine_now, mine_now, place.pair)
    copies.send(window_core_ids[0], mine_now, mine_now, place.core)
    before = window.at[BEFORE + place.q]
    copies.send(window_ids[1], mine_now, before, place.right, place.has_right)
    copies.send(window_ids[2], mine_now, before, place.right_cross, place.has_right)
    copies.send(window_ids[3], mine_now, window.at[0], place.far_right, place.has_far_right)
    for h in range(0, heads, 2):
        raw = project(h * head_size, 2 * head_size)
        for i in range(2):
            part = raw[:, i * head_size : (i + 1) * head_size] + wide(query_bias[h + i : h + i + 1])
            query[:, (h + i) * head_size : (h + i + 1) * head_size] = turned(part)
    keep_first = pltpu.make_async_copy(first_all, first_kept, local_sems.at[1])
    keep_first.start()
    for item in outs.items:
        outs.spread(*item)
    downs[0].start()
    ups[0].join()
    gates[0].arrive(1)
    copies.receive(window_ids[0], window.at[NOW + place.q_pair], place.pair)
    copies.send(
        window_core_ids[1],
        window.at[NOW + place.q_pair],
        window.at[NOW + place.q_pair],
        place.core,
    )

    def take_before():
        copies.receive(window_ids[1], window.at[BEFORE + place.q], place.left)
        copies.receive(window_ids[2], window.at[BEFORE + place.q_pair], place.left_cross)

    pl.when(place.has_left)(take_before)
    for i, at in ((2, BEFORE + place.q), (3, BEFORE + place.q_pair)):
        copies.send(window_core_ids[i], window.at[at], window.at[at], place.core, place.has_left)
    only(
        place.has_far_left,
        lambda: copies.receive(window_ids[3], window.at[0], place.far_left),
    )
    copies.receive(window_core_ids[0], window.at[NOW + place.q_core], place.core)
    copies.receive(window_core_ids[1], window.at[NOW + place.q_cross], place.core)

    def take_before_core():
        copies.receive(window_core_ids[2], window.at[BEFORE + place.q_core], place.core)
        copies.receive(window_core_ids[3], window.at[BEFORE + place.q_cross], place.core)

    pl.when(place.has_left)(take_before_core)
    cot_own = pltpu.make_async_copy(grad_out, grad_four.at[pl.ds(0, rows)], local_sems.at[8])
    cot_own.start()
    for i in range(PARTS):
        cot.send(i, grad_out.at[pl.ds(i * size, size)])

    own_marks[...] = marks[:, marks.shape[1] - own_marks.shape[0] :].T
    own_start = BACK * per_batch - (marks.shape[1] - own_marks.shape[0])
    every_key = (BACK + 1) * per_batch

    def take_window(b):
        for slot in range(BACK + 1):
            at, there = place.q + slot, slice(slot * per_batch, (slot + 1) * per_batch)
            keys[there] = window[at, b, :, :head_size]
            values[there] = window[at, b, :, head_size:]

    def probabilities(b, mine, columns):
        scores = times_transpose(query[mine, columns], keys[...]) * root
        at = batches + b
        own = own_marks[own_start : own_start + per_batch]
        same = own[:, b : b + 1] == marks[b : b + 1, :every_key]
        allowed = same & (marks[at : at + 1, :every_key] <= own[:, at : at + 1])
        scores = jnp.where(allowed, scores, NEGATIVE)
        weights = jnp.exp(scores - jnp.max(scores, axis=-1, keepdims=True))
        return weights * (1.0 / jnp.sum(weights, axis=-1, keepdims=True))

    part_own, part_other = mail.at[pl.ds(0, rows)], mail.at[pl.ds(rows, rows)]
    for b in range(batches):
        take_window(b)
        mine = slice(b * per_batch, (b + 1) * per_batch)

        def attend_head(h, carry, b=b, mine=mine):
            columns = pl.ds(pl.multiple_of(h * head_size, head_size), head_size)
            probs = low(probabilities(b, mine, columns))
            heads_out[mine, columns] = low(matmul(probs, values[...]))
            return carry

        lax.fori_loop(0, heads, attend_head, 0)
        if b == 0:
            for step in range(LINE):
                outs.crossing(step)
            outs.end()
            ups[0].arrive(1)
        part = low(times_transpose(heads_out[mine], w_out_all[...]))
        part_own[mine] = part
        for i in range(b * per_batch // size, (b + 1) * per_batch // size):
            block = pl.ds(i * size, size)
            copies.send(part_ids[i], part_own.at[block], part_other.at[block], place.other)
    early = copies.mark()

    for i in range(PARTS):
        block = pl.ds(i * size, size)
        copies.receive(part_ids[i], part_other.at[block], place.other)
        copies.left(part_ids[i])
        row_sum = wide(tokens[block]) + (wide(part_own[block]) + wide(part_other[block]))
        state[block] = row_sum
        scale_row = lax.rsqrt(jnp.mean(row_sum * row_sum, axis=-1, keepdims=True) + EPSILON)
        scales[block, 1:2] = scale_row
        second.slot(0, i)[...] = low(row_sum * scale_row * second_gain)
        second.send(i, second.slot(0, i))
        if i == 0:
            gates[0].arrive(2)
            downs[0].join()
        if i == PARTS // 2:
            ups[0].arrive(2)
    downs[0].arrive(1)
    for flow in (gates[1], ups[1], downs[1]):
        flow.start()
    for part in range(PARTS):
        cot.cross(part)
        cot.end(part)
    for part in range(PARTS):
        second.cross(part)
    downs[0].arrive(2)
    keep_first.wait()
    for i in range(PARTS):
        second.end(i)
    gates[0].arrive(3)
    ups[0].arrive(3)

    tile = 256

    def forward_half(half):
        columns = pl.ds(*halves[half])

        def forward_tile(t, carry):
            block = pl.ds(pl.multiple_of(t * tile, tile), tile)
            gate = matmul(normed_four[block], gate_all[:, columns])
            up = matmul(normed_four[block], up_all[:, columns])
            sigmoid = 1.0 / (1.0 + jnp.exp(-gate))
            silu = gate * sigmoid
            hidden[block, columns] = low(silu * up)
            grad_up[block, columns] = low(silu)
            grad_gate[block, columns] = low(up * sigmoid * (1.0 + gate * (1.0 - sigmoid)))
            return carry

        lax.fori_loop(0, 4 * rows // tile, forward_tile, 0)

    def backward_half(half):
        columns = pl.ds(*halves[half])

        def backward_tile(t, carry):
            block = pl.ds(pl.multiple_of(t * tile, tile), tile)
            back = matmul(grad_four[block], down_all[:, columns])
            grad_gate[block, columns] = low(back * wide(grad_gate[block, columns]))
            grad_up[block, columns] = low(back * wide(grad_up[block, columns]))
            return carry

        lax.fori_loop(0, 4 * rows // tile, backward_tile, 0)

    def columns_of(d):
        return pl.ds(pl.multiple_of(d * rows, rows), rows)

    def weight_grad(target, left_side, right_side, half):
        columns = pl.ds(*halves[half])

        def block(d, carry):
            part = contract_rows(left_side[:, columns_of(d)], right_side[:, columns])
            target[columns_of(d)] = low(part)
            return carry

        lax.fori_loop(0, LINE, block, 0)

    grad_down = first_all
    down_backs, up_backs, gate_backs = [
        [
            QuarterScatter(
                copies,
                place,
                grads[half],
                owner,
                halves[half],
                line_landing.at[i * 2 + half, :, :, :, pl.ds(0, halves[half][1])],
                stage.at[:, pl.ds(0, halves[half][1])],
                sem,
                (LineScatter, ShortScatter)[half],
            )
            for half in range(2)
        ]
        for i, (grads, owner) in enumerate(
            (
                ([part_of(grad_down, 0), part_of(grad_down, 1)], grad_w_down),
                ([early_up, part_of(up_all, 1)], grad_w_up),
                ([early_gate, part_of(gate_all, 1)], grad_w_gate),
            )
        )
    ]

    forward_half(0)
    copies.settle(early)
    cot_own.wait()
    for flow in (gates[1], ups[1], downs[1]):
        flow.join()
    weight_grad(down_backs[0].grad, grad_four, hidden, 0)
    down_backs[0].line.start()
    downs[0].arrive(3)
    backward_half(0)
    weight_grad(up_backs[0].grad, normed_four, grad_up, 0)
    up_backs[0].line.start()
    weight_grad(gate_backs[0].grad, normed_four, grad_gate, 0)
    gate_backs[0].line.start()
    for flow in (gates[1], ups[1], downs[1]):
        flow.arrive(1)

    first_columns, later_columns = pl.ds(*halves[0]), pl.ds(*halves[1])
    step = halves[1][1]
    spares = (hidden, grad_gate, grad_up)[: width // step]
    for i, spare in enumerate(spares):

        def first_normed_tile(t, carry, i=i, spare=spare):
            block = columns_of(t)
            spare[block, later_columns] = low(
                times_transpose(grad_gate[block, first_columns], gate_all[i * step : (i + 1) * step, first_columns])
                + times_transpose(grad_up[block, first_columns], up_all[i * step : (i + 1) * step, first_columns])
            )
            return carry

        lax.fori_loop(0, 4, first_normed_tile, 0)
    keeps = [
        pltpu.make_async_copy(
            spare.at[:, later_columns],
            normed_kept.at[:, pl.ds(i * step, step)],
            local_sems.at[10 + i],
        )
        for i, spare in enumerate(spares)
    ]
    for keep in keeps:
        keep.start()
    down_backs[0].line.step(2)
    for flow in (gates[1], ups[1], downs[1]):
        flow.arrive(2)
    down_backs[0].line.step(3)
    for keep in keeps:
        keep.wait()
    gates[1].arrive(3)
    ups[1].arrive(3)

    forward_half(1)
    weight_grad(down_backs[1].grad, grad_four, hidden, 1)
    down_backs[1].line.start()
    up_backs[0].line.step(2)
    downs[1].arrive(3)
    backward_half(1)
    for flow in (cot, second):
        for ids in flow.ids:
            copies.settle_of(ids)
    for flow in (gates[1], ups[1]):
        copies.settle_of(flow.line.ids.values())

    normed_grad = grad_four
    core_ids = [copies.new() for _ in range(2)]
    pair_ids = [copies.new() for _ in range(PARTS)]
    other_ids = [copies.new() for _ in range(PARTS)]

    def slot(which, part=0, parts=1):
        return pl.ds(which * rows + part * (rows // parts), rows // parts)

    order = (3, 1, 2, 0)
    backs = [
        pltpu.make_async_copy(
            normed_kept.at[slot(which)], normed_grad.at[slot(which)], local_sems.at[10 + which]
        )
        for which in range(4)
    ]
    for which in order:
        backs[which].start()

    def normed_slot(which):
        backs[which].wait()

        def column_tile(t, carry):
            columns = pl.ds(pl.multiple_of(t * NORMED_TILE, NORMED_TILE), NORMED_TILE)
            normed_grad[slot(which), columns] = low(
                wide(normed_grad[slot(which), columns])
                + times_transpose(grad_gate[slot(which), later_columns], gate_all[columns, later_columns])
                + times_transpose(grad_up[slot(which), later_columns], up_all[columns, later_columns])
            )
            return carry

        lax.fori_loop(0, width // NORMED_TILE, column_tile, 0)

    def send_core(i):
        copies.send(
            core_ids[i], normed_grad.at[slot(2 + i)], mail.at[pl.ds(i * rows, rows)], place.core
        )

    normed_slot(3)
    send_core(1)
    normed_slot(1)
    copies.receive(core_ids[1], mail.at[pl.ds(rows, rows)], place.core)
    for i in range(PARTS):
        block = slot(1, i, PARTS)
        add_to(normed_grad.at[block], mail.at[pl.ds(rows + i * size, size)])
        copies.send(
            pair_ids[i],
            normed_grad.at[block],
            pair_landing.at[pl.ds(i * size, size)],
            place.pair,
        )
    normed_slot(2)
    send_core(0)
    normed_slot(0)
    copies.receive(core_ids[0], mail.at[pl.ds(0, rows)], place.core)
    add_to(normed_grad.at[slot(0)], mail.at[pl.ds(0, rows)])
    weight_grad(up_backs[1].grad, normed_four, grad_up, 1)
    up_backs[1].line.start((1,))
    up_backs[1].line.start((-1,), "b")
    down_backs[0].finish()
    up_backs[0].line.step(3)
    out_sum = normed_four
    out_core_id, out_pair_id, out_other_id = copies.new(), copies.new(), copies.new()
    first_weights = hidden
    first_fetch = pltpu.make_async_copy(first_kept, first_weights, local_sems.at[9])

    def out_tile(t, carry):
        block = columns_of(t)
        out_sum[block] = low(times_transpose(hidden[block], down_all[...]))
        return carry

    for i in range(PARTS):
        block = pl.ds(i * size, size)
        copies.receive(pair_ids[i], pair_landing.at[block], place.pair)
        add_to(normed_grad.at[block], pair_landing.at[block])
        copies.send(other_ids[i], normed_grad.at[block], other_landing.at[block], place.other)
        if i == 0:
            weight_grad(gate_backs[1].grad, normed_four, grad_gate, 1)
            gate_backs[1].line.start((1,))
            gate_backs[1].line.start((-1,), "b")
        if i == 1:
            lax.fori_loop(0, 4, out_tile, 0)
            copies.send(
                out_core_id, out_sum.at[pl.ds(2 * rows, 2 * rows)], out_core_landing, place.core
            )
            first_fetch.start()
        if i == 2:
            gate_backs[0].line.step(2)
    spare = mail.at[pl.ds(rows, rows)]
    copies.receive(out_core_id, out_core_landing, place.core)
    fetch(out_core_landing.at[pl.ds(rows, rows)], spare, sem)
    add_to(out_sum.at[slot(1)], spare)
    copies.send(out_pair_id, out_sum.at[slot(1)], out_pair_landing, place.pair)
    grad_own = mail.at[pl.ds(rows, rows)]
    grad_branch = mail.at[pl.ds(0, rows)]
    fetch(grad_out, grad_own, sem)
    second_sum = totals.at[:, pl.ds(kv_width, width)]
    second_sum[...] = jnp.zeros_like(second_sum)
    for i in range(PARTS):
        block = pl.ds(i * size, size)
        copies.receive(other_ids[i], other_landing.at[block], place.other)
        back = wide(normed_grad[block]) + wide(other_landing[block])
        scale_row = scales[block, 1:2]
        unit = state[block] * scale_row
        second_sum[...] += eight_rows(back * unit)
        grad_state = wide(grad_own[block]) + norm_back(back, unit, scale_row, second_gain)
        input_grad[block] = grad_state
        grad_branch[block] = low(grad_state)

    grad_heads = grad_up.at[pl.ds(0, rows), pl.ds(0, query_width)]
    grad_raw = grad_up.at[pl.ds(rows, rows), pl.ds(0, kv_width)]
    grad_heads[...] = low(matmul(grad_branch[...], w_out_all[...]))
    back_ids = [copies.new() for _ in range(4)]
    back_core_ids = [copies.new() for _ in range(4)]
    for b in range(batches):
        take_window(b)
        mine = slice(b * per_batch, (b + 1) * per_batch)
        grad_keys[...] = jnp.zeros_like(grad_keys)
        grad_values[...] = jnp.zeros_like(grad_values)

        def attend_back_head(h, carry, b=b, mine=mine):
            columns = pl.ds(pl.multiple_of(h * head_size, head_size), head_size)
            probs = probabilities(b, mine, columns)
            grad_head = grad_heads[mine, columns]
            grad_probs = times_transpose(grad_head, values[...])
            row_inner = jnp.sum(probs * grad_probs, axis=-1, keepdims=True)
            grad_scores = low(probs * (grad_probs - row_inner))
            grad_raw[mine, columns] = turned_back(matmul(grad_scores, keys[...]) * root, mine)
            grad_keys[...] += contract_rows(grad_scores, query[mine, columns])
            grad_values[...] += contract_rows(low(probs), grad_head)
            return carry

        lax.fori_loop(0, heads, attend_back_head, 0)
        for at in range(NOW + 4):
            window[at, b] = jnp.zeros_like(window[at, b])
        for back in range(BACK + 1):
            at, there = place.q + back, slice(back * per_batch, (back + 1) * per_batch)
            window[at, b, :, :head_size] = low(grad_keys[there] * root)
            window[at, b, :, head_size:] = low(grad_values[there])
        own_grad[mine, :head_size] = grad_keys[there] * root
        own_grad[mine, head_size:] = grad_values[there]
    theirs = (NOW + place.q_core, NOW + place.q_cross, BEFORE + place.q_core, BEFORE + place.q_cross)
    ours = (NOW + place.q, NOW + place.q_pair, BEFORE + place.q, BEFORE + place.q_pair)
    for i in range(4):
        copies.send(back_core_ids[i], window.at[theirs[i]], core_window.at[i], place.core)
    copies.send(
        back_ids[3], window.at[0], window_landing.at[3], place.far_left, place.has_far_left
    )


    def add_own(landing):
        for b in range(batches):
            own_grad[b * per_batch : (b + 1) * per_batch] += wide(landing[b])

    for i in (1, 2, 3):
        copies.receive(back_core_ids[i], core_window.at[i], place.core)
        for b in range(batches):
            add_to(window.at[ours[i], b], core_window.at[i, b])
    copies.send(back_ids[0], window.at[ours[1]], window_landing.at[0], place.pair)
    copies.send(back_ids[1], window.at[ours[2]], window_landing.at[1], place.left, place.has_left)
    copies.send(
        back_ids[2], window.at[ours[3]], window_landing.at[2], place.left_cross, place.has_left
    )
    up_backs[0].finish()
    gate_backs[0].line.step(3)
    for name in "acd":
        up_backs[1].line.start((-1,), name)
        gate_backs[1].line.start((-1,), name)
    copies.receive(back_core_ids[0], core_window.at[0], place.core)
    add_own(core_window.at[0])
    wo_back = RowsScatter(
        copies, place, w_out_all, wo_core_landing, wo_pair_landing, wo_line_landing, stage, sem
    )
    for origin in range(LINE):
        branch = grad_branch[:, origin * rows : (origin + 1) * rows]
        wo_back.fill(origin, low(contract_rows(branch, heads_out[...])))
    wo_back.start()
    wo_back.halve()
    down_backs[1].line.step()
    up_backs[1].line.step((1,))
    fetch(out_core_landing.at[pl.ds(0, rows)], spare, sem)
    add_to(out_sum.at[slot(0)], spare)
    copies.receive(out_pair_id, out_pair_landing, place.pair)
    fetch(out_pair_landing, spare, sem)
    add_to(out_sum.at[slot(0)], spare)
    copies.send(out_other_id, out_sum.at[slot(0)], out_other_landing, place.other)
    first_at = kv_width + width
    bias_rows = kv_width // LANES
    gain_rows = first_shard.shape[0]
    shared = bias_rows + width // gain_rows

    def gain_sums(start, row):
        for r in range(width // gain_rows):
            part = totals[:, start + r * gain_rows : start + (r + 1) * gain_rows]
            sums[0, row + r : row + r + 1, :gain_rows] = jnp.sum(part, axis=0, keepdims=True)

    sums[0] = jnp.zeros_like(sums[0])
    gain_sums(kv_width, bias_rows)
    copies.receive(back_ids[0], window_landing.at[0], place.pair)
    add_own(window_landing.at[0])

    def take_after():
        copies.receive(back_ids[1], window_landing.at[1], place.right)
        add_own(window_landing.at[1])
        copies.receive(back_ids[2], window_landing.at[2], place.right_cross)
        add_own(window_landing.at[2])

    pl.when(place.has_right)(take_after)

    def take_far():
        copies.receive(back_ids[3], window_landing.at[3], place.far_right)
        add_own(window_landing.at[3])

    pl.when(place.has_far_right)(take_far)
    every = slice(0, rows)
    grad_raw[:, query_width : query_width + head_size] = turned_back(
        own_grad[:, :head_size], every
    )
    grad_raw[:, query_width + head_size :] = low(own_grad[:, head_size:])
    first_back = RowsScatter(
        copies,
        place,
        grad_gate,
        first_core_landing,
        first_pair_landing,
        first_line_landing,
        stage,
        sem,
    )
    first_normed[...] = low(wide(tokens[...]) * scales[:, 0:1] * first_gain)
    for origin in range(LINE):
        normed = first_normed[:, origin * rows : (origin + 1) * rows]
        first_back.fill(origin, low(contract_rows(normed, grad_raw[...])))
    first_back.start()

    first_ids = [copies.new() for _ in range(PARTS)]
    sum_ids = [copies.new() for _ in range(3)]
    first_own, first_other = mail.at[pl.ds(0, rows)], pair_landing
    first_fetch.wait()

    def first_tile(t, carry):
        block = pl.ds(pl.multiple_of(t * tile, tile), tile)
        part = times_transpose(grad_raw[...], first_weights[block, :kv_width])
        first_own[:, block] = low(part)
        unit = wide(tokens[:, block]) * scales[:, 0:1]
        at = pl.ds(pl.multiple_of(first_at + t * tile, tile), tile)
        totals[:, at] = eight_rows(part * unit)
        return carry

    lax.fori_loop(0, width // tile, first_tile, 0)
    totals[:, :kv_width] = eight_rows(wide(grad_raw[...]))

    def sum_row(t, carry):
        columns = pl.ds(pl.multiple_of(t * LANES, LANES), LANES)
        sums[0, pl.ds(t, 1)] = jnp.sum(totals[:, columns], axis=0, keepdims=True)
        return carry

    lax.fori_loop(0, bias_rows, sum_row, 0)
    gain_sums(first_at, shared)

    def sum_step(i, to):
        copies.send(sum_ids[i], sums.at[i], sums_landing.at[i], to)

    def sum_take(i, to):
        copies.receive(sum_ids[i], sums_landing.at[i], to)
        sums[i + 1] = sums[i]
        if i == 0:
            sums[1, shared:] += sums_landing[0, shared:]
        else:
            sums[i + 1] += sums_landing[i]

    def sum_line(way, far):
        return place.z + far < LINE if way == 1 else place.z >= far

    line_sum_ids = {(way, far): copies.new() for way in (1, -1) for far in range(1, LINE)}
    sum_step(0, place.other)
    for i in range(PARTS):
        block = pl.ds(i * size, size)
        copies.send(first_ids[i], first_own.at[block], first_other.at[block], place.other)
    first_back.halve()
    gate_backs[0].finish()
    gate_backs[1].line.step((1,))
    wo_back.quarter()
    wo_back.line.start()
    up_backs[1].line.step((-1,))
    first_back.quarter()
    gate_backs[1].line.step((-1,))
    first_back.line.start()
    sum_take(0, place.other)
    sum_step(1, place.pair)
    for i in range(PARTS):
        block = pl.ds(i * size, size)
        copies.receive(first_ids[i], first_other.at[block], place.other)
        unit = wide(tokens[block]) * scales[block, 0:1]
        back = wide(first_own[block]) + wide(first_other[block])
        input_grad[block] += norm_back(back, unit, scales[block, 0:1], first_gain)
    sum_take(1, place.pair)
    sum_step(2, place.core)
    sum_take(2, place.core)
    line_sums[place.z] = sums[3]
    for way in (1, -1):
        for far in range(1, LINE):
            copies.send(
                line_sum_ids[way, far],
                sums.at[3],
                line_sums.at[place.z],
                {RING: place.z + way * far},
                sum_line(way, far),
            )
    down_backs[1].finish()
    up_backs[1].finish()
    copies.receive(out_other_id, out_other_landing, place.other)
    fetch(out_other_landing, spare, sem)
    spare[...] = low(state[...] + (wide(out_sum[slot(0)]) + wide(spare[...])))
    fetch(spare, output, sem)
    gate_backs[1].finish()
    wo_back.finish(grad_w_out)
    first_back.finish(grad_query_weight, grad_key_weight, grad_value_weight)
    for way in (1, -1):
        for far in range(1, LINE):
            source = place.z - way * far

            def take_sums(way=way, far=far, source=source):
                copies.receive(line_sum_ids[way, far], line_sums.at[source], {RING: source})

            pl.when(sum_line(-way, far))(take_sums)
    total = line_sums[0]
    for origin in range(1, LINE):
        total += line_sums[origin]
    sums_landing[0] = total
    query_bias_sum[...] = sums_landing[0, :heads]
    key_bias_sum[...] = sums_landing[0, heads : heads + 1]
    value_bias_sum[...] = sums_landing[0, heads + 1 : heads + 2]
    second_gain_out[...] = sums_landing[0, pl.ds(bias_rows + place.z * 4 + place.q, 1)]
    first_gain_out[...] = sums_landing[0, pl.ds(shared + place.z * 4 + place.q, 1)]
    for scatter in down_backs + up_backs + gate_backs:
        scatter.end()
    copies.settle()


def layer_call(heads, head_size, operands):
    tokens, first_shard, out_shard, gate_shard = operands[:4]
    marks = operands[-1]
    rows, width = tokens.shape
    batches = marks.shape[0] // 4
    per_batch = rows // batches
    count, units = gate_shard.shape
    padded = -(-units // (4 * LANES)) * (4 * LANES)
    quarter = padded // 4
    first_half = -(-quarter // (2 * LANES)) * LANES
    query_width = heads * head_size
    kv_width = query_width + 2 * head_size
    low_type, wide_type = jnp.bfloat16, jnp.float32
    in_vmem, anywhere = pl.BlockSpec(memory_space=pltpu.VMEM), pl.BlockSpec(memory_space=pl.ANY)

    def shape(*dims, kind=low_type):
        return jax.ShapeDtypeStruct(dims, kind)

    def vmem(*dims, kind=low_type):
        return pltpu.VMEM(dims, kind)

    sum_rows = kv_width // LANES + 2 * (width // count)
    total_columns = kv_width + 2 * width
    own_rows = marks.shape[1] - BACK * per_batch // LANES * LANES
    outs = (
        (shape(rows, width), anywhere),
        (shape(rows, width, kind=wide_type), in_vmem),
        (shape(count, query_width, kind=wide_type), in_vmem),
        (shape(count, head_size, kind=wide_type), in_vmem),
        (shape(count, head_size, kind=wide_type), in_vmem),
        (shape(count, query_width, kind=wide_type), in_vmem),
        (shape(count, padded), anywhere),
        (shape(count, padded), anywhere),
        (shape(count, padded), anywhere),
        (shape(heads, head_size, kind=wide_type), in_vmem),
        (shape(1, head_size, kind=wide_type), in_vmem),
        (shape(1, head_size, kind=wide_type), in_vmem),
        (shape(1, LANES, kind=wide_type), in_vmem),
        (shape(1, LANES, kind=wide_type), in_vmem),
    )
    kept = (
        shape(width, first_shard.shape[1]),
        shape(4 * rows, width),
        shape(6, 2, LINE - 1, 4 * count, first_half),
        shape(2 * rows, width),
        shape(rows, width),
        shape(rows, width),
        shape(2 * LINE * count, kv_width),
        shape(LINE, count, kv_width),
        shape(2, LINE - 1, count, kv_width),
        shape(2 * LINE * count, query_width),
        shape(LINE, count, query_width),
        shape(2, LINE - 1, count, query_width),
    )
    scratch = (
        vmem(width, first_shard.shape[1]),
        vmem(width, query_width),
        vmem(rows, width, kind=wide_type),
        vmem(NOW + 4, batches, per_batch, 2 * head_size),
        vmem((BACK + 1) * per_batch, head_size),
        vmem((BACK + 1) * per_batch, head_size),
        vmem(2 * rows, width),
        vmem(rows, query_width),
        vmem(rows, query_width),
        vmem(width, quarter),
        vmem(width, quarter),
        vmem(width, quarter),
        vmem(4 * rows, width),
        vmem(4 * rows, width),
        vmem(4 * rows, quarter),
        vmem(4 * rows, quarter),
        vmem(4 * rows, quarter),
        vmem(width, first_half),
        vmem(width, first_half),
        vmem(rows, width),
        vmem(rows, width),
        vmem(4 * count, max(kv_width, first_half)),
        vmem((BACK + 1) * per_batch, head_size, kind=wide_type),
        vmem((BACK + 1) * per_batch, head_size, kind=wide_type),
        vmem(rows, 2 * head_size, kind=wide_type),
        vmem(4, batches, per_batch, 2 * head_size),
        vmem(4, batches, per_batch, 2 * head_size),
        vmem(own_rows, marks.shape[0], kind=wide_type),
        vmem(rows, 2, kind=wide_type),
        vmem(8, total_columns, kind=wide_type),
        vmem(4, sum_rows, LANES, kind=wide_type),
        vmem(3, sum_rows, LANES, kind=wide_type),
        vmem(LINE, sum_rows, LANES, kind=wide_type),
        pltpu.SemaphoreType.DMA((N_REMOTE,)),
        pltpu.SemaphoreType.DMA((N_REMOTE,)),
        pltpu.SemaphoreType.DMA((14,)),
    )
    results = pl.pallas_call(
        functools.partial(layer_kernel, heads, head_size),
        out_shape=[out[0] for out in outs] + list(kept),
        in_specs=[in_vmem] + [anywhere] * 6 + [in_vmem] * 6,
        out_specs=[out[1] for out in outs] + [anywhere] * len(kept),
        scratch_shapes=scratch,
        compiler_params=pltpu.CompilerParams(
            collective_id=0, has_side_effects=True, vmem_limit_bytes=VMEM_BYTES
        ),
    )(*operands)
    return results[: len(outs)]


def results_kernel(*refs):
    count = len(refs) // 2
    for source, target in zip(refs[:count], refs[count:]):
        if len(target.shape) == 1:
            target[...] = source[0, : target.shape[0]]
        else:
            target[...] = source[:, : target.shape[1]].astype(target.dtype)


def results_call(as_they_are, widened, units, vectors, vector_size):
    shapes = [jax.ShapeDtypeStruct(value.shape, value.dtype) for value in as_they_are]
    shapes += [jax.ShapeDtypeStruct((value.shape[0], units), jnp.float32) for value in widened]
    shapes += [jax.ShapeDtypeStruct((vector_size,), jnp.float32) for _ in vectors]
    in_vmem = pl.BlockSpec(memory_space=pltpu.VMEM)
    return pl.pallas_call(
        results_kernel,
        out_shape=shapes,
        in_specs=[in_vmem] * len(shapes),
        out_specs=[in_vmem] * len(shapes),
        compiler_params=pltpu.CompilerParams(vmem_limit_bytes=VMEM_BYTES),
    )(*as_they_are, *widened, *vectors)


def body(
    tokens,
    norm1_gain,
    query_weight,
    query_bias,
    key_weight,
    key_bias,
    value_weight,
    value_bias,
    output_weight,
    norm2_gain,
    gate_weight,
    up_weight,
    down_weight,
    cotangent,
    segments,
    positions,
):
    batches, count_rows, width = tokens.shape
    heads, head_size = query_bias.shape
    query_width = heads * head_size
    units = gate_weight.shape[1]
    place = lax.axis_index(FSDP)
    row_start = place * count_rows
    rows = batches * count_rows

    gains = jnp.stack([norm1_gain, norm2_gain], axis=1)
    gains = jnp.pad(gains, ((0, 0), (0, LANES - 2)))
    first_shard = jnp.concatenate([query_weight, key_weight, value_weight, gains], axis=1)
    kv_width = query_width + 2 * head_size
    padded = -(-units // (4 * LANES)) * (4 * LANES)

    def spaced(shard):
        return jnp.pad(shard, ((0, 0), (0, padded - units)))

    grad_out = cotangent.reshape(rows, width)
    inputs = wide(tokens.reshape(rows, width))
    biases = jnp.concatenate(
        [query_bias.reshape(-1), key_bias.reshape(-1), value_bias.reshape(-1)]
    )
    own_places = lax.dynamic_slice_in_dim(positions, row_start, count_rows, axis=1)
    cosine, sine_table = rotation(own_places.reshape(-1), head_size)
    if lax.axis_size(RING) == LINE:
        marks = jnp.concatenate([segments, positions]).astype(jnp.float32)
        lanes = -(-(BACK + 1) * count_rows // LANES) * LANES
        marks = jnp.pad(
            marks,
            ((0, 2 * batches), (BACK * count_rows, lanes - (BACK + 1) * count_rows)),
            constant_values=-1.0,
        )
        marks = lax.dynamic_slice_in_dim(marks, row_start, lanes, axis=1)
        (
            output,
            input_grad,
            grad_query_weight,
            grad_key_weight,
            grad_value_weight,
            grad_w_out,
            grad_w_down,
            grad_w_gate,
            grad_w_up,
            query_bias_sum,
            key_bias_sum,
            value_bias_sum,
            first_gain_sum,
            second_gain_sum,
        ) = layer_call(
            heads,
            head_size,
            (
                tokens.reshape(rows, width),
                first_shard,
                output_weight.T,
                gate_weight,
                up_weight,
                down_weight.T,
                grad_out,
                query_bias,
                key_bias,
                value_bias,
                cosine[:, 0],
                sine_table[:, 0],
                marks,
            ),
        )
        (
            output,
            input_grad,
            grad_query_weight,
            grad_key_weight,
            grad_value_weight,
            grad_w_out,
            query_bias_sum,
            key_bias_sum,
            value_bias_sum,
            grad_w_down,
            grad_w_gate,
            grad_w_up,
            first_total,
            second_total,
        ) = results_call(
            (
                output,
                input_grad,
                grad_query_weight,
                grad_key_weight,
                grad_value_weight,
                grad_w_out,
                query_bias_sum,
                key_bias_sum,
                value_bias_sum,
            ),
            (grad_w_down, grad_w_gate, grad_w_up),
            units,
            (first_gain_sum, second_gain_sum),
            norm1_gain.shape[0],
        )
    else:
        allowed = [
            visible(segments[b], positions[b], row_start, count_rows) for b in range(batches)
        ]
        first_all = gather_rows(first_shard)
        w_qkv = first_all[:, :kv_width]
        first_gain = wide(first_all[:, kv_width])
        second_gain = wide(first_all[:, kv_width + 1])
        w_out = gather_rows(output_weight.T)
        w_gate = quarter_columns(spaced(gate_weight))
        w_up = quarter_columns(spaced(up_weight))
        w_down = quarter_columns(spaced(down_weight.T))
        grad_out_four = four_blocks(grad_out)
        first_unit, first_scale = root_mean_square_parts(inputs)
        first_normed = low(first_unit * first_gain)
        raw = matmul(first_normed, w_qkv) + wide(biases)
        turned = rotate(
            raw[:, : query_width + head_size].reshape(rows, heads + 1, head_size),
            cosine,
            sine_table,
        )
        turned = low(turned)
        query_rows = turned[:, :heads].reshape(batches, count_rows, heads, head_size)
        key_value = jnp.concatenate(
            [turned[:, heads], low(raw[:, query_width + head_size :])], axis=1
        )
        key_value = key_value.reshape(batches, count_rows, 2 * head_size)
        window = jnp.concatenate(
            [shifted(key_value, back) for back in range(BACK, 0, -1)] + [key_value], axis=1
        )
        key_rows, value_rows = window[..., :head_size], window[..., head_size:]
        attended = [
            attend(query_rows[b], key_rows[b], value_rows[b], allowed[b]) for b in range(batches)
        ]
        log_totals = [log_total for _, log_total in attended]
        heads_out = jnp.concatenate([mixed for mixed, _ in attended], axis=0)
        residual = inputs + tensor_total(times_transpose(heads_out, w_out))
        second_unit, second_scale = root_mean_square_parts(residual)
        second_normed = four_blocks(low(second_unit * second_gain))

        second_unit, second_scale = root_mean_square_parts(residual)
        gate_value = matmul(second_normed, w_gate)
        up_part = matmul(second_normed, w_up)
        sigmoid_gate = jax.nn.sigmoid(gate_value)
        silu_gate = gate_value * sigmoid_gate
        hidden = low(silu_gate * up_part)
        grad_hidden = matmul(grad_out_four, w_down)
        grad_gate = low(
            grad_hidden * up_part * sigmoid_gate * (1.0 + gate_value * (1.0 - sigmoid_gate))
        )
        grad_up = low(grad_hidden * silu_gate)
        second_back = four_sums(times_transpose(grad_gate, w_gate) + times_transpose(grad_up, w_up))
        grad_w_down = quarter_to_owner(low(contract_rows(grad_out_four, hidden)))
        grad_w_gate = quarter_to_owner(low(contract_rows(second_normed, grad_gate)))
        grad_w_up = quarter_to_owner(low(contract_rows(second_normed, grad_up)))
        output = low(residual + four_sums(times_transpose(hidden, w_down)))

        second_gain_sum = jnp.sum(second_back * second_unit, axis=0)
        grad_state = wide(grad_out) + norm_back(second_back, second_unit, second_scale, second_gain)
        grad_branch = low(grad_state)
        grad_w_out = scatter_rows(contract_rows(grad_branch, heads_out))
        grad_heads = low(matmul(grad_branch, w_out)).reshape(query_rows.shape)
        backs = [
            attend_back(
                grad_heads[b], query_rows[b], key_rows[b], value_rows[b], allowed[b], log_totals[b]
            )
            for b in range(batches)
        ]
        grad_query = jnp.stack([back[0] for back in backs]).reshape(rows, heads, head_size)
        grad_window = jnp.stack([jnp.concatenate([back[1], back[2]], axis=1) for back in backs])
        own_grad = grad_window[:, BACK * count_rows :]
        for back in range(1, BACK + 1):
            first_row = (BACK - back) * count_rows
            own_grad = own_grad + wide(
                shifted(low(grad_window[:, first_row : first_row + count_rows]), -back)
            )
        own_grad = own_grad.reshape(rows, 2, head_size)
        turned_back = rotate_back(
            jnp.concatenate([grad_query, own_grad[:, :1]], axis=1), cosine, sine_table
        )
        grad_raw = low(jnp.concatenate([turned_back, own_grad[:, 1:]], axis=1).reshape(rows, -1))
        grad_w_qkv = scatter_rows(contract_rows(first_normed, grad_raw))
        bias_sum = jnp.sum(wide(grad_raw), axis=0)
        first_back_part = times_transpose(grad_raw, w_qkv)
        first_back = tensor_total(first_back_part)
        first_gain_sum = jnp.sum(first_back * first_unit, axis=0)
        input_grad = grad_state + norm_back(first_back, first_unit, first_scale, first_gain)
        sums = summed_over_fsdp(jnp.concatenate([bias_sum, second_gain_sum, first_gain_sum]))
        bias_total = sums[:kv_width]
        gain_rows = norm1_gain.shape[0]
        second_total = lax.dynamic_slice_in_dim(sums, kv_width + place * gain_rows, gain_rows)
        first_total = lax.dynamic_slice_in_dim(sums, kv_width + width + place * gain_rows, gain_rows)
        grad_query_weight = grad_w_qkv[:, :query_width]
        grad_key_weight = grad_w_qkv[:, query_width : query_width + head_size]
        grad_value_weight = grad_w_qkv[:, query_width + head_size :]
        query_bias_sum = bias_total[:query_width].reshape(query_bias.shape)
        key_bias_sum = bias_total[query_width : query_width + head_size].reshape(key_bias.shape)
        value_bias_sum = bias_total[query_width + head_size :].reshape(value_bias.shape)

    return (
        output.reshape(tokens.shape),
        input_grad.reshape(tokens.shape),
        first_total,
        grad_query_weight,
        query_bias_sum,
        grad_key_weight,
        key_bias_sum,
        grad_value_weight,
        value_bias_sum,
        grad_w_out.T,
        second_total,
        grad_w_gate[:, :units],
        grad_w_up[:, :units],
        grad_w_down[:, :units].T,
    )


def solution(mesh):
    fsdp, tensor = mesh.shape["fsdp"], mesh.shape["tensor"]
    fine = Mesh(mesh.devices.reshape(fsdp // 4, 2, 2, tensor), (RING, PAIR, CORE, TENSOR))
    by_rows, by_columns, by_tensor = P(FSDP, TENSOR), P(TENSOR, FSDP), P(TENSOR, None)
    by_tokens, by_gain = P(None, FSDP, None), P(FSDP)
    placed = (
        by_tokens,
        by_gain,
        by_rows,
        by_tensor,
        by_rows,
        by_tensor,
        by_rows,
        by_tensor,
        by_columns,
        by_gain,
        by_rows,
        by_rows,
        by_columns,
        by_tokens,
        P(),
        P(),
    )
    return jax.shard_map(
        body,
        mesh=fine,
        in_specs=placed,
        out_specs=(
            by_tokens,
            by_tokens,
            by_gain,
            by_rows,
            by_tensor,
            by_rows,
            by_tensor,
            by_rows,
            by_tensor,
            by_columns,
            by_gain,
            by_rows,
            by_rows,
            by_columns,
        ),
        check_vma=False,
    )
```

```python
import functools
import math

import jax
import jax.numpy as jnp
import numpy as np
from jax import lax
from jax.experimental import pallas as pl
from jax.experimental.pallas import tpu as pltpu
from jax.sharding import Mesh
from jax.sharding import PartitionSpec as P

BACK = 5
LINE = 4
LANES = 128
VMEM_BYTES = 65350 * 1024

EPSILON = 1e-06
THETA = 1000000.0
NEGATIVE = -1e30

RING, PAIR, CORE, TENSOR = "ring", "pair", "core", "tensor"
FSDP = (RING, PAIR, CORE)
SWAP = [(0, 1), (1, 0)]


def low(value):
    return value.astype(jnp.bfloat16)


def wide(value):
    return value.astype(jnp.float32)


def matmul(left_side, right_side):
    return jnp.dot(left_side, right_side, preferred_element_type=jnp.float32)


def contract_rows(left_side, right_side):
    return lax.dot_general(
        left_side, right_side, (((0,), (0,)), ((), ())), preferred_element_type=jnp.float32
    )


def times_transpose(left_side, right_side):
    return lax.dot_general(
        left_side, right_side, (((1,), (1,)), ((), ())), preferred_element_type=jnp.float32
    )


def swapped(value, axis):
    return lax.ppermute(value, axis, SWAP)


def in_order(own, other, place, axis):
    first = jnp.where(place == 0, own, other)
    second = jnp.where(place == 0, other, own)
    return jnp.stack([first, second], axis=axis)


def shifted(value, steps):
    count = lax.axis_size(FSDP)
    first, last = (max(0, -steps), min(count, count - steps))
    return lax.ppermute(value, FSDP, [(source, source + steps) for source in range(first, last)])


def summed_over_fsdp(value):
    count = lax.axis_size(FSDP)
    bit = 1
    while bit < count:
        value = value + lax.ppermute(value, FSDP, [(i, i ^ bit) for i in range(count)])
        bit *= 2
    return value


def line_gather(block):
    count, here = lax.axis_size(RING), lax.axis_index(RING)
    if count > LINE:
        return lax.all_gather(block, RING, axis=0)
    right, left = [block], [block]
    for step in range(1, count):
        right.append(
            lax.ppermute(right[-1], RING, [(i, i + 1) for i in range(step - 1, count - 1)])
        )
        left.append(
            lax.ppermute(left[-1], RING, [(i, i - 1) for i in range(1, count - step + 1)])
        )
    result = jnp.zeros((count,) + block.shape, block.dtype)
    for step in range(count):
        piece = block if step == 0 else jnp.where(here >= step, right[step], left[count - step])
        result = lax.dynamic_update_slice_in_dim(
            result, piece[None], (here - step + count) % count, axis=0
        )
    return result


def line_scatter(parts):
    count, here = lax.axis_size(RING), lax.axis_index(RING)
    if count > LINE:
        return wide(lax.psum_scatter(parts, RING, scatter_dimension=0, tiled=False))

    def part(place):
        return lax.dynamic_index_in_dim(parts, place, axis=0, keepdims=False)

    right, left = None, None
    for step in range(1, count):
        to_right, to_left = part(here + count - step), part(here - count + step)
        if step > 1:
            to_right = low(wide(to_right) + wide(right))
            to_left = low(wide(to_left) + wide(left))
        right = lax.ppermute(to_right, RING, [(i, i + 1) for i in range(step)])
        left = lax.ppermute(to_left, RING, [(i, i - 1) for i in range(count - step, count)])
    return wide(part(here)) + wide(right) + wide(left)


def gather_rows(shard):
    rows = line_gather(shard)
    rows = in_order(rows, swapped(rows, PAIR), lax.axis_index(PAIR), 1)
    rows = in_order(rows, swapped(rows, CORE), lax.axis_index(CORE), 2)
    return rows.reshape((-1,) + shard.shape[1:])


def scatter_rows(total):
    pair, core = lax.axis_index(PAIR), lax.axis_index(CORE)
    parts = low(total).reshape((lax.axis_size(RING), 2, 2, -1) + total.shape[1:])

    def halved(value, axis, place, name):
        mine = lax.dynamic_index_in_dim(value, place, axis=axis, keepdims=False)
        sent = lax.dynamic_index_in_dim(value, 1 - place, axis=axis, keepdims=False)
        return low(wide(mine) + wide(swapped(sent, name)))

    parts = halved(parts, 2, core, CORE)
    parts = halved(parts, 1, pair, PAIR)
    return line_scatter(parts)


def quarter_columns(shard):
    pair, core = lax.axis_index(PAIR), lax.axis_index(CORE)
    half = shard.shape[1] // 2

    def halved(value, place, width):
        mine = lax.dynamic_slice_in_dim(value, place * width, width, axis=value.ndim - 1)
        sent = lax.dynamic_slice_in_dim(value, (1 - place) * width, width, axis=value.ndim - 1)
        return mine, sent

    mine, sent = halved(shard, pair, half)
    rows = in_order(mine, swapped(sent, PAIR), pair, 0)
    mine, sent = halved(rows, core, half // 2)
    rows = in_order(mine, swapped(sent, CORE), core, 1)
    rows = line_gather(rows.reshape(-1, half // 2))
    return rows.reshape(-1, half // 2)


def quarter_to_owner(grad):
    pair, core = lax.axis_index(PAIR), lax.axis_index(CORE)
    width = grad.shape[1]
    block = lax.psum_scatter(
        grad.reshape(lax.axis_size(RING), -1, width), RING, scatter_dimension=0, tiled=False
    )
    block = block.reshape(2, 2, -1, width)

    def halved(value, axis, place):
        mine = lax.dynamic_index_in_dim(value, place, axis=axis, keepdims=False)
        sent = lax.dynamic_index_in_dim(value, 1 - place, axis=axis, keepdims=False)
        return mine, sent

    mine, sent = halved(block, 0, pair)
    block = in_order(mine, swapped(sent, PAIR), pair, 0)
    mine, sent = halved(block, 1, core)
    block = in_order(mine, swapped(sent, CORE), core, 1)
    return jnp.concatenate([wide(block[i, j]) for i in range(2) for j in range(2)], axis=1)


def four_blocks(value):
    over = swapped(value, PAIR)
    return jnp.concatenate([value, over, swapped(value, CORE), swapped(over, CORE)], axis=0)


def four_sums(total):
    half = total.shape[0] // 2
    total = total[:half] + wide(swapped(low(total[half:]), CORE))
    total = total[: half // 2] + wide(swapped(low(total[half // 2 :]), PAIR))
    return tensor_total(total)


def tensor_total(partial_sum):
    own = lax.reduce_precision(partial_sum, 8, 7)
    return own + wide(swapped(low(own), TENSOR))


def rotation(places, width):
    half_width = width // 2
    frequency = THETA ** (-(jnp.arange(half_width, dtype=jnp.float32) * 2.0) / width)
    angles = places.astype(jnp.float32)[:, None] * frequency[None, :]
    cosine = jnp.concatenate([jnp.cos(angles), jnp.cos(angles)], axis=-1)[:, None, :]
    sine_table = jnp.concatenate([jnp.sin(angles), jnp.sin(angles)], axis=-1)[:, None, :]
    return (cosine, sine_table)


def rotate(values, cosine, sine_table):
    half_width = values.shape[-1] // 2
    turned = jnp.concatenate([-values[..., half_width:], values[..., :half_width]], axis=-1)
    return values * cosine + turned * sine_table


def rotate_back(gradient, cosine, sine_table):
    half_width = gradient.shape[-1] // 2
    moved_part = gradient * sine_table
    return gradient * cosine + jnp.concatenate(
        [moved_part[..., half_width:], -moved_part[..., :half_width]], axis=-1
    )


def root_mean_square_parts(values):
    scale_row = lax.rsqrt(jnp.mean(values * values, axis=-1, keepdims=True) + EPSILON)
    return (values * scale_row, scale_row)


def norm_back(grad_normed, normalized, scale_row, gain):
    scaled = grad_normed * gain
    return scale_row * (scaled - normalized * jnp.mean(scaled * normalized, axis=-1, keepdims=True))


def visible(seg_row, pos_row, row_start, count_rows):
    pad_rows = BACK * count_rows
    seg_padded = jnp.concatenate([jnp.full((pad_rows,), -1, jnp.int32), seg_row])
    pos_padded = jnp.concatenate([jnp.zeros((pad_rows,), jnp.int32), pos_row])
    key_seg = lax.dynamic_slice_in_dim(seg_padded, row_start, pad_rows + count_rows)
    key_pos = lax.dynamic_slice_in_dim(pos_padded, row_start, pad_rows + count_rows)
    query_seg = lax.dynamic_slice_in_dim(seg_row, row_start, count_rows)
    query_pos = lax.dynamic_slice_in_dim(pos_row, row_start, count_rows)
    return (query_seg[:, None] == key_seg[None, :]) & (key_pos[None, :] <= query_pos[:, None])


def attend(query_rows, key_rows, value_rows, allowed):
    scores = jnp.einsum("thd,sd->hts", query_rows, key_rows, preferred_element_type=jnp.float32)
    scores = scores * (1.0 / math.sqrt(query_rows.shape[-1]))
    scores = jnp.where(allowed, scores, NEGATIVE)
    row_max = jnp.max(scores, axis=-1, keepdims=True)
    log_total = row_max + jnp.log(jnp.sum(jnp.exp(scores - row_max), axis=-1, keepdims=True))
    probs_low = low(jnp.exp(scores - log_total))
    mixed = jnp.einsum("hts,sd->thd", probs_low, value_rows, preferred_element_type=jnp.float32)
    return low(mixed.reshape(query_rows.shape[0], -1)), log_total


def log_total_of(query_rows, key_rows, allowed):
    scores = jnp.einsum("thd,sd->hts", query_rows, key_rows, preferred_element_type=jnp.float32)
    scores = scores * (1.0 / math.sqrt(query_rows.shape[-1]))
    scores = jnp.where(allowed, scores, NEGATIVE)
    row_max = jnp.max(scores, axis=-1, keepdims=True)
    return row_max + jnp.log(jnp.sum(jnp.exp(scores - row_max), axis=-1, keepdims=True))


def attend_back(grad_heads, query_rows, key_rows, value_rows, allowed, log_total):
    scale = 1.0 / math.sqrt(query_rows.shape[-1])
    scores = jnp.einsum("thd,sd->hts", query_rows, key_rows, preferred_element_type=jnp.float32)
    probs = jnp.exp(jnp.where(allowed, scores * scale, NEGATIVE) - log_total)
    grad_probs = jnp.einsum(
        "thd,sd->hts", grad_heads, value_rows, preferred_element_type=jnp.float32
    )
    row_inner = jnp.sum(probs * grad_probs, axis=-1, keepdims=True)
    grad_scores = low(probs * (grad_probs - row_inner))
    grad_query = jnp.einsum(
        "hts,sd->thd", grad_scores, key_rows, preferred_element_type=jnp.float32
    )
    grad_keys = jnp.einsum(
        "hts,thd->sd", grad_scores, query_rows, preferred_element_type=jnp.float32
    )
    grad_values = jnp.einsum(
        "hts,thd->sd", low(probs), grad_heads, preferred_element_type=jnp.float32
    )
    return grad_query * scale, grad_keys * scale, grad_values


def device(**coordinates):
    return {name: place for name, place in coordinates.items()}


class Copies:
    def __init__(self, send_sems, recv_sems):
        self.send_sems, self.recv_sems = send_sems, recv_sems
        self.used = 0
        self.sent = []

    def new(self):
        self.used += 1
        return self.used - 1

    def _make(self, which, source, target, to):
        return pltpu.make_async_remote_copy(
            src_ref=source,
            dst_ref=target,
            send_sem=self.send_sems.at[which],
            recv_sem=self.recv_sems.at[which],
            device_id=to,
            device_id_type=pl.DeviceIdType.MESH,
        )

    def send(self, which, source, target, to, cond=None):
        only(cond, lambda: self._make(which, source, target, to).start())
        self.sent.append((which, source, target, to, cond))

    def receive(self, which, target, via):
        self._make(which, target, target, via).wait_recv()

    def settle(self, until=None):
        until = len(self.sent) if until is None else until
        for i in range(until):
            if self.sent[i] is not None:
                which, source, target, to, cond = self.sent[i]
                only(cond, lambda: self._make(which, source, target, to).wait_send())
                self.sent[i] = None

    def left(self, which):
        for i, entry in enumerate(self.sent):
            if entry is not None and entry[0] == which:
                _, source, target, to, cond = entry
                only(cond, lambda: self._make(which, source, target, to).wait_send())
                self.sent[i] = None

    def settle_of(self, ids):
        for which in ids:
            self.left(which)

    def mark(self):
        return len(self.sent)


def only(cond, action):
    if cond is None:
        action()
    else:
        pl.when(cond)(action)


class Place:
    def __init__(self):
        self.z, self.p = lax.axis_index(RING), lax.axis_index(PAIR)
        self.c, self.y = lax.axis_index(CORE), lax.axis_index(TENSOR)
        self.q = self.p * 2 + self.c
        self.q_pair, self.q_core = (1 - self.p) * 2 + self.c, self.p * 2 + 1 - self.c
        self.q_cross = (1 - self.p) * 2 + 1 - self.c
        self.pair, self.core = {PAIR: 1 - self.p}, {CORE: 1 - self.c}
        self.cross = {PAIR: 1 - self.p, CORE: 1 - self.c}
        self.other = {TENSOR: 1 - self.y}
        self.near = {RING: self.z + 1 - 2 * (self.z % 2)}
        self.far = {RING: self.z + 2 - 4 * (self.z // 2)}
        self.right, self.left = {RING: self.z + 1}, {RING: self.z - 1}
        self.right_cross = {RING: self.z + 1, PAIR: 1 - self.p}
        self.left_cross = {RING: self.z - 1, PAIR: 1 - self.p}
        self.far_right = {RING: self.z + 2, PAIR: 0, CORE: 0}
        self.far_left = {RING: self.z - 2, PAIR: 1, CORE: 1}
        self.has_right, self.has_left = self.z < LINE - 1, self.z > 0
        self.has_far_right = (self.q == 3) & (self.z < LINE - 2)
        self.has_far_left = (self.q == 0) & (self.z > 1)

    def meet(self):
        barrier = pltpu.get_barrier_semaphore()

        def greet(to, cond=None):
            only(
                cond,
                lambda: pl.semaphore_signal(
                    barrier, inc=1, device_id=to, device_id_type=pl.DeviceIdType.MESH
                ),
            )

        for to in (self.pair, self.core, self.cross, self.other):
            greet(to)
        for far in (2, 3):
            greet({RING: self.z + far}, self.z + far < LINE)
            greet({RING: self.z - far}, self.z >= far)
        for there, to, cross in (
            (self.has_right, self.right, self.right_cross),
            (self.has_left, self.left, self.left_cross),
        ):
            greet(to, there)
            greet(cross, there)
        greet(self.far_right, self.has_far_right)
        greet(self.far_left, self.has_far_left)
        line = jnp.minimum(self.z, 1) + jnp.minimum(LINE - 1 - self.z, 1)
        upper = self.z // 2
        reach = self.p * self.c * (1 - upper) + (1 - self.p) * (1 - self.c) * upper
        pl.semaphore_wait(barrier, 4 + LINE - 1 + line + reach)


class LineFlow:
    def __init__(self, copies, place, block):
        self.copies, self.place, self.block = copies, place, block
        self.ids = {(way, step): copies.new() for way in (1, -1) for step in range(1, LINE)}

    def valid(self, way, step):
        z = self.place.z
        return z >= step if way == 1 else z + step <= LINE - 1

    def origin(self, way, step):
        return self.place.z - way * step

    def onward(self, way, step, source):
        if step == LINE - 1:
            return
        to = self.place.right if way == 1 else self.place.left
        there = self.place.has_right if way == 1 else self.place.has_left
        if step:
            there = there & self.valid(way, step)
        target = self.block(self.origin(way, step))
        self.copies.send(self.ids[way, step + 1], source, target, to, there)

    def start(self, source):
        self.onward(1, 0, source)
        self.onward(-1, 0, source)

    def arrive(self, step, then=None):
        for way in (1, -1):

            def take(way=way):
                target = self.block(self.origin(way, step))
                via = self.place.left if way == 1 else self.place.right
                self.copies.receive(self.ids[way, step], target, via)

            pl.when(self.valid(way, step))(take)
            if step < LINE - 1:
                self.onward(way, step, self.block(self.origin(way, step)))
            if then is not None:
                then(way, step)


class RowsFlow:
    def __init__(self, copies, place, shard, whole):
        self.copies, self.place, self.shard, self.whole = copies, place, shard, whole
        self.line = LineFlow(copies, place, lambda origin: self.rows(origin, place.p, place.c))
        items = [(0, 0)] + [(way, step) for step in range(1, LINE) for way in (1, -1)]
        self.items = items
        self.pair_ids = {item: copies.new() for item in items}
        self.core_ids = {item: copies.new() for item in items}
        self.cross_ids = {item: copies.new() for item in items}

    def rows(self, origin, p, c):
        count = self.shard.shape[0]
        return self.whole.at[pl.ds(pl.multiple_of((origin * 4 + p * 2 + c) * count, count), count)]

    def valid(self, item):
        return None if item == (0, 0) else self.line.valid(*item)

    def spread(self, way, step):
        item, place = (way, step), self.place
        here = self.rows(self.line.origin(way, step), place.p, place.c)
        self.copies.send(self.pair_ids[item], here, here, place.pair, self.valid(item))
        self.copies.send(self.core_ids[item], here, here, place.core, self.valid(item))

    def start(self, own_copy):
        self.line.start(self.shard)
        own_copy()
        self.spread(0, 0)

    def arrive(self, step):
        self.line.arrive(step, self.spread)

    def crossing(self, step):
        place = self.place
        for item in self.items:
            if item[1] != step:
                continue
            there = self.rows(self.line.origin(*item), 1 - place.p, place.c)
            only(
                self.valid(item),
                lambda: self.copies.receive(self.pair_ids[item], there, place.pair),
            )
            self.copies.send(self.cross_ids[item], there, there, place.core, self.valid(item))

    def end(self):
        place = self.place
        for item in self.items:
            origin = self.line.origin(*item)

            def take(item=item, origin=origin):
                mine = self.rows(origin, place.p, 1 - place.c)
                cross = self.rows(origin, 1 - place.p, 1 - place.c)
                self.copies.receive(self.core_ids[item], mine, place.core)
                self.copies.receive(self.cross_ids[item], cross, place.core)

            only(self.valid(item), take)


class QuarterFlow:
    def __init__(self, copies, place, shard, whole, columns, own_sem):
        self.copies, self.place, self.shard, self.whole = copies, place, shard, whole
        self.count, self.quarter = shard.shape[0], -(-shard.shape[1] // (4 * LANES)) * LANES
        self.start_column, self.width = columns
        self.last = min(self.width, shard.shape[1] - 3 * self.quarter - self.start_column)
        self.own_sem = own_sem
        self.near = (
            (copies.new(), 1 - place.p, place.c, place.pair),
            (copies.new(), place.p, 1 - place.c, place.core),
            (copies.new(), 1 - place.p, 1 - place.c, place.cross),
        )
        self.line = LineFlow(copies, place, self.block)

    def columns(self, q, width):
        start = q * self.quarter + self.start_column
        return self.shard.at[:, pl.ds(pl.multiple_of(start, LANES), width)]

    def rows(self, p, c, width):
        start = (self.place.z * 4 + p * 2 + c) * self.count
        rows = pl.ds(pl.multiple_of(start, self.count), self.count)
        return self.whole.at[rows, pl.ds(0, width)]

    def block(self, origin):
        count = 4 * self.count
        return self.whole.at[pl.ds(pl.multiple_of(origin * count, count), count)]

    def widths(self, q):
        if self.last == self.width:
            return ((None, self.width),)
        return ((q == 3, self.last), (q != 3, self.width))

    def own(self, width):
        place = self.place
        return pltpu.make_async_copy(
            self.columns(place.q, width), self.rows(place.p, place.c, width), self.own_sem
        )

    def start(self):
        place = self.place
        for cond, width in self.widths(place.q):
            only(cond, lambda: self.own(width).start())
        for which, p, c, to in self.near:
            for cond, width in self.widths(p * 2 + c):
                target = self.rows(place.p, place.c, width)
                self.copies.send(which, self.columns(p * 2 + c, width), target, to, cond)

    def join(self):
        def take(width):
            self.own(width).wait()
            for which, p, c, to in self.near:
                self.copies.receive(which, self.rows(p, c, width), to)

        for cond, width in self.widths(self.place.q):
            only(cond, lambda: take(width))
        self.line.start(self.block(self.place.z))

    def arrive(self, step):
        self.line.arrive(step)


class FourFlow:
    def __init__(self, copies, place, slots, parts):
        self.copies, self.place, self.slots = copies, place, slots
        self.rows = slots.shape[0] // 4
        self.size = self.rows // parts
        self.ids = [[copies.new() for _ in range(3)] for _ in range(parts)]

    def slot(self, which, part):
        return self.slots.at[pl.ds(which * self.rows + part * self.size, self.size)]

    def send(self, part, source):
        self.copies.send(self.ids[part][0], source, self.slot(1, part), self.place.pair)
        self.copies.send(self.ids[part][1], source, self.slot(2, part), self.place.core)

    def cross(self, part):
        got = self.slot(1, part)
        self.copies.receive(self.ids[part][0], got, self.place.pair)
        self.copies.send(self.ids[part][2], got, self.slot(3, part), self.place.core)

    def end(self, part):
        self.copies.receive(self.ids[part][1], self.slot(2, part), self.place.core)
        self.copies.receive(self.ids[part][2], self.slot(3, part), self.place.core)


def fetch(source, target, sem):
    copy = pltpu.make_async_copy(source, target, sem)
    copy.start()
    copy.wait()


def add_to(target, source):
    target[...] = low(wide(target[...]) + wide(source[...]))


class LineScatter:
    def __init__(self, copies, place, block, arrived, stage, sem):
        self.copies, self.place, self.block = copies, place, block
        self.arrived, self.stage, self.sem = arrived, stage, sem
        self.ids = {(way, step): copies.new() for way in (1, -1) for step in range(1, LINE)}

    def landing(self, way, step):
        return self.arrived.at[(1 - way) // 2, step - 1]

    def target(self, way, step):
        return self.block(self.place.z + way * (LINE - step))

    def takes(self, way, step):
        z = self.place.z
        if way == 1:
            return (z >= 1) & (z <= step)
        return (z <= LINE - 2) & (z >= LINE - 1 - step)

    def send(self, way, step, cond):
        to = self.place.right if way == 1 else self.place.left
        self.copies.send(
            self.ids[way, step], self.target(way, step), self.landing(way, step), to, cond
        )

    def start(self, ways=(1, -1)):
        for way in ways:
            for step in range(1, LINE):
                self.send(way, step, self.place.z == (0 if way == 1 else LINE - 1))

    def take(self, way, step):
        via = self.place.left if way == 1 else self.place.right
        self.copies.receive(self.ids[way, step], self.landing(way, step), via)
        fetch(self.landing(way, step), self.stage, self.sem)

    def step(self, step, ways=(1, -1)):
        for way in ways:
            there = self.takes(way, step - 1)

            def add(way=way):
                self.take(way, step - 1)
                add_to(self.target(way, step), self.stage)

            pl.when(there)(add)
            self.send(way, step, there)

    def finish(self, add):
        for way in (1, -1):

            def last(way=way):
                self.take(way, LINE - 1)
                add()

            pl.when(self.takes(way, LINE - 1))(last)


class QuarterScatter:
    def __init__(self, copies, place, grad, owner, columns, arrived, stage, sem, line=LineScatter):
        self.copies, self.place, self.grad, self.owner, self.sem = copies, place, grad, owner, sem
        self.stage = stage
        self.count, self.whole_width = owner.shape[0], owner.shape[1] // 4
        self.start_column, self.width = columns
        self.line = line(copies, place, self.block, arrived, stage, sem)
        self.near = (
            (copies.new(), 1 - place.p, place.c, place.pair),
            (copies.new(), place.p, 1 - place.c, place.core),
            (copies.new(), 1 - place.p, 1 - place.c, place.cross),
        )

    def block(self, origin):
        count = 4 * self.count
        return self.grad.at[pl.ds(pl.multiple_of(origin * count, count), count)]

    def rows(self, p, c):
        count = self.count
        start = (self.place.z * 4 + p * 2 + c) * count
        return self.grad.at[pl.ds(pl.multiple_of(start, count), count)]

    def columns(self, p, c):
        start = (p * 2 + c) * self.whole_width + self.start_column
        return self.owner.at[:, pl.ds(pl.multiple_of(start, LANES), self.width)]

    def finish(self):
        place = self.place
        self.line.finish(lambda: add_to(self.block(place.z), self.stage))
        for which, p, c, to in self.near:
            self.copies.send(which, self.rows(p, c), self.columns(place.p, place.c), to)
        fetch(self.rows(place.p, place.c), self.columns(place.p, place.c), self.sem)

    def end(self):
        for which, p, c, to in self.near:
            self.copies.receive(which, self.columns(p, c), to)


class ShortScatter:
    def __init__(self, copies, place, block, arrived, stage, sem):
        self.copies, self.place, self.block = copies, place, block
        self.arrived, self.stage, self.sem = arrived, stage, sem
        self.ids = {way: {name: copies.new() for name in "abcdef"} for way in (1, -1)}

    def at(self, way, k):
        return self.place.z == (k if way == 1 else LINE - 1 - k)

    def there(self, way, k):
        return k if way == 1 else LINE - 1 - k

    def landing(self, way, name):
        return self.arrived.at[(1 - way) // 2, 0 if name in "abc" else 1]

    def send(self, way, name, head, k, to):
        self.copies.send(
            self.ids[way][name],
            self.block(self.there(way, k)),
            self.landing(way, name),
            {RING: self.there(way, to)},
            self.at(way, head),
        )

    def take(self, way, name, source):
        landing = self.landing(way, name)
        self.copies.receive(self.ids[way][name], landing, {RING: self.there(way, source)})
        fetch(landing, self.stage, self.sem)

    def start(self, ways=(1, -1), names="abcd"):
        for name, head, k, to in (("a", 0, 2, 1), ("b", 1, 3, 2), ("c", 0, 3, 3), ("d", 0, 1, 1)):
            for way in ways:
                if name in names:
                    self.send(way, name, head, k, to)

    def step(self, ways=(1, -1)):
        for way in ways:
            for k, name, onward in ((1, "a", "e"), (2, "b", "f")):

                def add(way=way, k=k, name=name):
                    self.take(way, name, k - 1)
                    add_to(self.block(self.there(way, k + 1)), self.stage)

                pl.when(self.at(way, k))(add)
                self.send(way, onward, k, k + 1, k + 1)

    def finish(self, add):
        for way in (1, -1):
            for k, name, source in ((1, "d", 0), (2, "e", 1), (3, "c", 0), (3, "f", 2)):

                def last(way=way, name=name, source=source):
                    self.take(way, name, source)
                    add()

                pl.when(self.at(way, k))(last)


class DirectScatter:
    def __init__(self, copies, place, block, arrived, stage, sem):
        self.copies, self.place, self.block = copies, place, block
        self.arrived, self.stage, self.sem = arrived, stage, sem
        self.ids = {(way, far): copies.new() for way in (1, -1) for far in range(1, LINE)}

    def landing(self, way, far):
        return self.arrived.at[(1 - way) // 2, far - 1]

    def reaches(self, way, far):
        return self.place.z + far < LINE if way == 1 else self.place.z >= far

    def start(self):
        for far in range(LINE - 1, 0, -1):
            for way in (1, -1):
                there = self.place.z + way * far
                self.copies.send(
                    self.ids[way, far],
                    self.block(there),
                    self.landing(way, far),
                    {RING: there},
                    self.reaches(way, far),
                )

    def finish(self, add):
        for way in (1, -1):
            for far in range(1, LINE):

                def take(way=way, far=far):
                    via = {RING: self.place.z - way * far}
                    self.copies.receive(self.ids[way, far], self.landing(way, far), via)
                    fetch(self.landing(way, far), self.stage, self.sem)
                    add()

                pl.when(self.reaches(-way, far))(take)


class RowsScatter:
    def __init__(self, copies, place, whole, from_core, from_pair, arrived, stage, sem):
        self.copies, self.place, self.whole, self.sem = copies, place, whole, sem
        self.from_core, self.from_pair = from_core, from_pair
        self.count, self.columns = from_pair.shape[1], from_pair.shape[2]
        self.stage = stage
        self.core_id = copies.new()
        self.pair_ids = [copies.new() for _ in range(LINE)]
        self.line = DirectScatter(
            copies, place, lambda d: self.part(place.c, place.p, d), arrived, self.small(1), sem
        )

    def small(self, blocks):
        return self.stage.at[pl.ds(0, blocks * self.count), pl.ds(0, self.columns)]

    def part(self, c, p, origin, blocks=1):
        start = ((c * 2 + p) * LINE + origin) * self.count
        return self.whole.at[
            pl.ds(pl.multiple_of(start, self.count), blocks * self.count), pl.ds(0, self.columns)
        ]

    def fill(self, origin, value):
        for p in range(2):
            for c in range(2):
                start = (p * 2 + c) * self.count
                self.part(c, p, origin)[...] = value[start : start + self.count]

    def start(self):
        place = self.place
        self.copies.send(
            self.core_id, self.part(1 - place.c, 0, 0, 2 * LINE), self.from_core, place.core
        )

    def halve(self):
        place = self.place
        self.copies.receive(self.core_id, self.from_core, place.core)
        size = LINE * self.count
        for p in (1 - place.p, place.p):
            start = pl.multiple_of(p * size, size)
            fetch(self.from_core.at[pl.ds(start, size)], self.small(LINE), self.sem)
            add_to(self.part(place.c, p, 0, LINE), self.small(LINE))
            if p is place.p:
                continue
            for origin in (3, 0, 2, 1):
                self.copies.send(
                    self.pair_ids[origin],
                    self.part(place.c, p, origin),
                    self.from_pair.at[origin],
                    place.pair,
                )

    def quarter(self):
        place = self.place
        for origin in (3, 0, 2, 1):
            self.copies.receive(self.pair_ids[origin], self.from_pair.at[origin], place.pair)
            fetch(self.from_pair.at[origin], self.small(1), self.sem)
            add_to(self.part(place.c, place.p, origin), self.small(1))

    def finish(self, *outs):
        start = 0
        columns = []
        for out in outs:
            columns.append((out, slice(start, start + out.shape[1])))
            start += out.shape[1]
        for out, at in columns:
            out[...] = wide(self.part(self.place.c, self.place.p, self.place.z)[:, at])

        def add():
            for out, at in columns:
                out[...] += wide(self.small(1)[:, at])

        self.line.finish(add)


PARTS = 4
NORMED_TILE = 768
BEFORE, NOW = 1, 5
N_REMOTE = 360
SUM_ROWS = 32


def clear_last(*wholes_and_shard):
    *wholes, shard = wholes_and_shard
    quarter = wholes[0].shape[1]
    last = shard.shape[1] - 3 * quarter
    if last < quarter:
        for whole in wholes:
            whole[:, last:] = jnp.zeros((whole.shape[0], quarter - last), whole.dtype)


def eight_rows(value):
    return jnp.sum(value.reshape(-1, 8, value.shape[-1]), axis=0)


def layer_kernel(
    heads,
    head_size,
    tokens,
    first_shard,
    out_shard,
    gate_shard,
    up_shard,
    down_shard,
    grad_out,
    query_bias,
    key_bias,
    value_bias,
    frequency,
    marks,
    output,
    input_grad,
    grad_query_weight,
    grad_key_weight,
    grad_value_weight,
    grad_w_out,
    grad_w_down,
    grad_w_gate,
    grad_w_up,
    query_bias_sum,
    key_bias_sum,
    value_bias_sum,
    first_gain_out,
    second_gain_out,
    first_kept,
    normed_kept,
    line_landing,
    out_core_landing,
    out_pair_landing,
    out_other_landing,
    first_core_landing,
    first_pair_landing,
    first_line_landing,
    wo_core_landing,
    wo_pair_landing,
    wo_line_landing,
    first_all,
    w_out_all,
    state,
    window,
    keys,
    values,
    mail,
    query,
    heads_out,
    gate_all,
    up_all,
    down_all,
    normed_four,
    grad_four,
    hidden,
    grad_gate,
    grad_up,
    early_up,
    early_gate,
    pair_landing,
    other_landing,
    stage,
    grad_keys,
    grad_values,
    own_grad,
    window_landing,
    core_window,
    own_marks,
    cosine,
    sine,
    scales,
    totals,
    sums,
    sums_landing,
    line_sums,
    send_sems,
    recv_sems,
    local_sems,
):
    place = Place()
    copies = Copies(send_sems, recv_sems)
    rows, width = tokens.shape
    batches = marks.shape[0] // 4
    per_batch = rows // batches
    query_width = heads * head_size
    kv_width = query_width + 2 * head_size
    size = rows // PARTS
    root = 1.0 / math.sqrt(head_size)
    sem = local_sems.at[0]

    window[...] = jnp.zeros_like(window)
    clear_last(gate_all, up_all, down_all, gate_shard)
    place.meet()

    first = RowsFlow(copies, place, first_shard, first_all)
    outs = RowsFlow(copies, place, out_shard, w_out_all)
    quarter = gate_all.shape[1]
    first_half = -(-quarter // (2 * LANES)) * LANES
    halves = ((0, first_half), (first_half, quarter - first_half))

    def part_of(whole, half):
        return whole.at[:, pl.ds(*halves[half])]

    gates, ups, downs = [
        [
            QuarterFlow(
                copies, place, shard, part_of(whole, half), halves[half], local_sems.at[2 + i * 2 + half]
            )
            for half in range(2)
        ]
        for i, (shard, whole) in enumerate(
            ((gate_shard, gate_all), (up_shard, up_all), (down_shard, down_all))
        )
    ]
    cot = FourFlow(copies, place, grad_four, PARTS)
    second = FourFlow(copies, place, normed_four, PARTS)
    part_ids = [copies.new() for _ in range(PARTS)]
    window_ids = [copies.new() for _ in range(4)]
    window_core_ids = [copies.new() for _ in range(4)]

    def put(flow, sem):
        return lambda: fetch(flow.shard, flow.rows(place.z, place.p, place.c), sem)

    first.start(put(first, sem))
    gates[0].start()
    x = wide(tokens[...])
    scales[:, 0:1] = lax.rsqrt(jnp.mean(x * x, axis=-1, keepdims=True) + EPSILON)
    state[...] = x * scales[:, 0:1]
    outs.line.start(out_shard)
    own_marks[...] = marks[:, marks.shape[1] - own_marks.shape[0] :].T
    own_start = BACK * per_batch - (marks.shape[1] - own_marks.shape[0])
    every_key = (BACK + 1) * per_batch
    for b in range(batches):
        places = own_marks[own_start : own_start + per_batch, batches + b : batches + b + 1]
        angles = places * frequency[...]
        cosine[b * per_batch : (b + 1) * per_batch] = jnp.cos(angles)
        sine[b * per_batch : (b + 1) * per_batch] = jnp.sin(angles)
    first.crossing(0)
    first.arrive(1)
    outs.line.arrive(1)
    first.arrive(2)
    outs.line.arrive(2)
    first.arrive(3)
    ups[0].start()
    outs.line.arrive(3)
    gates[0].join()
    put(outs, sem)()
    for step in range(1, LINE):
        first.crossing(step)
    first.end()

    gains = wide(first_all[:, kv_width:]).T
    first_gain, second_gain = gains[0:1], gains[1:2]
    first_normed = mail.at[pl.ds(0, rows)]
    first_normed[...] = low(state[...] * first_gain)
    sign = jnp.where(
        lax.broadcasted_iota(jnp.int32, (1, head_size), 1) < head_size // 2, -1.0, 1.0
    )

    def project(start, size):
        return matmul(first_normed[...], first_all[:, start : start + size])

    def turned(raw):
        half_turn = pltpu.roll(raw, head_size // 2, 1)
        return low(raw * cosine[...] + half_turn * (sine[...] * sign))

    def turned_back(gradient, mine):
        half_turn = pltpu.roll(gradient * sine[mine], head_size // 2, 1)
        return low(gradient * cosine[mine] - half_turn * sign)

    kv = project(query_width, 2 * head_size)
    key_now = turned(kv[:, :head_size] + wide(key_bias[...]))
    value_now = low(kv[:, head_size:] + wide(value_bias[...]))
    for b in range(batches):
        mine = slice(b * per_batch, (b + 1) * per_batch)
        window[NOW + place.q, b, :, :head_size] = key_now[mine]
        window[NOW + place.q, b, :, head_size:] = value_now[mine]
    mine_now = window.at[NOW + place.q]
    copies.send(window_ids[0], mine_now, mine_now, place.pair)
    copies.send(window_core_ids[0], mine_now, mine_now, place.core)
    before = window.at[BEFORE + place.q]
    copies.send(window_ids[1], mine_now, before, place.right, place.has_right)
    copies.send(window_ids[2], mine_now, before, place.right_cross, place.has_right)
    copies.send(window_ids[3], mine_now, window.at[0], place.far_right, place.has_far_right)
    for h in range(0, heads, 2):
        raw = project(h * head_size, 2 * head_size)
        for i in range(2):
            part = raw[:, i * head_size : (i + 1) * head_size] + wide(query_bias[h + i : h + i + 1])
            query[:, (h + i) * head_size : (h + i + 1) * head_size] = turned(part)
    keep_first = pltpu.make_async_copy(first_all, first_kept, local_sems.at[1])
    keep_first.start()
    for item in outs.items:
        outs.spread(*item)
    downs[0].start()
    ups[0].join()
    gates[0].arrive(1)
    copies.receive(window_ids[0], window.at[NOW + place.q_pair], place.pair)
    copies.send(
        window_core_ids[1],
        window.at[NOW + place.q_pair],
        window.at[NOW + place.q_pair],
        place.core,
    )

    def take_before():
        copies.receive(window_ids[1], window.at[BEFORE + place.q], place.left)
        copies.receive(window_ids[2], window.at[BEFORE + place.q_pair], place.left_cross)

    pl.when(place.has_left)(take_before)
    for i, at in ((2, BEFORE + place.q), (3, BEFORE + place.q_pair)):
        copies.send(window_core_ids[i], window.at[at], window.at[at], place.core, place.has_left)
    only(
        place.has_far_left,
        lambda: copies.receive(window_ids[3], window.at[0], place.far_left),
    )
    copies.receive(window_core_ids[0], window.at[NOW + place.q_core], place.core)
    copies.receive(window_core_ids[1], window.at[NOW + place.q_cross], place.core)

    def take_before_core():
        copies.receive(window_core_ids[2], window.at[BEFORE + place.q_core], place.core)
        copies.receive(window_core_ids[3], window.at[BEFORE + place.q_cross], place.core)

    pl.when(place.has_left)(take_before_core)
    cot_own = pltpu.make_async_copy(grad_out, grad_four.at[pl.ds(0, rows)], local_sems.at[8])
    cot_own.start()
    for i in range(PARTS):
        cot.send(i, grad_out.at[pl.ds(i * size, size)])


    def take_window(b):
        for slot in range(BACK + 1):
            at, there = place.q + slot, slice(slot * per_batch, (slot + 1) * per_batch)
            keys[there] = window[at, b, :, :head_size]
            values[there] = window[at, b, :, head_size:]

    def probabilities(b, mine, columns):
        scores = times_transpose(query[mine, columns], keys[...]) * root
        at = batches + b
        own = own_marks[own_start : own_start + per_batch]
        same = own[:, b : b + 1] == marks[b : b + 1, :every_key]
        allowed = same & (marks[at : at + 1, :every_key] <= own[:, at : at + 1])
        scores = jnp.where(allowed, scores, NEGATIVE)
        weights = jnp.exp(scores - jnp.max(scores, axis=-1, keepdims=True))
        return weights * (1.0 / jnp.sum(weights, axis=-1, keepdims=True))

    part_own, part_other = mail.at[pl.ds(0, rows)], mail.at[pl.ds(rows, rows)]
    for b in range(batches):
        take_window(b)
        mine = slice(b * per_batch, (b + 1) * per_batch)

        def attend_head(h, carry, b=b, mine=mine):
            columns = pl.ds(pl.multiple_of(h * head_size, head_size), head_size)
            probs = low(probabilities(b, mine, columns))
            heads_out[mine, columns] = low(matmul(probs, values[...]))
            return carry

        lax.fori_loop(0, heads, attend_head, 0)
        if b == 0:
            for step in range(LINE):
                outs.crossing(step)
            outs.end()
            ups[0].arrive(1)
        part = low(times_transpose(heads_out[mine], w_out_all[...]))
        part_own[mine] = part
        for i in range(b * per_batch // size, (b + 1) * per_batch // size):
            block = pl.ds(i * size, size)
            copies.send(part_ids[i], part_own.at[block], part_other.at[block], place.other)
    early = copies.mark()

    for i in range(PARTS):
        block = pl.ds(i * size, size)
        copies.receive(part_ids[i], part_other.at[block], place.other)
        copies.left(part_ids[i])
        row_sum = wide(tokens[block]) + (wide(part_own[block]) + wide(part_other[block]))
        state[block] = row_sum
        scale_row = lax.rsqrt(jnp.mean(row_sum * row_sum, axis=-1, keepdims=True) + EPSILON)
        scales[block, 1:2] = scale_row
        second.slot(0, i)[...] = low(row_sum * scale_row * second_gain)
        second.send(i, second.slot(0, i))
        if i == 0:
            gates[0].arrive(2)
            downs[0].join()
        if i == PARTS // 2:
            ups[0].arrive(2)
    downs[0].arrive(1)
    for flow in (gates[1], ups[1], downs[1]):
        flow.start()
    for part in range(PARTS):
        cot.cross(part)
        cot.end(part)
    for part in range(PARTS):
        second.cross(part)
    downs[0].arrive(2)
    keep_first.wait()
    for i in range(PARTS):
        second.end(i)
    gates[0].arrive(3)
    ups[0].arrive(3)

    tile = 256

    def forward_half(half):
        columns = pl.ds(*halves[half])

        def forward_tile(t, carry):
            block = pl.ds(pl.multiple_of(t * tile, tile), tile)
            gate = matmul(normed_four[block], gate_all[:, columns])
            up = matmul(normed_four[block], up_all[:, columns])
            sigmoid = 1.0 / (1.0 + jnp.exp(-gate))
            silu = gate * sigmoid
            hidden[block, columns] = low(silu * up)
            grad_up[block, columns] = low(silu)
            grad_gate[block, columns] = low(up * sigmoid * (1.0 + gate * (1.0 - sigmoid)))
            return carry

        lax.fori_loop(0, 4 * rows // tile, forward_tile, 0)

    def backward_half(half):
        columns = pl.ds(*halves[half])

        def backward_tile(t, carry):
            block = pl.ds(pl.multiple_of(t * tile, tile), tile)
            back = matmul(grad_four[block], down_all[:, columns])
            grad_gate[block, columns] = low(back * wide(grad_gate[block, columns]))
            grad_up[block, columns] = low(back * wide(grad_up[block, columns]))
            return carry

        lax.fori_loop(0, 4 * rows // tile, backward_tile, 0)

    def columns_of(d):
        return pl.ds(pl.multiple_of(d * rows, rows), rows)

    def weight_grad(target, left_side, right_side, half):
        columns = pl.ds(*halves[half])

        def block(d, carry):
            part = contract_rows(left_side[:, columns_of(d)], right_side[:, columns])
            target[columns_of(d)] = low(part)
            return carry

        lax.fori_loop(0, LINE, block, 0)

    grad_down = first_all
    down_backs, up_backs, gate_backs = [
        [
            QuarterScatter(
                copies,
                place,
                grads[half],
                owner,
                halves[half],
                line_landing.at[i * 2 + half, :, :, :, pl.ds(0, halves[half][1])],
                stage.at[:, pl.ds(0, halves[half][1])],
                sem,
                (LineScatter, ShortScatter)[half],
            )
            for half in range(2)
        ]
        for i, (grads, owner) in enumerate(
            (
                ([part_of(grad_down, 0), part_of(grad_down, 1)], grad_w_down),
                ([early_up, part_of(up_all, 1)], grad_w_up),
                ([early_gate, part_of(gate_all, 1)], grad_w_gate),
            )
        )
    ]

    forward_half(0)
    copies.settle(early)
    cot_own.wait()
    for flow in (gates[1], ups[1], downs[1]):
        flow.join()
    weight_grad(down_backs[0].grad, grad_four, hidden, 0)
    down_backs[0].line.start()
    downs[0].arrive(3)
    backward_half(0)
    weight_grad(up_backs[0].grad, normed_four, grad_up, 0)
    up_backs[0].line.start()
    weight_grad(gate_backs[0].grad, normed_four, grad_gate, 0)
    gate_backs[0].line.start()
    for flow in (gates[1], ups[1], downs[1]):
        flow.arrive(1)

    first_columns, later_columns = pl.ds(*halves[0]), pl.ds(*halves[1])
    step = halves[1][1]
    spares = (hidden, grad_gate, grad_up)[: width // step]
    for i, spare in enumerate(spares):

        def first_normed_tile(t, carry, i=i, spare=spare):
            block = columns_of(t)
            spare[block, later_columns] = low(
                times_transpose(grad_gate[block, first_columns], gate_all[i * step : (i + 1) * step, first_columns])
                + times_transpose(grad_up[block, first_columns], up_all[i * step : (i + 1) * step, first_columns])
            )
            return carry

        lax.fori_loop(0, 4, first_normed_tile, 0)
    keeps = [
        pltpu.make_async_copy(
            spare.at[:, later_columns],
            normed_kept.at[:, pl.ds(i * step, step)],
            local_sems.at[10 + i],
        )
        for i, spare in enumerate(spares)
    ]
    for keep in keeps:
        keep.start()
    down_backs[0].line.step(2)
    for flow in (gates[1], ups[1], downs[1]):
        flow.arrive(2)
    down_backs[0].line.step(3)
    for keep in keeps:
        keep.wait()
    gates[1].arrive(3)
    ups[1].arrive(3)

    forward_half(1)
    weight_grad(down_backs[1].grad, grad_four, hidden, 1)
    down_backs[1].line.start()
    up_backs[0].line.step(2)
    downs[1].arrive(3)
    backward_half(1)
    for flow in (cot, second):
        for ids in flow.ids:
            copies.settle_of(ids)
    for flow in (gates[1], ups[1]):
        copies.settle_of(flow.line.ids.values())

    normed_grad = grad_four
    core_ids = [copies.new() for _ in range(2)]
    pair_ids = [copies.new() for _ in range(PARTS)]
    other_ids = [copies.new() for _ in range(PARTS)]

    def slot(which, part=0, parts=1):
        return pl.ds(which * rows + part * (rows // parts), rows // parts)

    order = (3, 1, 2, 0)
    backs = [
        pltpu.make_async_copy(
            normed_kept.at[slot(which)], normed_grad.at[slot(which)], local_sems.at[10 + which]
        )
        for which in range(4)
    ]
    for which in order:
        backs[which].start()

    def normed_slot(which):
        backs[which].wait()

        def column_tile(t, carry):
            columns = pl.ds(pl.multiple_of(t * NORMED_TILE, NORMED_TILE), NORMED_TILE)
            normed_grad[slot(which), columns] = low(
                wide(normed_grad[slot(which), columns])
                + times_transpose(grad_gate[slot(which), later_columns], gate_all[columns, later_columns])
                + times_transpose(grad_up[slot(which), later_columns], up_all[columns, later_columns])
            )
            return carry

        lax.fori_loop(0, width // NORMED_TILE, column_tile, 0)

    def send_core(i):
        copies.send(
            core_ids[i], normed_grad.at[slot(2 + i)], mail.at[pl.ds(i * rows, rows)], place.core
        )

    normed_slot(3)
    send_core(1)
    normed_slot(1)
    copies.receive(core_ids[1], mail.at[pl.ds(rows, rows)], place.core)
    for i in range(PARTS):
        block = slot(1, i, PARTS)
        add_to(normed_grad.at[block], mail.at[pl.ds(rows + i * size, size)])
        copies.send(
            pair_ids[i],
            normed_grad.at[block],
            pair_landing.at[pl.ds(i * size, size)],
            place.pair,
        )
    normed_slot(2)
    send_core(0)
    normed_slot(0)
    copies.receive(core_ids[0], mail.at[pl.ds(0, rows)], place.core)
    add_to(normed_grad.at[slot(0)], mail.at[pl.ds(0, rows)])
    weight_grad(up_backs[1].grad, normed_four, grad_up, 1)
    up_backs[1].line.start((1,))
    up_backs[1].line.start((-1,), "b")
    down_backs[0].finish()
    up_backs[0].line.step(3)
    out_sum = normed_four
    out_core_id, out_pair_id, out_other_id = copies.new(), copies.new(), copies.new()
    first_weights = hidden
    first_fetch = pltpu.make_async_copy(first_kept, first_weights, local_sems.at[9])

    def out_tile(t, carry):
        block = columns_of(t)
        out_sum[block] = low(times_transpose(hidden[block], down_all[...]))
        return carry

    for i in range(PARTS):
        block = pl.ds(i * size, size)
        copies.receive(pair_ids[i], pair_landing.at[block], place.pair)
        add_to(normed_grad.at[block], pair_landing.at[block])
        copies.send(other_ids[i], normed_grad.at[block], other_landing.at[block], place.other)
        if i == 0:
            weight_grad(gate_backs[1].grad, normed_four, grad_gate, 1)
            gate_backs[1].line.start((1,))
            gate_backs[1].line.start((-1,), "b")
        if i == 1:
            lax.fori_loop(0, 4, out_tile, 0)
            copies.send(
                out_core_id, out_sum.at[pl.ds(2 * rows, 2 * rows)], out_core_landing, place.core
            )
            first_fetch.start()
        if i == 2:
            gate_backs[0].line.step(2)
    spare = mail.at[pl.ds(rows, rows)]
    copies.receive(out_core_id, out_core_landing, place.core)
    fetch(out_core_landing.at[pl.ds(rows, rows)], spare, sem)
    add_to(out_sum.at[slot(1)], spare)
    copies.send(out_pair_id, out_sum.at[slot(1)], out_pair_landing, place.pair)
    grad_own = mail.at[pl.ds(rows, rows)]
    grad_branch = mail.at[pl.ds(0, rows)]
    fetch(grad_out, grad_own, sem)
    second_sum = totals.at[:, pl.ds(kv_width, width)]
    second_sum[...] = jnp.zeros_like(second_sum)
    for i in range(PARTS):
        block = pl.ds(i * size, size)
        copies.receive(other_ids[i], other_landing.at[block], place.other)
        back = wide(normed_grad[block]) + wide(other_landing[block])
        scale_row = scales[block, 1:2]
        unit = state[block] * scale_row
        second_sum[...] += eight_rows(back * unit)
        grad_state = wide(grad_own[block]) + norm_back(back, unit, scale_row, second_gain)
        input_grad[block] = grad_state
        grad_branch[block] = low(grad_state)

    grad_heads = grad_up.at[pl.ds(0, rows), pl.ds(0, query_width)]
    grad_raw = grad_up.at[pl.ds(rows, rows), pl.ds(0, kv_width)]
    grad_heads[...] = low(matmul(grad_branch[...], w_out_all[...]))
    back_ids = [copies.new() for _ in range(4)]
    back_core_ids = [copies.new() for _ in range(4)]
    for b in range(batches):
        take_window(b)
        mine = slice(b * per_batch, (b + 1) * per_batch)
        grad_keys[...] = jnp.zeros_like(grad_keys)
        grad_values[...] = jnp.zeros_like(grad_values)

        def attend_back_head(h, carry, b=b, mine=mine):
            columns = pl.ds(pl.multiple_of(h * head_size, head_size), head_size)
            probs = probabilities(b, mine, columns)
            grad_head = grad_heads[mine, columns]
            grad_probs = times_transpose(grad_head, values[...])
            row_inner = jnp.sum(probs * grad_probs, axis=-1, keepdims=True)
            grad_scores = low(probs * (grad_probs - row_inner))
            grad_raw[mine, columns] = turned_back(matmul(grad_scores, keys[...]) * root, mine)
            grad_keys[...] += contract_rows(grad_scores, query[mine, columns])
            grad_values[...] += contract_rows(low(probs), grad_head)
            return carry

        lax.fori_loop(0, heads, attend_back_head, 0)
        for at in range(NOW + 4):
            window[at, b] = jnp.zeros_like(window[at, b])
        for back in range(BACK + 1):
            at, there = place.q + back, slice(back * per_batch, (back + 1) * per_batch)
            window[at, b, :, :head_size] = low(grad_keys[there] * root)
            window[at, b, :, head_size:] = low(grad_values[there])
        own_grad[mine, :head_size] = grad_keys[there] * root
        own_grad[mine, head_size:] = grad_values[there]
    theirs = (NOW + place.q_core, NOW + place.q_cross, BEFORE + place.q_core, BEFORE + place.q_cross)
    ours = (NOW + place.q, NOW + place.q_pair, BEFORE + place.q, BEFORE + place.q_pair)
    for i in range(4):
        copies.send(back_core_ids[i], window.at[theirs[i]], core_window.at[i], place.core)
    copies.send(
        back_ids[3], window.at[0], window_landing.at[3], place.far_left, place.has_far_left
    )


    def add_own(landing):
        for b in range(batches):
            own_grad[b * per_batch : (b + 1) * per_batch] += wide(landing[b])

    for i in (1, 2, 3):
        copies.receive(back_core_ids[i], core_window.at[i], place.core)
        for b in range(batches):
            add_to(window.at[ours[i], b], core_window.at[i, b])
    copies.send(back_ids[0], window.at[ours[1]], window_landing.at[0], place.pair)
    copies.send(back_ids[1], window.at[ours[2]], window_landing.at[1], place.left, place.has_left)
    copies.send(
        back_ids[2], window.at[ours[3]], window_landing.at[2], place.left_cross, place.has_left
    )
    up_backs[0].finish()
    gate_backs[0].line.step(3)
    for name in "acd":
        up_backs[1].line.start((-1,), name)
        gate_backs[1].line.start((-1,), name)
    copies.receive(back_core_ids[0], core_window.at[0], place.core)
    add_own(core_window.at[0])
    wo_back = RowsScatter(
        copies, place, w_out_all, wo_core_landing, wo_pair_landing, wo_line_landing, stage, sem
    )
    for origin in range(LINE):
        branch = grad_branch[:, origin * rows : (origin + 1) * rows]
        wo_back.fill(origin, low(contract_rows(branch, heads_out[...])))
    wo_back.start()
    wo_back.halve()
    down_backs[1].line.step()
    up_backs[1].line.step((1,))
    first_at = kv_width + width
    bias_rows = kv_width // LANES
    gain_rows = first_shard.shape[0]
    shared = bias_rows + width // gain_rows

    def gain_sums(start, row):
        for r in range(width // gain_rows):
            part = totals[:, start + r * gain_rows : start + (r + 1) * gain_rows]
            sums[0, row + r : row + r + 1, :gain_rows] = jnp.sum(part, axis=0, keepdims=True)

    sums[0] = jnp.zeros_like(sums[0])
    gain_sums(kv_width, bias_rows)
    copies.receive(back_ids[0], window_landing.at[0], place.pair)
    add_own(window_landing.at[0])

    def take_after():
        copies.receive(back_ids[1], window_landing.at[1], place.right)
        add_own(window_landing.at[1])
        copies.receive(back_ids[2], window_landing.at[2], place.right_cross)
        add_own(window_landing.at[2])

    pl.when(place.has_right)(take_after)

    def take_far():
        copies.receive(back_ids[3], window_landing.at[3], place.far_right)
        add_own(window_landing.at[3])

    pl.when(place.has_far_right)(take_far)
    every = slice(0, rows)
    grad_raw[:, query_width : query_width + head_size] = turned_back(
        own_grad[:, :head_size], every
    )
    grad_raw[:, query_width + head_size :] = low(own_grad[:, head_size:])
    first_back = RowsScatter(
        copies,
        place,
        grad_gate,
        first_core_landing,
        first_pair_landing,
        first_line_landing,
        stage,
        sem,
    )
    first_normed[...] = low(wide(tokens[...]) * scales[:, 0:1] * first_gain)
    for origin in range(LINE):
        normed = first_normed[:, origin * rows : (origin + 1) * rows]
        first_back.fill(origin, low(contract_rows(normed, grad_raw[...])))
    first_back.start()

    first_ids = [copies.new() for _ in range(PARTS)]
    sum_ids = [copies.new() for _ in range(3)]
    first_own, first_other = mail.at[pl.ds(0, rows)], pair_landing
    first_fetch.wait()

    def first_tile(t, carry):
        block = pl.ds(pl.multiple_of(t * tile, tile), tile)
        part = times_transpose(grad_raw[...], first_weights[block, :kv_width])
        first_own[:, block] = low(part)
        unit = wide(tokens[:, block]) * scales[:, 0:1]
        at = pl.ds(pl.multiple_of(first_at + t * tile, tile), tile)
        totals[:, at] = eight_rows(part * unit)
        return carry

    lax.fori_loop(0, width // tile, first_tile, 0)
    totals[:, :kv_width] = eight_rows(wide(grad_raw[...]))

    def sum_row(t, carry):
        columns = pl.ds(pl.multiple_of(t * LANES, LANES), LANES)
        sums[0, pl.ds(t, 1)] = jnp.sum(totals[:, columns], axis=0, keepdims=True)
        return carry

    lax.fori_loop(0, bias_rows, sum_row, 0)
    gain_sums(first_at, shared)

    def sum_step(i, to):
        copies.send(sum_ids[i], sums.at[i], sums_landing.at[i], to)

    def sum_take(i, to):
        copies.receive(sum_ids[i], sums_landing.at[i], to)
        sums[i + 1] = sums[i]
        if i == 0:
            sums[1, shared:] += sums_landing[0, shared:]
        else:
            sums[i + 1] += sums_landing[i]

    def sum_line(way, far):
        return place.z + far < LINE if way == 1 else place.z >= far

    line_sum_ids = {(way, far): copies.new() for way in (1, -1) for far in range(1, LINE)}
    sum_step(0, place.other)
    for i in range(PARTS):
        block = pl.ds(i * size, size)
        copies.send(first_ids[i], first_own.at[block], first_other.at[block], place.other)
    first_back.halve()
    fetch(out_core_landing.at[pl.ds(0, rows)], spare, sem)
    add_to(out_sum.at[slot(0)], spare)
    copies.receive(out_pair_id, out_pair_landing, place.pair)
    fetch(out_pair_landing, spare, sem)
    add_to(out_sum.at[slot(0)], spare)
    copies.send(out_other_id, out_sum.at[slot(0)], out_other_landing, place.other)
    gate_backs[0].finish()
    up_backs[1].line.step((-1,))
    gate_backs[1].line.step((-1,))
    gate_backs[1].line.step((1,))
    wo_back.quarter()
    wo_back.line.start()
    first_back.quarter()
    first_back.line.start()
    sum_take(0, place.other)
    sum_step(1, place.pair)
    for i in range(PARTS):
        block = pl.ds(i * size, size)
        copies.receive(first_ids[i], first_other.at[block], place.other)
        unit = wide(tokens[block]) * scales[block, 0:1]
        back = wide(first_own[block]) + wide(first_other[block])
        input_grad[block] += norm_back(back, unit, scales[block, 0:1], first_gain)
    sum_take(1, place.pair)
    sum_step(2, place.core)
    sum_take(2, place.core)
    line_sums[place.z] = sums[3]
    for way in (1, -1):
        for far in range(1, LINE):
            copies.send(
                line_sum_ids[way, far],
                sums.at[3],
                line_sums.at[place.z],
                {RING: place.z + way * far},
                sum_line(way, far),
            )
    down_backs[1].finish()
    up_backs[1].finish()
    copies.receive(out_other_id, out_other_landing, place.other)
    fetch(out_other_landing, spare, sem)
    spare[...] = low(state[...] + (wide(out_sum[slot(0)]) + wide(spare[...])))
    fetch(spare, output, sem)
    gate_backs[1].finish()
    wo_back.finish(grad_w_out)
    first_back.finish(grad_query_weight, grad_key_weight, grad_value_weight)
    for way in (1, -1):
        for far in range(1, LINE):
            source = place.z - way * far

            def take_sums(way=way, far=far, source=source):
                copies.receive(line_sum_ids[way, far], line_sums.at[source], {RING: source})

            pl.when(sum_line(-way, far))(take_sums)
    total = line_sums[0]
    for origin in range(1, LINE):
        total += line_sums[origin]
    sums_landing[0] = total
    query_bias_sum[...] = sums_landing[0, :heads]
    key_bias_sum[...] = sums_landing[0, heads : heads + 1]
    value_bias_sum[...] = sums_landing[0, heads + 1 : heads + 2]
    second_gain_out[...] = sums_landing[0, pl.ds(bias_rows + place.z * 4 + place.q, 1)]
    first_gain_out[...] = sums_landing[0, pl.ds(shared + place.z * 4 + place.q, 1)]
    for scatter in down_backs + up_backs + gate_backs:
        scatter.end()
    copies.settle()


def layer_call(heads, head_size, operands):
    tokens, first_shard, out_shard, gate_shard = operands[:4]
    marks = operands[-1]
    rows, width = tokens.shape
    batches = marks.shape[0] // 4
    per_batch = rows // batches
    count, units = gate_shard.shape
    padded = -(-units // (4 * LANES)) * (4 * LANES)
    quarter = padded // 4
    first_half = -(-quarter // (2 * LANES)) * LANES
    query_width = heads * head_size
    kv_width = query_width + 2 * head_size
    low_type, wide_type = jnp.bfloat16, jnp.float32
    in_vmem, anywhere = pl.BlockSpec(memory_space=pltpu.VMEM), pl.BlockSpec(memory_space=pl.ANY)

    def shape(*dims, kind=low_type):
        return jax.ShapeDtypeStruct(dims, kind)

    def vmem(*dims, kind=low_type):
        return pltpu.VMEM(dims, kind)

    sum_rows = kv_width // LANES + 2 * (width // count)
    total_columns = kv_width + 2 * width
    own_rows = marks.shape[1] - BACK * per_batch // LANES * LANES
    outs = (
        (shape(rows, width), anywhere),
        (shape(rows, width, kind=wide_type), in_vmem),
        (shape(count, query_width, kind=wide_type), in_vmem),
        (shape(count, head_size, kind=wide_type), in_vmem),
        (shape(count, head_size, kind=wide_type), in_vmem),
        (shape(count, query_width, kind=wide_type), in_vmem),
        (shape(count, padded), anywhere),
        (shape(count, padded), anywhere),
        (shape(count, padded), anywhere),
        (shape(heads, head_size, kind=wide_type), in_vmem),
        (shape(1, head_size, kind=wide_type), in_vmem),
        (shape(1, head_size, kind=wide_type), in_vmem),
        (shape(1, LANES, kind=wide_type), in_vmem),
        (shape(1, LANES, kind=wide_type), in_vmem),
    )
    kept = (
        shape(width, first_shard.shape[1]),
        shape(4 * rows, width),
        shape(6, 2, LINE - 1, 4 * count, first_half),
        shape(2 * rows, width),
        shape(rows, width),
        shape(rows, width),
        shape(2 * LINE * count, kv_width),
        shape(LINE, count, kv_width),
        shape(2, LINE - 1, count, kv_width),
        shape(2 * LINE * count, query_width),
        shape(LINE, count, query_width),
        shape(2, LINE - 1, count, query_width),
    )
    scratch = (
        vmem(width, first_shard.shape[1]),
        vmem(width, query_width),
        vmem(rows, width, kind=wide_type),
        vmem(NOW + 4, batches, per_batch, 2 * head_size),
        vmem((BACK + 1) * per_batch, head_size),
        vmem((BACK + 1) * per_batch, head_size),
        vmem(2 * rows, width),
        vmem(rows, query_width),
        vmem(rows, query_width),
        vmem(width, quarter),
        vmem(width, quarter),
        vmem(width, quarter),
        vmem(4 * rows, width),
        vmem(4 * rows, width),
        vmem(4 * rows, quarter),
        vmem(4 * rows, quarter),
        vmem(4 * rows, quarter),
        vmem(width, first_half),
        vmem(width, first_half),
        vmem(rows, width),
        vmem(rows, width),
        vmem(4 * count, max(kv_width, first_half)),
        vmem((BACK + 1) * per_batch, head_size, kind=wide_type),
        vmem((BACK + 1) * per_batch, head_size, kind=wide_type),
        vmem(rows, 2 * head_size, kind=wide_type),
        vmem(4, batches, per_batch, 2 * head_size),
        vmem(4, batches, per_batch, 2 * head_size),
        vmem(own_rows, marks.shape[0], kind=wide_type),
        vmem(rows, head_size, kind=wide_type),
        vmem(rows, head_size, kind=wide_type),
        vmem(rows, 2, kind=wide_type),
        vmem(8, total_columns, kind=wide_type),
        vmem(4, sum_rows, LANES, kind=wide_type),
        vmem(3, sum_rows, LANES, kind=wide_type),
        vmem(LINE, sum_rows, LANES, kind=wide_type),
        pltpu.SemaphoreType.DMA((N_REMOTE,)),
        pltpu.SemaphoreType.DMA((N_REMOTE,)),
        pltpu.SemaphoreType.DMA((14,)),
    )
    results = pl.pallas_call(
        functools.partial(layer_kernel, heads, head_size),
        out_shape=[out[0] for out in outs] + list(kept),
        in_specs=[in_vmem] + [anywhere] * 6 + [in_vmem] * 5,
        out_specs=[out[1] for out in outs] + [anywhere] * len(kept),
        scratch_shapes=scratch,
        compiler_params=pltpu.CompilerParams(
            collective_id=0, has_side_effects=True, vmem_limit_bytes=VMEM_BYTES
        ),
    )(*operands)
    return results[: len(outs)]


def results_kernel(*refs):
    count = len(refs) // 2
    for source, target in zip(refs[:count], refs[count:]):
        if len(target.shape) == 1:
            target[...] = source[0, : target.shape[0]]
        else:
            target[...] = source[:, : target.shape[1]].astype(target.dtype)


def results_call(as_they_are, widened, units, vectors, vector_size):
    shapes = [jax.ShapeDtypeStruct(value.shape, value.dtype) for value in as_they_are]
    shapes += [jax.ShapeDtypeStruct((value.shape[0], units), jnp.float32) for value in widened]
    shapes += [jax.ShapeDtypeStruct((vector_size,), jnp.float32) for _ in vectors]
    in_vmem = pl.BlockSpec(memory_space=pltpu.VMEM)
    return pl.pallas_call(
        results_kernel,
        out_shape=shapes,
        in_specs=[in_vmem] * len(shapes),
        out_specs=[in_vmem] * len(shapes),
        compiler_params=pltpu.CompilerParams(vmem_limit_bytes=VMEM_BYTES),
    )(*as_they_are, *widened, *vectors)


def body(
    tokens,
    norm1_gain,
    query_weight,
    query_bias,
    key_weight,
    key_bias,
    value_weight,
    value_bias,
    output_weight,
    norm2_gain,
    gate_weight,
    up_weight,
    down_weight,
    cotangent,
    segments,
    positions,
):
    batches, count_rows, width = tokens.shape
    heads, head_size = query_bias.shape
    query_width = heads * head_size
    units = gate_weight.shape[1]
    place = lax.axis_index(FSDP)
    row_start = place * count_rows
    rows = batches * count_rows

    no_gain = jnp.zeros((norm1_gain.shape[0], LANES - 2), norm1_gain.dtype)
    first_shard = jnp.concatenate(
        [query_weight, key_weight, value_weight, norm1_gain[:, None], norm2_gain[:, None], no_gain],
        axis=1,
    )
    kv_width = query_width + 2 * head_size
    padded = -(-units // (4 * LANES)) * (4 * LANES)

    def spaced(shard):
        return jnp.pad(shard, ((0, 0), (0, padded - units)))

    grad_out = cotangent.reshape(rows, width)
    inputs = wide(tokens.reshape(rows, width))
    biases = jnp.concatenate(
        [query_bias.reshape(-1), key_bias.reshape(-1), value_bias.reshape(-1)]
    )
    if lax.axis_size(RING) == LINE:
        halves = np.arange(head_size // 2, dtype=np.float64)
        frequency = (THETA ** (-2.0 * halves / head_size)).astype(np.float32)
        marks = jnp.concatenate([segments, positions]).astype(jnp.float32)
        lanes = -(-(BACK + 1) * count_rows // LANES) * LANES
        marks = jnp.pad(
            marks,
            ((0, 2 * batches), (BACK * count_rows, lanes - (BACK + 1) * count_rows)),
            constant_values=-1.0,
        )
        marks = lax.dynamic_slice_in_dim(marks, row_start, lanes, axis=1)
        (
            output,
            input_grad,
            grad_query_weight,
            grad_key_weight,
            grad_value_weight,
            grad_w_out,
            grad_w_down,
            grad_w_gate,
            grad_w_up,
            query_bias_sum,
            key_bias_sum,
            value_bias_sum,
            first_gain_sum,
            second_gain_sum,
        ) = layer_call(
            heads,
            head_size,
            (
                tokens.reshape(rows, width),
                first_shard,
                output_weight.T,
                gate_weight,
                up_weight,
                down_weight.T,
                grad_out,
                query_bias,
                key_bias,
                value_bias,
                jnp.asarray(np.concatenate([frequency, frequency])[None]),
                marks,
            ),
        )
        (
            output,
            input_grad,
            grad_query_weight,
            grad_key_weight,
            grad_value_weight,
            grad_w_out,
            query_bias_sum,
            key_bias_sum,
            value_bias_sum,
            grad_w_down,
            grad_w_gate,
            grad_w_up,
            first_total,
            second_total,
        ) = results_call(
            (
                output,
                input_grad,
                grad_query_weight,
                grad_key_weight,
                grad_value_weight,
                grad_w_out,
                query_bias_sum,
                key_bias_sum,
                value_bias_sum,
            ),
            (grad_w_down, grad_w_gate, grad_w_up),
            units,
            (first_gain_sum, second_gain_sum),
            norm1_gain.shape[0],
        )
    else:
        own_places = lax.dynamic_slice_in_dim(positions, row_start, count_rows, axis=1)
        cosine, sine_table = rotation(own_places.reshape(-1), head_size)
        allowed = [
            visible(segments[b], positions[b], row_start, count_rows) for b in range(batches)
        ]
        first_all = gather_rows(first_shard)
        w_qkv = first_all[:, :kv_width]
        first_gain = wide(first_all[:, kv_width])
        second_gain = wide(first_all[:, kv_width + 1])
        w_out = gather_rows(output_weight.T)
        w_gate = quarter_columns(spaced(gate_weight))
        w_up = quarter_columns(spaced(up_weight))
        w_down = quarter_columns(spaced(down_weight.T))
        grad_out_four = four_blocks(grad_out)
        first_unit, first_scale = root_mean_square_parts(inputs)
        first_normed = low(first_unit * first_gain)
        raw = matmul(first_normed, w_qkv) + wide(biases)
        turned = rotate(
            raw[:, : query_width + head_size].reshape(rows, heads + 1, head_size),
            cosine,
            sine_table,
        )
        turned = low(turned)
        query_rows = turned[:, :heads].reshape(batches, count_rows, heads, head_size)
        key_value = jnp.concatenate(
            [turned[:, heads], low(raw[:, query_width + head_size :])], axis=1
        )
        key_value = key_value.reshape(batches, count_rows, 2 * head_size)
        window = jnp.concatenate(
            [shifted(key_value, back) for back in range(BACK, 0, -1)] + [key_value], axis=1
        )
        key_rows, value_rows = window[..., :head_size], window[..., head_size:]
        attended = [
            attend(query_rows[b], key_rows[b], value_rows[b], allowed[b]) for b in range(batches)
        ]
        log_totals = [log_total for _, log_total in attended]
        heads_out = jnp.concatenate([mixed for mixed, _ in attended], axis=0)
        residual = inputs + tensor_total(times_transpose(heads_out, w_out))
        second_unit, second_scale = root_mean_square_parts(residual)
        second_normed = four_blocks(low(second_unit * second_gain))

        second_unit, second_scale = root_mean_square_parts(residual)
        gate_value = matmul(second_normed, w_gate)
        up_part = matmul(second_normed, w_up)
        sigmoid_gate = jax.nn.sigmoid(gate_value)
        silu_gate = gate_value * sigmoid_gate
        hidden = low(silu_gate * up_part)
        grad_hidden = matmul(grad_out_four, w_down)
        grad_gate = low(
            grad_hidden * up_part * sigmoid_gate * (1.0 + gate_value * (1.0 - sigmoid_gate))
        )
        grad_up = low(grad_hidden * silu_gate)
        second_back = four_sums(times_transpose(grad_gate, w_gate) + times_transpose(grad_up, w_up))
        grad_w_down = quarter_to_owner(low(contract_rows(grad_out_four, hidden)))
        grad_w_gate = quarter_to_owner(low(contract_rows(second_normed, grad_gate)))
        grad_w_up = quarter_to_owner(low(contract_rows(second_normed, grad_up)))
        output = low(residual + four_sums(times_transpose(hidden, w_down)))

        second_gain_sum = jnp.sum(second_back * second_unit, axis=0)
        grad_state = wide(grad_out) + norm_back(second_back, second_unit, second_scale, second_gain)
        grad_branch = low(grad_state)
        grad_w_out = scatter_rows(contract_rows(grad_branch, heads_out))
        grad_heads = low(matmul(grad_branch, w_out)).reshape(query_rows.shape)
        backs = [
            attend_back(
                grad_heads[b], query_rows[b], key_rows[b], value_rows[b], allowed[b], log_totals[b]
            )
            for b in range(batches)
        ]
        grad_query = jnp.stack([back[0] for back in backs]).reshape(rows, heads, head_size)
        grad_window = jnp.stack([jnp.concatenate([back[1], back[2]], axis=1) for back in backs])
        own_grad = grad_window[:, BACK * count_rows :]
        for back in range(1, BACK + 1):
            first_row = (BACK - back) * count_rows
            own_grad = own_grad + wide(
                shifted(low(grad_window[:, first_row : first_row + count_rows]), -back)
            )
        own_grad = own_grad.reshape(rows, 2, head_size)
        turned_back = rotate_back(
            jnp.concatenate([grad_query, own_grad[:, :1]], axis=1), cosine, sine_table
        )
        grad_raw = low(jnp.concatenate([turned_back, own_grad[:, 1:]], axis=1).reshape(rows, -1))
        grad_w_qkv = scatter_rows(contract_rows(first_normed, grad_raw))
        bias_sum = jnp.sum(wide(grad_raw), axis=0)
        first_back_part = times_transpose(grad_raw, w_qkv)
        first_back = tensor_total(first_back_part)
        first_gain_sum = jnp.sum(first_back * first_unit, axis=0)
        input_grad = grad_state + norm_back(first_back, first_unit, first_scale, first_gain)
        sums = summed_over_fsdp(jnp.concatenate([bias_sum, second_gain_sum, first_gain_sum]))
        bias_total = sums[:kv_width]
        gain_rows = norm1_gain.shape[0]
        second_total = lax.dynamic_slice_in_dim(sums, kv_width + place * gain_rows, gain_rows)
        first_total = lax.dynamic_slice_in_dim(sums, kv_width + width + place * gain_rows, gain_rows)
        grad_query_weight = grad_w_qkv[:, :query_width]
        grad_key_weight = grad_w_qkv[:, query_width : query_width + head_size]
        grad_value_weight = grad_w_qkv[:, query_width + head_size :]
        query_bias_sum = bias_total[:query_width].reshape(query_bias.shape)
        key_bias_sum = bias_total[query_width : query_width + head_size].reshape(key_bias.shape)
        value_bias_sum = bias_total[query_width + head_size :].reshape(value_bias.shape)

    return (
        output.reshape(tokens.shape),
        input_grad.reshape(tokens.shape),
        first_total,
        grad_query_weight,
        query_bias_sum,
        grad_key_weight,
        key_bias_sum,
        grad_value_weight,
        value_bias_sum,
        grad_w_out.T,
        second_total,
        grad_w_gate[:, :units],
        grad_w_up[:, :units],
        grad_w_down[:, :units].T,
    )


def solution(mesh):
    fsdp, tensor = mesh.shape["fsdp"], mesh.shape["tensor"]
    fine = Mesh(mesh.devices.reshape(fsdp // 4, 2, 2, tensor), (RING, PAIR, CORE, TENSOR))
    by_rows, by_columns, by_tensor = P(FSDP, TENSOR), P(TENSOR, FSDP), P(TENSOR, None)
    by_tokens, by_gain = P(None, FSDP, None), P(FSDP)
    placed = (
        by_tokens,
        by_gain,
        by_rows,
        by_tensor,
        by_rows,
        by_tensor,
        by_rows,
        by_tensor,
        by_columns,
        by_gain,
        by_rows,
        by_rows,
        by_columns,
        by_tokens,
        P(),
        P(),
    )
    return jax.shard_map(
        body,
        mesh=fine,
        in_specs=placed,
        out_specs=(
            by_tokens,
            by_tokens,
            by_gain,
            by_rows,
            by_tensor,
            by_rows,
            by_tensor,
            by_rows,
            by_tensor,
            by_columns,
            by_gain,
            by_rows,
            by_rows,
            by_columns,
        ),
        check_vma=False,
    )
```
